32 devices in a mesh: dp: 16 (over z, y, x), tensor: 2 (over core).
Axes of the slice: x: 2, y: 2, z: 4, core: 2. Of those that a mesh axis runs over, the one named last changes fastest.
Arguments:
- tokens: bfloat16 [4096, 2048], P('dp'), may hold values from -6 to 6
- out_grad: bfloat16 [4096, 2048], P('dp'), may hold values from -6 to 6
- segments: int32 [1, 4096], replicated, may hold values from 0 to 7, never falling along the last dimension, each value on 1 to 3072 neighbouring positions
- routes: int32 [4096, 6], P('dp'), may hold values from 0 to 15, as said below
- attn_gain: bfloat16 [2048], P('dp'), may hold values from 0.5 to 1.5
- w_query: bfloat16 [2048, 3072], P('dp', 'tensor'), may hold values from -0.125 to 0.125
- w_latent: bfloat16 [2048, 576], P('dp'), may hold values from -0.125 to 0.125
- latent_gain: bfloat16 [512], P('dp'), may hold values from 0.5 to 1.5
- w_keyval: bfloat16 [512, 4096], P('dp', 'tensor'), may hold values from -0.25 to 0.25
- w_out: bfloat16 [2048, 2048], P('tensor', 'dp'), may hold values from -2 to 2
- moe_gain: bfloat16 [2048], P('dp'), may hold values from 0.5 to 1.5
- w_router: bfloat16 [2048, 16], P('dp'), may hold values from -0.0625 to 0.0625
- shared_gate: bfloat16 [2048, 2816], P('dp', 'tensor'), may hold values from -0.125 to 0.125
- shared_up: bfloat16 [2048, 2816], P('dp', 'tensor'), may hold values from -0.125 to 0.125
- shared_down: bfloat16 [2816, 2048], P('tensor', 'dp'), may hold values from -0.109375 to 0.109375
- expert_gate: bfloat16 [16, 2048, 1408], P('dp', None, 'tensor'), may hold values from -0.125 to 0.125
- routed_up_weight: bfloat16 [16, 2048, 1408], P('dp', None, 'tensor'), may hold values from -0.125 to 0.125
- expert_down: bfloat16 [16, 1408, 2048], P('dp', 'tensor'), may hold values from -1.5 to 1.5
Outputs:
- result: bfloat16 [4096, 2048], P('dp')
- token_input_gradient: float32 [4096, 2048], P('dp')
- grad_attn_gain: float32 [2048], P('dp')
- grad_w_query: float32 [2048, 3072], P('dp', 'tensor')
- grad_w_latent: float32 [2048, 576], P('dp')
- grad_latent_gain: float32 [512], P('dp')
- grad_w_keyval: float32 [512, 4096], P('dp', 'tensor')
- grad_w_out: float32 [2048, 2048], P('tensor', 'dp')
- grad_moe_gain: float32 [2048], P('dp')
- grad_w_router: float32 [2048, 16], P('dp')
- grad_shared_gate: float32 [2048, 2816], P('dp', 'tensor')
- grad_shared_up: float32 [2048, 2816], P('dp', 'tensor')
- grad_shared_down: float32 [2816, 2048], P('tensor', 'dp')
- grad_expert_gate: float32 [16, 2048, 1408], P('dp', None, 'tensor')
- grad_expert_up: float32 [16, 2048, 1408], P('dp', None, 'tensor')
- grad_expert_down: float32 [16, 1408, 2048], P('dp', 'tensor')
The draws below stay inside these ranges and needn't reach their ends.
Inputs may be any that keep to these rules, and one draw needn't show every extreme that they name: `routes`: each row names 6 different experts. Among the rows of one index of dp (aligned blocks of 256 rows) no expert is named more than 128 times, and in every draw one expert is named exactly 128 times by the rows of every block. `segments`: along each sequence the numbers never fall; a document has at most 3072 tokens and some document has exactly that many.
All inputs are finite; a program needn't handle non-finite values.
Results may differ from the reference program's by a relative error of at most 0.025.
Values may be sent and summed in bfloat16 or wider, within the bound.
A program may use at most 320 MiB of HBM per device.

```python
import math
import jax
import jax.numpy as jnp
import numpy as np
from jax import lax

D = 2048
HEADS = 16
NOPE = 128
ROPE = 64
VDIM = 128
RANK = 512
FFE = 1408
SHARED_FF = 2816
TOPK = 6
WINDOW = 1024
TOK_DEV = 256
EXPERTS = 16
TOKENS = 4096
SEQ_LEN = 4096
SEQS = 1
SEQ_DEVS = 16
CAP = 128
DOCS = 8
DOC_MOST = 3072


def draw_routes(key, part):
    block_count = TOKENS // TOK_DEV
    slot_count = TOK_DEV * TOPK
    hot_expert = jax.random.randint(jax.random.fold_in(key, 11), (), 0, EXPERTS)
    rest_count = slot_count - CAP
    base_load = rest_count // (EXPERTS - 1)
    extra_load = rest_count % (EXPERTS - 1)
    positions = jnp.arange(slot_count, dtype=jnp.int32)
    offsets = jax.random.randint(jax.random.fold_in(key, 12), (block_count, 1), 0, EXPERTS - 1)
    shifted = positions - CAP
    rank_big = shifted // (base_load + 1)
    rank_small = extra_load + (shifted - extra_load * (base_load + 1)) // max(base_load, 1)
    rank_all = jnp.where(shifted < extra_load * (base_load + 1), rank_big, rank_small)
    others = (hot_expert + 1 + (rank_all[None, :] + offsets) % (EXPERTS - 1)) % EXPERTS
    labels = jnp.where(positions[None, :] < CAP, hot_expert, others)
    table = jnp.transpose(labels.reshape(block_count, TOPK, TOK_DEV), (0, 2, 1))
    block_keys = jax.random.split(jax.random.fold_in(key, 13), block_count)
    row_perms = jax.vmap(lambda one_key: jax.random.permutation(one_key, TOK_DEV))(block_keys)
    shuffled = jnp.take_along_axis(table, row_perms[:, :, None], axis=1)
    return shuffled.reshape(TOKENS, TOPK).astype(jnp.int32)


def shard_levels(stream_key, dims, cuts, low, top_value):
    loudness = 1.0
    for dim, parts in cuts:
        draws = jax.random.uniform(jax.random.fold_in(jax.random.fold_in(stream_key, 6), dim), (parts,), jnp.float32, low / len(cuts), top_value / len(cuts))
        loudness = loudness * jnp.repeat(jnp.exp(draws), dims[dim] // parts).reshape((-1,) + (1,) * (len(dims) - 1 - dim))
    return loudness


def length_profile(count, total, most, lean):
    loads = [(1 << 20) // math.isqrt(grade ** lean) + 1 for grade in range(2, count + 1)]
    spare, holding = total - most - (count - 1), [1] * (count - 1)
    while spare > 0:
        free = [i for i in range(count - 1) if holding[i] < most]
        pool, budget = sum([loads[i] for i in free]), spare
        for i in free:
            more = min(most - holding[i], max(1, budget * loads[i] // pool), spare)
            holding[i] = holding[i] + more
            spare = spare - more
    return np.array([most] + holding)


def ragged(key, count, total, bound, lean):
    if count == 2:
        one = jax.random.randint(key, (), max(1, total - bound), min(bound, total - 1) + 1)
        return jnp.stack([one, total - one])
    tallies = jnp.asarray(length_profile(count, total, bound, lean), jnp.int32)
    twos = (count - 1) // 2
    giver, receiver = tallies[1:1 + 2 * twos:2], tallies[2:2 + 2 * twos:2]
    room = jnp.minimum(giver - 1, bound - receiver)
    moved = jax.random.randint(jax.random.fold_in(key, 1), (twos,), 0, 1 << 20) % (room + 1)
    tallies = tallies.at[1:1 + 2 * twos:2].set(giver - moved).at[2:2 + 2 * twos:2].set(receiver + moved)
    return tallies[jax.random.permutation(jax.random.fold_in(key, 2), count)]


def gaussian(own_key, extent, width, bound, cuts=(), kind=jnp.bfloat16):
    array = jax.random.normal(own_key, extent, jnp.float32) * width
    if len(cuts) > 0:
        array = shard_levels(own_key, extent, cuts, -0.22, 0.18) * array
    return jnp.clip(array, min=-bound, max=bound).astype(kind)


def setup_inputs(seed: int = 0) -> dict:
    seeds = jax.random.split(jax.random.key(seed), 19)
    tokens = gaussian(seeds[0], (TOKENS, D), 1.0, 6.0, ((0, 16),))
    out_grad = gaussian(seeds[1], (TOKENS, D), 1.0, 6.0, ((0, 16),))
    segments = jax.vmap(lambda own: jnp.searchsorted(jnp.cumsum(ragged(own, DOCS, SEQ_LEN, DOC_MOST, 1)), jnp.arange(SEQ_LEN), side="right"))(jax.random.split(seeds[2], SEQS)).reshape((SEQS, SEQ_LEN)).astype(jnp.int32)
    routes = draw_routes(jax.random.fold_in(seeds[18], 71), 0)
    attn_gain = jnp.clip(1.0 + 0.1 * jax.random.normal(seeds[4], (D,), jnp.float32), 0.5, 1.5).astype(jnp.bfloat16)
    w_query = gaussian(seeds[5], (D, HEADS * (NOPE + ROPE)), D ** -0.5, 0.125, ((0, 16), (1, 2)))
    w_latent = gaussian(seeds[6], (D, RANK + ROPE), D ** -0.5, 0.125, ((0, 16),))
    latent_gain = jnp.clip(1.0 + 0.1 * jax.random.normal(seeds[7], (RANK,), jnp.float32), 0.5, 1.5).astype(jnp.bfloat16)
    w_keyval = gaussian(seeds[8], (RANK, HEADS * (NOPE + VDIM)), RANK ** -0.5, 0.25, ((0, 16), (1, 2)))
    w_out = gaussian(seeds[9], (HEADS * VDIM, D), (max(HEADS * VDIM // 256, 1)) ** -0.5, 2.0, ((0, 2), (1, 16)))
    moe_gain = jnp.clip(1.0 + 0.1 * jax.random.normal(seeds[10], (D,), jnp.float32), 0.5, 1.5).astype(jnp.bfloat16)
    w_router = gaussian(seeds[11], (D, EXPERTS), (4 * D) ** -0.5, 0.0625, ((0, 16),))
    shared_gate = gaussian(seeds[12], (D, SHARED_FF), D ** -0.5, 0.125, ((0, 16), (1, 2)))
    shared_up = gaussian(seeds[13], (D, SHARED_FF), D ** -0.5, 0.125, ((0, 16), (1, 2)))
    shared_down = gaussian(seeds[14], (SHARED_FF, D), SHARED_FF ** -0.5, 0.109375, ((0, 2), (1, 16)))
    expert_gate = gaussian(seeds[15], (EXPERTS, D, FFE), D ** -0.5, 0.125, ((0, 16), (2, 2)))
    routed_up_weight = gaussian(seeds[16], (EXPERTS, D, FFE), D ** -0.5, 0.125, ((0, 16), (2, 2)))
    expert_down = gaussian(seeds[17], (EXPERTS, FFE, D), (max(3 * FFE // (EXPERTS * EXPERTS), 1)) ** -0.5, 1.5, ((0, 16), (1, 2)))
    return {"tokens": tokens, "out_grad": out_grad, "segments": segments, "routes": routes, "attn_gain": attn_gain, "w_query": w_query, "w_latent": w_latent, "latent_gain": latent_gain, "w_keyval": w_keyval, "w_out": w_out, "moe_gain": moe_gain, "w_router": w_router, "shared_gate": shared_gate, "shared_up": shared_up, "shared_down": shared_down, "expert_gate": expert_gate, "routed_up_weight": routed_up_weight, "expert_down": expert_down}


eps_norm = 1e-06
highest = lax.Precision.HIGHEST

@jax.custom_vjp
def low(v):
    return lax.optimization_barrier(v.astype(jnp.bfloat16)).astype(jnp.float32)

@jax.custom_vjp
def low_back(v):
    return v

def low_keep(v):
    return (low(v), None)

def low_pass(kept, grad):
    return (grad,)

def back_keep(v):
    return (v, None)

def back_low(kept, grad):
    return (low(grad),)
low.defvjp(low_keep, low_pass)
low_back.defvjp(back_keep, back_low)

def matmul(left_mat, right_mat):
    return jnp.dot(left_mat, right_mat, precision=highest, preferred_element_type=jnp.float32)

def rms_scale(values, gain_vec):
    inv_root = lax.rsqrt(lax.optimization_barrier(jnp.mean(values * values, axis=-1, keepdims=True)) + eps_norm)
    return values * inv_root * gain_vec

def rope_tables(positions):
    half_width = ROPE // 2
    frequency = jnp.exp(-jnp.arange(half_width, dtype=jnp.float32) * (2.0 * math.log(10000.0) / ROPE))
    angles = positions[:, None] * frequency[None, :]
    return (jnp.cos(angles), jnp.sin(angles))

def rotate(values, cos_tab, sin_tab):
    half_width = values.shape[-1] // 2
    first_half = values[..., :half_width]
    second = values[..., half_width:]
    return jnp.concatenate([first_half * cos_tab - second * sin_tab, second * cos_tab + first_half * sin_tab], axis=-1)

def attention(queries, key_nope, values, key_rope, seg_row):
    length = queries.shape[0]
    block_rows = min(512, length)
    margin = ((WINDOW - 1) // block_rows + 1) * block_rows
    score_scale = (NOPE + ROPE) ** (-0.5)
    pad_nope = jnp.concatenate([jnp.zeros((margin,) + key_nope.shape[1:], jnp.float32), key_nope], 0)
    pad_vals = jnp.concatenate([jnp.zeros((margin,) + values.shape[1:], jnp.float32), values], 0)
    pad_rope = jnp.concatenate([jnp.zeros((margin, ROPE), jnp.float32), key_rope], 0)
    pad_seg = jnp.concatenate([jnp.full((margin,), -1, jnp.int32), seg_row.astype(jnp.int32)])

    def one_block(row_start):
        q_blk = lax.dynamic_slice_in_dim(queries, row_start, block_rows, 0)
        key_blk = lax.dynamic_slice_in_dim(pad_nope, row_start, block_rows + margin, 0)
        val_blk = lax.dynamic_slice_in_dim(pad_vals, row_start, block_rows + margin, 0)
        rope_blk = lax.dynamic_slice_in_dim(pad_rope, row_start, block_rows + margin, 0)
        raw_scores = jnp.einsum('qhd,khd->hqk', q_blk[..., :NOPE], key_blk, precision=highest)
        raw_scores = raw_scores + jnp.einsum('qhr,kr->hqk', q_blk[..., NOPE:], rope_blk, precision=highest)
        scores = low_back(score_scale * raw_scores)
        q_pos = row_start + jnp.arange(block_rows, dtype=jnp.int32)
        k_pos = row_start - margin + jnp.arange(block_rows + margin, dtype=jnp.int32)
        q_seg = lax.dynamic_slice_in_dim(seg_row.astype(jnp.int32), row_start, block_rows, 0)
        k_seg = lax.dynamic_slice_in_dim(pad_seg, row_start, block_rows + margin, 0)
        allowed = (k_pos[None, :] >= 0) & (k_pos[None, :] <= q_pos[:, None])
        allowed = allowed & (q_pos[:, None] - k_pos[None, :] < WINDOW) & (q_seg[:, None] == k_seg[None, :])
        attn_probs = jax.nn.softmax(jnp.where(allowed[None], scores, -jnp.inf), axis=-1)
        block_out = jnp.einsum('hqk,khv->qhv', low(attn_probs), val_blk, precision=highest)
        return block_out.reshape(block_rows, -1)
    starts = (jnp.arange(length // block_rows) * block_rows).astype(jnp.int32)
    block_outs = lax.map(jax.checkpoint(one_block), starts)
    return block_outs.reshape(length, -1)

def routed_mix(moe_in, gate_w, route_rows, expert_gate, routed_up_weight, expert_down):
    length = moe_in.shape[0]
    flat_routes = route_rows.reshape(-1).astype(jnp.int32)
    flat_weights = gate_w.reshape(-1)
    rows_max = min(SEQ_DEVS * CAP, length * TOPK)

    def one_expert(running, scan_items):
        w_gate, w_up, w_down, expert = scan_items
        chosen = flat_routes == expert
        slot_order = jnp.argsort(jnp.where(chosen, 0, 1).astype(jnp.int32), stable=True)[:rows_max].astype(jnp.int32)
        token_ids = (slot_order // TOPK).astype(jnp.int32)
        weight = jnp.where(chosen[slot_order], flat_weights[slot_order], 0.0)
        row_data = moe_in[token_ids]
        gate_a = low_back(matmul(row_data, w_gate))
        up_b = low_back(matmul(row_data, w_up))
        act_low = low(jax.nn.silu(gate_a) * up_b)
        expert_out = low_back(matmul(act_low, w_down))
        return (running.at[token_ids].add(weight[:, None] * expert_out), None)
    running, unused = lax.scan(jax.checkpoint(one_expert), jnp.zeros_like(moe_in), (expert_gate, routed_up_weight, expert_down, jnp.arange(EXPERTS, dtype=jnp.int32)))
    return running

def block_layer(param_set, resid_in, seg_row, route_rows):
    attn_gain, w_query, w_latent, latent_gain, w_keyval, w_out, moe_gain, w_router, shared_gate, shared_up, shared_down, expert_gate, routed_up_weight, expert_down = param_set
    length = resid_in.shape[0]
    cos_tab, sin_tab = rope_tables(jnp.arange(length, dtype=jnp.float32))
    normed = low(rms_scale(resid_in, attn_gain))
    q_raw = low_back(matmul(normed, w_query)).reshape(length, HEADS, NOPE + ROPE)
    queries = low(jnp.concatenate([q_raw[..., :NOPE], rotate(q_raw[..., NOPE:], cos_tab[:, None], sin_tab[:, None])], -1))
    latent_raw = low_back(matmul(normed, w_latent))
    latent = low(rms_scale(latent_raw[:, :RANK], latent_gain))
    key_rope = low(rotate(latent_raw[:, RANK:], cos_tab, sin_tab))
    keyval = low(low_back(matmul(latent, w_keyval))).reshape(length, HEADS, NOPE + VDIM)
    attended = low(low_back(attention(queries, keyval[..., :NOPE], keyval[..., NOPE:], key_rope, seg_row)))
    middle = resid_in + low_back(matmul(attended, w_out))
    moe_in = low(rms_scale(middle, moe_gain))
    router = jax.nn.softmax(low_back(matmul(moe_in, w_router)), axis=-1)
    gate_w = jnp.take_along_axis(router, route_rows.astype(jnp.int32), axis=1)
    shared_a = low_back(matmul(moe_in, shared_gate))
    shared_b = low_back(matmul(moe_in, shared_up))
    shared_out = matmul(low(jax.nn.silu(shared_a) * shared_b), shared_down)
    return middle + routed_mix(moe_in, gate_w, route_rows, expert_gate, routed_up_weight, expert_down) + shared_out

def reference(tokens, out_grad, segments, routes, attn_gain, w_query, w_latent, latent_gain, w_keyval, w_out, moe_gain, w_router, shared_gate, shared_up, shared_down, expert_gate, routed_up_weight, expert_down):
    param_set = tuple((weight_arr.astype(jnp.float32) for weight_arr in (attn_gain, w_query, w_latent, latent_gain, w_keyval, w_out, moe_gain, w_router, shared_gate, shared_up, shared_down, expert_gate, routed_up_weight, expert_down)))
    seq_items = (tokens.astype(jnp.float32).reshape(SEQS, SEQ_LEN, D), out_grad.astype(jnp.float32).reshape(SEQS, SEQ_LEN, D), segments.astype(jnp.int32), routes.astype(jnp.int32).reshape(SEQS, SEQ_LEN, TOPK))

    def one_sequence(totals, scan_items):
        resid_in, cotangent, seg_row, route_rows = scan_items
        layer_out, pullback = jax.vjp(lambda params_now, resid_val: block_layer(params_now, resid_val, seg_row, route_rows), param_set, resid_in)
        param_grads, input_grad = pullback(cotangent)
        return (jax.tree.map(jnp.add, totals, param_grads), (layer_out.astype(jnp.bfloat16), input_grad))
    zero_grads = jax.tree.map(jnp.zeros_like, param_set)
    totals, (layer_outs, input_grads) = lax.scan(one_sequence, zero_grads, seq_items)
    return (layer_outs.reshape(TOKENS, D), input_grads.reshape(TOKENS, D), totals[0], totals[1], totals[2], totals[3], totals[4], totals[5], totals[6], totals[7], totals[8], totals[9], totals[10], totals[11], totals[12], totals[13])
```

```python
import functools
import math

import jax
import jax.numpy as jnp
from jax import lax
from jax.experimental import pallas as pl
from jax.experimental.pallas import tpu as pltpu
from jax.sharding import PartitionSpec as P

NOPE = 128
ROPE = 64
VDIM = 128
RANK = 512
TOPK = 6
WINDOW = 1024


eps_norm = 1e-06
highest = lax.Precision.HIGHEST


def passed_along(value, axis, steps):
    count = lax.axis_size(axis)
    leading, last = (max(0, -steps), min(count, count - steps))
    return lax.ppermute(value, axis, [(source, source + steps) for source in range(leading, last)])


def rms_scale(values, gain_vec):
    inv_root = lax.rsqrt(jnp.mean(values * values, axis=-1, keepdims=True) + eps_norm)
    return values * inv_root * gain_vec


def rope_tables(positions):
    half_width = ROPE // 2
    frequency = jnp.exp(
        -jnp.arange(half_width, dtype=jnp.float32) * (2.0 * math.log(10000.0) / ROPE)
    )
    angles = positions[:, None] * frequency[None, :]
    return (jnp.cos(angles), jnp.sin(angles))


def rotate(values, cos_tab, sin_tab):
    half_width = values.shape[-1] // 2
    first_half = values[..., :half_width]
    second = values[..., half_width:]
    return jnp.concatenate(
        [first_half * cos_tab - second * sin_tab, second * cos_tab + first_half * sin_tab], axis=-1
    )


def gated_act(gate_a, up_b):
    return jax.nn.silu(gate_a) * up_b


def matmul(left_mat, right_mat):
    return jnp.dot(left_mat, right_mat, preferred_element_type=jnp.float32)


def matmul_nt(left_mat, right_mat):
    return lax.dot_general(
        left_mat, right_mat, (((1,), (1,)), ((), ())), preferred_element_type=jnp.float32
    )


def matmul_tn(left_mat, right_mat):
    return lax.dot_general(
        left_mat, right_mat, (((0,), (0,)), ((), ())), preferred_element_type=jnp.float32
    )


def ranks_before(hot):
    count = hot.shape[0]
    below = jnp.arange(count)[:, None] > jnp.arange(count)[None, :]
    return matmul(below.astype(jnp.bfloat16), hot.astype(jnp.bfloat16)).astype(jnp.int32)


MESH = pl.DeviceIdType.MESH

def z_order(z, k):
    zz = jnp.where(z >= 2, 3 - z, z)
    o = [zz, 1 - zz, 2, 3][k]
    return jnp.where(z >= 2, 3 - o, o)

def ag_kernel(share, x_ref, o_ref, zsem_s, zsem_r, asem_s, asem_r, bsem_s, bsem_r, csem_s, csem_r, lsem):
    me = lax.axis_index("dp"); core = lax.axis_index("tensor")
    z = me // 4; y = (me // 2) % 2; x = me % 2
    xn = z*4 + y*2 + (1-x); yn = z*4 + (1-y)*2 + x
    up = jnp.minimum(z+1, 3)*4 + y*2 + x; dn = jnp.maximum(z-1, 0)*4 + y*2 + x
    slot = core if share else 0
    bar = pltpu.get_barrier_semaphore()
    def sig(d, c): pl.semaphore_signal(bar, inc=1, device_id=(d, c), device_id_type=MESH)
    sig(xn, core); sig(yn, core)
    pl.when(z < 3)(lambda: sig(up, core))
    pl.when(z > 0)(lambda: sig(dn, core))
    n = 2 + (z < 3).astype(jnp.int32) + (z > 0).astype(jnp.int32)
    if share:
        sig(me, 1-core); n = n + 1
    pl.semaphore_wait(bar, n)
    own = pltpu.make_async_copy(x_ref, o_ref.at[me, slot], lsem); own.start()

    def rc(src, dst, ss, rs, dev, c=None):
        return pltpu.make_async_remote_copy(src_ref=src, dst_ref=dst, send_sem=ss, recv_sem=rs,
                                            device_id=(dev, core if c is None else c), device_id_type=MESH)
    waits = []
    def zcopy(zp, dev, ss):
        b = zp*4 + y*2 + x
        return rc(o_ref.at[b, slot], o_ref.at[b, slot], zsem_s.at[ss], zsem_r.at[zp], dev)
    def xcopy(j, b, half, zp):
        return rc(o_ref.at[b, slot, half], o_ref.at[b, slot, half], asem_s.at[zp, j], asem_r.at[zp, j], xn)
    def ycopy(j, b, half, zp):
        return rc(o_ref.at[b, slot, half], o_ref.at[b, slot, half], bsem_s.at[zp, j], bsem_r.at[zp, j], yn)
    def sib(b):
        return rc(o_ref.at[b, slot], o_ref.at[b, slot], csem_s.at[b], csem_r.at[b], me, 1-core)

    own.wait()
    for k in range(4):
        zp = z_order(z, k)
        b = zp*4 + y*2 + x
        if k > 0:
            zcopy(zp, up, 0).wait_recv()
        @pl.when((zp <= z) & (z < 3))
        def _(): zcopy(zp, up, zp).start()
        @pl.when((zp >= z) & (z > 0))
        def _(): zcopy(zp, dn, 4 + zp).start()
        xcopy(0, b, 0, zp).start()
        ycopy(0, b, 1, zp).start()
        ycopy(1, b, 0, zp).start()
        xcopy(1, b, 1, zp).start()
        if share: sib(b).start()
        bx = zp*4 + y*2 + (1-x); by = zp*4 + (1-y)*2 + x
        if k > 0: hop(*prev)
        prev = (zp, bx, by)
        def hop(zp, bx, by):
            xcopy(0, bx, 0, zp).wait_recv()
            ycopy(2, bx, 0, zp).start()
            ycopy(0, by, 1, zp).wait_recv()
            xcopy(2, by, 1, zp).start()
            xcopy(1, bx, 1, zp).wait_recv()
            ycopy(1, by, 0, zp).wait_recv()
            if share:
                sib(bx).start(); sib(by).start()
    hop(*prev)
    for k in range(4):
        zp = z_order(z, k)
        bd = zp*4 + (1-y)*2 + (1-x)
        ycopy(2, bd, 0, zp).wait_recv()
        xcopy(2, bd, 1, zp).wait_recv()
        if share: sib(bd).start()
    for k in range(4):
        @pl.when((k <= z) & (z < 3))
        def _(): zcopy(k, up, k).wait_send()
        @pl.when((k >= z) & (z > 0))
        def _(): zcopy(k, dn, 4 + k).wait_send()
        for j in range(3):
            xcopy(j, 0, 0, k).wait_send(); ycopy(j, 0, 0, k).wait_send()
    if share:
        for b in range(16):
            sib(b).wait_send()
            pltpu.make_async_remote_copy(src_ref=o_ref.at[b, slot], dst_ref=o_ref.at[b, 1-slot], send_sem=csem_s.at[b], recv_sem=csem_r.at[b], device_id=(me, 1-core), device_id_type=MESH).wait_recv()

def ag16(x, share, cid):
    S = pltpu.SemaphoreType.DMA
    cores = 2 if share else 1
    return pl.pallas_call(functools.partial(ag_kernel, share),
        out_shape=jax.ShapeDtypeStruct((16, cores) + x.shape, x.dtype),
        in_specs=[pl.BlockSpec(memory_space=pl.ANY)], out_specs=pl.BlockSpec(memory_space=pl.ANY),
        scratch_shapes=[S((8,)), S((4,)), S((4,3)), S((4,3)), S((4,3)), S((4,3)), S((16,)), S((16,)), S],
        compiler_params=pltpu.CompilerParams(collective_id=cid, has_side_effects=True),
        )(x)


def add_into(dst, src, out=None):
    out = dst if out is None else out
    h = dst.shape[0]
    def step(i, _):
        r = pl.ds(pl.multiple_of(i * 16, 16), 16)
        out[r] = (dst[r].astype(jnp.float32) + src[r].astype(jnp.float32)).astype(out.dtype)
        return 0
    lax.fori_loop(0, h // 16, step, 0)

def rs_kernel(share, p_ref, o_ref, own, sibr, yr, xr, zr, lsem, cs, cr, xs, xrs, ys, yrs, zs, zrs, fs, fr):
    me = lax.axis_index("dp"); core = lax.axis_index("tensor")
    z = me // 4; y = (me // 2) % 2; x = me % 2
    xn = z*4 + y*2 + (1-x); yn = z*4 + (1-y)*2 + x
    up = jnp.minimum(z+1, 3)*4 + y*2 + x; dn = jnp.maximum(z-1, 0)*4 + y*2 + x
    slot = core if share else 0
    other = 1 - core
    def rc(src, dst, ss, rs, dev, c=None):
        return pltpu.make_async_remote_copy(src_ref=src, dst_ref=dst, send_sem=ss, recv_sem=rs,
                                            device_id=(dev, core if c is None else c), device_id_type=MESH)
    for k in range(4):
        zp = z_order(z, 3-k)
        pltpu.make_async_copy(p_ref.at[pl.ds(zp*4, 4), slot], own.at[pl.ds(zp*4, 4)], lsem.at[zp]).start()
    bar = pltpu.get_barrier_semaphore()
    def sig(d, c): pl.semaphore_signal(bar, inc=1, device_id=(d, c), device_id_type=MESH)
    sig(xn, core); sig(yn, core)
    pl.when(z < 3)(lambda: sig(up, core))
    pl.when(z > 0)(lambda: sig(dn, core))
    n = 2 + (z < 3).astype(jnp.int32) + (z > 0).astype(jnp.int32)
    if share:
        sig(me, other); n = n + 1
    pl.semaphore_wait(bar, n)
    def sib(zp):
        return rc(p_ref.at[pl.ds(zp*4, 4), other], sibr.at[pl.ds(zp*4, 4)], cs.at[zp], cr.at[zp], me, other)
    if share:
        for k in range(4): sib(z_order(z, 3-k)).start()
    def y_(j, b, half, zp): return rc(own.at[b, half], yr.at[zp, j], ys.at[zp, j], yrs.at[zp, j], yn)
    def x_(j, b, half, zp): return rc(own.at[b, half], xr.at[zp, j], xs.at[zp, j], xrs.at[zp, j], xn)
    def zc(zp, dev, d):
        b = zp*4 + y*2 + x
        return rc(own.at[b], zr.at[d, zp], zs.at[zp], zrs.at[d, zp], dev)
    def blk(zp, yy, xx): return zp*4 + yy*2 + xx
    def s1(k):
        zp = z_order(z, 3-k)
        pltpu.make_async_copy(p_ref.at[pl.ds(zp*4, 4), slot], own.at[pl.ds(zp*4, 4)], lsem.at[zp]).wait()
        if share:
            sib(zp).wait_recv()
            def one(q, _):
                b = zp*4 + q
                add_into(own.at[b, 0], sibr.at[b, 0]); add_into(own.at[b, 1], sibr.at[b, 1])
                return 0
            lax.fori_loop(0, 4, one, 0)
        y_(0, blk(zp, 1-y, 1-x), 0, zp).start()
        x_(0, blk(zp, 1-y, 1-x), 1, zp).start()
        y_(1, blk(zp, 1-y, x), 0, zp).start()
        x_(1, blk(zp, y, 1-x), 1, zp).start()
    def s2(k):
        zp = z_order(z, 3-k)
        y_(0, blk(zp, 1-y, 1-x), 0, zp).wait_recv()
        add_into(own.at[blk(zp, y, 1-x), 0], yr.at[zp, 0])
        x_(2, blk(zp, y, 1-x), 0, zp).start()
        x_(0, blk(zp, 1-y, 1-x), 1, zp).wait_recv()
        add_into(own.at[blk(zp, 1-y, x), 1], xr.at[zp, 0])
        y_(2, blk(zp, 1-y, x), 1, zp).start()
        mine = blk(zp, y, x)
        y_(1, blk(zp, 1-y, x), 0, zp).wait_recv()
        add_into(own.at[mine, 0], yr.at[zp, 1])
        x_(1, blk(zp, y, 1-x), 1, zp).wait_recv()
        add_into(own.at[mine, 1], xr.at[zp, 1])
    def s3(k):
        zp = z_order(z, 3-k)
        mine = blk(zp, y, x)
        x_(2, blk(zp, y, 1-x), 0, zp).wait_recv()
        add_into(own.at[mine, 0], xr.at[zp, 2])
        y_(2, blk(zp, 1-y, x), 1, zp).wait_recv()
        add_into(own.at[mine, 1], yr.at[zp, 2])
        def both(d):
            add_into(own.at[mine, 0], zr.at[d, zp, 0]); add_into(own.at[mine, 1], zr.at[d, zp, 1])
        if k < 3:
            @pl.when((zp < z) & (z < 3))
            def _():
                zc(zp, up, 1).wait_recv(); both(1)
            @pl.when((zp > z) & (z > 0))
            def _():
                zc(zp, dn, 0).wait_recv(); both(0)
            @pl.when(zp < z)
            def _(): zc(zp, dn, 1).start()
            @pl.when(zp > z)
            def _(): zc(zp, up, 0).start()
        else:
            @pl.when(z < 3)
            def _():
                zc(zp, up, 1).wait_recv(); both(1)
            @pl.when(z > 0)
            def _():
                zc(zp, dn, 0).wait_recv(); both(0)
    s1(0); s1(1); s2(0); s1(2); s2(1); s3(0); s1(3); s2(2); s3(1); s2(3); s3(2); s3(3)
    if share:
        mine = me
        for a in range(2):
            add = own.at[mine, a]
            def step(i, _):
                r = pl.ds(pl.multiple_of(i*16, 16), 16)
                o_ref[core, a, r] = add[r]
                return 0
            lax.fori_loop(0, add.shape[0]//16, step, 0)
        f = rc(o_ref.at[core], o_ref.at[core], fs, fr, me, other)
        f.start()
        pltpu.make_async_remote_copy(src_ref=o_ref.at[core], dst_ref=o_ref.at[other], send_sem=fs, recv_sem=fr, device_id=(me, other), device_id_type=MESH).wait_recv()
        f.wait_send()
        for k in range(4): sib(k).wait_send()
    else:
        for a in range(2):
            add = own.at[me, a]
            def step(i, _):
                r = pl.ds(pl.multiple_of(i*16, 16), 16)
                o_ref[0, a, r] = add[r].astype(o_ref.dtype)
                return 0
            lax.fori_loop(0, add.shape[0]//16, step, 0)
    for k in range(4):
        for j in range(3):
            x_(j, 0, 0, k).wait_send(); y_(j, 0, 0, k).wait_send()
        @pl.when(k != z)
        def _(): zc(k, up, 0).wait_send()

def rs16(p, share, cid):
    S = pltpu.SemaphoreType.DMA
    cores = 2 if share else 1
    blkshape = p.shape[2:]
    half = p.shape[3:]
    V = lambda s: pltpu.VMEM(s, p.dtype)
    return pl.pallas_call(functools.partial(rs_kernel, share),
        out_shape=jax.ShapeDtypeStruct((cores,) + blkshape, p.dtype),
        in_specs=[pl.BlockSpec(memory_space=pl.ANY)], out_specs=pl.BlockSpec(memory_space=pltpu.VMEM),
        scratch_shapes=[V((16,) + blkshape), V((16,) + blkshape) if share else V((1, 2, 16, 128)), V((4, 3) + half), V((4, 3) + half), V((2, 4) + blkshape),
            S((4,)), S((4,)), S((4,)), S((4,3)), S((4,3)), S((4,3)), S((4,3)), S((4,)), S((2,4)), S, S],
        compiler_params=pltpu.CompilerParams(collective_id=cid, has_side_effects=True, vmem_limit_bytes=60 << 20),
        )(p)


def swapped(v):
    return lax.ppermute(v, "tensor", [(0, 1), (1, 0)])


def summed(v):
    low = lax.reduce_precision(v, 8, 7)
    return low + swapped(low.astype(jnp.bfloat16)).astype(jnp.float32)


def my_half(v, rows):
    return lax.dynamic_slice_in_dim(v, lax.axis_index("tensor") * rows, rows, 0)


def gather_rows(v, cid):
    rows, width = v.shape[0] // 2, v.shape[1]
    moved = ag16(my_half(v, rows).reshape(2, rows // 2, width), True, cid)
    return moved.reshape(32 * rows, width)


def scatter_rows(v, cid):
    rows, width = v.shape[0] // 32, v.shape[1]
    return rs16(v.reshape(16, 2, 2, rows // 2, width), True, cid).reshape(2 * rows, width)


def exchange(parts):
    return lax.all_to_all(parts, "dp", split_axis=0, concat_axis=0, tiled=True)


def shards_sixteen(
    tokens,
    out_grad,
    segments,
    routes,
    attn_gain,
    w_query,
    w_latent,
    latent_gain,
    w_keyval,
    w_out,
    moe_gain,
    w_router,
    shared_gate,
    shared_up,
    shared_down,
    expert_gate,
    routed_up_weight,
    expert_down,
):
    n_rows, width = tokens.shape
    dp_count = lax.axis_size("dp")
    dp_index = lax.axis_index("dp")
    seq_len = segments.shape[1]
    total = n_rows * dp_count
    hop_count = (WINDOW - 1) // n_rows + 1
    n_keys = (hop_count + 1) * n_rows
    experts = w_router.shape[1]
    capacity = 4 * n_rows * TOPK // (3 * experts)
    score_scale = (NOPE + ROPE) ** (-0.5)
    row_start = dp_index * n_rows
    seg_row = segments[0]
    depth = w_query.shape[0]
    q_width, o_width, kv_width = w_query.shape[1], w_out.shape[0], w_keyval.shape[1]
    kv_rows = w_keyval.shape[0]
    kv_cuts = depth // kv_rows
    kv_part = kv_width // kv_cuts
    lat_width = w_latent.shape[1]
    small = (lat_width + experts + 3 + 127) // 128 * 128

    shared_part = shared_gate.shape[1] // dp_count
    shared_send = jnp.stack(
        [
            shared_gate.reshape(depth, dp_count, shared_part).transpose(1, 2, 0),
            shared_up.reshape(depth, dp_count, shared_part).transpose(1, 2, 0),
            shared_down.reshape(dp_count, shared_part, depth),
        ],
        1,
    )
    shared_all = exchange(shared_send).transpose(1, 2, 0, 3).reshape(3, shared_part, width)
    sg_t, su_t, sd = shared_all[0], shared_all[1], shared_all[2]
    all_routes = lax.all_gather(routes, "dp", axis=0, tiled=True)

    gains = jnp.stack(
        [attn_gain, moe_gain, jnp.pad(latent_gain, (0, depth - kv_rows))], 1
    )
    packed = jnp.concatenate(
        [
            w_query,
            w_out.T,
            w_keyval.reshape(kv_rows, kv_cuts, kv_part).transpose(1, 0, 2).reshape(depth, kv_part),
            w_latent,
            w_router,
            gains,
            jnp.zeros((depth, small - lat_width - experts - 3), jnp.bfloat16),
        ],
        1,
    )
    pack_width = packed.shape[1]
    weights = ag16(packed.reshape(2, depth // 2, pack_width), False, 1).reshape(width, pack_width)
    at = 0
    wq_full = weights[:, at : at + q_width]
    at += q_width
    wo_t = weights[:, at : at + o_width]
    at += o_width
    wkv_full = (
        weights[:, at : at + kv_part]
        .reshape(dp_count, kv_cuts, kv_rows, kv_part)
        .transpose(0, 2, 1, 3)
        .reshape(dp_count * kv_rows, kv_width)
    )
    at += kv_part
    wlat_full = weights[:, at : at + lat_width]
    at += lat_width
    wr_full = weights[:, at : at + experts]
    at += experts
    gain_attn = weights[:, at].astype(jnp.float32)
    gain_moe = weights[:, at + 1].astype(jnp.float32)
    gain_latent = (
        weights[:, at + 2].reshape(dp_count, depth)[:, :kv_rows].reshape(-1).astype(jnp.float32)
    )

    grad_all = gather_rows(out_grad, 2)

    local_heads = q_width // (NOPE + ROPE)
    positions = (row_start + jnp.arange(n_rows, dtype=jnp.int32)).astype(jnp.float32)
    cos_tab, sin_tab = rope_tables(positions)
    resid_in = tokens.astype(jnp.float32)
    normed, attn_norm_back = jax.vjp(rms_scale, resid_in, gain_attn)
    normed_low = normed.astype(jnp.bfloat16)

    def rope_queries(q_flat):
        shaped = q_flat.reshape(n_rows, local_heads, NOPE + ROPE)
        return jnp.concatenate(
            [shaped[..., :NOPE], rotate(shaped[..., NOPE:], cos_tab[:, None], sin_tab[:, None])], -1
        )

    queries, query_back = jax.vjp(rope_queries, matmul(normed_low, wq_full))
    query_low = queries.astype(jnp.bfloat16)

    def latent_piece(latent_raw, gain_vec):
        return (
            rms_scale(latent_raw[:, :RANK], gain_vec),
            rotate(latent_raw[:, RANK:], cos_tab, sin_tab),
        )

    (latent, key_rope), latent_back = jax.vjp(
        latent_piece, matmul(normed_low, wlat_full), gain_latent
    )
    own_keys = jnp.concatenate([latent.astype(jnp.bfloat16), key_rope.astype(jnp.bfloat16)], 1)
    keys_all = jnp.concatenate(
        [passed_along(own_keys, "dp", d) for d in range(hop_count, 0, -1)] + [own_keys], 0
    )
    keys_latent, keys_rope = keys_all[:, :RANK], keys_all[:, RANK:]
    keyval = (
        matmul(keys_latent, wkv_full).astype(jnp.bfloat16).reshape(n_keys, local_heads, NOPE + VDIM)
    )
    key_nope = keyval[..., :NOPE]
    values = keyval[..., NOPE:]
    key_pos = row_start - hop_count * n_rows + jnp.arange(n_keys, dtype=jnp.int32)
    query_pos = row_start + jnp.arange(n_rows, dtype=jnp.int32)
    padded_seg = jnp.concatenate([jnp.full((hop_count * n_rows,), -1, jnp.int32), seg_row])
    key_seg = lax.dynamic_slice_in_dim(padded_seg, row_start, n_keys, 0)
    query_seg = lax.dynamic_slice_in_dim(seg_row, row_start, n_rows, 0)
    allowed = (key_pos[None, :] >= 0) & (key_pos[None, :] <= query_pos[:, None])
    allowed = (
        allowed
        & (query_pos[:, None] - key_pos[None, :] < WINDOW)
        & (query_seg[:, None] == key_seg[None, :])
    )

    def masked_scores():
        nope_part = jnp.einsum(
            "qhd,khd->hqk", query_low[..., :NOPE], key_nope, preferred_element_type=jnp.float32
        )
        rope_part = jnp.einsum(
            "qhr,kr->hqk", query_low[..., NOPE:], keys_rope, preferred_element_type=jnp.float32
        )
        return jnp.where(allowed[None], score_scale * (nope_part + rope_part), -jnp.inf)

    scores = masked_scores()
    top_score = jnp.max(scores, axis=-1, keepdims=True)
    exp_scores = jnp.exp(scores - top_score)
    denom = jnp.sum(exp_scores, axis=-1, keepdims=True)
    attn_probs = exp_scores / denom
    log_total = top_score + jnp.log(denom)
    attended = jnp.einsum(
        "hqk,khv->qhv", attn_probs.astype(jnp.bfloat16), values, preferred_element_type=jnp.float32
    )
    attended_low = attended.astype(jnp.bfloat16).reshape(n_rows, local_heads * VDIM)
    middle = resid_in + summed(matmul_nt(attended_low, wo_t))
    moe_normed, moe_norm_back = jax.vjp(rms_scale, middle, gain_moe)
    moe_low = moe_normed.astype(jnp.bfloat16)
    router, router_back = jax.vjp(
        lambda logit_vals: jax.nn.softmax(logit_vals, axis=-1), matmul(moe_low, wr_full)
    )

    moe_all = gather_rows(moe_low, 3)
    chosen = jnp.any(all_routes == dp_index, axis=1).reshape(dp_count, n_rows)
    earlier = jnp.arange(n_rows)[:, None] < jnp.arange(n_rows)[None, :]
    rank = matmul(chosen.astype(jnp.bfloat16), earlier.astype(jnp.bfloat16)).astype(jnp.int32)
    pick = (
        (rank[:, None, :] == jnp.arange(capacity, dtype=jnp.int32)[None, :, None])
        & chosen[:, None, :]
    ).astype(jnp.bfloat16)

    def picked(v):
        return (
            jnp.einsum(
                "bst,btd->bsd",
                pick,
                v.reshape(dp_count, n_rows, width),
                preferred_element_type=jnp.float32,
            )
            .astype(jnp.bfloat16)
            .reshape(dp_count * capacity, width)
        )

    def put_back(v):
        return jnp.einsum(
            "bst,bsd->btd",
            pick,
            v.reshape(dp_count, capacity, v.shape[1]),
            preferred_element_type=jnp.float32,
        ).reshape(total, v.shape[1])

    w_gate, w_up, w_down = expert_gate[0], routed_up_weight[0], expert_down[0]
    rows_in = picked(moe_all)
    rows_grad = picked(grad_all)
    row_router = jax.nn.softmax(matmul(rows_in, wr_full), axis=-1)
    row_gate = lax.dynamic_slice_in_dim(row_router, dp_index, 1, 1)
    exp_act, exp_act_back = jax.vjp(gated_act, matmul(rows_in, w_gate), matmul(rows_in, w_up))
    act_low = exp_act.astype(jnp.bfloat16)
    exp_out = (row_gate * matmul(act_low, w_down)).astype(jnp.bfloat16)
    shared_act, shared_back = jax.vjp(
        gated_act, matmul_nt(moe_all, sg_t), matmul_nt(moe_all, su_t)
    )
    shared_low = shared_act.astype(jnp.bfloat16)
    out_part = (put_back(exp_out) + matmul(shared_low, sd)).astype(jnp.bfloat16)
    result = (middle + scatter_rows(out_part, 4).astype(jnp.float32)).astype(jnp.bfloat16)

    d_pre = matmul_nt(rows_grad, w_down)
    row_d_gate = jnp.sum(act_low.astype(jnp.float32) * d_pre, axis=1, keepdims=True)
    d_ea, d_eb = exp_act_back(row_gate * d_pre)
    d_ea_low, d_eb_low = d_ea.astype(jnp.bfloat16), d_eb.astype(jnp.bfloat16)
    d_slots = matmul_nt(d_ea_low, w_gate) + matmul_nt(d_eb_low, w_up)
    d_sa, d_sb = shared_back(matmul_nt(grad_all, sd))
    d_sa_low, d_sb_low = d_sa.astype(jnp.bfloat16), d_sb.astype(jnp.bfloat16)
    lane = jnp.arange(128, dtype=jnp.int32)[None, :]
    d_gate_cols = put_back(
        jnp.where(lane == dp_index, row_d_gate, 0.0).astype(jnp.bfloat16)
    )
    d_part = put_back(d_slots.astype(jnp.bfloat16)) + matmul(d_sa_low, sg_t) + matmul(d_sb_low, su_t)
    d_home = scatter_rows(jnp.concatenate([d_part, d_gate_cols], 1).astype(jnp.bfloat16), 5).astype(
        jnp.float32
    )
    scaled_act = (row_gate * act_low.astype(jnp.float32)).astype(jnp.bfloat16)
    grad_down = matmul_tn(scaled_act, rows_grad)[None]
    grad_gate = matmul_tn(rows_in, d_ea_low)[None]
    grad_up = matmul_tn(rows_in, d_eb_low)[None]
    shared_grads = jnp.stack(
        [matmul_tn(d_sa_low, moe_all), matmul_tn(d_sb_low, moe_all), matmul_tn(shared_low, grad_all)]
    ).astype(jnp.bfloat16)
    home = exchange(
        shared_grads.reshape(3, shared_part, dp_count, depth).transpose(2, 0, 1, 3)
    ).astype(jnp.float32)
    home = home.transpose(1, 0, 2, 3).reshape(3, dp_count * shared_part, depth)
    grad_sgate, grad_sup, grad_sdown = home[0].T, home[1].T, home[2]

    grad_y = out_grad.astype(jnp.float32)
    d_gate_all = d_home[:, width : width + experts]
    routed_here = jnp.any(
        routes[:, :, None] == jnp.arange(experts, dtype=jnp.int32)[None, None, :], axis=1
    )
    (d_logits,) = router_back(jnp.where(routed_here, d_gate_all, 0.0))
    d_logits_low = d_logits.astype(jnp.bfloat16)
    grad_router = matmul_tn(moe_low, d_logits_low)
    d_moe = d_home[:, :width] + matmul_nt(d_logits_low, wr_full)
    d_mid_norm, grad_gain_moe = moe_norm_back(d_moe)
    d_middle = grad_y + d_mid_norm
    d_middle_low = d_middle.astype(jnp.bfloat16)
    grad_wo_t = matmul_tn(d_middle_low, attended_low)
    d_att_low = matmul(d_middle_low, wo_t).astype(jnp.bfloat16).reshape(n_rows, local_heads, VDIM)
    again_probs = jnp.exp(masked_scores() - log_total)
    d_values = jnp.einsum(
        "hqk,qhv->khv",
        again_probs.astype(jnp.bfloat16),
        d_att_low,
        preferred_element_type=jnp.float32,
    )
    d_probs = jnp.einsum("qhv,khv->hqk", d_att_low, values, preferred_element_type=jnp.float32)
    d_scores = (
        again_probs * (d_probs - jnp.sum(d_probs * again_probs, axis=-1, keepdims=True))
    ).astype(jnp.bfloat16)
    d_query_nope = score_scale * jnp.einsum(
        "hqk,khd->qhd", d_scores, key_nope, preferred_element_type=jnp.float32
    )
    d_query_rope = score_scale * jnp.einsum(
        "hqk,kr->qhr", d_scores, keys_rope, preferred_element_type=jnp.float32
    )
    d_key_nope = score_scale * jnp.einsum(
        "hqk,qhd->khd", d_scores, query_low[..., :NOPE], preferred_element_type=jnp.float32
    )
    d_key_rope = score_scale * jnp.einsum(
        "hqk,qhr->kr", d_scores, query_low[..., NOPE:], preferred_element_type=jnp.float32
    )
    (d_q_raw,) = query_back(jnp.concatenate([d_query_nope, d_query_rope], -1))
    d_q_low = d_q_raw.astype(jnp.bfloat16)
    grad_wq = matmul_tn(normed_low, d_q_low)
    d_kv_low = (
        jnp.concatenate([d_key_nope, d_values], -1)
        .astype(jnp.bfloat16)
        .reshape(n_keys, local_heads * (NOPE + VDIM))
    )
    grad_wkv = matmul_tn(keys_latent, d_kv_low)
    d_keys = jnp.concatenate([matmul_nt(d_kv_low, wkv_full), d_key_rope], 1)
    d_own = d_keys[hop_count * n_rows :]
    d_keys_low = d_keys.astype(jnp.bfloat16)
    for distance in range(hop_count, 0, -1):
        lower = (hop_count - distance) * n_rows
        d_own = d_own + passed_along(
            d_keys_low[lower : lower + n_rows], "dp", -distance
        ).astype(jnp.float32)
    both = summed(jnp.concatenate([matmul_nt(d_q_low, wq_full), d_own], 1))
    d_normed, own_latent, own_rope = (
        both[:, :width],
        both[:, width : width + RANK],
        both[:, width + RANK :],
    )
    d_latent_raw, grad_gain_latent = latent_back((own_latent, own_rope))
    d_latent_low = d_latent_raw.astype(jnp.bfloat16)
    grad_wlat = matmul_tn(normed_low, d_latent_low)
    d_normed = d_normed + matmul_nt(d_latent_low, wlat_full)
    d_tokens_norm, grad_gain_attn = attn_norm_back(d_normed)
    token_input_gradient = d_middle + d_tokens_norm

    grad_gains = jnp.stack(
        [
            grad_gain_attn.reshape(dp_count, depth),
            grad_gain_moe.reshape(dp_count, depth),
            jnp.pad(grad_gain_latent.reshape(dp_count, kv_rows), ((0, 0), (0, depth - kv_rows))),
        ],
        2,
    ).reshape(width, 3)
    grads = jnp.concatenate(
        [
            grad_wq.astype(jnp.bfloat16),
            grad_wo_t.astype(jnp.bfloat16),
            grad_wkv.astype(jnp.bfloat16)
            .reshape(dp_count, kv_rows, kv_cuts, kv_part)
            .transpose(0, 2, 1, 3)
            .reshape(width, kv_part),
            grad_wlat.astype(jnp.bfloat16),
            grad_router.astype(jnp.bfloat16),
            grad_gains.astype(jnp.bfloat16),
            jnp.zeros((width, small - lat_width - experts - 3), jnp.bfloat16),
        ],
        1,
    )
    mine = (
        rs16(grads.reshape(dp_count, 1, 2, depth // 2, pack_width), False, 6)
        .reshape(depth, pack_width)
        .astype(jnp.float32)
    )
    at = 0
    out_wq = mine[:, at : at + q_width]
    at += q_width
    out_wo = mine[:, at : at + o_width].T
    at += o_width
    out_wkv = (
        mine[:, at : at + kv_part]
        .reshape(kv_cuts, kv_rows, kv_part)
        .transpose(1, 0, 2)
        .reshape(kv_rows, kv_width)
    )
    at += kv_part
    out_wlat = mine[:, at : at + lat_width]
    at += lat_width
    out_router = mine[:, at : at + experts]
    at += experts
    return (
        result,
        token_input_gradient,
        mine[:, at],
        out_wq,
        out_wlat,
        mine[:kv_rows, at + 2],
        out_wkv,
        out_wo,
        mine[:, at + 1],
        out_router,
        grad_sgate,
        grad_sup,
        grad_sdown,
        grad_gate,
        grad_up,
        grad_down,
    )


def shards_general(
    tokens,
    out_grad,
    segments,
    routes,
    attn_gain,
    w_query,
    w_latent,
    latent_gain,
    w_keyval,
    w_out,
    moe_gain,
    w_router,
    shared_gate,
    shared_up,
    shared_down,
    expert_gate,
    routed_up_weight,
    expert_down,
):
    n_rows = tokens.shape[0]
    model_width = tokens.shape[1]
    dp_count = lax.axis_size("dp")
    dp_index = lax.axis_index("dp")
    seq_len = segments.shape[1]
    seq_devs = seq_len // n_rows
    hop_count = (WINDOW - 1) // n_rows + 1
    n_keys = (hop_count + 1) * n_rows
    experts = w_router.shape[1]
    local_experts = expert_gate.shape[0]
    capacity = 4 * n_rows * TOPK // (3 * experts)
    slot_total = experts * capacity
    score_scale = (NOPE + ROPE) ** (-0.5)
    row_start = dp_index % seq_devs * n_rows
    seg_row = lax.dynamic_index_in_dim(segments, dp_index // seq_devs, 0, keepdims=False)
    gathered = (
        lax.all_gather(attn_gain, "dp", axis=0, tiled=True),
        lax.all_gather(w_query, "dp", axis=0, tiled=True),
        lax.all_gather(w_latent, "dp", axis=0, tiled=True),
        lax.all_gather(latent_gain, "dp", axis=0, tiled=True),
        lax.all_gather(w_keyval, "dp", axis=0, tiled=True),
        lax.all_gather(w_out, "dp", axis=1, tiled=True),
        lax.all_gather(moe_gain, "dp", axis=0, tiled=True),
        lax.all_gather(w_router, "dp", axis=0, tiled=True),
        lax.all_gather(shared_gate, "dp", axis=0, tiled=True),
        lax.all_gather(shared_up, "dp", axis=0, tiled=True),
        lax.all_gather(shared_down, "dp", axis=1, tiled=True),
    )
    (
        gain_attn,
        wq_full,
        wlat_full,
        gain_latent,
        wkv_full,
        wo_full,
        gain_moe,
        wr_full,
        sgate_full,
        sup_full,
        sdown_full,
    ) = gathered
    local_heads = wq_full.shape[1] // (NOPE + ROPE)
    positions = (row_start + jnp.arange(n_rows, dtype=jnp.int32)).astype(jnp.float32)
    cos_tab, sin_tab = rope_tables(positions)
    resid_in = tokens.astype(jnp.float32)
    normed, attn_norm_back = jax.vjp(rms_scale, resid_in, gain_attn.astype(jnp.float32))
    normed_low = normed.astype(jnp.bfloat16)

    def rope_queries(q_flat):
        shaped = q_flat.reshape(n_rows, local_heads, NOPE + ROPE)
        return jnp.concatenate(
            [shaped[..., :NOPE], rotate(shaped[..., NOPE:], cos_tab[:, None], sin_tab[:, None])], -1
        )

    queries, query_back = jax.vjp(rope_queries, matmul(normed_low, wq_full))
    query_low = queries.astype(jnp.bfloat16)

    def latent_piece(latent_raw, gain_vec):
        return (
            rms_scale(latent_raw[:, :RANK], gain_vec),
            rotate(latent_raw[:, RANK:], cos_tab, sin_tab),
        )

    (latent, key_rope), latent_back = jax.vjp(
        latent_piece, matmul(normed_low, wlat_full), gain_latent.astype(jnp.float32)
    )
    latent_low = latent.astype(jnp.bfloat16)
    rope_low = key_rope.astype(jnp.bfloat16)
    latent_parts = []
    rope_parts = []
    for distance in range(hop_count, 0, -1):
        moved_latent, moved_rope = passed_along((latent_low, rope_low), "dp", distance)
        latent_parts.append(moved_latent)
        rope_parts.append(moved_rope)
    keys_latent = jnp.concatenate(latent_parts + [latent_low], 0)
    keys_rope = jnp.concatenate(rope_parts + [rope_low], 0)
    keyval = (
        matmul(keys_latent, wkv_full).astype(jnp.bfloat16).reshape(n_keys, local_heads, NOPE + VDIM)
    )
    key_nope = keyval[..., :NOPE]
    values = keyval[..., NOPE:]
    key_pos = row_start - hop_count * n_rows + jnp.arange(n_keys, dtype=jnp.int32)
    query_pos = row_start + jnp.arange(n_rows, dtype=jnp.int32)
    padded_seg = jnp.concatenate([jnp.full((hop_count * n_rows,), -1, jnp.int32), seg_row])
    key_seg = lax.dynamic_slice_in_dim(padded_seg, row_start, n_keys, 0)
    query_seg = lax.dynamic_slice_in_dim(seg_row, row_start, n_rows, 0)
    allowed = (key_pos[None, :] >= 0) & (key_pos[None, :] <= query_pos[:, None])
    allowed = (
        allowed
        & (query_pos[:, None] - key_pos[None, :] < WINDOW)
        & (query_seg[:, None] == key_seg[None, :])
    )

    def masked_scores():
        nope_part = jnp.einsum(
            "qhd,khd->hqk", query_low[..., :NOPE], key_nope, preferred_element_type=jnp.float32
        )
        rope_part = jnp.einsum(
            "qhr,kr->hqk", query_low[..., NOPE:], keys_rope, preferred_element_type=jnp.float32
        )
        return jnp.where(allowed[None], score_scale * (nope_part + rope_part), -jnp.inf)

    scores = masked_scores()
    top_score = jnp.max(scores, axis=-1, keepdims=True)
    exp_scores = jnp.exp(scores - top_score)
    denom = jnp.sum(exp_scores, axis=-1, keepdims=True)
    attn_probs = exp_scores / denom
    log_total = top_score + jnp.log(denom)
    attended = jnp.einsum(
        "hqk,khv->qhv", attn_probs.astype(jnp.bfloat16), values, preferred_element_type=jnp.float32
    )
    attended_low = attended.astype(jnp.bfloat16).reshape(n_rows, local_heads * VDIM)
    attn_out = lax.psum(matmul(attended_low, wo_full).astype(jnp.bfloat16), "tensor").astype(
        jnp.float32
    )
    middle = resid_in + attn_out
    moe_normed, moe_norm_back = jax.vjp(rms_scale, middle, gain_moe.astype(jnp.float32))
    moe_low = moe_normed.astype(jnp.bfloat16)
    router, router_back = jax.vjp(
        lambda logit_vals: jax.nn.softmax(logit_vals, axis=-1), matmul(moe_low, wr_full)
    )
    expert_ids = jnp.arange(experts, dtype=jnp.int32)
    route_hot = (routes[:, :, None] == expert_ids[None, None, :]).astype(jnp.float32)
    gate_w = jnp.einsum("te,tke->tk", router, route_hot, precision=highest)
    flat_routes = routes.reshape(-1)
    assign_count = flat_routes.shape[0]
    flat_hot = (flat_routes[:, None] == expert_ids[None, :]).astype(jnp.int32)
    earlier = ranks_before(flat_hot)
    slot_in = jnp.sum(earlier * flat_hot, axis=1)
    target = flat_routes * capacity + slot_in
    assign_ids = jnp.arange(assign_count, dtype=jnp.int32)
    assign_of_slot = jnp.zeros((slot_total,), jnp.int32).at[target].set(assign_ids)
    slot_live = (
        jnp.zeros((slot_total,), jnp.bfloat16)
        .at[target]
        .set(jnp.ones((assign_count,), jnp.bfloat16))
    )
    send_rows = moe_low[assign_of_slot // TOPK] * slot_live[:, None]
    recv_rows = lax.all_to_all(
        send_rows.reshape(dp_count, local_experts * capacity, model_width),
        "dp",
        split_axis=0,
        concat_axis=0,
        tiled=True,
    )
    received_four_parts = recv_rows.reshape(dp_count, local_experts, capacity, model_width)
    exp_gate = jnp.einsum(
        "sjcd,jdf->sjcf", received_four_parts, expert_gate, preferred_element_type=jnp.float32
    )
    exp_up = jnp.einsum(
        "sjcd,jdf->sjcf", received_four_parts, routed_up_weight, preferred_element_type=jnp.float32
    )
    exp_act, exp_act_back = jax.vjp(gated_act, exp_gate, exp_up)
    exp_act_low = exp_act.astype(jnp.bfloat16)
    exp_result = jnp.einsum(
        "sjcf,jfd->sjcd", exp_act_low, expert_down, preferred_element_type=jnp.float32
    )
    returned = lax.all_to_all(
        exp_result.reshape(dp_count, local_experts * capacity, model_width).astype(jnp.bfloat16),
        "dp",
        split_axis=0,
        concat_axis=0,
        tiled=True,
    ).astype(jnp.float32)
    per_assign = returned.reshape(slot_total, model_width)[target].reshape(
        n_rows, TOPK, model_width
    )
    routed = jnp.einsum("tk,tkd->td", gate_w, per_assign, precision=highest)
    shared_a = matmul(moe_low, sgate_full)
    shared_b = matmul(moe_low, sup_full)
    shared_act, shared_back = jax.vjp(gated_act, shared_a, shared_b)
    shared_low = shared_act.astype(jnp.bfloat16)
    moe_out = lax.psum(
        (routed + matmul(shared_low, sdown_full)).astype(jnp.bfloat16), "tensor"
    ).astype(jnp.float32)
    result = (middle + moe_out).astype(jnp.bfloat16)
    grad_y = out_grad.astype(jnp.float32)
    grad_sdown = matmul_tn(shared_low, out_grad)
    d_shared_a, d_shared_b = shared_back(matmul_nt(out_grad, sdown_full))
    d_sa_low = d_shared_a.astype(jnp.bfloat16)
    d_sb_low = d_shared_b.astype(jnp.bfloat16)
    grad_sgate = matmul_tn(moe_low, d_sa_low)
    grad_sup = matmul_tn(moe_low, d_sb_low)
    d_moe = matmul_nt(d_sa_low, sgate_full) + matmul_nt(d_sb_low, sup_full)
    d_gate_part = jnp.einsum("td,tkd->tk", grad_y, per_assign, precision=highest)
    d_assign = (
        (gate_w[:, :, None] * grad_y[:, None, :])
        .astype(jnp.bfloat16)
        .reshape(assign_count, model_width)
    )
    send_grads = d_assign[assign_of_slot] * slot_live[:, None]
    recv_grads = lax.all_to_all(
        send_grads.reshape(dp_count, local_experts * capacity, model_width),
        "dp",
        split_axis=0,
        concat_axis=0,
        tiled=True,
    )
    recv_grads = recv_grads.reshape(dp_count, local_experts, capacity, model_width)
    expert_down_weight_gradient = jnp.einsum(
        "sjcf,sjcd->jfd", exp_act_low, recv_grads, preferred_element_type=jnp.float32
    )
    d_exp_act = jnp.einsum(
        "sjcd,jfd->sjcf", recv_grads, expert_down, preferred_element_type=jnp.float32
    )
    d_exp_gate, expert_up_act_gradient = exp_act_back(d_exp_act)
    d_egate_low = d_exp_gate.astype(jnp.bfloat16)
    expert_up_gradient_lowp = expert_up_act_gradient.astype(jnp.bfloat16)
    expert_gate_weight_gradient = jnp.einsum(
        "bmky,bmkx->myx", received_four_parts, d_egate_low, preferred_element_type=jnp.float32
    )
    expert_up_weight_gradient = jnp.einsum(
        "bmky,bmkx->myx",
        received_four_parts,
        expert_up_gradient_lowp,
        preferred_element_type=jnp.float32,
    )
    d_slots = jnp.einsum(
        "hteg,tmg->htem", d_egate_low, expert_gate, preferred_element_type=jnp.float32
    )
    d_slots = d_slots + jnp.einsum(
        "hteg,tmg->htem",
        expert_up_gradient_lowp,
        routed_up_weight,
        preferred_element_type=jnp.float32,
    )
    back_grads = lax.all_to_all(
        d_slots.reshape(dp_count, local_experts * capacity, model_width).astype(jnp.bfloat16),
        "dp",
        split_axis=0,
        concat_axis=0,
        tiled=True,
    ).astype(jnp.float32)
    d_moe = d_moe + jnp.sum(
        back_grads.reshape(slot_total, model_width)[target].reshape(n_rows, TOPK, model_width),
        axis=1,
    )
    d_moe, d_gate = (
        lax.psum(d_moe.astype(jnp.bfloat16), "tensor").astype(jnp.float32),
        lax.psum(d_gate_part.astype(jnp.bfloat16), "tensor").astype(jnp.float32),
    )
    d_router = jnp.einsum("tk,tke->te", d_gate, route_hot, precision=highest)
    (d_logits,) = router_back(d_router)
    d_logits_low = d_logits.astype(jnp.bfloat16)
    grad_router = matmul_tn(moe_low, d_logits_low)
    d_moe = d_moe + matmul_nt(d_logits_low, wr_full)
    d_mid_norm, grad_gain_moe = moe_norm_back(d_moe)
    d_middle = grad_y + d_mid_norm
    d_middle_low = d_middle.astype(jnp.bfloat16)
    grad_wout = matmul_tn(attended_low, d_middle_low)
    d_att_low = (
        matmul_nt(d_middle_low, wo_full).astype(jnp.bfloat16).reshape(n_rows, local_heads, VDIM)
    )
    again_probs = jnp.exp(masked_scores() - log_total)
    d_values = jnp.einsum(
        "hqk,qhv->khv",
        again_probs.astype(jnp.bfloat16),
        d_att_low,
        preferred_element_type=jnp.float32,
    )
    d_probs = jnp.einsum("qhv,khv->hqk", d_att_low, values, preferred_element_type=jnp.float32)
    d_scores = (
        again_probs * (d_probs - jnp.sum(d_probs * again_probs, axis=-1, keepdims=True))
    ).astype(jnp.bfloat16)
    d_query_nope = score_scale * jnp.einsum(
        "hqk,khd->qhd", d_scores, key_nope, preferred_element_type=jnp.float32
    )
    d_query_rope = score_scale * jnp.einsum(
        "hqk,kr->qhr", d_scores, keys_rope, preferred_element_type=jnp.float32
    )
    d_key_nope = score_scale * jnp.einsum(
        "hqk,qhd->khd", d_scores, query_low[..., :NOPE], preferred_element_type=jnp.float32
    )
    d_key_rope = score_scale * jnp.einsum(
        "hqk,qhr->kr", d_scores, query_low[..., NOPE:], preferred_element_type=jnp.float32
    )
    (d_q_raw,) = query_back(jnp.concatenate([d_query_nope, d_query_rope], -1))
    d_q_low = d_q_raw.astype(jnp.bfloat16)
    grad_wq = matmul_tn(normed_low, d_q_low)
    d_normed = matmul_nt(d_q_low, wq_full)
    d_kv_low = (
        jnp.concatenate([d_key_nope, d_values], -1)
        .astype(jnp.bfloat16)
        .reshape(n_keys, local_heads * (NOPE + VDIM))
    )
    grad_wkv = matmul_tn(keys_latent, d_kv_low)
    d_keys_latent = matmul_nt(d_kv_low, wkv_full)
    own_latent = d_keys_latent[hop_count * n_rows :]
    own_rope = d_key_rope[hop_count * n_rows :]
    for distance in range(hop_count, 0, -1):
        block_index = hop_count - distance
        lower = block_index * n_rows
        home_latent, home_rope = (
            passed_along(
                d_keys_latent[lower : lower + n_rows].astype(jnp.bfloat16), "dp", -distance
            ).astype(jnp.float32),
            passed_along(
                d_key_rope[lower : lower + n_rows].astype(jnp.bfloat16), "dp", -distance
            ).astype(jnp.float32),
        )
        own_latent = own_latent + home_latent
        own_rope = own_rope + home_rope
    d_normed, own_latent, own_rope = (
        lax.psum(d_normed.astype(jnp.bfloat16), "tensor").astype(jnp.float32),
        lax.psum(own_latent.astype(jnp.bfloat16), "tensor").astype(jnp.float32),
        lax.psum(own_rope.astype(jnp.bfloat16), "tensor").astype(jnp.float32),
    )
    d_latent_raw, grad_gain_latent = latent_back((own_latent, own_rope))
    d_latent_low = d_latent_raw.astype(jnp.bfloat16)
    grad_wlat = matmul_tn(normed_low, d_latent_low)
    d_normed = d_normed + matmul_nt(d_latent_low, wlat_full)
    d_tokens_norm, grad_gain_attn = attn_norm_back(d_normed)
    token_input_gradient = d_middle + d_tokens_norm
    reduced_result = tuple(
        (
            lax.psum_scatter(grad_gain_attn, "dp", scatter_dimension=0, tiled=True),
            lax.psum_scatter(grad_wq, "dp", scatter_dimension=0, tiled=True),
            lax.psum_scatter(grad_wlat, "dp", scatter_dimension=0, tiled=True),
            lax.psum_scatter(grad_gain_latent, "dp", scatter_dimension=0, tiled=True),
            lax.psum_scatter(grad_wkv, "dp", scatter_dimension=0, tiled=True),
            lax.psum_scatter(grad_wout, "dp", scatter_dimension=1, tiled=True),
            lax.psum_scatter(grad_gain_moe, "dp", scatter_dimension=0, tiled=True),
            lax.psum_scatter(grad_router, "dp", scatter_dimension=0, tiled=True),
            lax.psum_scatter(grad_sgate, "dp", scatter_dimension=0, tiled=True),
            lax.psum_scatter(grad_sup, "dp", scatter_dimension=0, tiled=True),
            lax.psum_scatter(grad_sdown, "dp", scatter_dimension=1, tiled=True),
        )
    )
    return (
        (result, token_input_gradient)
        + reduced_result
        + (expert_gate_weight_gradient, expert_up_weight_gradient, expert_down_weight_gradient)
    )


def solution(mesh):
    placed = (
        P("dp", None),
        P("dp", None),
        P(),
        P("dp", None),
        P("dp"),
        P("dp", "tensor"),
        P("dp", None),
        P("dp"),
        P("dp", "tensor"),
        P("tensor", "dp"),
        P("dp"),
        P("dp", None),
        P("dp", "tensor"),
        P("dp", "tensor"),
        P("tensor", "dp"),
        P("dp", None, "tensor"),
        P("dp", None, "tensor"),
        P("dp", "tensor", None),
    )
    body = shards_sixteen if mesh.shape["dp"] == 16 and mesh.shape["tensor"] == 2 else shards_general
    return jax.shard_map(
        body,
        mesh=mesh,
        in_specs=placed,
        out_specs=(
            P("dp", None),
            P("dp", None),
            P("dp"),
            P("dp", "tensor"),
            P("dp", None),
            P("dp"),
            P("dp", "tensor"),
            P("tensor", "dp"),
            P("dp"),
            P("dp", None),
            P("dp", "tensor"),
            P("dp", "tensor"),
            P("tensor", "dp"),
            P("dp", None, "tensor"),
            P("dp", None, "tensor"),
            P("dp", "tensor", None),
        ),
        check_vma=False,
    )
```

```python
import functools
import math

import jax
import jax.numpy as jnp
from jax import lax
from jax.experimental import pallas as pl
from jax.experimental.pallas import tpu as pltpu
from jax.sharding import PartitionSpec as P

NOPE = 128
ROPE = 64
VDIM = 128
RANK = 512
TOPK = 6
WINDOW = 1024


eps_norm = 1e-06
highest = lax.Precision.HIGHEST


def passed_along(value, axis, steps):
    count = lax.axis_size(axis)
    leading, last = (max(0, -steps), min(count, count - steps))
    return lax.ppermute(value, axis, [(source, source + steps) for source in range(leading, last)])


def rms_scale(values, gain_vec):
    inv_root = lax.rsqrt(jnp.mean(values * values, axis=-1, keepdims=True) + eps_norm)
    return values * inv_root * gain_vec


def rope_tables(positions):
    half_width = ROPE // 2
    frequency = jnp.exp(
        -jnp.arange(half_width, dtype=jnp.float32) * (2.0 * math.log(10000.0) / ROPE)
    )
    angles = positions[:, None] * frequency[None, :]
    return (jnp.cos(angles), jnp.sin(angles))


def rotate(values, cos_tab, sin_tab):
    half_width = values.shape[-1] // 2
    first_half = values[..., :half_width]
    second = values[..., half_width:]
    return jnp.concatenate(
        [first_half * cos_tab - second * sin_tab, second * cos_tab + first_half * sin_tab], axis=-1
    )


def gated_act(gate_a, up_b):
    return jax.nn.silu(gate_a) * up_b


def matmul(left_mat, right_mat):
    return jnp.dot(left_mat, right_mat, preferred_element_type=jnp.float32)


def matmul_nt(left_mat, right_mat):
    return lax.dot_general(
        left_mat, right_mat, (((1,), (1,)), ((), ())), preferred_element_type=jnp.float32
    )


def matmul_tn(left_mat, right_mat):
    return lax.dot_general(
        left_mat, right_mat, (((0,), (0,)), ((), ())), preferred_element_type=jnp.float32
    )


def ranks_before(hot):
    count = hot.shape[0]
    below = jnp.arange(count)[:, None] > jnp.arange(count)[None, :]
    return matmul(below.astype(jnp.bfloat16), hot.astype(jnp.bfloat16)).astype(jnp.int32)


MESH = pl.DeviceIdType.MESH

def z_order(z, k):
    zz = jnp.where(z >= 2, 3 - z, z)
    o = [zz, 1 - zz, 2, 3][k]
    return jnp.where(z >= 2, 3 - o, o)

def ag_kernel(share, x_ref, o_ref, zsem_s, zsem_r, asem_s, asem_r, bsem_s, bsem_r, csem_s, csem_r, lsem):
    me = lax.axis_index("dp"); core = lax.axis_index("tensor")
    z = me // 4; y = (me // 2) % 2; x = me % 2
    xn = z*4 + y*2 + (1-x); yn = z*4 + (1-y)*2 + x
    up = jnp.minimum(z+1, 3)*4 + y*2 + x; dn = jnp.maximum(z-1, 0)*4 + y*2 + x
    slot = core if share else 0
    bar = pltpu.get_barrier_semaphore()
    def sig(d, c): pl.semaphore_signal(bar, inc=1, device_id=(d, c), device_id_type=MESH)
    sig(xn, core); sig(yn, core)
    pl.when(z < 3)(lambda: sig(up, core))
    pl.when(z > 0)(lambda: sig(dn, core))
    n = 2 + (z < 3).astype(jnp.int32) + (z > 0).astype(jnp.int32)
    if share:
        sig(me, 1-core); n = n + 1
    pl.semaphore_wait(bar, n)
    own = pltpu.make_async_copy(x_ref, o_ref.at[me, slot], lsem); own.start()

    def rc(src, dst, ss, rs, dev, c=None):
        return pltpu.make_async_remote_copy(src_ref=src, dst_ref=dst, send_sem=ss, recv_sem=rs,
                                            device_id=(dev, core if c is None else c), device_id_type=MESH)
    waits = []
    def zcopy(zp, dev, ss):
        b = zp*4 + y*2 + x
        return rc(o_ref.at[b, slot], o_ref.at[b, slot], zsem_s.at[ss], zsem_r.at[zp], dev)
    def xcopy(j, b, half, zp):
        return rc(o_ref.at[b, slot, half], o_ref.at[b, slot, half], asem_s.at[zp, j], asem_r.at[zp, j], xn)
    def ycopy(j, b, half, zp):
        return rc(o_ref.at[b, slot, half], o_ref.at[b, slot, half], bsem_s.at[zp, j], bsem_r.at[zp, j], yn)
    def sib(b):
        return rc(o_ref.at[b, slot], o_ref.at[b, slot], csem_s.at[b], csem_r.at[b], me, 1-core)

    own.wait()
    for k in range(4):
        zp = z_order(z, k)
        b = zp*4 + y*2 + x
        if k > 0:
            zcopy(zp, up, 0).wait_recv()
        @pl.when((zp <= z) & (z < 3))
        def _(): zcopy(zp, up, zp).start()
        @pl.when((zp >= z) & (z > 0))
        def _(): zcopy(zp, dn, 4 + zp).start()
        xcopy(0, b, 0, zp).start()
        ycopy(0, b, 1, zp).start()
        ycopy(1, b, 0, zp).start()
        xcopy(1, b, 1, zp).start()
        if share: sib(b).start()
        bx = zp*4 + y*2 + (1-x); by = zp*4 + (1-y)*2 + x
        if k > 0: hop(*prev)
        prev = (zp, bx, by)
        def hop(zp, bx, by):
            xcopy(0, bx, 0, zp).wait_recv()
            ycopy(2, bx, 0, zp).start()
            ycopy(0, by, 1, zp).wait_recv()
            xcopy(2, by, 1, zp).start()
            xcopy(1, bx, 1, zp).wait_recv()
            ycopy(1, by, 0, zp).wait_recv()
            if share:
                sib(bx).start(); sib(by).start()
    hop(*prev)
    for k in range(4):
        zp = z_order(z, k)
        bd = zp*4 + (1-y)*2 + (1-x)
        ycopy(2, bd, 0, zp).wait_recv()
        xcopy(2, bd, 1, zp).wait_recv()
        if share: sib(bd).start()
    for k in range(4):
        @pl.when((k <= z) & (z < 3))
        def _(): zcopy(k, up, k).wait_send()
        @pl.when((k >= z) & (z > 0))
        def _(): zcopy(k, dn, 4 + k).wait_send()
        for j in range(3):
            xcopy(j, 0, 0, k).wait_send(); ycopy(j, 0, 0, k).wait_send()
    if share:
        for b in range(16):
            sib(b).wait_send()
            pltpu.make_async_remote_copy(src_ref=o_ref.at[b, slot], dst_ref=o_ref.at[b, 1-slot], send_sem=csem_s.at[b], recv_sem=csem_r.at[b], device_id=(me, 1-core), device_id_type=MESH).wait_recv()

def ag16(x, share, cid):
    S = pltpu.SemaphoreType.DMA
    cores = 2 if share else 1
    return pl.pallas_call(functools.partial(ag_kernel, share),
        out_shape=jax.ShapeDtypeStruct((16, cores) + x.shape, x.dtype),
        in_specs=[pl.BlockSpec(memory_space=pl.ANY)], out_specs=pl.BlockSpec(memory_space=pl.ANY),
        scratch_shapes=[S((8,)), S((4,)), S((4,3)), S((4,3)), S((4,3)), S((4,3)), S((16,)), S((16,)), S],
        compiler_params=pltpu.CompilerParams(collective_id=cid, has_side_effects=True),
        )(x)


def add_into(dst, src, out=None):
    out = dst if out is None else out
    h = dst.shape[0]
    def step(i, _):
        r = pl.ds(pl.multiple_of(i * 16, 16), 16)
        out[r] = (dst[r].astype(jnp.float32) + src[r].astype(jnp.float32)).astype(out.dtype)
        return 0
    lax.fori_loop(0, h // 16, step, 0)

def rs_kernel(share, p_ref, o_ref, own, sibr, yr, xr, zr, lsem, cs, cr, xs, xrs, ys, yrs, zs, zrs, fs, fr):
    me = lax.axis_index("dp"); core = lax.axis_index("tensor")
    z = me // 4; y = (me // 2) % 2; x = me % 2
    xn = z*4 + y*2 + (1-x); yn = z*4 + (1-y)*2 + x
    up = jnp.minimum(z+1, 3)*4 + y*2 + x; dn = jnp.maximum(z-1, 0)*4 + y*2 + x
    slot = core if share else 0
    other = 1 - core
    def rc(src, dst, ss, rs, dev, c=None):
        return pltpu.make_async_remote_copy(src_ref=src, dst_ref=dst, send_sem=ss, recv_sem=rs,
                                            device_id=(dev, core if c is None else c), device_id_type=MESH)
    for k in range(4):
        zp = z_order(z, 3-k)
        pltpu.make_async_copy(p_ref.at[pl.ds(zp*4, 4), slot], own.at[pl.ds(zp*4, 4)], lsem.at[zp]).start()
    bar = pltpu.get_barrier_semaphore()
    def sig(d, c): pl.semaphore_signal(bar, inc=1, device_id=(d, c), device_id_type=MESH)
    sig(xn, core); sig(yn, core)
    pl.when(z < 3)(lambda: sig(up, core))
    pl.when(z > 0)(lambda: sig(dn, core))
    n = 2 + (z < 3).astype(jnp.int32) + (z > 0).astype(jnp.int32)
    if share:
        sig(me, other); n = n + 1
    pl.semaphore_wait(bar, n)
    def sib(zp):
        return rc(p_ref.at[pl.ds(zp*4, 4), other], sibr.at[pl.ds(zp*4, 4)], cs.at[zp], cr.at[zp], me, other)
    if share:
        for k in range(4): sib(z_order(z, 3-k)).start()
    def y_(j, b, half, zp): return rc(own.at[b, half], yr.at[zp, j], ys.at[zp, j], yrs.at[zp, j], yn)
    def x_(j, b, half, zp): return rc(own.at[b, half], xr.at[zp, j], xs.at[zp, j], xrs.at[zp, j], xn)
    def zc(zp, dev, d):
        b = zp*4 + y*2 + x
        return rc(own.at[b], zr.at[d, zp], zs.at[zp], zrs.at[d, zp], dev)
    def blk(zp, yy, xx): return zp*4 + yy*2 + xx
    def s1(k):
        zp = z_order(z, 3-k)
        pltpu.make_async_copy(p_ref.at[pl.ds(zp*4, 4), slot], own.at[pl.ds(zp*4, 4)], lsem.at[zp]).wait()
        if share:
            sib(zp).wait_recv()
            def one(q, _):
                b = zp*4 + q
                add_into(own.at[b, 0], sibr.at[b, 0]); add_into(own.at[b, 1], sibr.at[b, 1])
                return 0
            lax.fori_loop(0, 4, one, 0)
        y_(0, blk(zp, 1-y, 1-x), 0, zp).start()
        x_(0, blk(zp, 1-y, 1-x), 1, zp).start()
        y_(1, blk(zp, 1-y, x), 0, zp).start()
        x_(1, blk(zp, y, 1-x), 1, zp).start()
    def s2(k):
        zp = z_order(z, 3-k)
        y_(0, blk(zp, 1-y, 1-x), 0, zp).wait_recv()
        add_into(own.at[blk(zp, y, 1-x), 0], yr.at[zp, 0])
        x_(2, blk(zp, y, 1-x), 0, zp).start()
        x_(0, blk(zp, 1-y, 1-x), 1, zp).wait_recv()
        add_into(own.at[blk(zp, 1-y, x), 1], xr.at[zp, 0])
        y_(2, blk(zp, 1-y, x), 1, zp).start()
        mine = blk(zp, y, x)
        y_(1, blk(zp, 1-y, x), 0, zp).wait_recv()
        add_into(own.at[mine, 0], yr.at[zp, 1])
        x_(1, blk(zp, y, 1-x), 1, zp).wait_recv()
        add_into(own.at[mine, 1], xr.at[zp, 1])
    def s3(k):
        zp = z_order(z, 3-k)
        mine = blk(zp, y, x)
        x_(2, blk(zp, y, 1-x), 0, zp).wait_recv()
        add_into(own.at[mine, 0], xr.at[zp, 2])
        y_(2, blk(zp, 1-y, x), 1, zp).wait_recv()
        add_into(own.at[mine, 1], yr.at[zp, 2])
        def both(d):
            add_into(own.at[mine, 0], zr.at[d, zp, 0]); add_into(own.at[mine, 1], zr.at[d, zp, 1])
        if k < 3:
            @pl.when((zp < z) & (z < 3))
            def _():
                zc(zp, up, 1).wait_recv(); both(1)
            @pl.when((zp > z) & (z > 0))
            def _():
                zc(zp, dn, 0).wait_recv(); both(0)
            @pl.when(zp < z)
            def _(): zc(zp, dn, 1).start()
            @pl.when(zp > z)
            def _(): zc(zp, up, 0).start()
        else:
            @pl.when(z < 3)
            def _():
                zc(zp, up, 1).wait_recv(); both(1)
            @pl.when(z > 0)
            def _():
                zc(zp, dn, 0).wait_recv(); both(0)
    s1(0); s1(1); s2(0); s1(2); s2(1); s3(0); s1(3); s2(2); s3(1); s2(3); s3(2); s3(3)
    if share:
        mine = me
        for a in range(2):
            add = own.at[mine, a]
            def step(i, _):
                r = pl.ds(pl.multiple_of(i*16, 16), 16)
                o_ref[core, a, r] = add[r]
                return 0
            lax.fori_loop(0, add.shape[0]//16, step, 0)
        f = rc(o_ref.at[core], o_ref.at[core], fs, fr, me, other)
        f.start()
        pltpu.make_async_remote_copy(src_ref=o_ref.at[core], dst_ref=o_ref.at[other], send_sem=fs, recv_sem=fr, device_id=(me, other), device_id_type=MESH).wait_recv()
        f.wait_send()
        for k in range(4): sib(k).wait_send()
    else:
        for a in range(2):
            add = own.at[me, a]
            def step(i, _):
                r = pl.ds(pl.multiple_of(i*16, 16), 16)
                o_ref[0, a, r] = add[r].astype(o_ref.dtype)
                return 0
            lax.fori_loop(0, add.shape[0]//16, step, 0)
    for k in range(4):
        for j in range(3):
            x_(j, 0, 0, k).wait_send(); y_(j, 0, 0, k).wait_send()
        @pl.when(k != z)
        def _(): zc(k, up, 0).wait_send()

def rs16(p, share, cid):
    S = pltpu.SemaphoreType.DMA
    cores = 2 if share else 1
    blkshape = p.shape[2:]
    half = p.shape[3:]
    V = lambda s: pltpu.VMEM(s, p.dtype)
    return pl.pallas_call(functools.partial(rs_kernel, share),
        out_shape=jax.ShapeDtypeStruct((cores,) + blkshape, p.dtype),
        in_specs=[pl.BlockSpec(memory_space=pl.ANY)], out_specs=pl.BlockSpec(memory_space=pltpu.VMEM),
        scratch_shapes=[V((16,) + blkshape), V((16,) + blkshape) if share else V((1, 2, 16, 128)), V((4, 3) + half), V((4, 3) + half), V((2, 4) + blkshape),
            S((4,)), S((4,)), S((4,)), S((4,3)), S((4,3)), S((4,3)), S((4,3)), S((4,)), S((2,4)), S, S],
        compiler_params=pltpu.CompilerParams(collective_id=cid, has_side_effects=True, vmem_limit_bytes=60 << 20),
        )(p)


def plane_at(z, k):
    edge = jnp.where(z >= 2, 3 - z, z)
    near = jnp.where(k == 0, edge, jnp.where(k == 1, 1 - edge, k))
    return jnp.where(z >= 2, 3 - near, near)


def nt(a, b):
    return lax.dot_general(a, b, (((1,), (1,)), ((), ())), preferred_element_type=jnp.float32)


def tn(a, b):
    return lax.dot_general(a, b, (((0,), (0,)), ((), ())), preferred_element_type=jnp.float32)


def mm(a, b):
    return jnp.dot(a, b, preferred_element_type=jnp.float32)


def gate_parts(a, b, dc):
    s = 1.0 / (1.0 + jnp.exp(-a))
    act = a * s
    return act * b, dc * b * (s * (1.0 + a * (1.0 - s))), dc * act


def moe_kernel(
    moe, grd, pick, pick_t, wg, wu, wd, wr, sgu, sdn,
    o_out, r_out, rg_out, act_out, da_out, db_out, sg_out, sibr, yr, xr, zr,
    own, sib, stage, xb, gb, pk, pt, rr, rg, ly, ld, ry, rd, acts, das, dbs,
    in_sem, out_sem, st_sem, cs, cr, xs, xrs, ys, yrs, zs, zrs, fs, fr,
):
    me = lax.axis_index("dp")
    core = lax.axis_index("tensor")
    other = 1 - core
    z = me // 4
    y = (me // 2) % 2
    x = me % 2
    xn = z * 4 + y * 2 + (1 - x)
    yn = z * 4 + (1 - y) * 2 + x
    up = jnp.minimum(z + 1, 3) * 4 + y * 2 + x
    dn = jnp.maximum(z - 1, 0) * 4 + y * 2 + x
    width = moe.shape[2]
    hid = 128
    cut = 512

    def rc(src, dst, ss, rs, dev, c):
        return pltpu.make_async_remote_copy(
            src_ref=src, dst_ref=dst, send_sem=ss, recv_sem=rs, device_id=(dev, c), device_id_type=MESH
        )

    def loads(i):
        k, half = i // 2, i % 2
        b = plane_at(z, 3 - k) * 4 + jnp.where(half == 0, 1 - y, y) * 2
        at = pl.ds(b, 2)
        return [
            pltpu.make_async_copy(moe.at[at], xb, in_sem.at[0]),
            pltpu.make_async_copy(grd.at[at], gb, in_sem.at[1]),
            pltpu.make_async_copy(pick.at[at], pk, in_sem.at[2]),
            pltpu.make_async_copy(pick_t.at[at], pt, in_sem.at[3]),
        ]

    for c in loads(0):
        c.start()
    bar = pltpu.get_barrier_semaphore()

    def sig(d, c):
        pl.semaphore_signal(bar, inc=1, device_id=(d, c), device_id_type=MESH)

    sig(xn, core)
    sig(yn, core)
    sig(me, other)
    pl.when(z < 3)(lambda: sig(up, core))
    pl.when(z > 0)(lambda: sig(dn, core))
    pl.semaphore_wait(bar, 3 + (z < 3).astype(jnp.int32) + (z > 0).astype(jnp.int32))

    for q in range(2):
        ry[q, hid:] = sdn[...]
        rd[q, hid:] = sgu[...]
    sg_out[...] = jnp.zeros_like(sg_out)

    def y_(j, b, half, zp):
        return rc(own.at[b, half], yr.at[zp, j], ys.at[zp, j], yrs.at[zp, j], yn, core)

    def x_(j, b, half, zp):
        return rc(own.at[b, half], xr.at[zp, j], xs.at[zp, j], xrs.at[zp, j], xn, core)

    def zc(zp, dev, d):
        b = zp * 4 + y * 2 + x
        return rc(own.at[b], zr.at[d, zp], zs.at[zp], zrs.at[d, zp], dev, core)

    def sib_send(i):
        return rc(sib, sibr.at[i], cs, cr.at[i], me, other)

    def outs(i):
        at = pl.ds(pl.multiple_of(i * 256, 256), 256)
        return [
            pltpu.make_async_copy(rr, r_out.at[at], out_sem.at[0]),
            pltpu.make_async_copy(rg, rg_out.at[at], out_sem.at[1]),
            pltpu.make_async_copy(acts, act_out.at[at], out_sem.at[2]),
            pltpu.make_async_copy(das, da_out.at[at], out_sem.at[3]),
            pltpu.make_async_copy(dbs, db_out.at[at], out_sem.at[4]),
        ]

    def columns(step):
        def one(n, _):
            step(pl.ds(pl.multiple_of(n * cut, cut), cut))
            return 0

        lax.fori_loop(0, width // cut, one, 0)

    def first_part(i):
        for c in loads(i):
            c.wait()

        @pl.when(i > 0)
        def _():
            for c in outs(i - 1):
                c.wait()

        def pick_rows(n):
            for q in range(2):
                rr[q * hid : (q + 1) * hid, n] = mm(pk[q], xb[q, :, n]).astype(jnp.bfloat16)
                rg[q * hid : (q + 1) * hid, n] = mm(pk[q], gb[q, :, n]).astype(jnp.bfloat16)

        columns(pick_rows)
        for q in range(2):
            ab = nt(xb[q], sgu[...])
            act, d_a, d_b = gate_parts(ab[:, :hid], ab[:, hid:], nt(gb[q], sdn[...]))
            ly[q, :, :hid] = pt[q]
            ly[q, :, hid:] = act.astype(jnp.bfloat16)
            ld[q, :, :hid] = pt[q]
            ld[q, :, hid : 2 * hid] = d_a.astype(jnp.bfloat16)
            ld[q, :, 2 * hid :] = d_b.astype(jnp.bfloat16)

        def shared_grads(n):
            sg_out[: 2 * hid, n] += tn(ld[0, :, hid:], xb[0, :, n]) + tn(ld[1, :, hid:], xb[1, :, n])
            sg_out[2 * hid :, n] += tn(ly[0, :, hid:], gb[0, :, n]) + tn(ly[1, :, hid:], gb[1, :, n])

        columns(shared_grads)

        @pl.when(i < 7)
        def _():
            for c in loads(i + 1):
                c.start()

    def second_part(i):
        logits = mm(rr[...], wr[...])
        lane = lax.broadcasted_iota(jnp.int32, logits.shape, 1)
        logits = jnp.where(lane < 16, logits, -jnp.inf)
        e = jnp.exp(logits - jnp.max(logits, axis=1, keepdims=True))
        gate = jnp.sum(jnp.where(lane == me, e, 0.0), axis=1, keepdims=True) / jnp.sum(
            e, axis=1, keepdims=True
        )
        pre = nt(rg[...], wd[...])
        act, d_a, d_b = gate_parts(mm(rr[...], wg[...]), mm(rr[...], wu[...]), gate * pre)
        low = act.astype(jnp.bfloat16)
        back = low.astype(jnp.float32)
        d_gate = jnp.sum(back * pre, axis=1, keepdims=True)
        acts[...] = (gate * back).astype(jnp.bfloat16)
        das[...] = d_a.astype(jnp.bfloat16)
        dbs[...] = d_b.astype(jnp.bfloat16)

        def spread(n):
            o = (gate * mm(low, wd[:, n])).astype(jnp.bfloat16)
            s = (nt(das[...], wg[n]) + nt(dbs[...], wu[n])).astype(jnp.bfloat16)
            for q in range(2):
                ry[q, :hid, n] = o[q * hid : (q + 1) * hid]
                rd[q, :hid, n] = s[q * hid : (q + 1) * hid]

        columns(spread)
        for c in outs(i):
            c.start()
        return jnp.where(lane == me, d_gate, 0.0).astype(jnp.bfloat16)

    def third_part(i, d_cols):
        k, half = i // 2, i % 2
        b = plane_at(z, 3 - k) * 4 + jnp.where(half == 0, 1 - y, y) * 2

        @pl.when(i > 0)
        def _():
            sib_send(i - 1).wait_send()

        def store(q, n, v):
            v = v.astype(jnp.bfloat16)
            mine = jnp.where(core == 0, v[:128], v[128:])
            theirs = jnp.where(core == 0, v[128:], v[:128])
            own[b + q, 0, :, n] = mine[:64]
            own[b + q, 1, :, n] = mine[64:]
            sib[q, 0, :, n] = theirs[:64]
            sib[q, 1, :, n] = theirs[64:]

        def put(m, _):
            n = pl.ds(pl.multiple_of(m * cut, cut), cut)
            n2 = pl.ds(pl.multiple_of(width + m * cut, cut), cut)
            for q in range(2):
                store(q, n, mm(ly[q], ry[q, :, n]))
                store(q, n2, mm(ld[q], rd[q, :, n]))
            return 0

        lax.fori_loop(0, width // cut, put, 0)
        for q in range(2):
            store(q, pl.ds(2 * width, 128), mm(pt_of(q), d_cols[q * hid : (q + 1) * hid]))
        sib_send(i).start()

    def pt_of(q):
        return ly[q, :, :hid]

    def staged(src, dst, sem):
        return pltpu.make_async_copy(src, dst, sem)

    def blk(zp, yy, xx):
        return zp * 4 + yy * 2 + xx

    def pair_sum(i):
        k, half = i // 2, i % 2
        zp = plane_at(z, 3 - k)
        b = zp * 4 + jnp.where(half == 0, 1 - y, y) * 2
        sib_send(i).wait_recv()
        c = staged(sibr.at[i], stage, st_sem.at[0])
        c.start()
        c.wait()

        def one(q, _):
            add_into(own.at[b + q, 0], stage.at[q, 0])
            add_into(own.at[b + q, 1], stage.at[q, 1])
            return 0

        lax.fori_loop(0, 2, one, 0)

        @pl.when(half == 0)
        def _():
            y_(0, blk(zp, 1 - y, 1 - x), 0, zp).start()
            x_(0, blk(zp, 1 - y, 1 - x), 1, zp).start()
            y_(1, blk(zp, 1 - y, x), 0, zp).start()

        @pl.when(half == 1)
        def _():
            x_(1, blk(zp, y, 1 - x), 1, zp).start()

    def second_hop(k):
        zp = plane_at(z, 3 - k)
        mine = blk(zp, y, x)
        y_(0, blk(zp, 1 - y, 1 - x), 0, zp).wait_recv()
        c0 = staged(yr.at[zp, 0], stage.at[0, 0], st_sem.at[0])
        c0.start()
        x_(0, blk(zp, 1 - y, 1 - x), 1, zp).wait_recv()
        c1 = staged(xr.at[zp, 0], stage.at[0, 1], st_sem.at[1])
        c1.start()
        c0.wait()
        add_into(own.at[blk(zp, y, 1 - x), 0], stage.at[0, 0])
        x_(2, blk(zp, y, 1 - x), 0, zp).start()
        c1.wait()
        add_into(own.at[blk(zp, 1 - y, x), 1], stage.at[0, 1])
        y_(2, blk(zp, 1 - y, x), 1, zp).start()
        y_(1, blk(zp, 1 - y, x), 0, zp).wait_recv()
        c2 = staged(yr.at[zp, 1], stage.at[1, 0], st_sem.at[2])
        c2.start()
        x_(1, blk(zp, y, 1 - x), 1, zp).wait_recv()
        c3 = staged(xr.at[zp, 1], stage.at[1, 1], st_sem.at[3])
        c3.start()
        c2.wait()
        add_into(own.at[mine, 0], stage.at[1, 0])
        c3.wait()
        add_into(own.at[mine, 1], stage.at[1, 1])

    def last_hop(k):
        zp = plane_at(z, 3 - k)
        mine = blk(zp, y, x)
        x_(2, blk(zp, y, 1 - x), 0, zp).wait_recv()
        c0 = staged(xr.at[zp, 2], stage.at[0, 0], st_sem.at[0])
        c0.start()
        y_(2, blk(zp, 1 - y, x), 1, zp).wait_recv()
        c1 = staged(yr.at[zp, 2], stage.at[0, 1], st_sem.at[1])
        c1.start()
        c0.wait()
        add_into(own.at[mine, 0], stage.at[0, 0])
        c1.wait()
        add_into(own.at[mine, 1], stage.at[0, 1])

        def arrived(d):
            zc(zp, me, d).wait_recv()
            c = staged(zr.at[d, zp], stage.at[1], st_sem.at[2])
            c.start()
            c.wait()
            add_into(own.at[mine, 0], stage.at[1, 0])
            add_into(own.at[mine, 1], stage.at[1, 1])

        pl.when((zp <= z) & (z < 3))(lambda: arrived(1))
        pl.when((zp >= z) & (z > 0))(lambda: arrived(0))
        pl.when(zp < z)(lambda: zc(zp, dn, 1).start())
        pl.when(zp > z)(lambda: zc(zp, up, 0).start())

    def step(i, _):
        pl.when(i < 8)(lambda: first_part(i))
        pl.when((i >= 1) & (i <= 8))(lambda: pair_sum(i - 1))
        pl.when((i % 2 == 0) & (i >= 4) & (i <= 10))(lambda: second_hop((i - 4) // 2))
        pl.when((i % 2 == 1) & (i >= 7) & (i <= 13))(lambda: last_hop((i - 7) // 2))

        @pl.when(i < 8)
        def _():
            third_part(i, second_part(i))

        return 0

    lax.fori_loop(0, 14, step, 0)
    for a in range(2):

        def row(n, _):
            r = pl.ds(pl.multiple_of(n * 16, 16), 16)
            o_out[core, a, r] = own[me, a, r]
            return 0

        lax.fori_loop(0, 4, row, 0)
    f = rc(o_out.at[core], o_out.at[core], fs, fr, me, other)
    f.start()
    for c in outs(7):
        c.wait()
    sib_send(7).wait_send()
    for k in range(4):
        for j in range(3):
            x_(j, 0, 0, k).wait_send()
            y_(j, 0, 0, k).wait_send()

        @pl.when(k != z)
        def _():
            zc(k, up, 0).wait_send()

    rc(o_out.at[core], o_out.at[other], fs, fr, me, other).wait_recv()
    f.wait_send()


def moe_call(moe, grd, pick, pick_t, wg, wu, wd, wr, sgu, sdn, cid):
    width, ffe = wg.shape
    total = 2 * width + 128
    slots = pick.shape[0] * pick.shape[1]
    low, S, V = jnp.bfloat16, pltpu.SemaphoreType.DMA, pltpu.VMEM
    any_, vmem = pl.BlockSpec(memory_space=pl.ANY), pl.BlockSpec(memory_space=pltpu.VMEM)
    shape = lambda *s: jax.ShapeDtypeStruct(s, low)
    blk = (2, 64, total)
    return pl.pallas_call(
        moe_kernel,
        out_shape=[
            shape(2, *blk), shape(slots, width), shape(slots, width), shape(slots, ffe), shape(slots, ffe),
            shape(slots, ffe), jax.ShapeDtypeStruct((384, width), jnp.float32),
            shape(8, 2, *blk), shape(4, 3, 64, total), shape(4, 3, 64, total), shape(2, 4, *blk),
        ],
        in_specs=[any_] * 4 + [vmem] * 6,
        out_specs=[vmem] + [any_] * 5 + [vmem] + [any_] * 4,
        scratch_shapes=[
            V((16,) + blk, low), V((2,) + blk, low), V((2,) + blk, low),
            V((2, 256, width), low), V((2, 256, width), low), V((2, 128, 256), low), V((2, 256, 128), low),
            V((256, width), low), V((256, width), low), V((2, 256, 256), low), V((2, 256, 384), low),
            V((2, 256, width), low), V((2, 384, width), low),
            V((256, ffe), low), V((256, ffe), low), V((256, ffe), low),
            S((4,)), S((5,)), S((4,)), S, S((8,)), S((4, 3)), S((4, 3)), S((4, 3)), S((4, 3)), S((4,)), S((2, 4)), S, S,
        ],
        compiler_params=pltpu.CompilerParams(collective_id=cid, has_side_effects=True, vmem_limit_bytes=60 << 20),
        cost_estimate=pl.CostEstimate(flops=65 * 10**9, bytes_accessed=80 * 10**6, transcendentals=0),
    )(moe, grd, pick, pick_t, wg, wu, wd, wr, sgu, sdn)


def swapped(v):
    return lax.ppermute(v, "tensor", [(0, 1), (1, 0)])


def summed(v):
    low = lax.reduce_precision(v, 8, 7)
    return low + swapped(low.astype(jnp.bfloat16)).astype(jnp.float32)


def my_half(v, rows):
    return lax.dynamic_slice_in_dim(v, lax.axis_index("tensor") * rows, rows, 0)


def gather_rows(v, cid):
    rows, width = v.shape[0] // 2, v.shape[1]
    moved = ag16(my_half(v, rows).reshape(2, rows // 2, width), True, cid)
    return moved.reshape(32 * rows, width)


def scatter_rows(v, cid):
    rows, width = v.shape[0] // 32, v.shape[1]
    return rs16(v.reshape(16, 2, 2, rows // 2, width), True, cid).reshape(2 * rows, width)


def gather_background(v):
    rows, width = v.shape[0] // 2, v.shape[1]
    moved = lax.all_gather(my_half(v, rows), "dp", axis=0)
    theirs = swapped(moved)
    core = lax.axis_index("tensor")
    pair = jnp.stack([jnp.where(core == 0, moved, theirs), jnp.where(core == 0, theirs, moved)], 1)
    return pair.reshape(-1, width)


def scatter_background(v):
    rows, width = v.shape[0] // 32, v.shape[1]
    core = lax.axis_index("tensor")
    cut = v.reshape(16, 2, rows, width)
    keep = lax.dynamic_index_in_dim(cut, core, 1, keepdims=False)
    give = lax.dynamic_index_in_dim(cut, 1 - core, 1, keepdims=False)
    pair = (keep.astype(jnp.float32) + swapped(give).astype(jnp.float32)).astype(jnp.bfloat16)
    mine = lax.psum_scatter(pair.reshape(16 * rows, width), "dp", scatter_dimension=0, tiled=True)
    theirs = swapped(mine)
    return jnp.where(
        core == 0, jnp.concatenate([mine, theirs]), jnp.concatenate([theirs, mine])
    ).astype(jnp.float32)


def exchange(parts):
    return lax.all_to_all(parts, "dp", split_axis=0, concat_axis=0, tiled=True)


def shards_sixteen(
    tokens,
    out_grad,
    segments,
    routes,
    attn_gain,
    w_query,
    w_latent,
    latent_gain,
    w_keyval,
    w_out,
    moe_gain,
    w_router,
    shared_gate,
    shared_up,
    shared_down,
    expert_gate,
    routed_up_weight,
    expert_down,
):
    n_rows, width = tokens.shape
    dp_count = lax.axis_size("dp")
    dp_index = lax.axis_index("dp")
    seq_len = segments.shape[1]
    total = n_rows * dp_count
    hop_count = (WINDOW - 1) // n_rows + 1
    n_keys = (hop_count + 1) * n_rows
    experts = w_router.shape[1]
    capacity = 4 * n_rows * TOPK // (3 * experts)
    score_scale = (NOPE + ROPE) ** (-0.5)
    row_start = dp_index * n_rows
    seg_row = segments[0]
    depth = w_query.shape[0]
    q_width, o_width, kv_width = w_query.shape[1], w_out.shape[0], w_keyval.shape[1]
    kv_rows = w_keyval.shape[0]
    kv_cuts = depth // kv_rows
    kv_part = kv_width // kv_cuts
    lat_width = w_latent.shape[1]
    route_width = n_rows * TOPK // depth
    small = (lat_width + experts + 3 + route_width + 127) // 128 * 128

    shared_part = shared_gate.shape[1] // dp_count
    shared_send = jnp.stack(
        [
            shared_gate.reshape(depth, dp_count, shared_part).transpose(1, 2, 0),
            shared_up.reshape(depth, dp_count, shared_part).transpose(1, 2, 0),
            shared_down.reshape(dp_count, shared_part, depth),
        ],
        1,
    )
    shared_all = exchange(shared_send).transpose(1, 2, 0, 3).reshape(3, shared_part, width)
    lead = jnp.pad(shared_all, ((0, 0), (0, 128 - shared_part), (0, 0)))
    shared_in, shared_out = lead[:2].reshape(256, width), lead[2]

    gains = jnp.stack(
        [attn_gain, moe_gain, jnp.pad(latent_gain, (0, depth - kv_rows))], 1
    )
    packed = jnp.concatenate(
        [
            w_query,
            w_out.T,
            w_keyval.reshape(kv_rows, kv_cuts, kv_part).transpose(1, 0, 2).reshape(depth, kv_part),
            w_latent,
            w_router,
            gains,
            routes.reshape(depth, route_width).astype(jnp.bfloat16),
            jnp.zeros((depth, small - lat_width - experts - 3 - route_width), jnp.bfloat16),
        ],
        1,
    )
    pack_width = packed.shape[1]
    weights = ag16(packed.reshape(2, depth // 2, pack_width), False, 1).reshape(width, pack_width)
    at = 0
    wq_full = weights[:, at : at + q_width]
    at += q_width
    wo_t = weights[:, at : at + o_width]
    at += o_width
    wkv_full = (
        weights[:, at : at + kv_part]
        .reshape(dp_count, kv_cuts, kv_rows, kv_part)
        .transpose(0, 2, 1, 3)
        .reshape(dp_count * kv_rows, kv_width)
    )
    at += kv_part
    wlat_full = weights[:, at : at + lat_width]
    at += lat_width
    wr_full = weights[:, at : at + experts]
    at += experts
    gain_attn = weights[:, at].astype(jnp.float32)
    gain_moe = weights[:, at + 1].astype(jnp.float32)
    gain_latent = (
        weights[:, at + 2].reshape(dp_count, depth)[:, :kv_rows].reshape(-1).astype(jnp.float32)
    )

    all_routes = (
        weights[:, at + 3 : at + 3 + route_width].reshape(total, TOPK).astype(jnp.int32)
    )
    grad_all = gather_background(out_grad)

    local_heads = q_width // (NOPE + ROPE)
    positions = (row_start + jnp.arange(n_rows, dtype=jnp.int32)).astype(jnp.float32)
    cos_tab, sin_tab = rope_tables(positions)
    resid_in = tokens.astype(jnp.float32)
    normed, attn_norm_back = jax.vjp(rms_scale, resid_in, gain_attn)
    normed_low = normed.astype(jnp.bfloat16)

    def rope_queries(q_flat):
        shaped = q_flat.reshape(n_rows, local_heads, NOPE + ROPE)
        return jnp.concatenate(
            [shaped[..., :NOPE], rotate(shaped[..., NOPE:], cos_tab[:, None], sin_tab[:, None])], -1
        )

    queries, query_back = jax.vjp(rope_queries, matmul(normed_low, wq_full))
    query_low = queries.astype(jnp.bfloat16)

    def latent_piece(latent_raw, gain_vec):
        return (
            rms_scale(latent_raw[:, :RANK], gain_vec),
            rotate(latent_raw[:, RANK:], cos_tab, sin_tab),
        )

    (latent, key_rope), latent_back = jax.vjp(
        latent_piece, matmul(normed_low, wlat_full), gain_latent
    )
    own_keys = jnp.concatenate([latent.astype(jnp.bfloat16), key_rope.astype(jnp.bfloat16)], 1)
    keys_all = jnp.concatenate(
        [passed_along(own_keys, "dp", d) for d in range(hop_count, 0, -1)] + [own_keys], 0
    )
    keys_latent, keys_rope = keys_all[:, :RANK], keys_all[:, RANK:]
    keyval = (
        matmul(keys_latent, wkv_full).astype(jnp.bfloat16).reshape(n_keys, local_heads, NOPE + VDIM)
    )
    key_nope = keyval[..., :NOPE]
    values = keyval[..., NOPE:]
    key_pos = row_start - hop_count * n_rows + jnp.arange(n_keys, dtype=jnp.int32)
    query_pos = row_start + jnp.arange(n_rows, dtype=jnp.int32)
    padded_seg = jnp.concatenate([jnp.full((hop_count * n_rows,), -1, jnp.int32), seg_row])
    key_seg = lax.dynamic_slice_in_dim(padded_seg, row_start, n_keys, 0)
    query_seg = lax.dynamic_slice_in_dim(seg_row, row_start, n_rows, 0)
    allowed = (key_pos[None, :] >= 0) & (key_pos[None, :] <= query_pos[:, None])
    allowed = (
        allowed
        & (query_pos[:, None] - key_pos[None, :] < WINDOW)
        & (query_seg[:, None] == key_seg[None, :])
    )

    def masked_scores():
        nope_part = jnp.einsum(
            "qhd,khd->hqk", query_low[..., :NOPE], key_nope, preferred_element_type=jnp.float32
        )
        rope_part = jnp.einsum(
            "qhr,kr->hqk", query_low[..., NOPE:], keys_rope, preferred_element_type=jnp.float32
        )
        return jnp.where(allowed[None], score_scale * (nope_part + rope_part), -jnp.inf)

    scores = masked_scores()
    top_score = jnp.max(scores, axis=-1, keepdims=True)
    exp_scores = jnp.exp(scores - top_score)
    denom = jnp.sum(exp_scores, axis=-1, keepdims=True)
    attn_probs = exp_scores / denom
    log_total = top_score + jnp.log(denom)
    attended = jnp.einsum(
        "hqk,khv->qhv", attn_probs.astype(jnp.bfloat16), values, preferred_element_type=jnp.float32
    )
    attended_low = attended.astype(jnp.bfloat16).reshape(n_rows, local_heads * VDIM)
    middle = resid_in + summed(matmul_nt(attended_low, wo_t))
    moe_normed, moe_norm_back = jax.vjp(rms_scale, middle, gain_moe)
    moe_low = moe_normed.astype(jnp.bfloat16)
    router, router_back = jax.vjp(
        lambda logit_vals: jax.nn.softmax(logit_vals, axis=-1), matmul(moe_low, wr_full)
    )

    moe_all = gather_rows(moe_low, 3)
    chosen = jnp.any(all_routes == dp_index, axis=1).reshape(dp_count, n_rows)
    earlier = jnp.arange(n_rows)[:, None] < jnp.arange(n_rows)[None, :]
    rank = matmul(chosen.astype(jnp.bfloat16), earlier.astype(jnp.bfloat16)).astype(jnp.int32)
    pick = (
        (rank[:, None, :] == jnp.arange(capacity, dtype=jnp.int32)[None, :, None])
        & chosen[:, None, :]
    ).astype(jnp.bfloat16)

    slot_rows = dp_count * capacity
    moe_wr = jnp.pad(wr_full, ((0, 0), (0, 128 - experts)))
    home, rows_in, rows_grad, scaled_act, d_ea_low, d_eb_low, shared_grads = moe_call(
        moe_all.reshape(dp_count, n_rows, width),
        grad_all.reshape(dp_count, n_rows, width),
        pick,
        pick.transpose(0, 2, 1),
        expert_gate[0],
        routed_up_weight[0],
        expert_down[0],
        moe_wr,
        shared_in,
        shared_out,
        4,
    )[:7]
    home = home.reshape(n_rows, 2 * width + 128)
    result = (middle + home[:, :width].astype(jnp.float32)).astype(jnp.bfloat16)
    d_home = home[:, width:].astype(jnp.float32)
    grad_down = matmul_tn(scaled_act, rows_grad)[None]
    grad_gate = matmul_tn(rows_in, d_ea_low)[None]
    grad_up = matmul_tn(rows_in, d_eb_low)[None]
    shared_home = exchange(
        shared_grads.astype(jnp.bfloat16)
        .reshape(3, 128, dp_count, depth)[:, :shared_part]
        .transpose(2, 0, 1, 3)
    ).astype(jnp.float32)
    shared_home = shared_home.transpose(1, 0, 2, 3).reshape(3, dp_count * shared_part, depth)
    grad_sgate, grad_sup, grad_sdown = shared_home[0].T, shared_home[1].T, shared_home[2]

    grad_y = out_grad.astype(jnp.float32)
    d_gate_all = d_home[:, width : width + experts]
    routed_here = jnp.any(
        routes[:, :, None] == jnp.arange(experts, dtype=jnp.int32)[None, None, :], axis=1
    )
    (d_logits,) = router_back(jnp.where(routed_here, d_gate_all, 0.0))
    d_logits_low = d_logits.astype(jnp.bfloat16)
    grad_router = matmul_tn(moe_low, d_logits_low)
    d_moe = d_home[:, :width] + matmul_nt(d_logits_low, wr_full)
    d_mid_norm, grad_gain_moe = moe_norm_back(d_moe)
    d_middle = grad_y + d_mid_norm
    d_middle_low = d_middle.astype(jnp.bfloat16)
    grad_wo_t = matmul_tn(d_middle_low, attended_low)
    d_att_low = matmul(d_middle_low, wo_t).astype(jnp.bfloat16).reshape(n_rows, local_heads, VDIM)
    again_probs = jnp.exp(masked_scores() - log_total)
    d_values = jnp.einsum(
        "hqk,qhv->khv",
        again_probs.astype(jnp.bfloat16),
        d_att_low,
        preferred_element_type=jnp.float32,
    )
    d_probs = jnp.einsum("qhv,khv->hqk", d_att_low, values, preferred_element_type=jnp.float32)
    d_scores = (
        again_probs * (d_probs - jnp.sum(d_probs * again_probs, axis=-1, keepdims=True))
    ).astype(jnp.bfloat16)
    d_query_nope = score_scale * jnp.einsum(
        "hqk,khd->qhd", d_scores, key_nope, preferred_element_type=jnp.float32
    )
    d_query_rope = score_scale * jnp.einsum(
        "hqk,kr->qhr", d_scores, keys_rope, preferred_element_type=jnp.float32
    )
    d_key_nope = score_scale * jnp.einsum(
        "hqk,qhd->khd", d_scores, query_low[..., :NOPE], preferred_element_type=jnp.float32
    )
    d_key_rope = score_scale * jnp.einsum(
        "hqk,qhr->kr", d_scores, query_low[..., NOPE:], preferred_element_type=jnp.float32
    )
    (d_q_raw,) = query_back(jnp.concatenate([d_query_nope, d_query_rope], -1))
    d_q_low = d_q_raw.astype(jnp.bfloat16)
    grad_wq = matmul_tn(normed_low, d_q_low)
    d_kv_low = (
        jnp.concatenate([d_key_nope, d_values], -1)
        .astype(jnp.bfloat16)
        .reshape(n_keys, local_heads * (NOPE + VDIM))
    )
    grad_wkv = matmul_tn(keys_latent, d_kv_low)
    d_keys = jnp.concatenate([matmul_nt(d_kv_low, wkv_full), d_key_rope], 1)
    d_own = d_keys[hop_count * n_rows :]
    d_keys_low = d_keys.astype(jnp.bfloat16)
    for distance in range(hop_count, 0, -1):
        lower = (hop_count - distance) * n_rows
        d_own = d_own + passed_along(
            d_keys_low[lower : lower + n_rows], "dp", -distance
        ).astype(jnp.float32)
    both = summed(jnp.concatenate([matmul_nt(d_q_low, wq_full), d_own], 1))
    d_normed, own_latent, own_rope = (
        both[:, :width],
        both[:, width : width + RANK],
        both[:, width + RANK :],
    )
    d_latent_raw, grad_gain_latent = latent_back((own_latent, own_rope))
    d_latent_low = d_latent_raw.astype(jnp.bfloat16)
    grad_wlat = matmul_tn(normed_low, d_latent_low)
    d_normed = d_normed + matmul_nt(d_latent_low, wlat_full)
    d_tokens_norm, grad_gain_attn = attn_norm_back(d_normed)
    token_input_gradient = d_middle + d_tokens_norm

    grad_gains = jnp.stack(
        [
            grad_gain_attn.reshape(dp_count, depth),
            grad_gain_moe.reshape(dp_count, depth),
            jnp.pad(grad_gain_latent.reshape(dp_count, kv_rows), ((0, 0), (0, depth - kv_rows))),
        ],
        2,
    ).reshape(width, 3)
    grads = jnp.concatenate(
        [
            grad_wq.astype(jnp.bfloat16),
            grad_wo_t.astype(jnp.bfloat16),
            grad_wkv.astype(jnp.bfloat16)
            .reshape(dp_count, kv_rows, kv_cuts, kv_part)
            .transpose(0, 2, 1, 3)
            .reshape(width, kv_part),
            grad_wlat.astype(jnp.bfloat16),
            grad_router.astype(jnp.bfloat16),
            grad_gains.astype(jnp.bfloat16),
            jnp.zeros((width, small - lat_width - experts - 3), jnp.bfloat16),
        ],
        1,
    )
    mine = (
        rs16(grads.reshape(dp_count, 1, 2, depth // 2, pack_width), False, 6)
        .reshape(depth, pack_width)
        .astype(jnp.float32)
    )
    at = 0
    out_wq = mine[:, at : at + q_width]
    at += q_width
    out_wo = mine[:, at : at + o_width].T
    at += o_width
    out_wkv = (
        mine[:, at : at + kv_part]
        .reshape(kv_cuts, kv_rows, kv_part)
        .transpose(1, 0, 2)
        .reshape(kv_rows, kv_width)
    )
    at += kv_part
    out_wlat = mine[:, at : at + lat_width]
    at += lat_width
    out_router = mine[:, at : at + experts]
    at += experts
    return (
        result,
        token_input_gradient,
        mine[:, at],
        out_wq,
        out_wlat,
        mine[:kv_rows, at + 2],
        out_wkv,
        out_wo,
        mine[:, at + 1],
        out_router,
        grad_sgate,
        grad_sup,
        grad_sdown,
        grad_gate,
        grad_up,
        grad_down,
    )


def shards_general(
    tokens,
    out_grad,
    segments,
    routes,
    attn_gain,
    w_query,
    w_latent,
    latent_gain,
    w_keyval,
    w_out,
    moe_gain,
    w_router,
    shared_gate,
    shared_up,
    shared_down,
    expert_gate,
    routed_up_weight,
    expert_down,
):
    n_rows = tokens.shape[0]
    model_width = tokens.shape[1]
    dp_count = lax.axis_size("dp")
    dp_index = lax.axis_index("dp")
    seq_len = segments.shape[1]
    seq_devs = seq_len // n_rows
    hop_count = (WINDOW - 1) // n_rows + 1
    n_keys = (hop_count + 1) * n_rows
    experts = w_router.shape[1]
    local_experts = expert_gate.shape[0]
    capacity = 4 * n_rows * TOPK // (3 * experts)
    slot_total = experts * capacity
    score_scale = (NOPE + ROPE) ** (-0.5)
    row_start = dp_index % seq_devs * n_rows
    seg_row = lax.dynamic_index_in_dim(segments, dp_index // seq_devs, 0, keepdims=False)
    gathered = (
        lax.all_gather(attn_gain, "dp", axis=0, tiled=True),
        lax.all_gather(w_query, "dp", axis=0, tiled=True),
        lax.all_gather(w_latent, "dp", axis=0, tiled=True),
        lax.all_gather(latent_gain, "dp", axis=0, tiled=True),
        lax.all_gather(w_keyval, "dp", axis=0, tiled=True),
        lax.all_gather(w_out, "dp", axis=1, tiled=True),
        lax.all_gather(moe_gain, "dp", axis=0, tiled=True),
        lax.all_gather(w_router, "dp", axis=0, tiled=True),
        lax.all_gather(shared_gate, "dp", axis=0, tiled=True),
        lax.all_gather(shared_up, "dp", axis=0, tiled=True),
        lax.all_gather(shared_down, "dp", axis=1, tiled=True),
    )
    (
        gain_attn,
        wq_full,
        wlat_full,
        gain_latent,
        wkv_full,
        wo_full,
        gain_moe,
        wr_full,
        sgate_full,
        sup_full,
        sdown_full,
    ) = gathered
    local_heads = wq_full.shape[1] // (NOPE + ROPE)
    positions = (row_start + jnp.arange(n_rows, dtype=jnp.int32)).astype(jnp.float32)
    cos_tab, sin_tab = rope_tables(positions)
    resid_in = tokens.astype(jnp.float32)
    normed, attn_norm_back = jax.vjp(rms_scale, resid_in, gain_attn.astype(jnp.float32))
    normed_low = normed.astype(jnp.bfloat16)

    def rope_queries(q_flat):
        shaped = q_flat.reshape(n_rows, local_heads, NOPE + ROPE)
        return jnp.concatenate(
            [shaped[..., :NOPE], rotate(shaped[..., NOPE:], cos_tab[:, None], sin_tab[:, None])], -1
        )

    queries, query_back = jax.vjp(rope_queries, matmul(normed_low, wq_full))
    query_low = queries.astype(jnp.bfloat16)

    def latent_piece(latent_raw, gain_vec):
        return (
            rms_scale(latent_raw[:, :RANK], gain_vec),
            rotate(latent_raw[:, RANK:], cos_tab, sin_tab),
        )

    (latent, key_rope), latent_back = jax.vjp(
        latent_piece, matmul(normed_low, wlat_full), gain_latent.astype(jnp.float32)
    )
    latent_low = latent.astype(jnp.bfloat16)
    rope_low = key_rope.astype(jnp.bfloat16)
    latent_parts = []
    rope_parts = []
    for distance in range(hop_count, 0, -1):
        moved_latent, moved_rope = passed_along((latent_low, rope_low), "dp", distance)
        latent_parts.append(moved_latent)
        rope_parts.append(moved_rope)
    keys_latent = jnp.concatenate(latent_parts + [latent_low], 0)
    keys_rope = jnp.concatenate(rope_parts + [rope_low], 0)
    keyval = (
        matmul(keys_latent, wkv_full).astype(jnp.bfloat16).reshape(n_keys, local_heads, NOPE + VDIM)
    )
    key_nope = keyval[..., :NOPE]
    values = keyval[..., NOPE:]
    key_pos = row_start - hop_count * n_rows + jnp.arange(n_keys, dtype=jnp.int32)
    query_pos = row_start + jnp.arange(n_rows, dtype=jnp.int32)
    padded_seg = jnp.concatenate([jnp.full((hop_count * n_rows,), -1, jnp.int32), seg_row])
    key_seg = lax.dynamic_slice_in_dim(padded_seg, row_start, n_keys, 0)
    query_seg = lax.dynamic_slice_in_dim(seg_row, row_start, n_rows, 0)
    allowed = (key_pos[None, :] >= 0) & (key_pos[None, :] <= query_pos[:, None])
    allowed = (
        allowed
        & (query_pos[:, None] - key_pos[None, :] < WINDOW)
        & (query_seg[:, None] == key_seg[None, :])
    )

    def masked_scores():
        nope_part = jnp.einsum(
            "qhd,khd->hqk", query_low[..., :NOPE], key_nope, preferred_element_type=jnp.float32
        )
        rope_part = jnp.einsum(
            "qhr,kr->hqk", query_low[..., NOPE:], keys_rope, preferred_element_type=jnp.float32
        )
        return jnp.where(allowed[None], score_scale * (nope_part + rope_part), -jnp.inf)

    scores = masked_scores()
    top_score = jnp.max(scores, axis=-1, keepdims=True)
    exp_scores = jnp.exp(scores - top_score)
    denom = jnp.sum(exp_scores, axis=-1, keepdims=True)
    attn_probs = exp_scores / denom
    log_total = top_score + jnp.log(denom)
    attended = jnp.einsum(
        "hqk,khv->qhv", attn_probs.astype(jnp.bfloat16), values, preferred_element_type=jnp.float32
    )
    attended_low = attended.astype(jnp.bfloat16).reshape(n_rows, local_heads * VDIM)
    attn_out = lax.psum(matmul(attended_low, wo_full).astype(jnp.bfloat16), "tensor").astype(
        jnp.float32
    )
    middle = resid_in + attn_out
    moe_normed, moe_norm_back = jax.vjp(rms_scale, middle, gain_moe.astype(jnp.float32))
    moe_low = moe_normed.astype(jnp.bfloat16)
    router, router_back = jax.vjp(
        lambda logit_vals: jax.nn.softmax(logit_vals, axis=-1), matmul(moe_low, wr_full)
    )
    expert_ids = jnp.arange(experts, dtype=jnp.int32)
    route_hot = (routes[:, :, None] == expert_ids[None, None, :]).astype(jnp.float32)
    gate_w = jnp.einsum("te,tke->tk", router, route_hot, precision=highest)
    flat_routes = routes.reshape(-1)
    assign_count = flat_routes.shape[0]
    flat_hot = (flat_routes[:, None] == expert_ids[None, :]).astype(jnp.int32)
    earlier = ranks_before(flat_hot)
    slot_in = jnp.sum(earlier * flat_hot, axis=1)
    target = flat_routes * capacity + slot_in
    assign_ids = jnp.arange(assign_count, dtype=jnp.int32)
    assign_of_slot = jnp.zeros((slot_total,), jnp.int32).at[target].set(assign_ids)
    slot_live = (
        jnp.zeros((slot_total,), jnp.bfloat16)
        .at[target]
        .set(jnp.ones((assign_count,), jnp.bfloat16))
    )
    send_rows = moe_low[assign_of_slot // TOPK] * slot_live[:, None]
    recv_rows = lax.all_to_all(
        send_rows.reshape(dp_count, local_experts * capacity, model_width),
        "dp",
        split_axis=0,
        concat_axis=0,
        tiled=True,
    )
    received_four_parts = recv_rows.reshape(dp_count, local_experts, capacity, model_width)
    exp_gate = jnp.einsum(
        "sjcd,jdf->sjcf", received_four_parts, expert_gate, preferred_element_type=jnp.float32
    )
    exp_up = jnp.einsum(
        "sjcd,jdf->sjcf", received_four_parts, routed_up_weight, preferred_element_type=jnp.float32
    )
    exp_act, exp_act_back = jax.vjp(gated_act, exp_gate, exp_up)
    exp_act_low = exp_act.astype(jnp.bfloat16)
    exp_result = jnp.einsum(
        "sjcf,jfd->sjcd", exp_act_low, expert_down, preferred_element_type=jnp.float32
    )
    returned = lax.all_to_all(
        exp_result.reshape(dp_count, local_experts * capacity, model_width).astype(jnp.bfloat16),
        "dp",
        split_axis=0,
        concat_axis=0,
        tiled=True,
    ).astype(jnp.float32)
    per_assign = returned.reshape(slot_total, model_width)[target].reshape(
        n_rows, TOPK, model_width
    )
    routed = jnp.einsum("tk,tkd->td", gate_w, per_assign, precision=highest)
    shared_a = matmul(moe_low, sgate_full)
    shared_b = matmul(moe_low, sup_full)
    shared_act, shared_back = jax.vjp(gated_act, shared_a, shared_b)
    shared_low = shared_act.astype(jnp.bfloat16)
    moe_out = lax.psum(
        (routed + matmul(shared_low, sdown_full)).astype(jnp.bfloat16), "tensor"
    ).astype(jnp.float32)
    result = (middle + moe_out).astype(jnp.bfloat16)
    grad_y = out_grad.astype(jnp.float32)
    grad_sdown = matmul_tn(shared_low, out_grad)
    d_shared_a, d_shared_b = shared_back(matmul_nt(out_grad, sdown_full))
    d_sa_low = d_shared_a.astype(jnp.bfloat16)
    d_sb_low = d_shared_b.astype(jnp.bfloat16)
    grad_sgate = matmul_tn(moe_low, d_sa_low)
    grad_sup = matmul_tn(moe_low, d_sb_low)
    d_moe = matmul_nt(d_sa_low, sgate_full) + matmul_nt(d_sb_low, sup_full)
    d_gate_part = jnp.einsum("td,tkd->tk", grad_y, per_assign, precision=highest)
    d_assign = (
        (gate_w[:, :, None] * grad_y[:, None, :])
        .astype(jnp.bfloat16)
        .reshape(assign_count, model_width)
    )
    send_grads = d_assign[assign_of_slot] * slot_live[:, None]
    recv_grads = lax.all_to_all(
        send_grads.reshape(dp_count, local_experts * capacity, model_width),
        "dp",
        split_axis=0,
        concat_axis=0,
        tiled=True,
    )
    recv_grads = recv_grads.reshape(dp_count, local_experts, capacity, model_width)
    expert_down_weight_gradient = jnp.einsum(
        "sjcf,sjcd->jfd", exp_act_low, recv_grads, preferred_element_type=jnp.float32
    )
    d_exp_act = jnp.einsum(
        "sjcd,jfd->sjcf", recv_grads, expert_down, preferred_element_type=jnp.float32
    )
    d_exp_gate, expert_up_act_gradient = exp_act_back(d_exp_act)
    d_egate_low = d_exp_gate.astype(jnp.bfloat16)
    expert_up_gradient_lowp = expert_up_act_gradient.astype(jnp.bfloat16)
    expert_gate_weight_gradient = jnp.einsum(
        "bmky,bmkx->myx", received_four_parts, d_egate_low, preferred_element_type=jnp.float32
    )
    expert_up_weight_gradient = jnp.einsum(
        "bmky,bmkx->myx",
        received_four_parts,
        expert_up_gradient_lowp,
        preferred_element_type=jnp.float32,
    )
    d_slots = jnp.einsum(
        "hteg,tmg->htem", d_egate_low, expert_gate, preferred_element_type=jnp.float32
    )
    d_slots = d_slots + jnp.einsum(
        "hteg,tmg->htem",
        expert_up_gradient_lowp,
        routed_up_weight,
        preferred_element_type=jnp.float32,
    )
    back_grads = lax.all_to_all(
        d_slots.reshape(dp_count, local_experts * capacity, model_width).astype(jnp.bfloat16),
        "dp",
        split_axis=0,
        concat_axis=0,
        tiled=True,
    ).astype(jnp.float32)
    d_moe = d_moe + jnp.sum(
        back_grads.reshape(slot_total, model_width)[target].reshape(n_rows, TOPK, model_width),
        axis=1,
    )
    d_moe, d_gate = (
        lax.psum(d_moe.astype(jnp.bfloat16), "tensor").astype(jnp.float32),
        lax.psum(d_gate_part.astype(jnp.bfloat16), "tensor").astype(jnp.float32),
    )
    d_router = jnp.einsum("tk,tke->te", d_gate, route_hot, precision=highest)
    (d_logits,) = router_back(d_router)
    d_logits_low = d_logits.astype(jnp.bfloat16)
    grad_router = matmul_tn(moe_low, d_logits_low)
    d_moe = d_moe + matmul_nt(d_logits_low, wr_full)
    d_mid_norm, grad_gain_moe = moe_norm_back(d_moe)
    d_middle = grad_y + d_mid_norm
    d_middle_low = d_middle.astype(jnp.bfloat16)
    grad_wout = matmul_tn(attended_low, d_middle_low)
    d_att_low = (
        matmul_nt(d_middle_low, wo_full).astype(jnp.bfloat16).reshape(n_rows, local_heads, VDIM)
    )
    again_probs = jnp.exp(masked_scores() - log_total)
    d_values = jnp.einsum(
        "hqk,qhv->khv",
        again_probs.astype(jnp.bfloat16),
        d_att_low,
        preferred_element_type=jnp.float32,
    )
    d_probs = jnp.einsum("qhv,khv->hqk", d_att_low, values, preferred_element_type=jnp.float32)
    d_scores = (
        again_probs * (d_probs - jnp.sum(d_probs * again_probs, axis=-1, keepdims=True))
    ).astype(jnp.bfloat16)
    d_query_nope = score_scale * jnp.einsum(
        "hqk,khd->qhd", d_scores, key_nope, preferred_element_type=jnp.float32
    )
    d_query_rope = score_scale * jnp.einsum(
        "hqk,kr->qhr", d_scores, keys_rope, preferred_element_type=jnp.float32
    )
    d_key_nope = score_scale * jnp.einsum(
        "hqk,qhd->khd", d_scores, query_low[..., :NOPE], preferred_element_type=jnp.float32
    )
    d_key_rope = score_scale * jnp.einsum(
        "hqk,qhr->kr", d_scores, query_low[..., NOPE:], preferred_element_type=jnp.float32
    )
    (d_q_raw,) = query_back(jnp.concatenate([d_query_nope, d_query_rope], -1))
    d_q_low = d_q_raw.astype(jnp.bfloat16)
    grad_wq = matmul_tn(normed_low, d_q_low)
    d_normed = matmul_nt(d_q_low, wq_full)
    d_kv_low = (
        jnp.concatenate([d_key_nope, d_values], -1)
        .astype(jnp.bfloat16)
        .reshape(n_keys, local_heads * (NOPE + VDIM))
    )
    grad_wkv = matmul_tn(keys_latent, d_kv_low)
    d_keys_latent = matmul_nt(d_kv_low, wkv_full)
    own_latent = d_keys_latent[hop_count * n_rows :]
    own_rope = d_key_rope[hop_count * n_rows :]
    for distance in range(hop_count, 0, -1):
        block_index = hop_count - distance
        lower = block_index * n_rows
        home_latent, home_rope = (
            passed_along(
                d_keys_latent[lower : lower + n_rows].astype(jnp.bfloat16), "dp", -distance
            ).astype(jnp.float32),
            passed_along(
                d_key_rope[lower : lower + n_rows].astype(jnp.bfloat16), "dp", -distance
            ).astype(jnp.float32),
        )
        own_latent = own_latent + home_latent
        own_rope = own_rope + home_rope
    d_normed, own_latent, own_rope = (
        lax.psum(d_normed.astype(jnp.bfloat16), "tensor").astype(jnp.float32),
        lax.psum(own_latent.astype(jnp.bfloat16), "tensor").astype(jnp.float32),
        lax.psum(own_rope.astype(jnp.bfloat16), "tensor").astype(jnp.float32),
    )
    d_latent_raw, grad_gain_latent = latent_back((own_latent, own_rope))
    d_latent_low = d_latent_raw.astype(jnp.bfloat16)
    grad_wlat = matmul_tn(normed_low, d_latent_low)
    d_normed = d_normed + matmul_nt(d_latent_low, wlat_full)
    d_tokens_norm, grad_gain_attn = attn_norm_back(d_normed)
    token_input_gradient = d_middle + d_tokens_norm
    reduced_result = tuple(
        (
            lax.psum_scatter(grad_gain_attn, "dp", scatter_dimension=0, tiled=True),
            lax.psum_scatter(grad_wq, "dp", scatter_dimension=0, tiled=True),
            lax.psum_scatter(grad_wlat, "dp", scatter_dimension=0, tiled=True),
            lax.psum_scatter(grad_gain_latent, "dp", scatter_dimension=0, tiled=True),
            lax.psum_scatter(grad_wkv, "dp", scatter_dimension=0, tiled=True),
            lax.psum_scatter(grad_wout, "dp", scatter_dimension=1, tiled=True),
            lax.psum_scatter(grad_gain_moe, "dp", scatter_dimension=0, tiled=True),
            lax.psum_scatter(grad_router, "dp", scatter_dimension=0, tiled=True),
            lax.psum_scatter(grad_sgate, "dp", scatter_dimension=0, tiled=True),
            lax.psum_scatter(grad_sup, "dp", scatter_dimension=0, tiled=True),
            lax.psum_scatter(grad_sdown, "dp", scatter_dimension=1, tiled=True),
        )
    )
    return (
        (result, token_input_gradient)
        + reduced_result
        + (expert_gate_weight_gradient, expert_up_weight_gradient, expert_down_weight_gradient)
    )


def solution(mesh):
    placed = (
        P("dp", None),
        P("dp", None),
        P(),
        P("dp", None),
        P("dp"),
        P("dp", "tensor"),
        P("dp", None),
        P("dp"),
        P("dp", "tensor"),
        P("tensor", "dp"),
        P("dp"),
        P("dp", None),
        P("dp", "tensor"),
        P("dp", "tensor"),
        P("tensor", "dp"),
        P("dp", None, "tensor"),
        P("dp", None, "tensor"),
        P("dp", "tensor", None),
    )
    sixteen = mesh.shape["dp"] == 16 and mesh.shape["tensor"] == 2

    def body(*args):
        fits_sixteen = sixteen and args[2].shape[0] == 1 and args[15].shape[0] == 1
        return (shards_sixteen if fits_sixteen else shards_general)(*args)

    return jax.shard_map(
        body,
        mesh=mesh,
        in_specs=placed,
        out_specs=(
            P("dp", None),
            P("dp", None),
            P("dp"),
            P("dp", "tensor"),
            P("dp", None),
            P("dp"),
            P("dp", "tensor"),
            P("tensor", "dp"),
            P("dp"),
            P("dp", None),
            P("dp", "tensor"),
            P("dp", "tensor"),
            P("tensor", "dp"),
            P("dp", None, "tensor"),
            P("dp", None, "tensor"),
            P("dp", "tensor", None),
        ),
        check_vma=False,
    )
```

```python
import functools
import math

import jax
import jax.numpy as jnp
from jax import lax
from jax.experimental import pallas as pl
from jax.experimental.pallas import tpu as pltpu
from jax.sharding import PartitionSpec as P

NOPE = 128
ROPE = 64
VDIM = 128
RANK = 512
TOPK = 6
WINDOW = 1024


eps_norm = 1e-06
highest = lax.Precision.HIGHEST


def passed_along(value, axis, steps):
    count = lax.axis_size(axis)
    leading, last = (max(0, -steps), min(count, count - steps))
    return lax.ppermute(value, axis, [(source, source + steps) for source in range(leading, last)])


def rms_scale(values, gain_vec):
    inv_root = lax.rsqrt(jnp.mean(values * values, axis=-1, keepdims=True) + eps_norm)
    return values * inv_root * gain_vec


def rope_tables(positions):
    half_width = ROPE // 2
    frequency = jnp.exp(
        -jnp.arange(half_width, dtype=jnp.float32) * (2.0 * math.log(10000.0) / ROPE)
    )
    angles = positions[:, None] * frequency[None, :]
    return (jnp.cos(angles), jnp.sin(angles))


def rotate(values, cos_tab, sin_tab):
    half_width = values.shape[-1] // 2
    first_half = values[..., :half_width]
    second = values[..., half_width:]
    return jnp.concatenate(
        [first_half * cos_tab - second * sin_tab, second * cos_tab + first_half * sin_tab], axis=-1
    )


def gated_act(gate_a, up_b):
    return jax.nn.silu(gate_a) * up_b


def matmul(left_mat, right_mat):
    return jnp.dot(left_mat, right_mat, preferred_element_type=jnp.float32)


def matmul_nt(left_mat, right_mat):
    return lax.dot_general(
        left_mat, right_mat, (((1,), (1,)), ((), ())), preferred_element_type=jnp.float32
    )


def matmul_tn(left_mat, right_mat):
    return lax.dot_general(
        left_mat, right_mat, (((0,), (0,)), ((), ())), preferred_element_type=jnp.float32
    )


def ranks_before(hot):
    count = hot.shape[0]
    below = jnp.arange(count)[:, None] > jnp.arange(count)[None, :]
    return matmul(below.astype(jnp.bfloat16), hot.astype(jnp.bfloat16)).astype(jnp.int32)


MESH = pl.DeviceIdType.MESH


def plane_at(z, k):
    edge = jnp.where(z >= 2, 3 - z, z)
    near = jnp.where(k == 0, edge, jnp.where(k == 1, 1 - edge, k))
    return jnp.where(z >= 2, 3 - near, near)


def ag_kernel(kinds, cuts, *refs):
    n = len(kinds)
    ins, outs, lands, sems = refs[:n], refs[n : 2 * n], refs[2 * n : 3 * n], refs[3 * n :]
    me = lax.axis_index("dp")
    core = lax.axis_index("tensor")
    z = me // 4
    y = (me // 2) % 2
    x = me % 2
    xn = z * 4 + y * 2 + (1 - x)
    yn = z * 4 + (1 - y) * 2 + x
    up = jnp.minimum(z + 1, 3) * 4 + y * 2 + x
    dn = jnp.maximum(z - 1, 0) * 4 + y * 2 + x
    bar = pltpu.get_barrier_semaphore()

    def sig(d, c):
        pl.semaphore_signal(bar, inc=1, device_id=(d, c), device_id_type=MESH)

    sig(xn, core)
    sig(yn, core)
    sig(me, 1 - core)
    pl.when(z < 3)(lambda: sig(up, core))
    pl.when(z > 0)(lambda: sig(dn, core))

    def rc(src, dst, ss, rs, dev, c):
        return pltpu.make_async_remote_copy(
            src_ref=src, dst_ref=dst, send_sem=ss, recv_sem=rs, device_id=(dev, c), device_id_type=MESH
        )

    class Part:
        def __init__(self, at, cut):
            self.share = kinds[at]
            self.x, self.o, self.hbm = ins[at], lands[at], outs[at]
            rows = self.x.shape[1] // cuts[at]
            self.rows = pl.ds(cut * rows, rows)
            self.zs, self.zr, self.xs, self.xr, self.ys, self.yr, self.cs, self.cr, self.own, self.out = (
                s.at[cut] for s in sems[10 * at : 10 * at + 10]
            )
            self.slot = core if self.share else 0
            self.copy = pltpu.make_async_copy(self.x.at[:, self.rows], self.whole(me), self.own)

        def whole(self, b):
            return self.o.at[b, self.slot, :, self.rows]

        def z_(self, zp, dev, s):
            b = zp * 4 + y * 2 + x
            return rc(self.whole(b), self.whole(b), self.zs.at[s], self.zr.at[zp], dev, core)

        def x_(self, j, b, half, zp):
            r = self.o.at[b, self.slot, half, self.rows]
            return rc(r, r, self.xs.at[zp, j], self.xr.at[zp, j], xn, core)

        def y_(self, j, b, half, zp):
            r = self.o.at[b, self.slot, half, self.rows]
            return rc(r, r, self.ys.at[zp, j], self.yr.at[zp, j], yn, core)

        def twin(self, b):
            return rc(self.whole(b), self.whole(b), self.cs.at[b], self.cr.at[b], me, 1 - core)

        def first(self, k):
            zp = plane_at(z, k)
            b = zp * 4 + y * 2 + x
            if k > 0:
                self.z_(zp, up, 0).wait_recv()
            pl.when((zp <= z) & (z < 3))(lambda: self.z_(zp, up, zp).start())
            pl.when((zp >= z) & (z > 0))(lambda: self.z_(zp, dn, 4 + zp).start())
            self.x_(0, b, 0, zp).start()
            self.y_(0, b, 1, zp).start()
            self.y_(1, b, 0, zp).start()
            self.x_(1, b, 1, zp).start()
            if self.share:
                self.twin(b).start()

        def second(self, k):
            zp = plane_at(z, k)
            bx = zp * 4 + y * 2 + (1 - x)
            by = zp * 4 + (1 - y) * 2 + x
            self.x_(0, bx, 0, zp).wait_recv()
            self.y_(2, bx, 0, zp).start()
            self.y_(0, by, 1, zp).wait_recv()
            self.x_(2, by, 1, zp).start()
            self.x_(1, bx, 1, zp).wait_recv()
            self.y_(1, by, 0, zp).wait_recv()
            if self.share:
                self.twin(bx).start()
                self.twin(by).start()

        def third(self, k):
            zp = plane_at(z, k)
            bd = zp * 4 + (1 - y) * 2 + (1 - x)
            self.y_(2, bd, 0, zp).wait_recv()
            self.x_(2, bd, 1, zp).wait_recv()
            if self.share:
                self.twin(bd).start()

        def save(self, k):
            at = pl.ds(plane_at(z, k) * 4, 4)
            return pltpu.make_async_copy(
                self.o.at[at, :, :, self.rows], self.hbm.at[at, :, :, self.rows], self.out.at[k]
            )

        def fourth(self, k):
            if self.share:
                for q in range(4):
                    b = plane_at(z, k) * 4 + q
                    src, dst = self.o.at[b, core, :, self.rows], self.o.at[b, 1 - core, :, self.rows]
                    rc(src, dst, self.cs.at[b], self.cr.at[b], me, 1 - core).wait_recv()
            self.save(k).start()

        def end(self):
            for k in range(4):
                self.save(k).wait()
                pl.when((k <= z) & (z < 3))(lambda k=k: self.z_(k, up, k).wait_send())
                pl.when((k >= z) & (z > 0))(lambda k=k: self.z_(k, dn, 4 + k).wait_send())
                for j in range(3):
                    self.x_(j, 0, 0, k).wait_send()
                    self.y_(j, 0, 0, k).wait_send()
            if self.share:
                for b in range(16):
                    self.twin(b).wait_send()

    groups = [[Part(at, cut) for cut in range(cuts[at])] for at in range(n)]
    parts = [p for g in groups for p in g]
    for p in parts:
        p.copy.start()
    pl.semaphore_wait(bar, 3 + (z < 3).astype(jnp.int32) + (z > 0).astype(jnp.int32))
    for p in parts:
        p.copy.wait()
    turns = [(p, k) for g in groups for k in range(4) for p in g]
    lag = max(cuts)
    for t in range(len(turns) + lag):
        if t < len(turns):
            turns[t][0].first(turns[t][1])
        if t >= lag:
            turns[t - lag][0].second(turns[t - lag][1])
    for p, k in turns:
        p.third(k)
        if not p.share:
            p.fourth(k)
    for p, k in turns:
        if p.share:
            p.fourth(k)
    for p in parts:
        p.end()


def ag16(arrays, kinds, cid, cuts=None):
    S = pltpu.SemaphoreType.DMA
    any_ = pl.BlockSpec(memory_space=pl.ANY)
    cuts = cuts or (1,) * len(arrays)
    counts = ((8,), (4,), (4, 3), (4, 3), (4, 3), (4, 3), (16,), (16,), (), (4,))
    shapes = [(16, 2 if share else 1) + v.shape for v, share in zip(arrays, kinds)]
    return pl.pallas_call(
        functools.partial(ag_kernel, kinds, cuts),
        out_shape=[jax.ShapeDtypeStruct(s, v.dtype) for s, v in zip(shapes, arrays)],
        in_specs=[any_] * len(arrays),
        out_specs=[any_] * len(arrays),
        scratch_shapes=[pltpu.VMEM(s, v.dtype) for s, v in zip(shapes, arrays)]
        + [S((c,) + s) for c in cuts for s in counts],
        compiler_params=pltpu.CompilerParams(collective_id=cid, has_side_effects=True, vmem_limit_bytes=60 << 20),
    )(*arrays)


def add_into(dst, src):
    def step(i, _):
        r = pl.ds(pl.multiple_of(i * 16, 16), 16)
        dst[r] = dst[r] + src[r]
        return 0

    lax.fori_loop(0, dst.shape[0] // 16, step, 0)


def rs_kernel(a_ref, b_ref, o_ref, own, yr, xr, zr, lsem, xs, xrs, ys, yrs, zs, zrs):
    me = lax.axis_index("dp")
    core = lax.axis_index("tensor")
    z = me // 4
    y = (me // 2) % 2
    x = me % 2
    xn = z * 4 + y * 2 + (1 - x)
    yn = z * 4 + (1 - y) * 2 + x
    up = jnp.minimum(z + 1, 3) * 4 + y * 2 + x
    dn = jnp.maximum(z - 1, 0) * 4 + y * 2 + x
    wide = a_ref.shape[3]

    def rc(src, dst, ss, rs, dev):
        return pltpu.make_async_remote_copy(
            src_ref=src, dst_ref=dst, send_sem=ss, recv_sem=rs, device_id=(dev, core), device_id_type=MESH
        )

    def loads(zp):
        at = pl.ds(zp * 4, 4)
        return [
            pltpu.make_async_copy(a_ref.at[at], own.at[at, :, :, 0:wide], lsem.at[zp, 0]),
            pltpu.make_async_copy(b_ref.at[at], own.at[at, :, :, wide:], lsem.at[zp, 1]),
        ]

    for k in range(4):
        for c in loads(plane_at(z, 3 - k)):
            c.start()
    bar = pltpu.get_barrier_semaphore()

    def sig(d):
        pl.semaphore_signal(bar, inc=1, device_id=(d, core), device_id_type=MESH)

    sig(xn)
    sig(yn)
    pl.when(z < 3)(lambda: sig(up))
    pl.when(z > 0)(lambda: sig(dn))
    pl.semaphore_wait(bar, 2 + (z < 3).astype(jnp.int32) + (z > 0).astype(jnp.int32))

    def y_(j, b, half, zp):
        return rc(own.at[b, half], yr.at[zp, j], ys.at[zp, j], yrs.at[zp, j], yn)

    def x_(j, b, half, zp):
        return rc(own.at[b, half], xr.at[zp, j], xs.at[zp, j], xrs.at[zp, j], xn)

    def zc(zp, dev, d):
        return rc(own.at[zp * 4 + y * 2 + x], zr.at[d, zp], zs.at[zp], zrs.at[d, zp], dev)

    def blk(zp, yy, xx):
        return zp * 4 + yy * 2 + xx

    def s1(k):
        zp = plane_at(z, 3 - k)
        for c in loads(zp):
            c.wait()
        y_(0, blk(zp, 1 - y, 1 - x), 0, zp).start()
        x_(0, blk(zp, 1 - y, 1 - x), 1, zp).start()
        y_(1, blk(zp, 1 - y, x), 0, zp).start()
        x_(1, blk(zp, y, 1 - x), 1, zp).start()

    def s2(k):
        zp = plane_at(z, 3 - k)
        mine = blk(zp, y, x)
        y_(0, blk(zp, 1 - y, 1 - x), 0, zp).wait_recv()
        add_into(own.at[blk(zp, y, 1 - x), 0], yr.at[zp, 0])
        x_(2, blk(zp, y, 1 - x), 0, zp).start()
        x_(0, blk(zp, 1 - y, 1 - x), 1, zp).wait_recv()
        add_into(own.at[blk(zp, 1 - y, x), 1], xr.at[zp, 0])
        y_(2, blk(zp, 1 - y, x), 1, zp).start()
        y_(1, blk(zp, 1 - y, x), 0, zp).wait_recv()
        add_into(own.at[mine, 0], yr.at[zp, 1])
        x_(1, blk(zp, y, 1 - x), 1, zp).wait_recv()
        add_into(own.at[mine, 1], xr.at[zp, 1])

    def s3(k):
        zp = plane_at(z, 3 - k)
        mine = blk(zp, y, x)
        x_(2, blk(zp, y, 1 - x), 0, zp).wait_recv()
        add_into(own.at[mine, 0], xr.at[zp, 2])
        y_(2, blk(zp, 1 - y, x), 1, zp).wait_recv()
        add_into(own.at[mine, 1], yr.at[zp, 2])

        def arrived(d):
            zc(zp, me, d).wait_recv()
            add_into(own.at[mine, 0], zr.at[d, zp, 0])
            add_into(own.at[mine, 1], zr.at[d, zp, 1])

        pl.when((zp <= z) & (z < 3))(lambda: arrived(1))
        pl.when((zp >= z) & (z > 0))(lambda: arrived(0))
        pl.when(zp < z)(lambda: zc(zp, dn, 1).start())
        pl.when(zp > z)(lambda: zc(zp, up, 0).start())

    s1(0)
    s1(1)
    s2(0)
    s1(2)
    s2(1)
    s3(0)
    s1(3)
    s2(2)
    s3(1)
    s2(3)
    s3(2)
    s3(3)
    for a in range(2):

        def row(i, _):
            r = pl.ds(pl.multiple_of(i * 16, 16), 16)
            o_ref[a, r] = own[me, a, r].astype(jnp.float32)
            return 0

        lax.fori_loop(0, o_ref.shape[1] // 16, row, 0)
    for k in range(4):
        for j in range(3):
            x_(j, 0, 0, k).wait_send()
            y_(j, 0, 0, k).wait_send()

        @pl.when(k != z)
        def _():
            zc(k, up, 0).wait_send()


def rs16(a, b, cid):
    S = pltpu.SemaphoreType.DMA
    half = (a.shape[2], a.shape[3] + b.shape[3])
    blkshape = (2,) + half
    V = lambda s: pltpu.VMEM(s, a.dtype)
    return pl.pallas_call(
        rs_kernel,
        out_shape=jax.ShapeDtypeStruct(blkshape, jnp.float32),
        in_specs=[pl.BlockSpec(memory_space=pl.ANY)] * 2,
        out_specs=pl.BlockSpec(memory_space=pltpu.VMEM),
        scratch_shapes=[
            V((16,) + blkshape), V((4, 3) + half), V((4, 3) + half), V((2, 4) + blkshape),
            S((4, 2)), S((4, 3)), S((4, 3)), S((4, 3)), S((4, 3)), S((4,)), S((2, 4)),
        ],
        compiler_params=pltpu.CompilerParams(collective_id=cid, has_side_effects=True, vmem_limit_bytes=60 << 20),
    )(a, b)


def nt(a, b):
    return lax.dot_general(a, b, (((1,), (1,)), ((), ())), preferred_element_type=jnp.float32)


def tn(a, b):
    return lax.dot_general(a, b, (((0,), (0,)), ((), ())), preferred_element_type=jnp.float32)


def mm(a, b):
    return jnp.dot(a, b, preferred_element_type=jnp.float32)


def gate_parts(a, b, dc):
    s = 1.0 / (1.0 + jnp.exp(-a))
    act = a * s
    return act * b, dc * b * (s * (1.0 + a * (1.0 - s))), dc * act


def moe_kernel(
    moe, grd, pick, pick_t, wg, wu, wd, wr, sgu, sdn,
    o_out, r_out, rg_out, act_out, da_out, db_out, sg_out, yr, xr, zr,
    own, sib, sibr, stage, xb, gb, pk, pt, rr, rg, ly, ld, ry, rd, acts, das, dbs, dgs,
    in_sem, out_sem, st_sem, free, cs, cr, xs, xrs, ys, yrs, zs, zrs, fs, fr,
):
    me = lax.axis_index("dp")
    core = lax.axis_index("tensor")
    other = 1 - core
    z = me // 4
    y = (me // 2) % 2
    x = me % 2
    xn = z * 4 + y * 2 + (1 - x)
    yn = z * 4 + (1 - y) * 2 + x
    up = jnp.minimum(z + 1, 3) * 4 + y * 2 + x
    dn = jnp.maximum(z - 1, 0) * 4 + y * 2 + x
    width = moe.shape[2]
    hid = 128
    cut = 512

    def rc(src, dst, ss, rs, dev, c):
        return pltpu.make_async_remote_copy(
            src_ref=src, dst_ref=dst, send_sem=ss, recv_sem=rs, device_id=(dev, c), device_id_type=MESH
        )

    def loads(i):
        k, half = i // 2, i % 2
        b = plane_at(z, 3 - k) * 4 + jnp.where(half == 0, 1 - y, y) * 2
        at = pl.ds(b, 2)
        return [
            pltpu.make_async_copy(moe.at[at], xb, in_sem.at[0]),
            pltpu.make_async_copy(grd.at[at], gb, in_sem.at[1]),
            pltpu.make_async_copy(pick.at[at], pk, in_sem.at[2]),
            pltpu.make_async_copy(pick_t.at[at], pt, in_sem.at[3]),
        ]

    for c in loads(0):
        c.start()
    bar = pltpu.get_barrier_semaphore()

    def sig(d, c):
        pl.semaphore_signal(bar, inc=1, device_id=(d, c), device_id_type=MESH)

    sig(xn, core)
    sig(yn, core)
    sig(me, other)
    pl.when(z < 3)(lambda: sig(up, core))
    pl.when(z > 0)(lambda: sig(dn, core))
    pl.semaphore_wait(bar, 3 + (z < 3).astype(jnp.int32) + (z > 0).astype(jnp.int32))

    for q in range(2):
        ry[q, hid:] = sdn[...]
        rd[q, hid:] = sgu[...]
    sg_out[...] = jnp.zeros_like(sg_out)

    def y_(j, b, half, zp):
        return rc(own.at[b, half], yr.at[zp, j], ys.at[zp, j], yrs.at[zp, j], yn, core)

    def x_(j, b, half, zp):
        return rc(own.at[b, half], xr.at[zp, j], xs.at[zp, j], xrs.at[zp, j], xn, core)

    def zc(zp, dev, d):
        b = zp * 4 + y * 2 + x
        return rc(own.at[b], zr.at[d, zp], zs.at[zp], zrs.at[d, zp], dev, core)

    def sib_send(i):
        return rc(sib, sibr, cs, cr, me, other)

    def outs(i):
        at = pl.ds(pl.multiple_of(i * 256, 256), 256)
        return [
            pltpu.make_async_copy(rr, r_out.at[at], out_sem.at[0]),
            pltpu.make_async_copy(rg, rg_out.at[at], out_sem.at[1]),
            pltpu.make_async_copy(acts, act_out.at[at], out_sem.at[2]),
            pltpu.make_async_copy(das, da_out.at[at], out_sem.at[3]),
            pltpu.make_async_copy(dbs, db_out.at[at], out_sem.at[4]),
        ]

    def columns(step):
        def one(n, _):
            step(pl.ds(pl.multiple_of(n * cut, cut), cut))
            return 0

        lax.fori_loop(0, width // cut, one, 0)

    def first_part(i):
        for c in loads(i):
            c.wait()

        @pl.when(i > 0)
        def _():
            for c in outs(i - 1):
                c.wait()

        def pick_rows(n):
            for q in range(2):
                rr[q * hid : (q + 1) * hid, n] = mm(pk[q], xb[q, :, n]).astype(jnp.bfloat16)
                rg[q * hid : (q + 1) * hid, n] = mm(pk[q], gb[q, :, n]).astype(jnp.bfloat16)

        columns(pick_rows)
        for q in range(2):
            ab = nt(xb[q], sgu[...])
            act, d_a, d_b = gate_parts(ab[:, :hid], ab[:, hid:], nt(gb[q], sdn[...]))
            ly[q, :, :hid] = pt[q]
            ly[q, :, hid:] = act.astype(jnp.bfloat16)
            ld[q, :, :hid] = pt[q]
            ld[q, :, hid : 2 * hid] = d_a.astype(jnp.bfloat16)
            ld[q, :, 2 * hid :] = d_b.astype(jnp.bfloat16)

        def shared_grads(n):
            sg_out[: 2 * hid, n] += tn(ld[0, :, hid:], xb[0, :, n]) + tn(ld[1, :, hid:], xb[1, :, n])
            sg_out[2 * hid :, n] += tn(ly[0, :, hid:], gb[0, :, n]) + tn(ly[1, :, hid:], gb[1, :, n])

        columns(shared_grads)

        @pl.when(i < 7)
        def _():
            for c in loads(i + 1):
                c.start()

    def second_part(i):
        logits = mm(rr[...], wr[...])
        lane = lax.broadcasted_iota(jnp.int32, logits.shape, 1)
        logits = jnp.where(lane < 16, logits, -jnp.inf)
        e = jnp.exp(logits - jnp.max(logits, axis=1, keepdims=True))
        gate = jnp.sum(jnp.where(lane == me, e, 0.0), axis=1, keepdims=True) / jnp.sum(
            e, axis=1, keepdims=True
        )
        pre = nt(rg[...], wd[...])
        act, d_a, d_b = gate_parts(mm(rr[...], wg[...]), mm(rr[...], wu[...]), gate * pre)
        low = act.astype(jnp.bfloat16)
        back = low.astype(jnp.float32)
        d_gate = jnp.sum(back * pre, axis=1, keepdims=True)
        acts[...] = (gate * back).astype(jnp.bfloat16)
        das[...] = d_a.astype(jnp.bfloat16)
        dbs[...] = d_b.astype(jnp.bfloat16)

        def spread(n):
            o = (gate * mm(low, wd[:, n])).astype(jnp.bfloat16)
            s = (nt(das[...], wg[n]) + nt(dbs[...], wu[n])).astype(jnp.bfloat16)
            for q in range(2):
                ry[q, :hid, n] = o[q * hid : (q + 1) * hid]
                rd[q, :hid, n] = s[q * hid : (q + 1) * hid]

        columns(spread)
        for c in outs(i):
            c.start()
        dgs[...] = jnp.where(lane == me, d_gate, 0.0).astype(jnp.bfloat16)

    def third_part(i):
        k, half = i // 2, i % 2
        b = plane_at(z, 3 - k) * 4 + jnp.where(half == 0, 1 - y, y) * 2

        @pl.when(i > 0)
        def _():
            sib_send(i - 1).wait_send()

        def store(q, n, v):
            v = v.astype(jnp.bfloat16)
            mine = jnp.where(core == 0, v[:128], v[128:])
            theirs = jnp.where(core == 0, v[128:], v[:128])
            own[b + q, 0, :, n] = mine[:64]
            own[b + q, 1, :, n] = mine[64:]
            sib[q, 0, :, n] = theirs[:64]
            sib[q, 1, :, n] = theirs[64:]

        def put(m, _):
            n = pl.ds(pl.multiple_of(m * cut, cut), cut)
            n2 = pl.ds(pl.multiple_of(width + m * cut, cut), cut)
            for q in range(2):
                store(q, n, mm(ly[q], ry[q, :, n]))
                store(q, n2, mm(ld[q], rd[q, :, n]))
            return 0

        lax.fori_loop(0, width // cut, put, 0)
        for q in range(2):
            store(q, pl.ds(2 * width, 128), mm(pt_of(q), dgs[q * hid : (q + 1) * hid]))

        @pl.when(i > 0)
        def _():
            pl.semaphore_wait(free, 1)

        sib_send(i).start()

    def pt_of(q):
        return ly[q, :, :hid]

    def staged(src, dst, sem):
        return pltpu.make_async_copy(src, dst, sem)

    def blk(zp, yy, xx):
        return zp * 4 + yy * 2 + xx

    def pair_sum(i):
        k, half = i // 2, i % 2
        zp = plane_at(z, 3 - k)
        b = zp * 4 + jnp.where(half == 0, 1 - y, y) * 2
        sib_send(i).wait_recv()

        def one(q, _):
            add_into(own.at[b + q, 0], sibr.at[q, 0])
            add_into(own.at[b + q, 1], sibr.at[q, 1])
            return 0

        lax.fori_loop(0, 2, one, 0)

        @pl.when(i < 7)
        def _():
            pl.semaphore_signal(free, inc=1, device_id=(me, other), device_id_type=MESH)

        @pl.when(half == 0)
        def _():
            y_(0, blk(zp, 1 - y, 1 - x), 0, zp).start()
            x_(0, blk(zp, 1 - y, 1 - x), 1, zp).start()
            y_(1, blk(zp, 1 - y, x), 0, zp).start()

        @pl.when(half == 1)
        def _():
            x_(1, blk(zp, y, 1 - x), 1, zp).start()

    def second_staging(k):
        zp = plane_at(z, 3 - k)
        return [
            staged(yr.at[zp, 0], stage.at[0, 0], st_sem.at[0]),
            staged(xr.at[zp, 0], stage.at[0, 1], st_sem.at[1]),
            staged(yr.at[zp, 1], stage.at[1, 0], st_sem.at[2]),
            staged(xr.at[zp, 1], stage.at[1, 1], st_sem.at[3]),
        ]

    def second_fetch(k):
        zp = plane_at(z, 3 - k)
        c = second_staging(k)
        y_(0, blk(zp, 1 - y, 1 - x), 0, zp).wait_recv()
        c[0].start()
        x_(0, blk(zp, 1 - y, 1 - x), 1, zp).wait_recv()
        c[1].start()
        y_(1, blk(zp, 1 - y, x), 0, zp).wait_recv()
        c[2].start()
        x_(1, blk(zp, y, 1 - x), 1, zp).wait_recv()
        c[3].start()

    def second_hop(k):
        zp = plane_at(z, 3 - k)
        mine = blk(zp, y, x)
        c = second_staging(k)
        c[0].wait()
        add_into(own.at[blk(zp, y, 1 - x), 0], stage.at[0, 0])
        x_(2, blk(zp, y, 1 - x), 0, zp).start()
        c[1].wait()
        add_into(own.at[blk(zp, 1 - y, x), 1], stage.at[0, 1])
        y_(2, blk(zp, 1 - y, x), 1, zp).start()
        c[2].wait()
        add_into(own.at[mine, 0], stage.at[1, 0])
        c[3].wait()
        add_into(own.at[mine, 1], stage.at[1, 1])

    def last_staging(k):
        zp = plane_at(z, 3 - k)
        return [
            staged(xr.at[zp, 2], stage.at[0, 0], st_sem.at[0]),
            staged(yr.at[zp, 2], stage.at[0, 1], st_sem.at[1]),
            staged(zr.at[1, zp], stage.at[1], st_sem.at[2]),
            staged(zr.at[0, zp], stage.at[2], st_sem.at[3]),
        ]

    def last_fetch(k):
        zp = plane_at(z, 3 - k)
        c = last_staging(k)
        x_(2, blk(zp, y, 1 - x), 0, zp).wait_recv()
        c[0].start()
        y_(2, blk(zp, 1 - y, x), 1, zp).wait_recv()
        c[1].start()

        @pl.when((zp <= z) & (z < 3))
        def _():
            zc(zp, me, 1).wait_recv()
            c[2].start()

        @pl.when((zp >= z) & (z > 0))
        def _():
            zc(zp, me, 0).wait_recv()
            c[3].start()

    def last_hop(k):
        zp = plane_at(z, 3 - k)
        mine = blk(zp, y, x)
        c = last_staging(k)
        c[0].wait()
        add_into(own.at[mine, 0], stage.at[0, 0])
        c[1].wait()
        add_into(own.at[mine, 1], stage.at[0, 1])

        def arrived(d):
            c[3 - d].wait()
            add_into(own.at[mine, 0], stage.at[2 - d, 0])
            add_into(own.at[mine, 1], stage.at[2 - d, 1])

        pl.when((zp <= z) & (z < 3))(lambda: arrived(1))
        pl.when((zp >= z) & (z > 0))(lambda: arrived(0))
        pl.when(zp < z)(lambda: zc(zp, dn, 1).start())
        pl.when(zp > z)(lambda: zc(zp, up, 0).start())

    def step(i, _):
        pl.when(i < 8)(lambda: first_part(i))
        pl.when((i >= 1) & (i <= 8))(lambda: pair_sum(i - 1))
        seconds = (i % 2 == 0) & (i >= 4) & (i <= 10)
        lasts = (i % 2 == 1) & (i >= 7) & (i <= 13)
        pl.when(seconds)(lambda: second_fetch((i - 4) // 2))
        pl.when(lasts)(lambda: last_fetch((i - 7) // 2))
        pl.when(i < 8)(lambda: second_part(i))
        pl.when(seconds)(lambda: second_hop((i - 4) // 2))
        pl.when(lasts)(lambda: last_hop((i - 7) // 2))
        pl.when(i < 8)(lambda: third_part(i))
        return 0

    lax.fori_loop(0, 14, step, 0)
    for a in range(2):

        def row(n, _):
            r = pl.ds(pl.multiple_of(n * 16, 16), 16)
            o_out[core, a, r] = own[me, a, r]
            return 0

        lax.fori_loop(0, 4, row, 0)
    f = rc(o_out.at[core], o_out.at[core], fs, fr, me, other)
    f.start()
    for c in outs(7):
        c.wait()
    sib_send(7).wait_send()
    for k in range(4):
        for j in range(3):
            x_(j, 0, 0, k).wait_send()
            y_(j, 0, 0, k).wait_send()

        @pl.when(k != z)
        def _():
            zc(k, up, 0).wait_send()

    rc(o_out.at[core], o_out.at[other], fs, fr, me, other).wait_recv()
    f.wait_send()


def moe_call(moe, grd, pick, pick_t, wg, wu, wd, wr, sgu, sdn, cid):
    width, ffe = wg.shape
    total = 2 * width + 128
    slots = pick.shape[0] * pick.shape[1]
    low, S, V = jnp.bfloat16, pltpu.SemaphoreType.DMA, pltpu.VMEM
    any_, vmem = pl.BlockSpec(memory_space=pl.ANY), pl.BlockSpec(memory_space=pltpu.VMEM)
    shape = lambda *s: jax.ShapeDtypeStruct(s, low)
    blk = (2, 64, total)
    return pl.pallas_call(
        moe_kernel,
        out_shape=[
            shape(2, *blk), shape(slots, width), shape(slots, width), shape(slots, ffe), shape(slots, ffe),
            shape(slots, ffe), jax.ShapeDtypeStruct((384, width), jnp.float32),
            shape(4, 3, 64, total), shape(4, 3, 64, total), shape(2, 4, *blk),
        ],
        in_specs=[any_] * 4 + [vmem] * 6,
        out_specs=[vmem] + [any_] * 5 + [vmem] + [any_] * 3,
        scratch_shapes=[
            V((16,) + blk, low), V((2,) + blk, low), V((2,) + blk, low), V((3,) + blk, low),
            V((2, 256, width), low), V((2, 256, width), low), V((2, 128, 256), low), V((2, 256, 128), low),
            V((256, width), low), V((256, width), low), V((2, 256, 256), low), V((2, 256, 384), low),
            V((2, 256, width), low), V((2, 384, width), low),
            V((256, ffe), low), V((256, ffe), low), V((256, ffe), low), V((256, 128), low),
            S((4,)), S((5,)), S((4,)), pltpu.SemaphoreType.REGULAR, S, S, S((4, 3)), S((4, 3)), S((4, 3)), S((4, 3)), S((4,)), S((2, 4)), S, S,
        ],
        compiler_params=pltpu.CompilerParams(collective_id=cid, has_side_effects=True, vmem_limit_bytes=60 << 20),
        cost_estimate=pl.CostEstimate(flops=65 * 10**9, bytes_accessed=80 * 10**6, transcendentals=0),
    )(moe, grd, pick, pick_t, wg, wu, wd, wr, sgu, sdn)


SLOTS = 5
KEYS = SLOTS * 256


def turned(v, cos, sin):
    n = v.shape[1]
    lane = lax.broadcasted_iota(jnp.int32, v.shape, 1) % 64
    swap = jnp.where(lane < 32, -pltpu.roll(v, n - 32, 1), pltpu.roll(v, 32, 1))
    return v * cos + swap * sin


def root(v):
    return lax.rsqrt(jnp.mean(v * v, axis=1, keepdims=True) + eps_norm)


def neighbours(me, core, bar):
    count = jnp.int32(1)
    pl.semaphore_signal(bar, inc=1, device_id=(me, 1 - core), device_id_type=MESH)
    for d in range(1, SLOTS):

        @pl.when(me + d < 16)
        def _():
            pl.semaphore_signal(bar, inc=1, device_id=(jnp.minimum(me + d, 15), core), device_id_type=MESH)

        @pl.when(me >= d)
        def _():
            pl.semaphore_signal(bar, inc=1, device_id=(jnp.maximum(me - d, 0), core), device_id_type=MESH)

        count = count + (me + d < 16).astype(jnp.int32) + (me >= d).astype(jnp.int32)
    return count


def slab_copies(w4, w2, wq, wo, wkv, wlat, sem):
    pairs = [
        (w2.at[:, 2560:3200], wlat, sem.at[0]),
        (w2.at[:, 0:1536], wq, sem.at[1]),
        (w2.at[:, 1536:2560], wo, sem.at[2]),
    ]
    for c in range(4):
        pairs.append((w4.at[:, c, :, w4.shape[3] - 512 :], wkv.at[:, :, c * 512 : (c + 1) * 512], sem.at[3 + c]))
    return pairs


def att_fwd_kernel(
    tok, w4, w2, g_att, g_moe, g_lat, cos, sin, bias,
    middle, moe_low, normed, lat_raw, qcat, keys, kv_out, lse, att,
    kv, wq, wo, wkv, wlat, part, arrived, w_sem, kv_sem, ks, kr, cs, cr,
):
    me = lax.axis_index("dp")
    core = lax.axis_index("tensor")
    loads = [pltpu.make_async_copy(h, v, s) for h, v, s in slab_copies(w4, w2, wq, wo, wkv, wlat, w_sem)]
    for c in loads:
        c.start()
    bar = pltpu.get_barrier_semaphore()
    pl.semaphore_wait(bar, neighbours(me, core, bar))
    t = tok[...].astype(jnp.float32)
    normed[...] = (t * root(t) * g_att[...]).astype(jnp.bfloat16)
    loads[0].wait()
    lat = mm(normed[...], wlat[...])
    lat_raw[...] = lat
    first = lat[:, :RANK]
    rot = turned(lat[:, RANK:], cos[:, :128], sin[:, :128])
    rot = jnp.where(lax.broadcasted_iota(jnp.int32, rot.shape, 1) < 64, rot, 0.0)
    keys[SLOTS - 1, :, :RANK] = (first * root(first) * g_lat[...]).astype(jnp.bfloat16)
    keys[SLOTS - 1, :, RANK:] = (rot + pltpu.roll(rot, 64, 1)).astype(jnp.bfloat16)

    def send(d):
        return pltpu.make_async_remote_copy(
            src_ref=keys.at[SLOTS - 1], dst_ref=keys.at[SLOTS - 1 - d], send_sem=ks.at[d - 1], recv_sem=kr.at[d - 1],
            device_id=(jnp.minimum(me + d, 15), core), device_id_type=MESH,
        )

    for d in range(1, SLOTS):
        pl.when(me + d < 16)(lambda d=d: send(d).start())

        @pl.when(me < d)
        def _():
            keys[SLOTS - 1 - d] = jnp.zeros((256, 640), jnp.bfloat16)

    loads[1].wait()
    half = lax.broadcasted_iota(jnp.int32, (256, 128), 1) < 64
    q_nope = mm(normed[...], wq[:, :1024])
    q_rope = turned(mm(normed[...], wq[:, 1024:]), cos[...], sin[...])
    for h in range(8):
        qcat[h, :, :128] = q_nope[:, h * 128 : (h + 1) * 128].astype(jnp.bfloat16)
        pair = q_rope[:, h // 2 * 128 : (h // 2 + 1) * 128]
        qcat[h, :, 128:] = jnp.where(half == (h % 2 == 0), pair, 0.0).astype(jnp.bfloat16)
    for c in loads[3:]:
        c.wait()
    for s in range(SLOTS - 1, -1, -1):
        if s < SLOTS - 1:
            pl.when(me >= SLOTS - 1 - s)(lambda s=s: send(SLOTS - 1 - s).wait_recv())
        kv[s * 256 : (s + 1) * 256] = mm(keys[s, :, :RANK], wkv[...].reshape(RANK, 2048)).astype(jnp.bfloat16)
    save = pltpu.make_async_copy(kv, kv_out, kv_sem)
    save.start()

    def head(h, _):
        kn = kv[:, pl.ds(pl.multiple_of(h * 256, 256), 128)]
        v = kv[:, pl.ds(pl.multiple_of(h * 256 + 128, 128), 128)]
        rope = keys[:, :, RANK:].reshape(KEYS, 128)
        s = nt(qcat[h], jnp.concatenate([kn, rope], 1)) * ((NOPE + ROPE) ** -0.5) + bias[...]
        top = jnp.max(s, axis=1, keepdims=True)
        e = jnp.exp(s - top)
        den = jnp.sum(e, axis=1, keepdims=True)
        lse[h] = top + jnp.log(den)
        p = (e * (1.0 / den)).astype(jnp.bfloat16)
        att[:, pl.ds(pl.multiple_of(h * 128, 128), 128)] = mm(p, v).astype(jnp.bfloat16)
        return 0

    lax.fori_loop(0, 8, head, 0)
    loads[2].wait()

    def out(n, _):
        r = pl.ds(pl.multiple_of(n * 512, 512), 512)
        part[:, r] = nt(att[...], wo[r]).astype(jnp.bfloat16)
        return 0

    lax.fori_loop(0, 4, out, 0)
    swap = pltpu.make_async_remote_copy(
        src_ref=part, dst_ref=arrived, send_sem=cs, recv_sem=cr, device_id=(me, 1 - core), device_id_type=MESH
    )
    swap.start()
    swap.wait()
    m = tok[...].astype(jnp.float32) + (part[...].astype(jnp.float32) + arrived[...].astype(jnp.float32))
    middle[...] = m
    moe_low[...] = (m * root(m) * g_moe[...]).astype(jnp.bfloat16)
    save.wait()
    for d in range(1, SLOTS):
        pl.when(me + d < 16)(lambda d=d: send(d).wait_send())


def att_fwd(tok, weights, g_att, g_moe, g_lat, cos, sin, bias, cid):
    low, f32, S, V = jnp.bfloat16, jnp.float32, pltpu.SemaphoreType.DMA, pltpu.VMEM
    any_, vmem = pl.BlockSpec(memory_space=pl.ANY), pl.BlockSpec(memory_space=pltpu.VMEM)
    shape = lambda kind, *s: jax.ShapeDtypeStruct(s, kind)
    rows, width = tok.shape
    pack = weights.shape[1]
    return pl.pallas_call(
        att_fwd_kernel,
        out_shape=[
            shape(f32, rows, width), shape(low, rows, width), shape(low, rows, width), shape(f32, rows, 640),
            shape(low, 8, rows, 256), shape(low, SLOTS, rows, 640), shape(low, KEYS, 2048), shape(f32, 8, rows, 1),
            shape(low, rows, 1024),
        ],
        in_specs=[vmem, any_, any_] + [vmem] * 6,
        out_specs=[vmem] * 6 + [any_] + [vmem] * 2,
        scratch_shapes=[
            V((KEYS, 2048), low), V((width, 1536), low), V((width, 1024), low), V((16, 32, 2048), low), V((width, 640), low),
            V((rows, width), low), V((rows, width), low), S((7,)), S, S((4,)), S((4,)), S, S,
        ],
        compiler_params=pltpu.CompilerParams(collective_id=cid, has_side_effects=True, vmem_limit_bytes=60 << 20),
        cost_estimate=pl.CostEstimate(flops=10**10, bytes_accessed=40 * 10**6, transcendentals=0),
    )(tok, weights.reshape(16, 4, 32, pack), weights, g_att, g_moe, g_lat, cos, sin, bias)


def att_bwd_kernel(
    w4, w2, home, grad, middle, moe_low, tok, normed, lat_raw, qcat, keys, kv_in, lse, att, wr,
    g_att, g_moe, g_lat, cos, sin, bias,
    tok_grad, packed, p4,
    kv, wq, wo, wkv, wlat, dmid, dnorm, dmid_low, d_att, dq, dqr, dkr, dk_out, dk_in, own_dk, part, arrived,
    w_sem, kv_sem, ks, kr, cs, cr, o_sem,
):
    me = lax.axis_index("dp")
    core = lax.axis_index("tensor")
    width = tok.shape[1]
    scale = (NOPE + ROPE) ** -0.5
    loads = [pltpu.make_async_copy(h, v, s) for h, v, s in slab_copies(w4, w2, wq, wo, wkv, wlat, w_sem)]
    stores = [pltpu.make_async_copy(v, h, s) for h, v, s in slab_copies(p4, packed, wq, wo, wkv, wlat, o_sem)]
    kv_load = pltpu.make_async_copy(kv_in, kv, kv_sem)
    loads[2].start()
    kv_load.start()
    for n in (1, 3, 4, 5, 6, 0):
        loads[n].start()
    bar = pltpu.get_barrier_semaphore()
    pl.semaphore_wait(bar, neighbours(me, core, bar))
    lane = lax.broadcasted_iota(jnp.int32, (256, 128), 1)

    logits = jnp.where(lane < 16, mm(moe_low[...], wr[...]), -jnp.inf)
    e = jnp.exp(logits - jnp.max(logits, axis=1, keepdims=True))
    router = e / jnp.sum(e, axis=1, keepdims=True)
    d_router = jnp.where(lane < 16, home[:, width:].astype(jnp.float32), 0.0)
    d_logits = (router * (d_router - jnp.sum(router * d_router, axis=1, keepdims=True))).astype(jnp.bfloat16)

    def norm_back(v, gain, dy):
        r = root(v)
        hat = v * r
        up = dy * gain
        return r * (up - hat * jnp.mean(up * hat, axis=1, keepdims=True)), dy * hat

    def one_lane(n):
        return (lane == n).astype(jnp.bfloat16)

    d_moe = home[:, :width].astype(jnp.float32) + nt(d_logits, wr[...])
    d_norm2, gain_rows = norm_back(middle[...], g_moe[...], d_moe)
    d_middle = grad[...].astype(jnp.float32) + d_norm2
    dmid[...] = d_middle
    dmid_low[...] = d_middle.astype(jnp.bfloat16)
    gains = gain_rows.astype(jnp.bfloat16)
    moved = pltpu.roll(d_logits.astype(jnp.float32), 64, 1).astype(jnp.bfloat16)
    small = tn(moe_low[...], moved) + tn(gains, one_lane(81))

    loads[2].wait()
    d_att[...] = mm(dmid_low[...], wo[...]).astype(jnp.bfloat16)

    def wo_rows(n, _):
        r = pl.ds(pl.multiple_of(n * 256, 256), 256)
        wo[r] = tn(dmid_low[:, r], att[...]).astype(jnp.bfloat16)
        return 0

    lax.fori_loop(0, width // 256, wo_rows, 0)
    stores[2].start()
    kv_load.wait()
    dkr[...] = jnp.zeros_like(dkr)
    dqr[...] = jnp.zeros_like(dqr)

    def head(h, _):
        cols = pl.ds(pl.multiple_of(h * 128, 128), 128)
        nope_at = pl.ds(pl.multiple_of(h * 256, 256), 128)
        value_at = pl.ds(pl.multiple_of(h * 256 + 128, 128), 128)
        pair = pl.ds(pl.multiple_of(h // 2 * 128, 128), 128)
        kc = jnp.concatenate([kv[:, nope_at], keys[:, :, RANK:].reshape(KEYS, 128)], 1)
        p = jnp.exp(nt(qcat[h], kc) * scale + bias[...] - lse[h])
        dv = tn(p.astype(jnp.bfloat16), d_att[:, cols])
        dp = nt(d_att[:, cols], kv[:, value_at])
        ds = (p * (dp - jnp.sum(p * dp, axis=1, keepdims=True))).astype(jnp.bfloat16)
        dqc = mm(ds, kc) * scale
        dkc = tn(ds, qcat[h]) * scale
        dq[:, cols] = dqc[:, :128].astype(jnp.bfloat16)
        dqr[:, pair] += jnp.where((lane < 64) == (h % 2 == 0), dqc[:, 128:], 0.0)
        kv[:, nope_at] = dkc[:, :128].astype(jnp.bfloat16)
        kv[:, value_at] = dv.astype(jnp.bfloat16)
        dkr[...] += dkc[:, 128:]
        return 0

    lax.fori_loop(0, 8, head, 0)
    for n in (3, 4, 5, 6):
        loads[n].wait()

    def send(d):
        return pltpu.make_async_remote_copy(
            src_ref=dk_out.at[d - 1], dst_ref=dk_in.at[d - 1], send_sem=ks.at[d - 1], recv_sem=kr.at[d - 1],
            device_id=(jnp.maximum(me - d, 0), core), device_id_type=MESH,
        )

    for s in range(SLOTS):
        r = slice(s * 256, (s + 1) * 256)
        d_lat = nt(kv[r], wkv[...].reshape(RANK, 2048))
        d_rope = dkr[r] + pltpu.roll(dkr[r], 64, 1)
        if s == SLOTS - 1:
            own_dk[:, :RANK] = d_lat
            own_dk[:, RANK:] = d_rope
        else:
            d = SLOTS - 1 - s
            dk_out[d - 1, :, :RANK] = d_lat.astype(jnp.bfloat16)
            dk_out[d - 1, :, RANK:] = d_rope.astype(jnp.bfloat16)
            pl.when(me >= d)(lambda d=d: send(d).start())
    dq[:, 1024:] = turned(dqr[...], cos[...], -sin[...]).astype(jnp.bfloat16)
    loads[1].wait()

    def normed_cols(n, _):
        r = pl.ds(pl.multiple_of(n * 512, 512), 512)
        v = nt(dq[...], wq[r])
        part[:, r] = v.astype(jnp.bfloat16)
        wq[r] = tn(normed[:, r], dq[...]).astype(jnp.bfloat16)
        return 0

    lax.fori_loop(0, 4, normed_cols, 0)
    stores[1].start()
    latent_all = keys[:, :, :RANK].reshape(KEYS, RANK)
    for c in range(4):
        g = tn(latent_all, kv[:, c * 512 : (c + 1) * 512]).astype(jnp.bfloat16)
        wkv[:, :, c * 512 : (c + 1) * 512] = g.reshape(16, 32, 512)
        stores[3 + c].start()
    for d in range(1, SLOTS):

        @pl.when(me + d < 16)
        def _():
            pltpu.make_async_remote_copy(
                src_ref=dk_out.at[d - 1], dst_ref=dk_in.at[d - 1], send_sem=ks.at[d - 1], recv_sem=kr.at[d - 1],
                device_id=(jnp.minimum(me + d, 15), core), device_id_type=MESH,
            ).wait_recv()
            own_dk[...] += dk_in[d - 1].astype(jnp.float32)

    part[:, width:] = own_dk[...].astype(jnp.bfloat16)
    swap = pltpu.make_async_remote_copy(
        src_ref=part, dst_ref=arrived, send_sem=cs, recv_sem=cr, device_id=(me, 1 - core), device_id_type=MESH
    )
    swap.start()
    swap.wait()
    dnorm[...] = part[:, :width].astype(jnp.float32) + arrived[:, :width].astype(jnp.float32)
    d_keys = part[:, width:].astype(jnp.float32) + arrived[:, width:].astype(jnp.float32)

    d_first, lat_gain_rows = norm_back(lat_raw[:, :RANK], g_lat[...], d_keys[:, :RANK])
    d_second = turned(d_keys[:, RANK:], cos[:, :128], -sin[:, :128])
    d_second = jnp.where(lane < 64, d_second, 0.0)
    d_lat_low = jnp.concatenate([d_first, d_second], 1).astype(jnp.bfloat16)
    loads[0].wait()
    d_normed = dnorm[...] + nt(d_lat_low, wlat[...])
    d_norm1, att_gain_rows = norm_back(tok[...].astype(jnp.float32), g_att[...], d_normed)
    tok_grad[...] = dmid[...] + d_norm1
    small = small + tn(normed[...], d_lat_low[:, RANK:]) + tn(att_gain_rows.astype(jnp.bfloat16), one_lane(80))
    wlat[:, :RANK] = tn(normed[...], d_lat_low[:, :RANK]).astype(jnp.bfloat16)
    wlat[:, RANK:] = small.astype(jnp.bfloat16)
    lat_col = tn(lat_gain_rows.astype(jnp.bfloat16), one_lane(82))
    for b in range(16):
        r = slice(b * 128, b * 128 + 32)
        wlat[r, RANK:] = (small[r] + lat_col[b * 32 : (b + 1) * 32]).astype(jnp.bfloat16)
    stores[0].start()
    for c in stores:
        c.wait()
    for d in range(1, SLOTS):
        pl.when(me >= d)(lambda d=d: send(d).wait_send())


def att_bwd(weights, home, grad, middle, moe_low, tok, normed, lat_raw, qcat, keys, kv, lse, att, wr, g_att, g_moe, g_lat, cos, sin, bias, cid):
    low, f32, S, V = jnp.bfloat16, jnp.float32, pltpu.SemaphoreType.DMA, pltpu.VMEM
    any_, vmem = pl.BlockSpec(memory_space=pl.ANY), pl.BlockSpec(memory_space=pltpu.VMEM)
    shape = lambda kind, *s: jax.ShapeDtypeStruct(s, kind)
    rows, width = tok.shape
    pack = weights.shape[1]
    return pl.pallas_call(
        att_bwd_kernel,
        out_shape=[shape(f32, rows, width), shape(low, width, pack - 512), shape(low, 16, 4, 32, 512)],
        in_specs=[any_, any_] + [vmem] * 9 + [any_] + [vmem] * 9,
        out_specs=[vmem, any_, any_],
        scratch_shapes=[
            V((KEYS, 2048), low), V((width, 1536), low), V((width, 1024), low), V((16, 32, 2048), low),
            V((width, 640), low), V((rows, width), f32), V((rows, width), f32), V((rows, width), low), V((rows, 1024), low),
            V((rows, 1536), low), V((rows, 512), f32), V((KEYS, 128), f32), V((4, rows, 640), low), V((4, rows, 640), low),
            V((rows, 640), f32), V((rows, width + 640), low), V((rows, width + 640), low),
            S((7,)), S, S((4,)), S((4,)), S, S, S((7,)),
        ],
        compiler_params=pltpu.CompilerParams(collective_id=cid, has_side_effects=True, vmem_limit_bytes=60 << 20),
        cost_estimate=pl.CostEstimate(flops=25 * 10**9, bytes_accessed=70 * 10**6, transcendentals=0),
    )(
        weights.reshape(16, 4, 32, pack), weights, home, grad, middle, moe_low, tok, normed, lat_raw, qcat, keys, kv, lse, att, wr,
        g_att, g_moe, g_lat, cos, sin, bias,
    )


def swapped(v):
    return lax.ppermute(v, "tensor", [(0, 1), (1, 0)])


def my_half(v, rows):
    return lax.dynamic_slice_in_dim(v, lax.axis_index("tensor") * rows, rows, 0)


def row_halves(v):
    rows = v.shape[0] // 2
    return my_half(v, rows).reshape(2, rows // 2, v.shape[1])


def exchange(parts):
    return lax.all_to_all(parts, "dp", split_axis=0, concat_axis=0, tiled=True)


def nope_first(w):
    heads = w.reshape(w.shape[0], -1, NOPE + ROPE)
    return jnp.concatenate(
        [heads[:, :, :NOPE].reshape(w.shape[0], -1), heads[:, :, NOPE:].reshape(w.shape[0], -1)], 1
    )


def heads_first(w):
    heads = w.shape[1] // (NOPE + ROPE)
    nope = w[:, : heads * NOPE].reshape(w.shape[0], heads, NOPE)
    rope = w[:, heads * NOPE :].reshape(w.shape[0], heads, ROPE)
    return jnp.concatenate([nope, rope], 2).reshape(w.shape[0], -1)


def shards_sixteen(
    tokens,
    out_grad,
    segments,
    routes,
    attn_gain,
    w_query,
    w_latent,
    latent_gain,
    w_keyval,
    w_out,
    moe_gain,
    w_router,
    shared_gate,
    shared_up,
    shared_down,
    expert_gate,
    routed_up_weight,
    expert_down,
):
    n_rows, width = tokens.shape
    dp_count = lax.axis_size("dp")
    dp_index = lax.axis_index("dp")
    seq_len = segments.shape[1]
    total = n_rows * dp_count
    hop_count = (WINDOW - 1) // n_rows + 1
    n_keys = (hop_count + 1) * n_rows
    experts = w_router.shape[1]
    capacity = 4 * n_rows * TOPK // (3 * experts)
    row_start = dp_index * n_rows
    seg_row = segments[0]
    depth = w_query.shape[0]
    q_width, o_width, kv_width = w_query.shape[1], w_out.shape[0], w_keyval.shape[1]
    kv_rows = w_keyval.shape[0]
    kv_cuts = depth // kv_rows
    kv_part = kv_width // kv_cuts
    lat_width = w_latent.shape[1]
    route_width = n_rows * TOPK // depth
    small = (lat_width + experts + 3 + route_width + 127) // 128 * 128

    gains = jnp.stack(
        [attn_gain, moe_gain, jnp.pad(latent_gain, (0, depth - kv_rows))], 1
    )
    packed = jnp.concatenate(
        [
            nope_first(w_query),
            w_out.T,
            w_latent,
            w_router,
            gains,
            routes.reshape(depth, route_width).astype(jnp.bfloat16),
            jnp.zeros((depth, small - lat_width - experts - 3 - route_width), jnp.bfloat16),
            w_keyval.reshape(kv_rows, kv_cuts, kv_part).transpose(1, 0, 2).reshape(depth, kv_part),
        ],
        1,
    )
    pack_width = packed.shape[1]
    weights, grad_all = ag16(
        [packed.reshape(2, depth // 2, pack_width), row_halves(out_grad)], (False, True), 1
    )
    weights = weights.reshape(width, pack_width)
    shared_part = shared_gate.shape[1] // dp_count
    shared_send = jnp.stack(
        [
            shared_gate.reshape(depth, dp_count, shared_part).transpose(1, 2, 0),
            shared_up.reshape(depth, dp_count, shared_part).transpose(1, 2, 0),
            shared_down.reshape(dp_count, shared_part, depth),
        ],
        1,
    )
    shared_send, weights = lax.optimization_barrier((shared_send, weights))
    shared_all = exchange(shared_send).transpose(1, 2, 0, 3).reshape(3, shared_part, width)
    lead = jnp.pad(shared_all, ((0, 0), (0, 128 - shared_part), (0, 0)))
    shared_in, shared_out = lead[:2].reshape(256, width), lead[2]

    at = q_width + o_width + lat_width
    wr_full = weights[:, at : at + experts]
    at += experts
    gain_attn = weights[:, at].astype(jnp.float32)
    gain_moe = weights[:, at + 1].astype(jnp.float32)
    gain_latent = (
        weights[:, at + 2].reshape(dp_count, depth)[:, :kv_rows].reshape(-1).astype(jnp.float32)
    )

    all_routes = (
        weights[:, at + 3 : at + 3 + route_width].reshape(total, TOPK).astype(jnp.int32)
    )

    local_heads = q_width // (NOPE + ROPE)
    positions = (row_start + jnp.arange(n_rows, dtype=jnp.int32)).astype(jnp.float32)
    cos_tab, sin_tab = rope_tables(positions)
    cos_lanes, sin_lanes = jnp.tile(cos_tab, (1, 2 * local_heads)), jnp.tile(sin_tab, (1, 2 * local_heads))
    key_pos = row_start - hop_count * n_rows + jnp.arange(n_keys, dtype=jnp.int32)
    query_pos = row_start + jnp.arange(n_rows, dtype=jnp.int32)
    padded_seg = jnp.concatenate([jnp.full((hop_count * n_rows,), -1, jnp.int32), seg_row])
    key_seg = lax.dynamic_slice_in_dim(padded_seg, row_start, n_keys, 0)
    query_seg = lax.dynamic_slice_in_dim(seg_row, row_start, n_rows, 0)
    allowed = (key_pos[None, :] >= 0) & (key_pos[None, :] <= query_pos[:, None])
    allowed = (
        allowed
        & (query_pos[:, None] - key_pos[None, :] < WINDOW)
        & (query_seg[:, None] == key_seg[None, :])
    )

    bias = jnp.where(allowed, 0.0, -jnp.inf)
    middle, moe_low, normed_low, lat_raw, qcat, keys, kv, lse, attended_low = att_fwd(
        tokens, weights, gain_attn[None], gain_moe[None], gain_latent[None], cos_lanes, sin_lanes, bias, 7
    )
    moe_low, shared_in, shared_out = lax.optimization_barrier((moe_low, shared_in, shared_out))
    (moe_all,) = ag16([row_halves(moe_low)], (True,), 3)
    chosen = jnp.any(all_routes == dp_index, axis=1).reshape(dp_count, n_rows)
    earlier = jnp.arange(n_rows)[:, None] < jnp.arange(n_rows)[None, :]
    rank = matmul(chosen.astype(jnp.bfloat16), earlier.astype(jnp.bfloat16)).astype(jnp.int32)
    pick = (
        (rank[:, None, :] == jnp.arange(capacity, dtype=jnp.int32)[None, :, None])
        & chosen[:, None, :]
    ).astype(jnp.bfloat16)

    slot_rows = dp_count * capacity
    moe_wr = jnp.pad(wr_full, ((0, 0), (0, 128 - experts)))
    home, rows_in, rows_grad, scaled_act, d_ea_low, d_eb_low, shared_grads = moe_call(
        moe_all.reshape(dp_count, n_rows, width),
        grad_all.reshape(dp_count, n_rows, width),
        pick,
        pick.transpose(0, 2, 1),
        expert_gate[0],
        routed_up_weight[0],
        expert_down[0],
        moe_wr,
        shared_in,
        shared_out,
        4,
    )[:7]
    home = home.reshape(n_rows, 2 * width + 128)
    result = (middle + home[:, :width].astype(jnp.float32)).astype(jnp.bfloat16)
    grad_down = matmul_tn(scaled_act, rows_grad)[None]
    grad_gate = matmul_tn(rows_in, d_ea_low)[None]
    grad_up = matmul_tn(rows_in, d_eb_low)[None]
    shared_home = exchange(
        shared_grads.astype(jnp.bfloat16)
        .reshape(3, 128, dp_count, depth)[:, :shared_part]
        .transpose(2, 0, 1, 3)
    ).astype(jnp.float32)
    shared_home = shared_home.transpose(1, 0, 2, 3).reshape(3, dp_count * shared_part, depth)

    token_input_gradient, packed_grads, kv_grads = att_bwd(
        weights, home[:, width:], out_grad, middle, moe_low, tokens, normed_low, lat_raw, qcat, keys, kv, lse,
        attended_low, moe_wr, gain_attn[None], gain_moe[None], gain_latent[None], cos_lanes, sin_lanes, bias, 8
    )
    packed_grads, shared_home = lax.optimization_barrier((packed_grads, shared_home))
    mine = rs16(
        packed_grads.reshape(dp_count, 2, depth // 2, pack_width - kv_part),
        kv_grads.reshape(dp_count, 2, depth // 2, kv_part),
        6,
    ).reshape(depth, pack_width)
    grad_sgate, grad_sup, grad_sdown = shared_home[0].T, shared_home[1].T, shared_home[2]
    out_wq = heads_first(mine[:, :q_width])
    at = q_width
    out_wo = mine[:, at : at + o_width].T
    at += o_width
    out_wlat = mine[:, at : at + lat_width]
    at += lat_width
    out_router = mine[:, at : at + experts]
    at += experts
    out_wkv = (
        mine[:, pack_width - kv_part :]
        .reshape(kv_cuts, kv_rows, kv_part)
        .transpose(1, 0, 2)
        .reshape(kv_rows, kv_width)
    )
    return (
        result,
        token_input_gradient,
        mine[:, at],
        out_wq,
        out_wlat,
        mine[:kv_rows, at + 2],
        out_wkv,
        out_wo,
        mine[:, at + 1],
        out_router,
        grad_sgate,
        grad_sup,
        grad_sdown,
        grad_gate,
        grad_up,
        grad_down,
    )


def shards_general(
    tokens,
    out_grad,
    segments,
    routes,
    attn_gain,
    w_query,
    w_latent,
    latent_gain,
    w_keyval,
    w_out,
    moe_gain,
    w_router,
    shared_gate,
    shared_up,
    shared_down,
    expert_gate,
    routed_up_weight,
    expert_down,
):
    n_rows = tokens.shape[0]
    model_width = tokens.shape[1]
    dp_count = lax.axis_size("dp")
    dp_index = lax.axis_index("dp")
    seq_len = segments.shape[1]
    seq_devs = seq_len // n_rows
    hop_count = (WINDOW - 1) // n_rows + 1
    n_keys = (hop_count + 1) * n_rows
    experts = w_router.shape[1]
    local_experts = expert_gate.shape[0]
    capacity = 4 * n_rows * TOPK // (3 * experts)
    slot_total = experts * capacity
    score_scale = (NOPE + ROPE) ** (-0.5)
    row_start = dp_index % seq_devs * n_rows
    seg_row = lax.dynamic_index_in_dim(segments, dp_index // seq_devs, 0, keepdims=False)
    gathered = (
        lax.all_gather(attn_gain, "dp", axis=0, tiled=True),
        lax.all_gather(w_query, "dp", axis=0, tiled=True),
        lax.all_gather(w_latent, "dp", axis=0, tiled=True),
        lax.all_gather(latent_gain, "dp", axis=0, tiled=True),
        lax.all_gather(w_keyval, "dp", axis=0, tiled=True),
        lax.all_gather(w_out, "dp", axis=1, tiled=True),
        lax.all_gather(moe_gain, "dp", axis=0, tiled=True),
        lax.all_gather(w_router, "dp", axis=0, tiled=True),
        lax.all_gather(shared_gate, "dp", axis=0, tiled=True),
        lax.all_gather(shared_up, "dp", axis=0, tiled=True),
        lax.all_gather(shared_down, "dp", axis=1, tiled=True),
    )
    (
        gain_attn,
        wq_full,
        wlat_full,
        gain_latent,
        wkv_full,
        wo_full,
        gain_moe,
        wr_full,
        sgate_full,
        sup_full,
        sdown_full,
    ) = gathered
    local_heads = wq_full.shape[1] // (NOPE + ROPE)
    positions = (row_start + jnp.arange(n_rows, dtype=jnp.int32)).astype(jnp.float32)
    cos_tab, sin_tab = rope_tables(positions)
    resid_in = tokens.astype(jnp.float32)
    normed, attn_norm_back = jax.vjp(rms_scale, resid_in, gain_attn.astype(jnp.float32))
    normed_low = normed.astype(jnp.bfloat16)

    def rope_queries(q_flat):
        shaped = q_flat.reshape(n_rows, local_heads, NOPE + ROPE)
        return jnp.concatenate(
            [shaped[..., :NOPE], rotate(shaped[..., NOPE:], cos_tab[:, None], sin_tab[:, None])], -1
        )

    queries, query_back = jax.vjp(rope_queries, matmul(normed_low, wq_full))
    query_low = queries.astype(jnp.bfloat16)

    def latent_piece(latent_raw, gain_vec):
        return (
            rms_scale(latent_raw[:, :RANK], gain_vec),
            rotate(latent_raw[:, RANK:], cos_tab, sin_tab),
        )

    (latent, key_rope), latent_back = jax.vjp(
        latent_piece, matmul(normed_low, wlat_full), gain_latent.astype(jnp.float32)
    )
    latent_low = latent.astype(jnp.bfloat16)
    rope_low = key_rope.astype(jnp.bfloat16)
    latent_parts = []
    rope_parts = []
    for distance in range(hop_count, 0, -1):
        moved_latent, moved_rope = passed_along((latent_low, rope_low), "dp", distance)
        latent_parts.append(moved_latent)
        rope_parts.append(moved_rope)
    keys_latent = jnp.concatenate(latent_parts + [latent_low], 0)
    keys_rope = jnp.concatenate(rope_parts + [rope_low], 0)
    keyval = (
        matmul(keys_latent, wkv_full).astype(jnp.bfloat16).reshape(n_keys, local_heads, NOPE + VDIM)
    )
    key_nope = keyval[..., :NOPE]
    values = keyval[..., NOPE:]
    key_pos = row_start - hop_count * n_rows + jnp.arange(n_keys, dtype=jnp.int32)
    query_pos = row_start + jnp.arange(n_rows, dtype=jnp.int32)
    padded_seg = jnp.concatenate([jnp.full((hop_count * n_rows,), -1, jnp.int32), seg_row])
    key_seg = lax.dynamic_slice_in_dim(padded_seg, row_start, n_keys, 0)
    query_seg = lax.dynamic_slice_in_dim(seg_row, row_start, n_rows, 0)
    allowed = (key_pos[None, :] >= 0) & (key_pos[None, :] <= query_pos[:, None])
    allowed = (
        allowed
        & (query_pos[:, None] - key_pos[None, :] < WINDOW)
        & (query_seg[:, None] == key_seg[None, :])
    )

    def masked_scores():
        nope_part = jnp.einsum(
            "qhd,khd->hqk", query_low[..., :NOPE], key_nope, preferred_element_type=jnp.float32
        )
        rope_part = jnp.einsum(
            "qhr,kr->hqk", query_low[..., NOPE:], keys_rope, preferred_element_type=jnp.float32
        )
        return jnp.where(allowed[None], score_scale * (nope_part + rope_part), -jnp.inf)

    scores = masked_scores()
    top_score = jnp.max(scores, axis=-1, keepdims=True)
    exp_scores = jnp.exp(scores - top_score)
    denom = jnp.sum(exp_scores, axis=-1, keepdims=True)
    attn_probs = exp_scores / denom
    log_total = top_score + jnp.log(denom)
    attended = jnp.einsum(
        "hqk,khv->qhv", attn_probs.astype(jnp.bfloat16), values, preferred_element_type=jnp.float32
    )
    attended_low = attended.astype(jnp.bfloat16).reshape(n_rows, local_heads * VDIM)
    attn_out = lax.psum(matmul(attended_low, wo_full).astype(jnp.bfloat16), "tensor").astype(
        jnp.float32
    )
    middle = resid_in + attn_out
    moe_normed, moe_norm_back = jax.vjp(rms_scale, middle, gain_moe.astype(jnp.float32))
    moe_low = moe_normed.astype(jnp.bfloat16)
    router, router_back = jax.vjp(
        lambda logit_vals: jax.nn.softmax(logit_vals, axis=-1), matmul(moe_low, wr_full)
    )
    expert_ids = jnp.arange(experts, dtype=jnp.int32)
    route_hot = (routes[:, :, None] == expert_ids[None, None, :]).astype(jnp.float32)
    gate_w = jnp.einsum("te,tke->tk", router, route_hot, precision=highest)
    flat_routes = routes.reshape(-1)
    assign_count = flat_routes.shape[0]
    flat_hot = (flat_routes[:, None] == expert_ids[None, :]).astype(jnp.int32)
    earlier = ranks_before(flat_hot)
    slot_in = jnp.sum(earlier * flat_hot, axis=1)
    target = flat_routes * capacity + slot_in
    assign_ids = jnp.arange(assign_count, dtype=jnp.int32)
    assign_of_slot = jnp.zeros((slot_total,), jnp.int32).at[target].set(assign_ids)
    slot_live = (
        jnp.zeros((slot_total,), jnp.bfloat16)
        .at[target]
        .set(jnp.ones((assign_count,), jnp.bfloat16))
    )
    send_rows = moe_low[assign_of_slot // TOPK] * slot_live[:, None]
    recv_rows = lax.all_to_all(
        send_rows.reshape(dp_count, local_experts * capacity, model_width),
        "dp",
        split_axis=0,
        concat_axis=0,
        tiled=True,
    )
    received_four_parts = recv_rows.reshape(dp_count, local_experts, capacity, model_width)
    exp_gate = jnp.einsum(
        "sjcd,jdf->sjcf", received_four_parts, expert_gate, preferred_element_type=jnp.float32
    )
    exp_up = jnp.einsum(
        "sjcd,jdf->sjcf", received_four_parts, routed_up_weight, preferred_element_type=jnp.float32
    )
    exp_act, exp_act_back = jax.vjp(gated_act, exp_gate, exp_up)
    exp_act_low = exp_act.astype(jnp.bfloat16)
    exp_result = jnp.einsum(
        "sjcf,jfd->sjcd", exp_act_low, expert_down, preferred_element_type=jnp.float32
    )
    returned = lax.all_to_all(
        exp_result.reshape(dp_count, local_experts * capacity, model_width).astype(jnp.bfloat16),
        "dp",
        split_axis=0,
        concat_axis=0,
        tiled=True,
    ).astype(jnp.float32)
    per_assign = returned.reshape(slot_total, model_width)[target].reshape(
        n_rows, TOPK, model_width
    )
    routed = jnp.einsum("tk,tkd->td", gate_w, per_assign, precision=highest)
    shared_a = matmul(moe_low, sgate_full)
    shared_b = matmul(moe_low, sup_full)
    shared_act, shared_back = jax.vjp(gated_act, shared_a, shared_b)
    shared_low = shared_act.astype(jnp.bfloat16)
    moe_out = lax.psum(
        (routed + matmul(shared_low, sdown_full)).astype(jnp.bfloat16), "tensor"
    ).astype(jnp.float32)
    result = (middle + moe_out).astype(jnp.bfloat16)
    grad_y = out_grad.astype(jnp.float32)
    grad_sdown = matmul_tn(shared_low, out_grad)
    d_shared_a, d_shared_b = shared_back(matmul_nt(out_grad, sdown_full))
    d_sa_low = d_shared_a.astype(jnp.bfloat16)
    d_sb_low = d_shared_b.astype(jnp.bfloat16)
    grad_sgate = matmul_tn(moe_low, d_sa_low)
    grad_sup = matmul_tn(moe_low, d_sb_low)
    d_moe = matmul_nt(d_sa_low, sgate_full) + matmul_nt(d_sb_low, sup_full)
    d_gate_part = jnp.einsum("td,tkd->tk", grad_y, per_assign, precision=highest)
    d_assign = (
        (gate_w[:, :, None] * grad_y[:, None, :])
        .astype(jnp.bfloat16)
        .reshape(assign_count, model_width)
    )
    send_grads = d_assign[assign_of_slot] * slot_live[:, None]
    recv_grads = lax.all_to_all(
        send_grads.reshape(dp_count, local_experts * capacity, model_width),
        "dp",
        split_axis=0,
        concat_axis=0,
        tiled=True,
    )
    recv_grads = recv_grads.reshape(dp_count, local_experts, capacity, model_width)
    expert_down_weight_gradient = jnp.einsum(
        "sjcf,sjcd->jfd", exp_act_low, recv_grads, preferred_element_type=jnp.float32
    )
    d_exp_act = jnp.einsum(
        "sjcd,jfd->sjcf", recv_grads, expert_down, preferred_element_type=jnp.float32
    )
    d_exp_gate, expert_up_act_gradient = exp_act_back(d_exp_act)
    d_egate_low = d_exp_gate.astype(jnp.bfloat16)
    expert_up_gradient_lowp = expert_up_act_gradient.astype(jnp.bfloat16)
    expert_gate_weight_gradient = jnp.einsum(
        "bmky,bmkx->myx", received_four_parts, d_egate_low, preferred_element_type=jnp.float32
    )
    expert_up_weight_gradient = jnp.einsum(
        "bmky,bmkx->myx",
        received_four_parts,
        expert_up_gradient_lowp,
        preferred_element_type=jnp.float32,
    )
    d_slots = jnp.einsum(
        "hteg,tmg->htem", d_egate_low, expert_gate, preferred_element_type=jnp.float32
    )
    d_slots = d_slots + jnp.einsum(
        "hteg,tmg->htem",
        expert_up_gradient_lowp,
        routed_up_weight,
        preferred_element_type=jnp.float32,
    )
    back_grads = lax.all_to_all(
        d_slots.reshape(dp_count, local_experts * capacity, model_width).astype(jnp.bfloat16),
        "dp",
        split_axis=0,
        concat_axis=0,
        tiled=True,
    ).astype(jnp.float32)
    d_moe = d_moe + jnp.sum(
        back_grads.reshape(slot_total, model_width)[target].reshape(n_rows, TOPK, model_width),
        axis=1,
    )
    d_moe, d_gate = (
        lax.psum(d_moe.astype(jnp.bfloat16), "tensor").astype(jnp.float32),
        lax.psum(d_gate_part.astype(jnp.bfloat16), "tensor").astype(jnp.float32),
    )
    d_router = jnp.einsum("tk,tke->te", d_gate, route_hot, precision=highest)
    (d_logits,) = router_back(d_router)
    d_logits_low = d_logits.astype(jnp.bfloat16)
    grad_router = matmul_tn(moe_low, d_logits_low)
    d_moe = d_moe + matmul_nt(d_logits_low, wr_full)
    d_mid_norm, grad_gain_moe = moe_norm_back(d_moe)
    d_middle = grad_y + d_mid_norm
    d_middle_low = d_middle.astype(jnp.bfloat16)
    grad_wout = matmul_tn(attended_low, d_middle_low)
    d_att_low = (
        matmul_nt(d_middle_low, wo_full).astype(jnp.bfloat16).reshape(n_rows, local_heads, VDIM)
    )
    again_probs = jnp.exp(masked_scores() - log_total)
    d_values = jnp.einsum(
        "hqk,qhv->khv",
        again_probs.astype(jnp.bfloat16),
        d_att_low,
        preferred_element_type=jnp.float32,
    )
    d_probs = jnp.einsum("qhv,khv->hqk", d_att_low, values, preferred_element_type=jnp.float32)
    d_scores = (
        again_probs * (d_probs - jnp.sum(d_probs * again_probs, axis=-1, keepdims=True))
    ).astype(jnp.bfloat16)
    d_query_nope = score_scale * jnp.einsum(
        "hqk,khd->qhd", d_scores, key_nope, preferred_element_type=jnp.float32
    )
    d_query_rope = score_scale * jnp.einsum(
        "hqk,kr->qhr", d_scores, keys_rope, preferred_element_type=jnp.float32
    )
    d_key_nope = score_scale * jnp.einsum(
        "hqk,qhd->khd", d_scores, query_low[..., :NOPE], preferred_element_type=jnp.float32
    )
    d_key_rope = score_scale * jnp.einsum(
        "hqk,qhr->kr", d_scores, query_low[..., NOPE:], preferred_element_type=jnp.float32
    )
    (d_q_raw,) = query_back(jnp.concatenate([d_query_nope, d_query_rope], -1))
    d_q_low = d_q_raw.astype(jnp.bfloat16)
    grad_wq = matmul_tn(normed_low, d_q_low)
    d_normed = matmul_nt(d_q_low, wq_full)
    d_kv_low = (
        jnp.concatenate([d_key_nope, d_values], -1)
        .astype(jnp.bfloat16)
        .reshape(n_keys, local_heads * (NOPE + VDIM))
    )
    grad_wkv = matmul_tn(keys_latent, d_kv_low)
    d_keys_latent = matmul_nt(d_kv_low, wkv_full)
    own_latent = d_keys_latent[hop_count * n_rows :]
    own_rope = d_key_rope[hop_count * n_rows :]
    for distance in range(hop_count, 0, -1):
        block_index = hop_count - distance
        lower = block_index * n_rows
        home_latent, home_rope = (
            passed_along(
                d_keys_latent[lower : lower + n_rows].astype(jnp.bfloat16), "dp", -distance
            ).astype(jnp.float32),
            passed_along(
                d_key_rope[lower : lower + n_rows].astype(jnp.bfloat16), "dp", -distance
            ).astype(jnp.float32),
        )
        own_latent = own_latent + home_latent
        own_rope = own_rope + home_rope
    d_normed, own_latent, own_rope = (
        lax.psum(d_normed.astype(jnp.bfloat16), "tensor").astype(jnp.float32),
        lax.psum(own_latent.astype(jnp.bfloat16), "tensor").astype(jnp.float32),
        lax.psum(own_rope.astype(jnp.bfloat16), "tensor").astype(jnp.float32),
    )
    d_latent_raw, grad_gain_latent = latent_back((own_latent, own_rope))
    d_latent_low = d_latent_raw.astype(jnp.bfloat16)
    grad_wlat = matmul_tn(normed_low, d_latent_low)
    d_normed = d_normed + matmul_nt(d_latent_low, wlat_full)
    d_tokens_norm, grad_gain_attn = attn_norm_back(d_normed)
    token_input_gradient = d_middle + d_tokens_norm
    reduced_result = tuple(
        (
            lax.psum_scatter(grad_gain_attn, "dp", scatter_dimension=0, tiled=True),
            lax.psum_scatter(grad_wq, "dp", scatter_dimension=0, tiled=True),
            lax.psum_scatter(grad_wlat, "dp", scatter_dimension=0, tiled=True),
            lax.psum_scatter(grad_gain_latent, "dp", scatter_dimension=0, tiled=True),
            lax.psum_scatter(grad_wkv, "dp", scatter_dimension=0, tiled=True),
            lax.psum_scatter(grad_wout, "dp", scatter_dimension=1, tiled=True),
            lax.psum_scatter(grad_gain_moe, "dp", scatter_dimension=0, tiled=True),
            lax.psum_scatter(grad_router, "dp", scatter_dimension=0, tiled=True),
            lax.psum_scatter(grad_sgate, "dp", scatter_dimension=0, tiled=True),
            lax.psum_scatter(grad_sup, "dp", scatter_dimension=0, tiled=True),
            lax.psum_scatter(grad_sdown, "dp", scatter_dimension=1, tiled=True),
        )
    )
    return (
        (result, token_input_gradient)
        + reduced_result
        + (expert_gate_weight_gradient, expert_up_weight_gradient, expert_down_weight_gradient)
    )


def solution(mesh):
    placed = (
        P("dp", None),
        P("dp", None),
        P(),
        P("dp", None),
        P("dp"),
        P("dp", "tensor"),
        P("dp", None),
        P("dp"),
        P("dp", "tensor"),
        P("tensor", "dp"),
        P("dp"),
        P("dp", None),
        P("dp", "tensor"),
        P("dp", "tensor"),
        P("tensor", "dp"),
        P("dp", None, "tensor"),
        P("dp", None, "tensor"),
        P("dp", "tensor", None),
    )
    sixteen = mesh.shape["dp"] == 16 and mesh.shape["tensor"] == 2

    def body(*args):
        fits_sixteen = sixteen and args[2].shape[0] == 1 and args[15].shape[0] == 1 and args[0].shape[0] == 256
        return (shards_sixteen if fits_sixteen else shards_general)(*args)

    return jax.shard_map(
        body,
        mesh=mesh,
        in_specs=placed,
        out_specs=(
            P("dp", None),
            P("dp", None),
            P("dp"),
            P("dp", "tensor"),
            P("dp", None),
            P("dp"),
            P("dp", "tensor"),
            P("tensor", "dp"),
            P("dp"),
            P("dp", None),
            P("dp", "tensor"),
            P("dp", "tensor"),
            P("tensor", "dp"),
            P("dp", None, "tensor"),
            P("dp", None, "tensor"),
            P("dp", "tensor", None),
        ),
        check_vma=False,
    )
```

```python
import functools
import math

import jax
import jax.numpy as jnp
from jax import lax
from jax.experimental import pallas as pl
from jax.experimental.pallas import tpu as pltpu
from jax.sharding import PartitionSpec as P

NOPE = 128
ROPE = 64
VDIM = 128
RANK = 512
TOPK = 6
WINDOW = 1024


eps_norm = 1e-06
highest = lax.Precision.HIGHEST


def passed_along(value, axis, steps):
    count = lax.axis_size(axis)
    leading, last = (max(0, -steps), min(count, count - steps))
    return lax.ppermute(value, axis, [(source, source + steps) for source in range(leading, last)])


def rms_scale(values, gain_vec):
    inv_root = lax.rsqrt(jnp.mean(values * values, axis=-1, keepdims=True) + eps_norm)
    return values * inv_root * gain_vec


def rope_tables(positions):
    half_width = ROPE // 2
    frequency = jnp.exp(
        -jnp.arange(half_width, dtype=jnp.float32) * (2.0 * math.log(10000.0) / ROPE)
    )
    angles = positions[:, None] * frequency[None, :]
    return (jnp.cos(angles), jnp.sin(angles))


def rotate(values, cos_tab, sin_tab):
    half_width = values.shape[-1] // 2
    first_half = values[..., :half_width]
    second = values[..., half_width:]
    return jnp.concatenate(
        [first_half * cos_tab - second * sin_tab, second * cos_tab + first_half * sin_tab], axis=-1
    )


def gated_act(gate_a, up_b):
    return jax.nn.silu(gate_a) * up_b


def matmul(left_mat, right_mat):
    return jnp.dot(left_mat, right_mat, preferred_element_type=jnp.float32)


def matmul_nt(left_mat, right_mat):
    return lax.dot_general(
        left_mat, right_mat, (((1,), (1,)), ((), ())), preferred_element_type=jnp.float32
    )


def matmul_tn(left_mat, right_mat):
    return lax.dot_general(
        left_mat, right_mat, (((0,), (0,)), ((), ())), preferred_element_type=jnp.float32
    )


def ranks_before(hot):
    count = hot.shape[0]
    below = jnp.arange(count)[:, None] > jnp.arange(count)[None, :]
    return matmul(below.astype(jnp.bfloat16), hot.astype(jnp.bfloat16)).astype(jnp.int32)


MESH = pl.DeviceIdType.MESH


def plane_at(z, k):
    edge = jnp.where(z >= 2, 3 - z, z)
    near = jnp.where(k == 0, edge, jnp.where(k == 1, 1 - edge, k))
    return jnp.where(z >= 2, 3 - near, near)


def ag_kernel(kinds, cuts, *refs):
    n = len(kinds)
    ins, outs, lands, sems = refs[:n], refs[n : 2 * n], refs[2 * n : 3 * n], refs[3 * n :]
    me = lax.axis_index("dp")
    core = lax.axis_index("tensor")
    z = me // 4
    y = (me // 2) % 2
    x = me % 2
    xn = z * 4 + y * 2 + (1 - x)
    yn = z * 4 + (1 - y) * 2 + x
    up = jnp.minimum(z + 1, 3) * 4 + y * 2 + x
    dn = jnp.maximum(z - 1, 0) * 4 + y * 2 + x
    bar = pltpu.get_barrier_semaphore()

    def sig(d, c):
        pl.semaphore_signal(bar, inc=1, device_id=(d, c), device_id_type=MESH)

    sig(xn, core)
    sig(yn, core)
    sig(me, 1 - core)
    pl.when(z < 3)(lambda: sig(up, core))
    pl.when(z > 0)(lambda: sig(dn, core))

    def rc(src, dst, ss, rs, dev, c):
        return pltpu.make_async_remote_copy(
            src_ref=src, dst_ref=dst, send_sem=ss, recv_sem=rs, device_id=(dev, c), device_id_type=MESH
        )

    class Part:
        def __init__(self, at, rows):
            self.share = kinds[at]
            self.x, self.o, self.hbm = ins[at], lands[at], outs[at]
            self.rows = rows
            self.zs, self.zr, self.xs, self.xr, self.ys, self.yr, self.cs, self.cr, self.own, self.out = sems[20 * at + 10 : 20 * at + 20]
            self.slot = core if self.share else 0
            self.copy = pltpu.make_async_copy(self.x.at[:, self.rows], self.whole(me), self.own)

        def whole(self, b):
            return self.o.at[b, self.slot, :, self.rows]

        def z_(self, zp, dev, s):
            b = zp * 4 + y * 2 + x
            return rc(self.whole(b), self.whole(b), self.zs.at[s], self.zr.at[zp], dev, core)

        def x_(self, j, b, half, zp):
            r = self.o.at[b, self.slot, half, self.rows]
            return rc(r, r, self.xs.at[zp, j], self.xr.at[zp, j], xn, core)

        def y_(self, j, b, half, zp):
            r = self.o.at[b, self.slot, half, self.rows]
            return rc(r, r, self.ys.at[zp, j], self.yr.at[zp, j], yn, core)

        def twin(self, b):
            return rc(self.whole(b), self.whole(b), self.cs.at[b], self.cr.at[b], me, 1 - core)

        def first(self, k):
            zp = plane_at(z, k)
            b = zp * 4 + y * 2 + x
            if k > 0:
                self.z_(zp, up, 0).wait_recv()
            pl.when((zp <= z) & (z < 3))(lambda: self.z_(zp, up, zp).start())
            pl.when((zp >= z) & (z > 0))(lambda: self.z_(zp, dn, 4 + zp).start())
            self.x_(0, b, 0, zp).start()
            self.y_(0, b, 1, zp).start()
            self.y_(1, b, 0, zp).start()
            self.x_(1, b, 1, zp).start()
            if self.share:
                self.twin(b).start()

        def second(self, k):
            zp = plane_at(z, k)
            bx = zp * 4 + y * 2 + (1 - x)
            by = zp * 4 + (1 - y) * 2 + x
            self.x_(0, bx, 0, zp).wait_recv()
            self.y_(2, bx, 0, zp).start()
            self.y_(0, by, 1, zp).wait_recv()
            self.x_(2, by, 1, zp).start()
            self.x_(1, bx, 1, zp).wait_recv()
            self.y_(1, by, 0, zp).wait_recv()
            if self.share:
                self.twin(bx).start()
                self.twin(by).start()

        def third(self, k):
            zp = plane_at(z, k)
            bd = zp * 4 + (1 - y) * 2 + (1 - x)
            self.y_(2, bd, 0, zp).wait_recv()
            self.x_(2, bd, 1, zp).wait_recv()
            if self.share:
                self.twin(bd).start()

        def save(self, k):
            at = pl.ds(plane_at(z, k) * 4, 4)
            return pltpu.make_async_copy(
                self.o.at[at, :, :, self.rows], self.hbm.at[at, :, :, self.rows], self.out.at[k]
            )

        def fourth(self, k):
            if self.share:
                for q in range(4):
                    b = plane_at(z, k) * 4 + q
                    src, dst = self.o.at[b, core, :, self.rows], self.o.at[b, 1 - core, :, self.rows]
                    rc(src, dst, self.cs.at[b], self.cr.at[b], me, 1 - core).wait_recv()
            self.save(k).start()

        def end(self):
            for k in range(4):
                self.save(k).wait()
                pl.when((k <= z) & (z < 3))(lambda k=k: self.z_(k, up, k).wait_send())
                pl.when((k >= z) & (z > 0))(lambda k=k: self.z_(k, dn, 4 + k).wait_send())
                for j in range(3):
                    self.x_(j, 0, 0, k).wait_send()
                    self.y_(j, 0, 0, k).wait_send()
            if self.share:
                for b in range(16):
                    self.twin(b).wait_send()

    class Cross:
        def __init__(self, at, rows):
            self.share = kinds[at]
            self.x, self.o, self.hbm = ins[at], lands[at], outs[at]
            self.rows = rows
            self.fs, self.fr, self.zs, self.zr, self.ls, self.lr, self.cs, self.cr, self.own, self.out = sems[20 * at : 20 * at + 10]
            self.slot = core if self.share else 0
            self.copy = pltpu.make_async_copy(self.x.at[:, rows], self.o.at[me, self.slot, :, rows], self.own)

        def ref(self, b, half):
            return self.o.at[b, self.slot, half, self.rows]

        def block(self, zp, half, p):
            if half == 0:
                return zp * 4 + y * 2 + (x if p == 0 else 1 - x)
            return zp * 4 + (y if p == 0 else 1 - y) * 2 + x

        def hop(self, half):
            r = self.ref(me, half)
            return rc(r, r, self.fs.at[half], self.fr.at[half], xn if half == 0 else yn, core)

        def line(self, zp, half, p, d):
            r = self.ref(self.block(zp, half, p), half)
            return rc(r, r, self.zs.at[d, zp, half, p], self.zr.at[zp, half, p], up if d == 0 else dn, core)

        def last(self, zp, half, p):
            r = self.ref(self.block(zp, half, p), half)
            return rc(r, r, self.ls.at[zp, half, p], self.lr.at[zp, half, p], yn if half == 0 else xn, core)

        def twin(self, b, half):
            r = self.ref(b, half)
            return rc(r, r, self.cs.at[b, half], self.cr.at[b, half], me, 1 - core)

        def pass_on(self, zp, half, p):
            pl.when((zp <= z) & (z < 3))(lambda: self.line(zp, half, p, 0).start())
            pl.when((zp >= z) & (z > 0))(lambda: self.line(zp, half, p, 1).start())
            self.last(zp, half, p).start()
            if self.share:
                self.twin(self.block(zp, half, p), half).start()

        def first(self, k):
            zp = plane_at(z, k)
            if k == 0:
                for half in range(2):
                    self.hop(half).start()
                for half in range(2):
                    self.pass_on(zp, half, 0)
                for half in range(2):
                    self.hop(half).wait_recv()
                    self.pass_on(zp, half, 1)
            else:
                for p in range(2):
                    for half in range(2):
                        self.line(zp, half, p, 0).wait_recv()
                        self.pass_on(zp, half, p)

        def second(self, k):
            pass

        def third(self, k):
            zp = plane_at(z, k)
            for p in range(2):
                for half in range(2):
                    self.last(zp, half, p).wait_recv()
                    if self.share:
                        far = zp * 4 + (1 - y) * 2 + (x if p == 0 else 1 - x)
                        if half == 1:
                            far = zp * 4 + (y if p == 0 else 1 - y) * 2 + (1 - x)
                        self.twin(far, half).start()

        def save(self, k):
            at = pl.ds(plane_at(z, k) * 4, 4)
            return pltpu.make_async_copy(
                self.o.at[at, :, :, self.rows], self.hbm.at[at, :, :, self.rows], self.out.at[k]
            )

        def fourth(self, k):
            if self.share:
                for q in range(4):
                    b = plane_at(z, k) * 4 + q
                    for half in range(2):
                        src, dst = self.o.at[b, core, half, self.rows], self.o.at[b, 1 - core, half, self.rows]
                        rc(src, dst, self.cs.at[b, half], self.cr.at[b, half], me, 1 - core).wait_recv()
            self.save(k).start()

        def end(self):
            for half in range(2):
                self.hop(half).wait_send()
            for k in range(4):
                self.save(k).wait()
                for half in range(2):
                    for p in range(2):
                        pl.when((k <= z) & (z < 3))(lambda k=k, h=half, p=p: self.line(k, h, p, 0).wait_send())
                        pl.when((k >= z) & (z > 0))(lambda k=k, h=half, p=p: self.line(k, h, p, 1).wait_send())
                        self.last(k, half, p).wait_send()
            if self.share:
                for b in range(16):
                    for half in range(2):
                        self.twin(b, half).wait_send()

    groups = []
    for at in range(n):
        height = ins[at].shape[1]
        group = [Cross(at, pl.ds(0, cuts[at]))] if cuts[at] > 0 else []
        if cuts[at] < height:
            group.append(Part(at, pl.ds(cuts[at], height - cuts[at])))
        groups.append(group)
    parts = [p for g in groups for p in g]
    for p in parts:
        p.copy.start()
    pl.semaphore_wait(bar, 3 + (z < 3).astype(jnp.int32) + (z > 0).astype(jnp.int32))
    for p in parts:
        p.copy.wait()
    turns = [(p, k) for k in range(4) for p in parts]
    lag = len(parts)
    for t in range(len(turns) + lag):
        if t < len(turns):
            turns[t][0].first(turns[t][1])
        if t >= lag:
            turns[t - lag][0].second(turns[t - lag][1])
    for p, k in turns:
        p.third(k)
        if not p.share:
            p.fourth(k)
    for p, k in turns:
        if p.share:
            p.fourth(k)
    for p in parts:
        p.end()


def ag16(arrays, kinds, cid, cuts=None):
    S = pltpu.SemaphoreType.DMA
    any_ = pl.BlockSpec(memory_space=pl.ANY)
    cuts = cuts or tuple(v.shape[1] // 2 for v in arrays)
    counts = (
        ((2,), (2,), (2, 4, 2, 2), (4, 2, 2), (4, 2, 2), (4, 2, 2), (16, 2), (16, 2), (), (4,))
        + ((8,), (4,), (4, 3), (4, 3), (4, 3), (4, 3), (16,), (16,), (), (4,))
    )
    shapes = [(16, 2 if share else 1) + v.shape for v, share in zip(arrays, kinds)]
    return pl.pallas_call(
        functools.partial(ag_kernel, kinds, cuts),
        out_shape=[jax.ShapeDtypeStruct(s, v.dtype) for s, v in zip(shapes, arrays)],
        in_specs=[any_] * len(arrays),
        out_specs=[any_] * len(arrays),
        scratch_shapes=[pltpu.VMEM(s, v.dtype) for s, v in zip(shapes, arrays)]
        + [S(s) for _ in arrays for s in counts],
        compiler_params=pltpu.CompilerParams(collective_id=cid, has_side_effects=True, vmem_limit_bytes=60 << 20),
    )(*arrays)


def add_into(dst, src):
    def step(i, _):
        r = pl.ds(pl.multiple_of(i * 16, 16), 16)
        dst[r] = dst[r] + src[r]
        return 0

    lax.fori_loop(0, dst.shape[0] // 16, step, 0)


def rs_kernel(a_ref, b_ref, o_ref, own, fr, zr, lr, yr, xr, z2r, lsem, fs, frs, zs, zrs, ls, lrs, xs, xrs, ys, yrs, z2s, z2rs):
    me = lax.axis_index("dp")
    core = lax.axis_index("tensor")
    z = me // 4
    y = (me // 2) % 2
    x = me % 2
    xn = z * 4 + y * 2 + (1 - x)
    yn = z * 4 + (1 - y) * 2 + x
    up = jnp.minimum(z + 1, 3) * 4 + y * 2 + x
    dn = jnp.maximum(z - 1, 0) * 4 + y * 2 + x
    wide = a_ref.shape[3]
    cut = fr.shape[3]
    crossing, rest = pl.ds(0, cut), pl.ds(cut, own.shape[2] - cut)

    def rc(src, dst, ss, rs, dev):
        return pltpu.make_async_remote_copy(
            src_ref=src, dst_ref=dst, send_sem=ss, recv_sem=rs, device_id=(dev, core), device_id_type=MESH
        )

    def loads(zp):
        at = pl.ds(zp * 4, 4)
        return [
            pltpu.make_async_copy(a_ref.at[at], own.at[at, :, :, 0:wide], lsem.at[zp, 0]),
            pltpu.make_async_copy(b_ref.at[at], own.at[at, :, :, wide:], lsem.at[zp, 1]),
        ]

    for k in range(4):
        for c in loads(plane_at(z, 3 - k)):
            c.start()
    bar = pltpu.get_barrier_semaphore()

    def sig(d):
        pl.semaphore_signal(bar, inc=1, device_id=(d, core), device_id_type=MESH)

    sig(xn)
    sig(yn)
    pl.when(z < 3)(lambda: sig(up))
    pl.when(z > 0)(lambda: sig(dn))
    pl.semaphore_wait(bar, 2 + (z < 3).astype(jnp.int32) + (z > 0).astype(jnp.int32))

    def blk(zp, yy, xx):
        return zp * 4 + yy * 2 + xx

    def place(zp, half, p):
        if half == 0:
            return blk(zp, y, x if p == 0 else 1 - x)
        return blk(zp, y if p == 0 else 1 - y, x)

    def hop(zp, half, p):
        b = blk(zp, 1 - y, x if p == 0 else 1 - x) if half == 0 else blk(zp, y if p == 0 else 1 - y, 1 - x)
        return rc(
            own.at[b, half, crossing], fr.at[zp, half, p], fs.at[zp, half, p], frs.at[zp, half, p], yn if half == 0 else xn
        )

    def line(zp, half, p, dev, slot):
        b = place(zp, half, p)
        return rc(own.at[b, half, crossing], zr.at[slot, half, p], zs.at[zp, half, p], zrs.at[slot, half, p], dev)

    def last(half):
        b = place(z, half, 1)
        return rc(own.at[b, half, crossing], lr.at[half], ls.at[half], lrs.at[half], xn if half == 0 else yn)

    def y_(j, b, half, zp):
        return rc(own.at[b, half, rest], yr.at[zp, j], ys.at[zp, j], yrs.at[zp, j], yn)

    def x_(j, b, half, zp):
        return rc(own.at[b, half, rest], xr.at[zp, j], xs.at[zp, j], xrs.at[zp, j], xn)

    def zc(zp, dev, d):
        return rc(own.at[zp * 4 + y * 2 + x, :, rest], z2r.at[d, zp], z2s.at[zp], z2rs.at[d, zp], dev)

    def s1(k):
        zp = plane_at(z, 3 - k)
        for c in loads(zp):
            c.wait()
        for p in range(2):
            for half in range(2):
                hop(zp, half, 1 - p).start()
        y_(0, blk(zp, 1 - y, 1 - x), 0, zp).start()
        x_(0, blk(zp, 1 - y, 1 - x), 1, zp).start()
        y_(1, blk(zp, 1 - y, x), 0, zp).start()
        x_(1, blk(zp, y, 1 - x), 1, zp).start()

    def arrive(zp, half, p, slot):
        line(zp, half, p, me, slot).wait_recv()
        add_into(own.at[place(zp, half, p), half, crossing], zr.at[slot, half, p])

    def s2(k):
        zp = plane_at(z, 3 - k)
        for p in (1, 0):
            for half in range(2):
                hop(zp, half, p).wait_recv()
                add_into(own.at[place(zp, half, p), half, crossing], fr.at[zp, half, p])
                pl.when((zp <= z) & (z < 3))(lambda h=half, p=p: arrive(zp, h, p, jnp.where(zp == z, 4, zp)))
                pl.when((zp >= z) & (z > 0))(lambda h=half, p=p: arrive(zp, h, p, zp))
                pl.when(zp < z)(lambda h=half, p=p: line(zp, h, p, dn, jnp.where(zp == z - 1, 4, zp)).start())
                pl.when(zp > z)(lambda h=half, p=p: line(zp, h, p, up, zp).start())
                if k == 3 and p == 1:
                    last(half).start()
        mine = blk(zp, y, x)
        y_(0, blk(zp, 1 - y, 1 - x), 0, zp).wait_recv()
        add_into(own.at[blk(zp, y, 1 - x), 0, rest], yr.at[zp, 0])
        x_(2, blk(zp, y, 1 - x), 0, zp).start()
        x_(0, blk(zp, 1 - y, 1 - x), 1, zp).wait_recv()
        add_into(own.at[blk(zp, 1 - y, x), 1, rest], xr.at[zp, 0])
        y_(2, blk(zp, 1 - y, x), 1, zp).start()
        y_(1, blk(zp, 1 - y, x), 0, zp).wait_recv()
        add_into(own.at[mine, 0, rest], yr.at[zp, 1])
        x_(1, blk(zp, y, 1 - x), 1, zp).wait_recv()
        add_into(own.at[mine, 1, rest], xr.at[zp, 1])

    def s3(k):
        zp = plane_at(z, 3 - k)
        mine = blk(zp, y, x)
        x_(2, blk(zp, y, 1 - x), 0, zp).wait_recv()
        add_into(own.at[mine, 0, rest], xr.at[zp, 2])
        y_(2, blk(zp, 1 - y, x), 1, zp).wait_recv()
        add_into(own.at[mine, 1, rest], yr.at[zp, 2])

        def arrived(d):
            zc(zp, me, d).wait_recv()
            add_into(own.at[mine, 0, rest], z2r.at[d, zp, 0])
            add_into(own.at[mine, 1, rest], z2r.at[d, zp, 1])

        pl.when((zp <= z) & (z < 3))(lambda: arrived(1))
        pl.when((zp >= z) & (z > 0))(lambda: arrived(0))
        pl.when(zp < z)(lambda: zc(zp, dn, 1).start())
        pl.when(zp > z)(lambda: zc(zp, up, 0).start())

    s1(0)
    s1(1)
    s2(0)
    s1(2)
    s2(1)
    s3(0)
    s1(3)
    s2(2)
    s3(1)
    s2(3)
    s3(2)
    s3(3)
    for half in range(2):
        last(half).wait_recv()
        add_into(own.at[me, half, crossing], lr.at[half])
    for a in range(2):

        def row(i, _):
            r = pl.ds(pl.multiple_of(i * 16, 16), 16)
            o_ref[a, r] = own[me, a, r].astype(jnp.float32)
            return 0

        lax.fori_loop(0, o_ref.shape[1] // 16, row, 0)
    for half in range(2):
        last(half).wait_send()
    for k in range(4):
        for half in range(2):
            for p in range(2):
                hop(k, half, p).wait_send()
                pl.when(k != z)(lambda k=k, h=half, p=p: line(k, h, p, me, 0).wait_send())
        for j in range(3):
            x_(j, 0, 0, k).wait_send()
            y_(j, 0, 0, k).wait_send()
        pl.when(k != z)(lambda k=k: zc(k, up, 0).wait_send())


def rs16(a, b, cid):
    S = pltpu.SemaphoreType.DMA
    high, total = a.shape[2], a.shape[3] + b.shape[3]
    blkshape = (2, high, total)
    cross, half = (high // 2, total), (high - high // 2, total)
    V = lambda s: pltpu.VMEM(s, a.dtype)
    return pl.pallas_call(
        rs_kernel,
        out_shape=jax.ShapeDtypeStruct(blkshape, jnp.float32),
        in_specs=[pl.BlockSpec(memory_space=pl.ANY)] * 2,
        out_specs=pl.BlockSpec(memory_space=pltpu.VMEM),
        scratch_shapes=[
            V((16,) + blkshape), V((4, 2, 2) + cross), V((5, 2, 2) + cross), V((2,) + cross),
            V((4, 3) + half), V((4, 3) + half), V((2, 4, 2) + half),
            S((4, 2)), S((4, 2, 2)), S((4, 2, 2)), S((4, 2, 2)), S((5, 2, 2)), S((2,)), S((2,)),
            S((4, 3)), S((4, 3)), S((4, 3)), S((4, 3)), S((4,)), S((2, 4)),
        ],
        compiler_params=pltpu.CompilerParams(collective_id=cid, has_side_effects=True, vmem_limit_bytes=60 << 20),
    )(a, b)


def nt(a, b):
    return lax.dot_general(a, b, (((1,), (1,)), ((), ())), preferred_element_type=jnp.float32)


def tn(a, b):
    return lax.dot_general(a, b, (((0,), (0,)), ((), ())), preferred_element_type=jnp.float32)


def mm(a, b):
    return jnp.dot(a, b, preferred_element_type=jnp.float32)


def gate_parts(a, b, dc):
    s = 1.0 / (1.0 + jnp.exp(-a))
    act = a * s
    return act * b, dc * b * (s * (1.0 + a * (1.0 - s))), dc * act


def moe_kernel(
    moe, grd, pick, pick_t, wg, wu, wd, wr, sgu, sdn,
    o_out, r_out, rg_out, act_out, da_out, db_out, sg_out, yr, xr, zr,
    own, sib, sibr, stage, xb, gb, pk, pt, rr, rg, ly, ld, ry, rd, acts, das, dbs, dgs,
    in_sem, out_sem, st_sem, free, cs, cr, xs, xrs, ys, yrs, zs, zrs, fs, fr,
):
    me = lax.axis_index("dp")
    core = lax.axis_index("tensor")
    other = 1 - core
    z = me // 4
    y = (me // 2) % 2
    x = me % 2
    xn = z * 4 + y * 2 + (1 - x)
    yn = z * 4 + (1 - y) * 2 + x
    up = jnp.minimum(z + 1, 3) * 4 + y * 2 + x
    dn = jnp.maximum(z - 1, 0) * 4 + y * 2 + x
    width = moe.shape[2]
    hid = 128
    cut = 512

    def rc(src, dst, ss, rs, dev, c):
        return pltpu.make_async_remote_copy(
            src_ref=src, dst_ref=dst, send_sem=ss, recv_sem=rs, device_id=(dev, c), device_id_type=MESH
        )

    def loads(i):
        k, half = i // 2, i % 2
        b = plane_at(z, 3 - k) * 4 + jnp.where(half == 0, 1 - y, y) * 2
        at = pl.ds(b, 2)
        return [
            pltpu.make_async_copy(moe.at[at], xb, in_sem.at[0]),
            pltpu.make_async_copy(grd.at[at], gb, in_sem.at[1]),
            pltpu.make_async_copy(pick.at[at], pk, in_sem.at[2]),
            pltpu.make_async_copy(pick_t.at[at], pt, in_sem.at[3]),
        ]

    for c in loads(0):
        c.start()
    bar = pltpu.get_barrier_semaphore()

    def sig(d, c):
        pl.semaphore_signal(bar, inc=1, device_id=(d, c), device_id_type=MESH)

    sig(xn, core)
    sig(yn, core)
    sig(me, other)
    pl.when(z < 3)(lambda: sig(up, core))
    pl.when(z > 0)(lambda: sig(dn, core))
    pl.semaphore_wait(bar, 3 + (z < 3).astype(jnp.int32) + (z > 0).astype(jnp.int32))

    for q in range(2):
        ry[q, hid:] = sdn[...]
        rd[q, hid:] = sgu[...]
    sg_out[...] = jnp.zeros_like(sg_out)

    def y_(j, b, half, zp):
        return rc(own.at[b, half], yr.at[zp, j], ys.at[zp, j], yrs.at[zp, j], yn, core)

    def x_(j, b, half, zp):
        return rc(own.at[b, half], xr.at[zp, j], xs.at[zp, j], xrs.at[zp, j], xn, core)

    def zc(zp, dev, d):
        b = zp * 4 + y * 2 + x
        return rc(own.at[b], zr.at[d, zp], zs.at[zp], zrs.at[d, zp], dev, core)

    def sib_send(i):
        return rc(sib, sibr, cs, cr, me, other)

    def outs(i):
        at = pl.ds(pl.multiple_of(i * 256, 256), 256)
        return [
            pltpu.make_async_copy(rr, r_out.at[at], out_sem.at[0]),
            pltpu.make_async_copy(rg, rg_out.at[at], out_sem.at[1]),
            pltpu.make_async_copy(acts, act_out.at[at], out_sem.at[2]),
            pltpu.make_async_copy(das, da_out.at[at], out_sem.at[3]),
            pltpu.make_async_copy(dbs, db_out.at[at], out_sem.at[4]),
        ]

    def columns(step):
        def one(n, _):
            step(pl.ds(pl.multiple_of(n * cut, cut), cut))
            return 0

        lax.fori_loop(0, width // cut, one, 0)

    def first_part(i):
        for c in loads(i):
            c.wait()

        @pl.when(i > 0)
        def _():
            for c in outs(i - 1):
                c.wait()

        def pick_rows(n):
            for q in range(2):
                rr[q * hid : (q + 1) * hid, n] = mm(pk[q], xb[q, :, n]).astype(jnp.bfloat16)
                rg[q * hid : (q + 1) * hid, n] = mm(pk[q], gb[q, :, n]).astype(jnp.bfloat16)

        columns(pick_rows)
        for q in range(2):
            ab = nt(xb[q], sgu[...])
            act, d_a, d_b = gate_parts(ab[:, :hid], ab[:, hid:], nt(gb[q], sdn[...]))
            ly[q, :, :hid] = pt[q]
            ly[q, :, hid:] = act.astype(jnp.bfloat16)
            ld[q, :, :hid] = pt[q]
            ld[q, :, hid : 2 * hid] = d_a.astype(jnp.bfloat16)
            ld[q, :, 2 * hid :] = d_b.astype(jnp.bfloat16)

        def shared_grads(n):
            sg_out[: 2 * hid, n] += tn(ld[0, :, hid:], xb[0, :, n]) + tn(ld[1, :, hid:], xb[1, :, n])
            sg_out[2 * hid :, n] += tn(ly[0, :, hid:], gb[0, :, n]) + tn(ly[1, :, hid:], gb[1, :, n])

        columns(shared_grads)

        @pl.when(i < 7)
        def _():
            for c in loads(i + 1):
                c.start()

    def second_part(i):
        logits = mm(rr[...], wr[...])
        lane = lax.broadcasted_iota(jnp.int32, logits.shape, 1)
        logits = jnp.where(lane < 16, logits, -jnp.inf)
        e = jnp.exp(logits - jnp.max(logits, axis=1, keepdims=True))
        gate = jnp.sum(jnp.where(lane == me, e, 0.0), axis=1, keepdims=True) / jnp.sum(
            e, axis=1, keepdims=True
        )
        pre = nt(rg[...], wd[...])
        act, d_a, d_b = gate_parts(nt(rr[...], wg[...]), nt(rr[...], wu[...]), gate * pre)
        low = act.astype(jnp.bfloat16)
        back = low.astype(jnp.float32)
        d_gate = jnp.sum(back * pre, axis=1, keepdims=True)
        acts[...] = (gate * back).astype(jnp.bfloat16)
        das[...] = d_a.astype(jnp.bfloat16)
        dbs[...] = d_b.astype(jnp.bfloat16)

        def spread(n):
            o = (gate * mm(low, wd[:, n])).astype(jnp.bfloat16)
            s = (mm(das[...], wg[:, n]) + mm(dbs[...], wu[:, n])).astype(jnp.bfloat16)
            for q in range(2):
                ry[q, :hid, n] = o[q * hid : (q + 1) * hid]
                rd[q, :hid, n] = s[q * hid : (q + 1) * hid]

        columns(spread)
        for c in outs(i):
            c.start()
        dgs[...] = jnp.where(lane == me, d_gate, 0.0).astype(jnp.bfloat16)

    def third_part(i):
        k, half = i // 2, i % 2
        b = plane_at(z, 3 - k) * 4 + jnp.where(half == 0, 1 - y, y) * 2

        @pl.when(i > 0)
        def _():
            sib_send(i - 1).wait_send()

        def store(q, n, v):
            v = v.astype(jnp.bfloat16)
            mine = jnp.where(core == 0, v[:128], v[128:])
            theirs = jnp.where(core == 0, v[128:], v[:128])
            own[b + q, 0, :, n] = mine[:64]
            own[b + q, 1, :, n] = mine[64:]
            sib[q, 0, :, n] = theirs[:64]
            sib[q, 1, :, n] = theirs[64:]

        def put(m, _):
            n = pl.ds(pl.multiple_of(m * cut, cut), cut)
            n2 = pl.ds(pl.multiple_of(width + m * cut, cut), cut)
            for q in range(2):
                store(q, n, mm(ly[q], ry[q, :, n]))
                store(q, n2, mm(ld[q], rd[q, :, n]))
            return 0

        lax.fori_loop(0, width // cut, put, 0)
        for q in range(2):
            store(q, pl.ds(2 * width, 128), mm(pt_of(q), dgs[q * hid : (q + 1) * hid]))

        @pl.when(i > 0)
        def _():
            pl.semaphore_wait(free, 1)

        sib_send(i).start()

    def pt_of(q):
        return ly[q, :, :hid]

    def staged(src, dst, sem):
        return pltpu.make_async_copy(src, dst, sem)

    def blk(zp, yy, xx):
        return zp * 4 + yy * 2 + xx

    def pair_sum(i):
        k, half = i // 2, i % 2
        zp = plane_at(z, 3 - k)
        b = zp * 4 + jnp.where(half == 0, 1 - y, y) * 2
        sib_send(i).wait_recv()

        def one(q, _):
            add_into(own.at[b + q, 0], sibr.at[q, 0])
            add_into(own.at[b + q, 1], sibr.at[q, 1])
            return 0

        lax.fori_loop(0, 2, one, 0)

        @pl.when(i < 7)
        def _():
            pl.semaphore_signal(free, inc=1, device_id=(me, other), device_id_type=MESH)

        @pl.when(half == 0)
        def _():
            y_(0, blk(zp, 1 - y, 1 - x), 0, zp).start()
            x_(0, blk(zp, 1 - y, 1 - x), 1, zp).start()
            y_(1, blk(zp, 1 - y, x), 0, zp).start()

        @pl.when(half == 1)
        def _():
            x_(1, blk(zp, y, 1 - x), 1, zp).start()

    def second_staging(k):
        zp = plane_at(z, 3 - k)
        return [
            staged(yr.at[zp, 0], stage.at[0, 0], st_sem.at[0]),
            staged(xr.at[zp, 0], stage.at[0, 1], st_sem.at[1]),
            staged(yr.at[zp, 1], stage.at[1, 0], st_sem.at[2]),
            staged(xr.at[zp, 1], stage.at[1, 1], st_sem.at[3]),
        ]

    def second_fetch(k):
        zp = plane_at(z, 3 - k)
        c = second_staging(k)
        y_(0, blk(zp, 1 - y, 1 - x), 0, zp).wait_recv()
        c[0].start()
        x_(0, blk(zp, 1 - y, 1 - x), 1, zp).wait_recv()
        c[1].start()
        y_(1, blk(zp, 1 - y, x), 0, zp).wait_recv()
        c[2].start()
        x_(1, blk(zp, y, 1 - x), 1, zp).wait_recv()
        c[3].start()

    def second_hop(k):
        zp = plane_at(z, 3 - k)
        mine = blk(zp, y, x)
        c = second_staging(k)
        c[0].wait()
        add_into(own.at[blk(zp, y, 1 - x), 0], stage.at[0, 0])
        x_(2, blk(zp, y, 1 - x), 0, zp).start()
        c[1].wait()
        add_into(own.at[blk(zp, 1 - y, x), 1], stage.at[0, 1])
        y_(2, blk(zp, 1 - y, x), 1, zp).start()
        c[2].wait()
        add_into(own.at[mine, 0], stage.at[1, 0])
        c[3].wait()
        add_into(own.at[mine, 1], stage.at[1, 1])

    def last_staging(k):
        zp = plane_at(z, 3 - k)
        return [
            staged(xr.at[zp, 2], stage.at[0, 0], st_sem.at[0]),
            staged(yr.at[zp, 2], stage.at[0, 1], st_sem.at[1]),
            staged(zr.at[1, zp], stage.at[1], st_sem.at[2]),
            staged(zr.at[0, zp], stage.at[2], st_sem.at[3]),
        ]

    def last_fetch(k):
        zp = plane_at(z, 3 - k)
        c = last_staging(k)
        x_(2, blk(zp, y, 1 - x), 0, zp).wait_recv()
        c[0].start()
        y_(2, blk(zp, 1 - y, x), 1, zp).wait_recv()
        c[1].start()

        @pl.when((zp <= z) & (z < 3))
        def _():
            zc(zp, me, 1).wait_recv()
            c[2].start()

        @pl.when((zp >= z) & (z > 0))
        def _():
            zc(zp, me, 0).wait_recv()
            c[3].start()

    def last_hop(k):
        zp = plane_at(z, 3 - k)
        mine = blk(zp, y, x)
        c = last_staging(k)
        c[0].wait()
        add_into(own.at[mine, 0], stage.at[0, 0])
        c[1].wait()
        add_into(own.at[mine, 1], stage.at[0, 1])

        def arrived(d):
            c[3 - d].wait()
            add_into(own.at[mine, 0], stage.at[2 - d, 0])
            add_into(own.at[mine, 1], stage.at[2 - d, 1])

        pl.when((zp <= z) & (z < 3))(lambda: arrived(1))
        pl.when((zp >= z) & (z > 0))(lambda: arrived(0))
        pl.when(zp < z)(lambda: zc(zp, dn, 1).start())
        pl.when(zp > z)(lambda: zc(zp, up, 0).start())

    def step(i, _):
        pl.when(i < 8)(lambda: first_part(i))
        pl.when((i >= 1) & (i <= 8))(lambda: pair_sum(i - 1))
        seconds = (i % 2 == 0) & (i >= 4) & (i <= 10)
        lasts = (i % 2 == 1) & (i >= 7) & (i <= 13)
        pl.when(seconds)(lambda: second_fetch((i - 4) // 2))
        pl.when(lasts)(lambda: last_fetch((i - 7) // 2))
        pl.when(i < 8)(lambda: second_part(i))
        pl.when(seconds)(lambda: second_hop((i - 4) // 2))
        pl.when(lasts)(lambda: last_hop((i - 7) // 2))
        pl.when(i < 8)(lambda: third_part(i))
        return 0

    lax.fori_loop(0, 14, step, 0)
    for a in range(2):

        def row(n, _):
            r = pl.ds(pl.multiple_of(n * 16, 16), 16)
            o_out[core, a, r] = own[me, a, r]
            return 0

        lax.fori_loop(0, 4, row, 0)
    f = rc(o_out.at[core], o_out.at[core], fs, fr, me, other)
    f.start()
    for c in outs(7):
        c.wait()
    sib_send(7).wait_send()
    for k in range(4):
        for j in range(3):
            x_(j, 0, 0, k).wait_send()
            y_(j, 0, 0, k).wait_send()

        @pl.when(k != z)
        def _():
            zc(k, up, 0).wait_send()

    rc(o_out.at[core], o_out.at[other], fs, fr, me, other).wait_recv()
    f.wait_send()


def moe_call(moe, grd, pick, pick_t, wg, wu, wd, wr, sgu, sdn, cid):
    ffe, width = wg.shape
    total = 2 * width + 128
    slots = pick.shape[0] * pick.shape[1]
    low, S, V = jnp.bfloat16, pltpu.SemaphoreType.DMA, pltpu.VMEM
    any_, vmem = pl.BlockSpec(memory_space=pl.ANY), pl.BlockSpec(memory_space=pltpu.VMEM)
    shape = lambda *s: jax.ShapeDtypeStruct(s, low)
    blk = (2, 64, total)
    return pl.pallas_call(
        moe_kernel,
        out_shape=[
            shape(2, *blk), shape(slots, width), shape(slots, width), shape(slots, ffe), shape(slots, ffe),
            shape(slots, ffe), jax.ShapeDtypeStruct((384, width), jnp.float32),
            shape(4, 3, 64, total), shape(4, 3, 64, total), shape(2, 4, *blk),
        ],
        in_specs=[any_] * 4 + [vmem] * 6,
        out_specs=[vmem] + [any_] * 5 + [vmem] + [any_] * 3,
        scratch_shapes=[
            V((16,) + blk, low), V((2,) + blk, low), V((2,) + blk, low), V((3,) + blk, low),
            V((2, 256, width), low), V((2, 256, width), low), V((2, 128, 256), low), V((2, 256, 128), low),
            V((256, width), low), V((256, width), low), V((2, 256, 256), low), V((2, 256, 384), low),
            V((2, 256, width), low), V((2, 384, width), low),
            V((256, ffe), low), V((256, ffe), low), V((256, ffe), low), V((256, 128), low),
            S((4,)), S((5,)), S((4,)), pltpu.SemaphoreType.REGULAR, S, S, S((4, 3)), S((4, 3)), S((4, 3)), S((4, 3)), S((4,)), S((2, 4)), S, S,
        ],
        compiler_params=pltpu.CompilerParams(collective_id=cid, has_side_effects=True, vmem_limit_bytes=60 << 20),
        cost_estimate=pl.CostEstimate(flops=65 * 10**9, bytes_accessed=80 * 10**6, transcendentals=0),
    )(moe, grd, pick, pick_t, wg, wu, wd, wr, sgu, sdn)


SLOTS = 5
KEYS = SLOTS * 256


def turned(v, cos, sin):
    n = v.shape[1]
    lane = lax.broadcasted_iota(jnp.int32, v.shape, 1) % 64
    swap = jnp.where(lane < 32, -pltpu.roll(v, n - 32, 1), pltpu.roll(v, 32, 1))
    return v * cos + swap * sin


def root(v):
    return lax.rsqrt(jnp.mean(v * v, axis=1, keepdims=True) + eps_norm)


def neighbours(me, core, bar):
    count = jnp.int32(1)
    pl.semaphore_signal(bar, inc=1, device_id=(me, 1 - core), device_id_type=MESH)
    for d in range(1, SLOTS):

        @pl.when(me + d < 16)
        def _():
            pl.semaphore_signal(bar, inc=1, device_id=(jnp.minimum(me + d, 15), core), device_id_type=MESH)

        @pl.when(me >= d)
        def _():
            pl.semaphore_signal(bar, inc=1, device_id=(jnp.maximum(me - d, 0), core), device_id_type=MESH)

        count = count + (me + d < 16).astype(jnp.int32) + (me >= d).astype(jnp.int32)
    return count


def slab_copies(w4, w2, wq, wo, wkv, wlat, sem):
    pairs = [
        (w2.at[:, 2560:3200], wlat, sem.at[0]),
        (w2.at[:, 0:1536], wq, sem.at[1]),
        (w2.at[:, 1536:2560], wo, sem.at[2]),
    ]
    for c in range(4):
        pairs.append((w4.at[:, c, :, w4.shape[3] - 512 :], wkv.at[:, :, c * 512 : (c + 1) * 512], sem.at[3 + c]))
    return pairs


def att_fwd_kernel(
    tok, w4, w2, g_att, g_moe, g_lat, cos, sin, bias,
    middle, moe_low, normed, lat_raw, qcat, keys, kv_out, lse, att,
    kv, wq, wo, wkv, wlat, part, arrived, w_sem, kv_sem, ks, kr, ts, tr, cs, cr,
):
    me = lax.axis_index("dp")
    core = lax.axis_index("tensor")
    loads = [pltpu.make_async_copy(h, v, s) for h, v, s in slab_copies(w4, w2, wq, wo, wkv, wlat, w_sem)]
    for c in loads:
        c.start()
    bar = pltpu.get_barrier_semaphore()
    pl.semaphore_wait(bar, neighbours(me, core, bar))
    t = tok[...].astype(jnp.float32)
    normed[...] = (t * root(t) * g_att[...]).astype(jnp.bfloat16)
    loads[0].wait()
    lat = mm(normed[...], wlat[...])
    lat_raw[...] = lat
    first = lat[:, :RANK]
    rot = turned(lat[:, RANK:], cos[:, :128], sin[:, :128])
    rot = jnp.where(lax.broadcasted_iota(jnp.int32, rot.shape, 1) < 64, rot, 0.0)
    keys[SLOTS - 1, :, :RANK] = (first * root(first) * g_lat[...]).astype(jnp.bfloat16)
    keys[SLOTS - 1, :, RANK:] = (rot + pltpu.roll(rot, 64, 1)).astype(jnp.bfloat16)

    mine = pl.ds(pl.multiple_of(core * 128, 128), 128)

    def send(d):
        return pltpu.make_async_remote_copy(
            src_ref=keys.at[SLOTS - 1, mine], dst_ref=keys.at[SLOTS - 1 - d, mine], send_sem=ks.at[d - 1],
            recv_sem=kr.at[d - 1], device_id=(jnp.minimum(me + d, 15), core), device_id_type=MESH,
        )

    def hand(d):
        return pltpu.make_async_remote_copy(
            src_ref=keys.at[SLOTS - 1 - d, mine], dst_ref=keys.at[SLOTS - 1 - d, mine], send_sem=ts.at[d - 1],
            recv_sem=tr.at[d - 1], device_id=(me, 1 - core), device_id_type=MESH,
        )

    def handed(d):
        other = keys.at[SLOTS - 1 - d, pl.ds(pl.multiple_of((1 - core) * 128, 128), 128)]
        return pltpu.make_async_remote_copy(
            src_ref=other, dst_ref=other, send_sem=ts.at[d - 1], recv_sem=tr.at[d - 1],
            device_id=(me, 1 - core), device_id_type=MESH,
        )

    for d in range(1, SLOTS):
        pl.when(me + d < 16)(lambda d=d: send(d).start())

        @pl.when(me < d)
        def _():
            keys[SLOTS - 1 - d] = jnp.zeros((256, 640), jnp.bfloat16)

    loads[1].wait()
    half = lax.broadcasted_iota(jnp.int32, (256, 128), 1) < 64
    q_nope = mm(normed[...], wq[:, :1024])
    q_rope = turned(mm(normed[...], wq[:, 1024:]), cos[...], sin[...])
    for h in range(8):
        qcat[h, :, :128] = q_nope[:, h * 128 : (h + 1) * 128].astype(jnp.bfloat16)
        pair = q_rope[:, h // 2 * 128 : (h // 2 + 1) * 128]
        qcat[h, :, 128:] = jnp.where(half == (h % 2 == 0), pair, 0.0).astype(jnp.bfloat16)
    for c in loads[3:]:
        c.wait()
    def project(s):
        kv[s * 256 : (s + 1) * 256] = mm(keys[s, :, :RANK], wkv[...].reshape(RANK, 2048)).astype(jnp.bfloat16)

    project(SLOTS - 1)
    for d in range(1, SLOTS + 1):
        if d < SLOTS:

            @pl.when(me >= d)
            def _(d=d):
                send(d).wait_recv()
                hand(d).start()

        if d > 1:
            pl.when(me >= d - 1)(lambda d=d: handed(d - 1).wait_recv())
            project(SLOTS - d)
    save = pltpu.make_async_copy(kv, kv_out, kv_sem)
    save.start()

    def head(h, _):
        kn = kv[:, pl.ds(pl.multiple_of(h * 256, 256), 128)]
        v = kv[:, pl.ds(pl.multiple_of(h * 256 + 128, 128), 128)]
        rope = keys[:, :, RANK:].reshape(KEYS, 128)
        s = nt(qcat[h], jnp.concatenate([kn, rope], 1)) * ((NOPE + ROPE) ** -0.5) + bias[...]
        top = jnp.max(s, axis=1, keepdims=True)
        e = jnp.exp(s - top)
        den = jnp.sum(e, axis=1, keepdims=True)
        lse[h] = top + jnp.log(den)
        p = (e * (1.0 / den)).astype(jnp.bfloat16)
        att[:, pl.ds(pl.multiple_of(h * 128, 128), 128)] = mm(p, v).astype(jnp.bfloat16)
        return 0

    lax.fori_loop(0, 8, head, 0)
    loads[2].wait()

    def out(n, _):
        r = pl.ds(pl.multiple_of(n * 512, 512), 512)
        part[:, r] = nt(att[...], wo[r]).astype(jnp.bfloat16)
        return 0

    lax.fori_loop(0, 4, out, 0)
    swap = pltpu.make_async_remote_copy(
        src_ref=part, dst_ref=arrived, send_sem=cs, recv_sem=cr, device_id=(me, 1 - core), device_id_type=MESH
    )
    swap.start()
    swap.wait()
    m = tok[...].astype(jnp.float32) + (part[...].astype(jnp.float32) + arrived[...].astype(jnp.float32))
    middle[...] = m
    moe_low[...] = (m * root(m) * g_moe[...]).astype(jnp.bfloat16)
    save.wait()
    for d in range(1, SLOTS):
        pl.when(me + d < 16)(lambda d=d: send(d).wait_send())
        pl.when(me >= d)(lambda d=d: hand(d).wait_send())


def att_fwd(tok, weights, g_att, g_moe, g_lat, cos, sin, bias, cid):
    low, f32, S, V = jnp.bfloat16, jnp.float32, pltpu.SemaphoreType.DMA, pltpu.VMEM
    any_, vmem = pl.BlockSpec(memory_space=pl.ANY), pl.BlockSpec(memory_space=pltpu.VMEM)
    shape = lambda kind, *s: jax.ShapeDtypeStruct(s, kind)
    rows, width = tok.shape
    pack = weights.shape[1]
    return pl.pallas_call(
        att_fwd_kernel,
        out_shape=[
            shape(f32, rows, width), shape(low, rows, width), shape(low, rows, width), shape(f32, rows, 640),
            shape(low, 8, rows, 256), shape(low, SLOTS, rows, 640), shape(low, KEYS, 2048), shape(f32, 8, rows, 1),
            shape(low, rows, 1024),
        ],
        in_specs=[vmem, any_, any_] + [vmem] * 6,
        out_specs=[vmem] * 6 + [any_] + [vmem] * 2,
        scratch_shapes=[
            V((KEYS, 2048), low), V((width, 1536), low), V((width, 1024), low), V((16, 32, 2048), low), V((width, 640), low),
            V((rows, width), low), V((rows, width), low), S((7,)), S, S((4,)), S((4,)), S((4,)), S((4,)), S, S,
        ],
        compiler_params=pltpu.CompilerParams(collective_id=cid, has_side_effects=True, vmem_limit_bytes=60 << 20),
        cost_estimate=pl.CostEstimate(flops=10**10, bytes_accessed=40 * 10**6, transcendentals=0),
    )(tok, weights.reshape(16, 4, 32, pack), weights, g_att, g_moe, g_lat, cos, sin, bias)


def att_bwd_kernel(
    w4, w2, home, grad, middle, moe_low, tok, normed, lat_raw, qcat, keys, kv_in, lse, att, wr,
    g_att, g_moe, g_lat, cos, sin, bias,
    tok_grad, packed, p4,
    kv, wq, wo, wkv, wlat, dmid, dnorm, dmid_low, d_att, dq, dqr, dkr, dk_out, dk_pair, dk_in, own_dk, part, arrived, d_keys,
    w_sem, kv_sem, ks, kr, cs, cr, ps, pr, hs, hr, o_sem,
):
    me = lax.axis_index("dp")
    core = lax.axis_index("tensor")
    width = tok.shape[1]
    scale = (NOPE + ROPE) ** -0.5
    loads = [pltpu.make_async_copy(h, v, s) for h, v, s in slab_copies(w4, w2, wq, wo, wkv, wlat, w_sem)]
    stores = [pltpu.make_async_copy(v, h, s) for h, v, s in slab_copies(p4, packed, wq, wo, wkv, wlat, o_sem)]
    kv_load = pltpu.make_async_copy(kv_in, kv, kv_sem)
    loads[2].start()
    kv_load.start()
    for n in (1, 3, 4, 5, 6, 0):
        loads[n].start()
    bar = pltpu.get_barrier_semaphore()
    pl.semaphore_wait(bar, neighbours(me, core, bar))
    lane = lax.broadcasted_iota(jnp.int32, (256, 128), 1)

    logits = jnp.where(lane < 16, mm(moe_low[...], wr[...]), -jnp.inf)
    e = jnp.exp(logits - jnp.max(logits, axis=1, keepdims=True))
    router = e / jnp.sum(e, axis=1, keepdims=True)
    d_router = jnp.where(lane < 16, home[:, width:].astype(jnp.float32), 0.0)
    d_logits = (router * (d_router - jnp.sum(router * d_router, axis=1, keepdims=True))).astype(jnp.bfloat16)

    def norm_back(v, gain, dy):
        r = root(v)
        hat = v * r
        up = dy * gain
        return r * (up - hat * jnp.mean(up * hat, axis=1, keepdims=True)), dy * hat

    def one_lane(n):
        return (lane == n).astype(jnp.bfloat16)

    d_moe = home[:, :width].astype(jnp.float32) + nt(d_logits, wr[...])
    d_norm2, gain_rows = norm_back(middle[...], g_moe[...], d_moe)
    d_middle = grad[...].astype(jnp.float32) + d_norm2
    dmid[...] = d_middle
    dmid_low[...] = d_middle.astype(jnp.bfloat16)
    gains = gain_rows.astype(jnp.bfloat16)
    moved = pltpu.roll(d_logits.astype(jnp.float32), 64, 1).astype(jnp.bfloat16)
    small = tn(moe_low[...], moved) + tn(gains, one_lane(81))

    loads[2].wait()
    d_att[...] = mm(dmid_low[...], wo[...]).astype(jnp.bfloat16)

    def wo_rows(n, _):
        r = pl.ds(pl.multiple_of(n * 256, 256), 256)
        wo[r] = tn(dmid_low[:, r], att[...]).astype(jnp.bfloat16)
        return 0

    lax.fori_loop(0, width // 256, wo_rows, 0)
    stores[2].start()
    kv_load.wait()
    dkr[...] = jnp.zeros_like(dkr)
    dqr[...] = jnp.zeros_like(dqr)

    def head(h, _):
        cols = pl.ds(pl.multiple_of(h * 128, 128), 128)
        nope_at = pl.ds(pl.multiple_of(h * 256, 256), 128)
        value_at = pl.ds(pl.multiple_of(h * 256 + 128, 128), 128)
        pair = pl.ds(pl.multiple_of(h // 2 * 128, 128), 128)
        kc = jnp.concatenate([kv[:, nope_at], keys[:, :, RANK:].reshape(KEYS, 128)], 1)
        p = jnp.exp(nt(qcat[h], kc) * scale + bias[...] - lse[h])
        dv = tn(p.astype(jnp.bfloat16), d_att[:, cols])
        dp = nt(d_att[:, cols], kv[:, value_at])
        ds = (p * (dp - jnp.sum(p * dp, axis=1, keepdims=True))).astype(jnp.bfloat16)
        dqc = mm(ds, kc) * scale
        dkc = tn(ds, qcat[h]) * scale
        dq[:, cols] = dqc[:, :128].astype(jnp.bfloat16)
        dqr[:, pair] += jnp.where((lane < 64) == (h % 2 == 0), dqc[:, 128:], 0.0)
        kv[:, nope_at] = dkc[:, :128].astype(jnp.bfloat16)
        kv[:, value_at] = dv.astype(jnp.bfloat16)
        dkr[...] += dkc[:, 128:]
        return 0

    lax.fori_loop(0, 8, head, 0)
    for n in (3, 4, 5, 6):
        loads[n].wait()

    mine = pl.ds(pl.multiple_of(core * 128, 128), 128)
    others = pl.ds(pl.multiple_of((1 - core) * 128, 128), 128)

    def send(d, to):
        return pltpu.make_async_remote_copy(
            src_ref=dk_out.at[d - 1, mine], dst_ref=dk_in.at[d - 1], send_sem=ks.at[d - 1], recv_sem=kr.at[d - 1],
            device_id=(jnp.clip(to, 0, 15), core), device_id_type=MESH,
        )

    pair = pltpu.make_async_remote_copy(
        src_ref=dk_out.at[:, others], dst_ref=dk_pair, send_sem=ps, recv_sem=pr, device_id=(me, 1 - core), device_id_type=MESH
    )
    for s in range(SLOTS):
        r = slice(s * 256, (s + 1) * 256)
        d = SLOTS - 1 - s if s < SLOTS - 1 else SLOTS
        dk_out[d - 1, :, :RANK] = nt(kv[r], wkv[...].reshape(RANK, 2048)).astype(jnp.bfloat16)
        dk_out[d - 1, :, RANK:] = (dkr[r] + pltpu.roll(dkr[r], 64, 1)).astype(jnp.bfloat16)
    pair.start()
    dq[:, 1024:] = turned(dqr[...], cos[...], -sin[...]).astype(jnp.bfloat16)
    loads[1].wait()

    def normed_cols(n, _):
        r = pl.ds(pl.multiple_of(n * 512, 512), 512)
        v = nt(dq[...], wq[r])
        part[:, r] = v.astype(jnp.bfloat16)
        wq[r] = tn(normed[:, r], dq[...]).astype(jnp.bfloat16)
        return 0

    normed_cols(0, 0)
    pair.wait_recv()
    for d in range(1, SLOTS):
        dk_out[d - 1, mine] = dk_out[d - 1, mine] + dk_pair[d - 1]
        pl.when(me >= d)(lambda d=d: send(d, me - d).start())
    own_dk[...] = dk_out[SLOTS - 1, mine].astype(jnp.float32) + dk_pair[SLOTS - 1].astype(jnp.float32)
    lax.fori_loop(1, 4, normed_cols, 0)
    swap = pltpu.make_async_remote_copy(
        src_ref=part, dst_ref=arrived, send_sem=cs, recv_sem=cr, device_id=(me, 1 - core), device_id_type=MESH
    )
    swap.start()
    stores[1].start()
    latent_all = keys[:, :, :RANK].reshape(KEYS, RANK)
    for c in range(4):
        g = tn(latent_all, kv[:, c * 512 : (c + 1) * 512]).astype(jnp.bfloat16)
        wkv[:, :, c * 512 : (c + 1) * 512] = g.reshape(16, 32, 512)
        stores[3 + c].start()
    for d in range(1, SLOTS):

        @pl.when(me + d < 16)
        def _():
            send(d, me + d).wait_recv()
            own_dk[...] += dk_in[d - 1].astype(jnp.float32)

    d_keys[mine] = own_dk[...].astype(jnp.bfloat16)

    def half(rows):
        return pltpu.make_async_remote_copy(
            src_ref=d_keys.at[rows], dst_ref=d_keys.at[rows], send_sem=hs, recv_sem=hr,
            device_id=(me, 1 - core), device_id_type=MESH,
        )

    half(mine).start()
    swap.wait_recv()
    dnorm[...] = part[...].astype(jnp.float32) + arrived[...].astype(jnp.float32)
    half(others).wait_recv()

    d_first, lat_gain_rows = norm_back(lat_raw[:, :RANK], g_lat[...], d_keys[:, :RANK].astype(jnp.float32))
    d_second = turned(d_keys[:, RANK:].astype(jnp.float32), cos[:, :128], -sin[:, :128])
    d_second = jnp.where(lane < 64, d_second, 0.0)
    d_lat_low = jnp.concatenate([d_first, d_second], 1).astype(jnp.bfloat16)
    loads[0].wait()
    d_normed = dnorm[...] + nt(d_lat_low, wlat[...])
    d_norm1, att_gain_rows = norm_back(tok[...].astype(jnp.float32), g_att[...], d_normed)
    tok_grad[...] = dmid[...] + d_norm1
    small = small + tn(normed[...], d_lat_low[:, RANK:]) + tn(att_gain_rows.astype(jnp.bfloat16), one_lane(80))
    wlat[:, :RANK] = tn(normed[...], d_lat_low[:, :RANK]).astype(jnp.bfloat16)
    wlat[:, RANK:] = small.astype(jnp.bfloat16)
    lat_col = tn(lat_gain_rows.astype(jnp.bfloat16), one_lane(82))
    for b in range(16):
        r = slice(b * 128, b * 128 + 32)
        wlat[r, RANK:] = (small[r] + lat_col[b * 32 : (b + 1) * 32]).astype(jnp.bfloat16)
    stores[0].start()
    for c in stores:
        c.wait()
    for d in range(1, SLOTS):
        pl.when(me >= d)(lambda d=d: send(d, me - d).wait_send())
    pair.wait_send()
    swap.wait_send()
    half(mine).wait_send()


def att_bwd(weights, home, grad, middle, moe_low, tok, normed, lat_raw, qcat, keys, kv, lse, att, wr, g_att, g_moe, g_lat, cos, sin, bias, cid):
    low, f32, S, V = jnp.bfloat16, jnp.float32, pltpu.SemaphoreType.DMA, pltpu.VMEM
    any_, vmem = pl.BlockSpec(memory_space=pl.ANY), pl.BlockSpec(memory_space=pltpu.VMEM)
    shape = lambda kind, *s: jax.ShapeDtypeStruct(s, kind)
    rows, width = tok.shape
    pack = weights.shape[1]
    return pl.pallas_call(
        att_bwd_kernel,
        out_shape=[shape(f32, rows, width), shape(low, width, pack - 512), shape(low, 16, 4, 32, 512)],
        in_specs=[any_, any_] + [vmem] * 9 + [any_] + [vmem] * 9,
        out_specs=[vmem, any_, any_],
        scratch_shapes=[
            V((KEYS, 2048), low), V((width, 1536), low), V((width, 1024), low), V((16, 32, 2048), low),
            V((width, 640), low), V((rows, width), f32), V((rows, width), f32), V((rows, width), low), V((rows, 1024), low),
            V((rows, 1536), low), V((rows, 512), f32), V((KEYS, 128), f32), V((SLOTS, rows, 640), low), V((SLOTS, rows // 2, 640), low),
            V((4, rows // 2, 640), low), V((rows // 2, 640), f32), V((rows, width), low), V((rows, width), low), V((rows, 640), low),
            S((7,)), S, S((4,)), S((4,)), S, S, S, S, S, S, S((7,)),
        ],
        compiler_params=pltpu.CompilerParams(collective_id=cid, has_side_effects=True, vmem_limit_bytes=60 << 20),
        cost_estimate=pl.CostEstimate(flops=25 * 10**9, bytes_accessed=70 * 10**6, transcendentals=0),
    )(
        weights.reshape(16, 4, 32, pack), weights, home, grad, middle, moe_low, tok, normed, lat_raw, qcat, keys, kv, lse, att, wr,
        g_att, g_moe, g_lat, cos, sin, bias,
    )


def swapped(v):
    return lax.ppermute(v, "tensor", [(0, 1), (1, 0)])


def my_half(v, rows):
    return lax.dynamic_slice_in_dim(v, lax.axis_index("tensor") * rows, rows, 0)


def row_halves(v):
    rows = v.shape[0] // 2
    return my_half(v, rows).reshape(2, rows // 2, v.shape[1])


def exchange(parts):
    return lax.all_to_all(parts, "dp", split_axis=0, concat_axis=0, tiled=True)


def nope_first(w):
    heads = w.reshape(w.shape[0], -1, NOPE + ROPE)
    return jnp.concatenate(
        [heads[:, :, :NOPE].reshape(w.shape[0], -1), heads[:, :, NOPE:].reshape(w.shape[0], -1)], 1
    )


def heads_first(w):
    heads = w.shape[1] // (NOPE + ROPE)
    nope = w[:, : heads * NOPE].reshape(w.shape[0], heads, NOPE)
    rope = w[:, heads * NOPE :].reshape(w.shape[0], heads, ROPE)
    return jnp.concatenate([nope, rope], 2).reshape(w.shape[0], -1)


def shards_sixteen(
    tokens,
    out_grad,
    segments,
    routes,
    attn_gain,
    w_query,
    w_latent,
    latent_gain,
    w_keyval,
    w_out,
    moe_gain,
    w_router,
    shared_gate,
    shared_up,
    shared_down,
    expert_gate,
    routed_up_weight,
    expert_down,
):
    n_rows, width = tokens.shape
    dp_count = lax.axis_size("dp")
    dp_index = lax.axis_index("dp")
    seq_len = segments.shape[1]
    total = n_rows * dp_count
    hop_count = (WINDOW - 1) // n_rows + 1
    n_keys = (hop_count + 1) * n_rows
    experts = w_router.shape[1]
    capacity = 4 * n_rows * TOPK // (3 * experts)
    row_start = dp_index * n_rows
    seg_row = segments[0]
    depth = w_query.shape[0]
    q_width, o_width, kv_width = w_query.shape[1], w_out.shape[0], w_keyval.shape[1]
    kv_rows = w_keyval.shape[0]
    kv_cuts = depth // kv_rows
    kv_part = kv_width // kv_cuts
    lat_width = w_latent.shape[1]
    route_width = n_rows * TOPK // depth
    small = (lat_width + experts + 3 + route_width + 127) // 128 * 128

    gains = jnp.stack(
        [attn_gain, moe_gain, jnp.pad(latent_gain, (0, depth - kv_rows))], 1
    )
    packed = jnp.concatenate(
        [
            nope_first(w_query),
            w_out.T,
            w_latent,
            w_router,
            gains,
            routes.reshape(depth, route_width).astype(jnp.bfloat16),
            jnp.zeros((depth, small - lat_width - experts - 3 - route_width), jnp.bfloat16),
            w_keyval.reshape(kv_rows, kv_cuts, kv_part).transpose(1, 0, 2).reshape(depth, kv_part),
        ],
        1,
    )
    pack_width = packed.shape[1]
    weights, grad_all = ag16(
        [packed.reshape(2, depth // 2, pack_width), row_halves(out_grad)], (False, True), 1
    )
    weights = weights.reshape(width, pack_width)
    shared_part = shared_gate.shape[1] // dp_count
    shared_send = jnp.stack(
        [
            shared_gate.reshape(depth, dp_count, shared_part).transpose(1, 2, 0),
            shared_up.reshape(depth, dp_count, shared_part).transpose(1, 2, 0),
            shared_down.reshape(dp_count, shared_part, depth),
        ],
        1,
    )
    shared_send, weights = lax.optimization_barrier((shared_send, weights))
    shared_all = exchange(shared_send).transpose(1, 2, 0, 3).reshape(3, shared_part, width)
    lead = jnp.pad(shared_all, ((0, 0), (0, 128 - shared_part), (0, 0)))
    shared_in, shared_out = lead[:2].reshape(256, width), lead[2]

    at = q_width + o_width + lat_width
    wr_full = weights[:, at : at + experts]
    at += experts
    gain_attn = weights[:, at].astype(jnp.float32)
    gain_moe = weights[:, at + 1].astype(jnp.float32)
    gain_latent = (
        weights[:, at + 2].reshape(dp_count, depth)[:, :kv_rows].reshape(-1).astype(jnp.float32)
    )

    all_routes = (
        weights[:, at + 3 : at + 3 + route_width].reshape(total, TOPK).astype(jnp.int32)
    )

    local_heads = q_width // (NOPE + ROPE)
    positions = (row_start + jnp.arange(n_rows, dtype=jnp.int32)).astype(jnp.float32)
    cos_tab, sin_tab = rope_tables(positions)
    cos_lanes, sin_lanes = jnp.tile(cos_tab, (1, 2 * local_heads)), jnp.tile(sin_tab, (1, 2 * local_heads))
    key_pos = row_start - hop_count * n_rows + jnp.arange(n_keys, dtype=jnp.int32)
    query_pos = row_start + jnp.arange(n_rows, dtype=jnp.int32)
    padded_seg = jnp.concatenate([jnp.full((hop_count * n_rows,), -1, jnp.int32), seg_row])
    key_seg = lax.dynamic_slice_in_dim(padded_seg, row_start, n_keys, 0)
    query_seg = lax.dynamic_slice_in_dim(seg_row, row_start, n_rows, 0)
    allowed = (key_pos[None, :] >= 0) & (key_pos[None, :] <= query_pos[:, None])
    allowed = (
        allowed
        & (query_pos[:, None] - key_pos[None, :] < WINDOW)
        & (query_seg[:, None] == key_seg[None, :])
    )

    bias = jnp.where(allowed, 0.0, -jnp.inf)
    middle, moe_low, normed_low, lat_raw, qcat, keys, kv, lse, attended_low = att_fwd(
        tokens, weights, gain_attn[None], gain_moe[None], gain_latent[None], cos_lanes, sin_lanes, bias, 7
    )
    moe_low, shared_in, shared_out = lax.optimization_barrier((moe_low, shared_in, shared_out))
    (moe_all,) = ag16([row_halves(moe_low)], (True,), 3)
    chosen = jnp.any(all_routes == dp_index, axis=1).reshape(dp_count, n_rows)
    earlier = jnp.arange(n_rows)[:, None] < jnp.arange(n_rows)[None, :]
    rank = matmul(chosen.astype(jnp.bfloat16), earlier.astype(jnp.bfloat16)).astype(jnp.int32)
    pick = (
        (rank[:, None, :] == jnp.arange(capacity, dtype=jnp.int32)[None, :, None])
        & chosen[:, None, :]
    ).astype(jnp.bfloat16)

    slot_rows = dp_count * capacity
    moe_wr = jnp.pad(wr_full, ((0, 0), (0, 128 - experts)))
    home, rows_in, rows_grad, scaled_act, d_ea_low, d_eb_low, shared_grads = moe_call(
        moe_all.reshape(dp_count, n_rows, width),
        grad_all.reshape(dp_count, n_rows, width),
        pick,
        pick.transpose(0, 2, 1),
        expert_gate[0].T,
        routed_up_weight[0].T,
        expert_down[0],
        moe_wr,
        shared_in,
        shared_out,
        4,
    )[:7]
    home = home.reshape(n_rows, 2 * width + 128)
    result = (middle + home[:, :width].astype(jnp.float32)).astype(jnp.bfloat16)
    grad_down = matmul_tn(scaled_act, rows_grad)[None]
    grad_gate = matmul_tn(rows_in, d_ea_low)[None]
    grad_up = matmul_tn(rows_in, d_eb_low)[None]
    shared_home = exchange(
        shared_grads.astype(jnp.bfloat16)
        .reshape(3, 128, dp_count, depth)[:, :shared_part]
        .transpose(2, 0, 1, 3)
    ).astype(jnp.float32)
    shared_home = shared_home.transpose(1, 0, 2, 3).reshape(3, dp_count * shared_part, depth)

    token_input_gradient, packed_grads, kv_grads = att_bwd(
        weights, home[:, width:], out_grad, middle, moe_low, tokens, normed_low, lat_raw, qcat, keys, kv, lse,
        attended_low, moe_wr, gain_attn[None], gain_moe[None], gain_latent[None], cos_lanes, sin_lanes, bias, 8
    )
    packed_grads, shared_home = lax.optimization_barrier((packed_grads, shared_home))
    mine = rs16(
        packed_grads.reshape(dp_count, 2, depth // 2, pack_width - kv_part),
        kv_grads.reshape(dp_count, 2, depth // 2, kv_part),
        6,
    ).reshape(depth, pack_width)
    grad_sgate, grad_sup, grad_sdown = shared_home[0].T, shared_home[1].T, shared_home[2]
    out_wq = heads_first(mine[:, :q_width])
    at = q_width
    out_wo = mine[:, at : at + o_width].T
    at += o_width
    out_wlat = mine[:, at : at + lat_width]
    at += lat_width
    out_router = mine[:, at : at + experts]
    at += experts
    out_wkv = (
        mine[:, pack_width - kv_part :]
        .reshape(kv_cuts, kv_rows, kv_part)
        .transpose(1, 0, 2)
        .reshape(kv_rows, kv_width)
    )
    return (
        result,
        token_input_gradient,
        mine[:, at],
        out_wq,
        out_wlat,
        mine[:kv_rows, at + 2],
        out_wkv,
        out_wo,
        mine[:, at + 1],
        out_router,
        grad_sgate,
        grad_sup,
        grad_sdown,
        grad_gate,
        grad_up,
        grad_down,
    )


def shards_general(
    tokens,
    out_grad,
    segments,
    routes,
    attn_gain,
    w_query,
    w_latent,
    latent_gain,
    w_keyval,
    w_out,
    moe_gain,
    w_router,
    shared_gate,
    shared_up,
    shared_down,
    expert_gate,
    routed_up_weight,
    expert_down,
):
    n_rows = tokens.shape[0]
    model_width = tokens.shape[1]
    dp_count = lax.axis_size("dp")
    dp_index = lax.axis_index("dp")
    seq_len = segments.shape[1]
    seq_devs = seq_len // n_rows
    hop_count = (WINDOW - 1) // n_rows + 1
    n_keys = (hop_count + 1) * n_rows
    experts = w_router.shape[1]
    local_experts = expert_gate.shape[0]
    capacity = 4 * n_rows * TOPK // (3 * experts)
    slot_total = experts * capacity
    score_scale = (NOPE + ROPE) ** (-0.5)
    row_start = dp_index % seq_devs * n_rows
    seg_row = lax.dynamic_index_in_dim(segments, dp_index // seq_devs, 0, keepdims=False)
    gathered = (
        lax.all_gather(attn_gain, "dp", axis=0, tiled=True),
        lax.all_gather(w_query, "dp", axis=0, tiled=True),
        lax.all_gather(w_latent, "dp", axis=0, tiled=True),
        lax.all_gather(latent_gain, "dp", axis=0, tiled=True),
        lax.all_gather(w_keyval, "dp", axis=0, tiled=True),
        lax.all_gather(w_out, "dp", axis=1, tiled=True),
        lax.all_gather(moe_gain, "dp", axis=0, tiled=True),
        lax.all_gather(w_router, "dp", axis=0, tiled=True),
        lax.all_gather(shared_gate, "dp", axis=0, tiled=True),
        lax.all_gather(shared_up, "dp", axis=0, tiled=True),
        lax.all_gather(shared_down, "dp", axis=1, tiled=True),
    )
    (
        gain_attn,
        wq_full,
        wlat_full,
        gain_latent,
        wkv_full,
        wo_full,
        gain_moe,
        wr_full,
        sgate_full,
        sup_full,
        sdown_full,
    ) = gathered
    local_heads = wq_full.shape[1] // (NOPE + ROPE)
    positions = (row_start + jnp.arange(n_rows, dtype=jnp.int32)).astype(jnp.float32)
    cos_tab, sin_tab = rope_tables(positions)
    resid_in = tokens.astype(jnp.float32)
    normed, attn_norm_back = jax.vjp(rms_scale, resid_in, gain_attn.astype(jnp.float32))
    normed_low = normed.astype(jnp.bfloat16)

    def rope_queries(q_flat):
        shaped = q_flat.reshape(n_rows, local_heads, NOPE + ROPE)
        return jnp.concatenate(
            [shaped[..., :NOPE], rotate(shaped[..., NOPE:], cos_tab[:, None], sin_tab[:, None])], -1
        )

    queries, query_back = jax.vjp(rope_queries, matmul(normed_low, wq_full))
    query_low = queries.astype(jnp.bfloat16)

    def latent_piece(latent_raw, gain_vec):
        return (
            rms_scale(latent_raw[:, :RANK], gain_vec),
            rotate(latent_raw[:, RANK:], cos_tab, sin_tab),
        )

    (latent, key_rope), latent_back = jax.vjp(
        latent_piece, matmul(normed_low, wlat_full), gain_latent.astype(jnp.float32)
    )
    latent_low = latent.astype(jnp.bfloat16)
    rope_low = key_rope.astype(jnp.bfloat16)
    latent_parts = []
    rope_parts = []
    for distance in range(hop_count, 0, -1):
        moved_latent, moved_rope = passed_along((latent_low, rope_low), "dp", distance)
        latent_parts.append(moved_latent)
        rope_parts.append(moved_rope)
    keys_latent = jnp.concatenate(latent_parts + [latent_low], 0)
    keys_rope = jnp.concatenate(rope_parts + [rope_low], 0)
    keyval = (
        matmul(keys_latent, wkv_full).astype(jnp.bfloat16).reshape(n_keys, local_heads, NOPE + VDIM)
    )
    key_nope = keyval[..., :NOPE]
    values = keyval[..., NOPE:]
    key_pos = row_start - hop_count * n_rows + jnp.arange(n_keys, dtype=jnp.int32)
    query_pos = row_start + jnp.arange(n_rows, dtype=jnp.int32)
    padded_seg = jnp.concatenate([jnp.full((hop_count * n_rows,), -1, jnp.int32), seg_row])
    key_seg = lax.dynamic_slice_in_dim(padded_seg, row_start, n_keys, 0)
    query_seg = lax.dynamic_slice_in_dim(seg_row, row_start, n_rows, 0)
    allowed = (key_pos[None, :] >= 0) & (key_pos[None, :] <= query_pos[:, None])
    allowed = (
        allowed
        & (query_pos[:, None] - key_pos[None, :] < WINDOW)
        & (query_seg[:, None] == key_seg[None, :])
    )

    def masked_scores():
        nope_part = jnp.einsum(
            "qhd,khd->hqk", query_low[..., :NOPE], key_nope, preferred_element_type=jnp.float32
        )
        rope_part = jnp.einsum(
            "qhr,kr->hqk", query_low[..., NOPE:], keys_rope, preferred_element_type=jnp.float32
        )
        return jnp.where(allowed[None], score_scale * (nope_part + rope_part), -jnp.inf)

    scores = masked_scores()
    top_score = jnp.max(scores, axis=-1, keepdims=True)
    exp_scores = jnp.exp(scores - top_score)
    denom = jnp.sum(exp_scores, axis=-1, keepdims=True)
    attn_probs = exp_scores / denom
    log_total = top_score + jnp.log(denom)
    attended = jnp.einsum(
        "hqk,khv->qhv", attn_probs.astype(jnp.bfloat16), values, preferred_element_type=jnp.float32
    )
    attended_low = attended.astype(jnp.bfloat16).reshape(n_rows, local_heads * VDIM)
    attn_out = lax.psum(matmul(attended_low, wo_full).astype(jnp.bfloat16), "tensor").astype(
        jnp.float32
    )
    middle = resid_in + attn_out
    moe_normed, moe_norm_back = jax.vjp(rms_scale, middle, gain_moe.astype(jnp.float32))
    moe_low = moe_normed.astype(jnp.bfloat16)
    router, router_back = jax.vjp(
        lambda logit_vals: jax.nn.softmax(logit_vals, axis=-1), matmul(moe_low, wr_full)
    )
    expert_ids = jnp.arange(experts, dtype=jnp.int32)
    route_hot = (routes[:, :, None] == expert_ids[None, None, :]).astype(jnp.float32)
    gate_w = jnp.einsum("te,tke->tk", router, route_hot, precision=highest)
    flat_routes = routes.reshape(-1)
    assign_count = flat_routes.shape[0]
    flat_hot = (flat_routes[:, None] == expert_ids[None, :]).astype(jnp.int32)
    earlier = ranks_before(flat_hot)
    slot_in = jnp.sum(earlier * flat_hot, axis=1)
    target = flat_routes * capacity + slot_in
    assign_ids = jnp.arange(assign_count, dtype=jnp.int32)
    assign_of_slot = jnp.zeros((slot_total,), jnp.int32).at[target].set(assign_ids)
    slot_live = (
        jnp.zeros((slot_total,), jnp.bfloat16)
        .at[target]
        .set(jnp.ones((assign_count,), jnp.bfloat16))
    )
    send_rows = moe_low[assign_of_slot // TOPK] * slot_live[:, None]
    recv_rows = lax.all_to_all(
        send_rows.reshape(dp_count, local_experts * capacity, model_width),
        "dp",
        split_axis=0,
        concat_axis=0,
        tiled=True,
    )
    received_four_parts = recv_rows.reshape(dp_count, local_experts, capacity, model_width)
    exp_gate = jnp.einsum(
        "sjcd,jdf->sjcf", received_four_parts, expert_gate, preferred_element_type=jnp.float32
    )
    exp_up = jnp.einsum(
        "sjcd,jdf->sjcf", received_four_parts, routed_up_weight, preferred_element_type=jnp.float32
    )
    exp_act, exp_act_back = jax.vjp(gated_act, exp_gate, exp_up)
    exp_act_low = exp_act.astype(jnp.bfloat16)
    exp_result = jnp.einsum(
        "sjcf,jfd->sjcd", exp_act_low, expert_down, preferred_element_type=jnp.float32
    )
    returned = lax.all_to_all(
        exp_result.reshape(dp_count, local_experts * capacity, model_width).astype(jnp.bfloat16),
        "dp",
        split_axis=0,
        concat_axis=0,
        tiled=True,
    ).astype(jnp.float32)
    per_assign = returned.reshape(slot_total, model_width)[target].reshape(
        n_rows, TOPK, model_width
    )
    routed = jnp.einsum("tk,tkd->td", gate_w, per_assign, precision=highest)
    shared_a = matmul(moe_low, sgate_full)
    shared_b = matmul(moe_low, sup_full)
    shared_act, shared_back = jax.vjp(gated_act, shared_a, shared_b)
    shared_low = shared_act.astype(jnp.bfloat16)
    moe_out = lax.psum(
        (routed + matmul(shared_low, sdown_full)).astype(jnp.bfloat16), "tensor"
    ).astype(jnp.float32)
    result = (middle + moe_out).astype(jnp.bfloat16)
    grad_y = out_grad.astype(jnp.float32)
    grad_sdown = matmul_tn(shared_low, out_grad)
    d_shared_a, d_shared_b = shared_back(matmul_nt(out_grad, sdown_full))
    d_sa_low = d_shared_a.astype(jnp.bfloat16)
    d_sb_low = d_shared_b.astype(jnp.bfloat16)
    grad_sgate = matmul_tn(moe_low, d_sa_low)
    grad_sup = matmul_tn(moe_low, d_sb_low)
    d_moe = matmul_nt(d_sa_low, sgate_full) + matmul_nt(d_sb_low, sup_full)
    d_gate_part = jnp.einsum("td,tkd->tk", grad_y, per_assign, precision=highest)
    d_assign = (
        (gate_w[:, :, None] * grad_y[:, None, :])
        .astype(jnp.bfloat16)
        .reshape(assign_count, model_width)
    )
    send_grads = d_assign[assign_of_slot] * slot_live[:, None]
    recv_grads = lax.all_to_all(
        send_grads.reshape(dp_count, local_experts * capacity, model_width),
        "dp",
        split_axis=0,
        concat_axis=0,
        tiled=True,
    )
    recv_grads = recv_grads.reshape(dp_count, local_experts, capacity, model_width)
    expert_down_weight_gradient = jnp.einsum(
        "sjcf,sjcd->jfd", exp_act_low, recv_grads, preferred_element_type=jnp.float32
    )
    d_exp_act = jnp.einsum(
        "sjcd,jfd->sjcf", recv_grads, expert_down, preferred_element_type=jnp.float32
    )
    d_exp_gate, expert_up_act_gradient = exp_act_back(d_exp_act)
    d_egate_low = d_exp_gate.astype(jnp.bfloat16)
    expert_up_gradient_lowp = expert_up_act_gradient.astype(jnp.bfloat16)
    expert_gate_weight_gradient = jnp.einsum(
        "bmky,bmkx->myx", received_four_parts, d_egate_low, preferred_element_type=jnp.float32
    )
    expert_up_weight_gradient = jnp.einsum(
        "bmky,bmkx->myx",
        received_four_parts,
        expert_up_gradient_lowp,
        preferred_element_type=jnp.float32,
    )
    d_slots = jnp.einsum(
        "hteg,tmg->htem", d_egate_low, expert_gate, preferred_element_type=jnp.float32
    )
    d_slots = d_slots + jnp.einsum(
        "hteg,tmg->htem",
        expert_up_gradient_lowp,
        routed_up_weight,
        preferred_element_type=jnp.float32,
    )
    back_grads = lax.all_to_all(
        d_slots.reshape(dp_count, local_experts * capacity, model_width).astype(jnp.bfloat16),
        "dp",
        split_axis=0,
        concat_axis=0,
        tiled=True,
    ).astype(jnp.float32)
    d_moe = d_moe + jnp.sum(
        back_grads.reshape(slot_total, model_width)[target].reshape(n_rows, TOPK, model_width),
        axis=1,
    )
    d_moe, d_gate = (
        lax.psum(d_moe.astype(jnp.bfloat16), "tensor").astype(jnp.float32),
        lax.psum(d_gate_part.astype(jnp.bfloat16), "tensor").astype(jnp.float32),
    )
    d_router = jnp.einsum("tk,tke->te", d_gate, route_hot, precision=highest)
    (d_logits,) = router_back(d_router)
    d_logits_low = d_logits.astype(jnp.bfloat16)
    grad_router = matmul_tn(moe_low, d_logits_low)
    d_moe = d_moe + matmul_nt(d_logits_low, wr_full)
    d_mid_norm, grad_gain_moe = moe_norm_back(d_moe)
    d_middle = grad_y + d_mid_norm
    d_middle_low = d_middle.astype(jnp.bfloat16)
    grad_wout = matmul_tn(attended_low, d_middle_low)
    d_att_low = (
        matmul_nt(d_middle_low, wo_full).astype(jnp.bfloat16).reshape(n_rows, local_heads, VDIM)
    )
    again_probs = jnp.exp(masked_scores() - log_total)
    d_values = jnp.einsum(
        "hqk,qhv->khv",
        again_probs.astype(jnp.bfloat16),
        d_att_low,
        preferred_element_type=jnp.float32,
    )
    d_probs = jnp.einsum("qhv,khv->hqk", d_att_low, values, preferred_element_type=jnp.float32)
    d_scores = (
        again_probs * (d_probs - jnp.sum(d_probs * again_probs, axis=-1, keepdims=True))
    ).astype(jnp.bfloat16)
    d_query_nope = score_scale * jnp.einsum(
        "hqk,khd->qhd", d_scores, key_nope, preferred_element_type=jnp.float32
    )
    d_query_rope = score_scale * jnp.einsum(
        "hqk,kr->qhr", d_scores, keys_rope, preferred_element_type=jnp.float32
    )
    d_key_nope = score_scale * jnp.einsum(
        "hqk,qhd->khd", d_scores, query_low[..., :NOPE], preferred_element_type=jnp.float32
    )
    d_key_rope = score_scale * jnp.einsum(
        "hqk,qhr->kr", d_scores, query_low[..., NOPE:], preferred_element_type=jnp.float32
    )
    (d_q_raw,) = query_back(jnp.concatenate([d_query_nope, d_query_rope], -1))
    d_q_low = d_q_raw.astype(jnp.bfloat16)
    grad_wq = matmul_tn(normed_low, d_q_low)
    d_normed = matmul_nt(d_q_low, wq_full)
    d_kv_low = (
        jnp.concatenate([d_key_nope, d_values], -1)
        .astype(jnp.bfloat16)
        .reshape(n_keys, local_heads * (NOPE + VDIM))
    )
    grad_wkv = matmul_tn(keys_latent, d_kv_low)
    d_keys_latent = matmul_nt(d_kv_low, wkv_full)
    own_latent = d_keys_latent[hop_count * n_rows :]
    own_rope = d_key_rope[hop_count * n_rows :]
    for distance in range(hop_count, 0, -1):
        block_index = hop_count - distance
        lower = block_index * n_rows
        home_latent, home_rope = (
            passed_along(
                d_keys_latent[lower : lower + n_rows].astype(jnp.bfloat16), "dp", -distance
            ).astype(jnp.float32),
            passed_along(
                d_key_rope[lower : lower + n_rows].astype(jnp.bfloat16), "dp", -distance
            ).astype(jnp.float32),
        )
        own_latent = own_latent + home_latent
        own_rope = own_rope + home_rope
    d_normed, own_latent, own_rope = (
        lax.psum(d_normed.astype(jnp.bfloat16), "tensor").astype(jnp.float32),
        lax.psum(own_latent.astype(jnp.bfloat16), "tensor").astype(jnp.float32),
        lax.psum(own_rope.astype(jnp.bfloat16), "tensor").astype(jnp.float32),
    )
    d_latent_raw, grad_gain_latent = latent_back((own_latent, own_rope))
    d_latent_low = d_latent_raw.astype(jnp.bfloat16)
    grad_wlat = matmul_tn(normed_low, d_latent_low)
    d_normed = d_normed + matmul_nt(d_latent_low, wlat_full)
    d_tokens_norm, grad_gain_attn = attn_norm_back(d_normed)
    token_input_gradient = d_middle + d_tokens_norm
    reduced_result = tuple(
        (
            lax.psum_scatter(grad_gain_attn, "dp", scatter_dimension=0, tiled=True),
            lax.psum_scatter(grad_wq, "dp", scatter_dimension=0, tiled=True),
            lax.psum_scatter(grad_wlat, "dp", scatter_dimension=0, tiled=True),
            lax.psum_scatter(grad_gain_latent, "dp", scatter_dimension=0, tiled=True),
            lax.psum_scatter(grad_wkv, "dp", scatter_dimension=0, tiled=True),
            lax.psum_scatter(grad_wout, "dp", scatter_dimension=1, tiled=True),
            lax.psum_scatter(grad_gain_moe, "dp", scatter_dimension=0, tiled=True),
            lax.psum_scatter(grad_router, "dp", scatter_dimension=0, tiled=True),
            lax.psum_scatter(grad_sgate, "dp", scatter_dimension=0, tiled=True),
            lax.psum_scatter(grad_sup, "dp", scatter_dimension=0, tiled=True),
            lax.psum_scatter(grad_sdown, "dp", scatter_dimension=1, tiled=True),
        )
    )
    return (
        (result, token_input_gradient)
        + reduced_result
        + (expert_gate_weight_gradient, expert_up_weight_gradient, expert_down_weight_gradient)
    )


def solution(mesh):
    placed = (
        P("dp", None),
        P("dp", None),
        P(),
        P("dp", None),
        P("dp"),
        P("dp", "tensor"),
        P("dp", None),
        P("dp"),
        P("dp", "tensor"),
        P("tensor", "dp"),
        P("dp"),
        P("dp", None),
        P("dp", "tensor"),
        P("dp", "tensor"),
        P("tensor", "dp"),
        P("dp", None, "tensor"),
        P("dp", None, "tensor"),
        P("dp", "tensor", None),
    )
    sixteen = mesh.shape["dp"] == 16 and mesh.shape["tensor"] == 2

    def body(*args):
        fits_sixteen = sixteen and args[2].shape[0] == 1 and args[15].shape[0] == 1 and args[0].shape[0] == 256
        return (shards_sixteen if fits_sixteen else shards_general)(*args)

    return jax.shard_map(
        body,
        mesh=mesh,
        in_specs=placed,
        out_specs=(
            P("dp", None),
            P("dp", None),
            P("dp"),
            P("dp", "tensor"),
            P("dp", None),
            P("dp"),
            P("dp", "tensor"),
            P("tensor", "dp"),
            P("dp"),
            P("dp", None),
            P("dp", "tensor"),
            P("dp", "tensor"),
            P("tensor", "dp"),
            P("dp", None, "tensor"),
            P("dp", None, "tensor"),
            P("dp", "tensor", None),
        ),
        check_vma=False,
    )
```

```python
import functools
import math

import jax
import jax.numpy as jnp
from jax import lax
from jax.experimental import pallas as pl
from jax.experimental.pallas import tpu as pltpu
from jax.sharding import PartitionSpec as P

NOPE = 128
ROPE = 64
VDIM = 128
RANK = 512
TOPK = 6
WINDOW = 1024


eps_norm = 1e-06
highest = lax.Precision.HIGHEST


def passed_along(value, axis, steps):
    count = lax.axis_size(axis)
    leading, last = (max(0, -steps), min(count, count - steps))
    return lax.ppermute(value, axis, [(source, source + steps) for source in range(leading, last)])


def rms_scale(values, gain_vec):
    inv_root = lax.rsqrt(jnp.mean(values * values, axis=-1, keepdims=True) + eps_norm)
    return values * inv_root * gain_vec


def rope_tables(positions):
    half_width = ROPE // 2
    frequency = jnp.exp(
        -jnp.arange(half_width, dtype=jnp.float32) * (2.0 * math.log(10000.0) / ROPE)
    )
    angles = positions[:, None] * frequency[None, :]
    return (jnp.cos(angles), jnp.sin(angles))


def rotate(values, cos_tab, sin_tab):
    half_width = values.shape[-1] // 2
    first_half = values[..., :half_width]
    second = values[..., half_width:]
    return jnp.concatenate(
        [first_half * cos_tab - second * sin_tab, second * cos_tab + first_half * sin_tab], axis=-1
    )


def gated_act(gate_a, up_b):
    return jax.nn.silu(gate_a) * up_b


def matmul(left_mat, right_mat):
    return jnp.dot(left_mat, right_mat, preferred_element_type=jnp.float32)


def matmul_nt(left_mat, right_mat):
    return lax.dot_general(
        left_mat, right_mat, (((1,), (1,)), ((), ())), preferred_element_type=jnp.float32
    )


def matmul_tn(left_mat, right_mat):
    return lax.dot_general(
        left_mat, right_mat, (((0,), (0,)), ((), ())), preferred_element_type=jnp.float32
    )


def ranks_before(hot):
    count = hot.shape[0]
    below = jnp.arange(count)[:, None] > jnp.arange(count)[None, :]
    return matmul(below.astype(jnp.bfloat16), hot.astype(jnp.bfloat16)).astype(jnp.int32)


MESH = pl.DeviceIdType.MESH


def plane_at(z, k):
    edge = jnp.where(z >= 2, 3 - z, z)
    near = jnp.where(k == 0, edge, jnp.where(k == 1, 1 - edge, k))
    return jnp.where(z >= 2, 3 - near, near)


def ag_kernel(kinds, cuts, *refs):
    n = len(kinds)
    ins, outs, lands, sems = refs[:n], refs[n : 2 * n], refs[2 * n : 3 * n], refs[3 * n :]
    me = lax.axis_index("dp")
    core = lax.axis_index("tensor")
    z = me // 4
    y = (me // 2) % 2
    x = me % 2
    xn = z * 4 + y * 2 + (1 - x)
    yn = z * 4 + (1 - y) * 2 + x
    up = jnp.minimum(z + 1, 3) * 4 + y * 2 + x
    dn = jnp.maximum(z - 1, 0) * 4 + y * 2 + x
    bar = pltpu.get_barrier_semaphore()

    def sig(d, c):
        pl.semaphore_signal(bar, inc=1, device_id=(d, c), device_id_type=MESH)

    sig(xn, core)
    sig(yn, core)
    sig(me, 1 - core)
    pl.when(z < 3)(lambda: sig(up, core))
    pl.when(z > 0)(lambda: sig(dn, core))

    def rc(src, dst, ss, rs, dev, c):
        return pltpu.make_async_remote_copy(
            src_ref=src, dst_ref=dst, send_sem=ss, recv_sem=rs, device_id=(dev, c), device_id_type=MESH
        )

    class Part:
        def __init__(self, at, rows):
            self.share = kinds[at]
            self.x, self.o, self.hbm = ins[at], lands[at], outs[at]
            self.rows = rows
            self.zs, self.zr, self.xs, self.xr, self.ys, self.yr, self.cs, self.cr, self.own, self.out = sems[20 * at + 10 : 20 * at + 20]
            self.slot = core if self.share else 0
            self.copy = pltpu.make_async_copy(self.x.at[:, self.rows], self.whole(me), self.own)

        def whole(self, b):
            return self.o.at[b, self.slot, :, self.rows]

        def z_(self, zp, dev, s):
            b = zp * 4 + y * 2 + x
            return rc(self.whole(b), self.whole(b), self.zs.at[s], self.zr.at[zp], dev, core)

        def x_(self, j, b, half, zp):
            r = self.o.at[b, self.slot, half, self.rows]
            return rc(r, r, self.xs.at[zp, j], self.xr.at[zp, j], xn, core)

        def y_(self, j, b, half, zp):
            r = self.o.at[b, self.slot, half, self.rows]
            return rc(r, r, self.ys.at[zp, j], self.yr.at[zp, j], yn, core)

        def twin(self, b):
            return rc(self.whole(b), self.whole(b), self.cs.at[b], self.cr.at[b], me, 1 - core)

        def first(self, k):
            zp = plane_at(z, k)
            b = zp * 4 + y * 2 + x
            if k > 0:
                self.z_(zp, up, 0).wait_recv()
            pl.when((zp <= z) & (z < 3))(lambda: self.z_(zp, up, zp).start())
            pl.when((zp >= z) & (z > 0))(lambda: self.z_(zp, dn, 4 + zp).start())
            self.x_(0, b, 0, zp).start()
            self.y_(0, b, 1, zp).start()
            self.y_(1, b, 0, zp).start()
            self.x_(1, b, 1, zp).start()
            if self.share:
                self.twin(b).start()

        def second(self, k):
            zp = plane_at(z, k)
            bx = zp * 4 + y * 2 + (1 - x)
            by = zp * 4 + (1 - y) * 2 + x
            self.x_(0, bx, 0, zp).wait_recv()
            self.y_(2, bx, 0, zp).start()
            self.y_(0, by, 1, zp).wait_recv()
            self.x_(2, by, 1, zp).start()
            self.x_(1, bx, 1, zp).wait_recv()
            self.y_(1, by, 0, zp).wait_recv()
            if self.share:
                self.twin(bx).start()
                self.twin(by).start()

        def third(self, k):
            zp = plane_at(z, k)
            bd = zp * 4 + (1 - y) * 2 + (1 - x)
            self.y_(2, bd, 0, zp).wait_recv()
            self.x_(2, bd, 1, zp).wait_recv()
            if self.share:
                self.twin(bd).start()

        def save(self, k):
            at = pl.ds(plane_at(z, k) * 4, 4)
            return pltpu.make_async_copy(
                self.o.at[at, :, :, self.rows], self.hbm.at[at, :, :, self.rows], self.out.at[k]
            )

        def fourth(self, k):
            if self.share:
                for q in range(4):
                    b = plane_at(z, k) * 4 + q
                    src, dst = self.o.at[b, core, :, self.rows], self.o.at[b, 1 - core, :, self.rows]
                    rc(src, dst, self.cs.at[b], self.cr.at[b], me, 1 - core).wait_recv()
            self.save(k).start()

        def end(self):
            for k in range(4):
                self.save(k).wait()
                pl.when((k <= z) & (z < 3))(lambda k=k: self.z_(k, up, k).wait_send())
                pl.when((k >= z) & (z > 0))(lambda k=k: self.z_(k, dn, 4 + k).wait_send())
                for j in range(3):
                    self.x_(j, 0, 0, k).wait_send()
                    self.y_(j, 0, 0, k).wait_send()
            if self.share:
                for b in range(16):
                    self.twin(b).wait_send()

    class Cross:
        def __init__(self, at, rows):
            self.share = kinds[at]
            self.x, self.o, self.hbm = ins[at], lands[at], outs[at]
            self.rows = rows
            self.fs, self.fr, self.zs, self.zr, self.ls, self.lr, self.cs, self.cr, self.own, self.out = sems[20 * at : 20 * at + 10]
            self.slot = core if self.share else 0
            self.copy = pltpu.make_async_copy(self.x.at[:, rows], self.o.at[me, self.slot, :, rows], self.own)

        def ref(self, b, half):
            return self.o.at[b, self.slot, half, self.rows]

        def block(self, zp, half, p):
            if half == 0:
                return zp * 4 + y * 2 + (x if p == 0 else 1 - x)
            return zp * 4 + (y if p == 0 else 1 - y) * 2 + x

        def hop(self, half):
            r = self.ref(me, half)
            return rc(r, r, self.fs.at[half], self.fr.at[half], xn if half == 0 else yn, core)

        def line(self, zp, half, p, d):
            r = self.ref(self.block(zp, half, p), half)
            return rc(r, r, self.zs.at[d, zp, half, p], self.zr.at[zp, half, p], up if d == 0 else dn, core)

        def last(self, zp, half, p):
            r = self.ref(self.block(zp, half, p), half)
            return rc(r, r, self.ls.at[zp, half, p], self.lr.at[zp, half, p], yn if half == 0 else xn, core)

        def twin(self, b, half):
            r = self.ref(b, half)
            return rc(r, r, self.cs.at[b, half], self.cr.at[b, half], me, 1 - core)

        def pass_on(self, zp, half, p):
            pl.when((zp <= z) & (z < 3))(lambda: self.line(zp, half, p, 0).start())
            pl.when((zp >= z) & (z > 0))(lambda: self.line(zp, half, p, 1).start())
            self.last(zp, half, p).start()
            if self.share:
                self.twin(self.block(zp, half, p), half).start()

        def first(self, k):
            zp = plane_at(z, k)
            if k == 0:
                for half in range(2):
                    self.hop(half).start()
                for half in range(2):
                    self.pass_on(zp, half, 0)
                for half in range(2):
                    self.hop(half).wait_recv()
                    self.pass_on(zp, half, 1)
            else:
                for p in range(2):
                    for half in range(2):
                        self.line(zp, half, p, 0).wait_recv()
                        self.pass_on(zp, half, p)

        def second(self, k):
            pass

        def third(self, k):
            zp = plane_at(z, k)
            for p in range(2):
                for half in range(2):
                    self.last(zp, half, p).wait_recv()
                    if self.share:
                        far = zp * 4 + (1 - y) * 2 + (x if p == 0 else 1 - x)
                        if half == 1:
                            far = zp * 4 + (y if p == 0 else 1 - y) * 2 + (1 - x)
                        self.twin(far, half).start()

        def save(self, k):
            at = pl.ds(plane_at(z, k) * 4, 4)
            return pltpu.make_async_copy(
                self.o.at[at, :, :, self.rows], self.hbm.at[at, :, :, self.rows], self.out.at[k]
            )

        def fourth(self, k):
            if self.share:
                for q in range(4):
                    b = plane_at(z, k) * 4 + q
                    for half in range(2):
                        src, dst = self.o.at[b, core, half, self.rows], self.o.at[b, 1 - core, half, self.rows]
                        rc(src, dst, self.cs.at[b, half], self.cr.at[b, half], me, 1 - core).wait_recv()
            self.save(k).start()

        def end(self):
            for half in range(2):
                self.hop(half).wait_send()
            for k in range(4):
                self.save(k).wait()
                for half in range(2):
                    for p in range(2):
                        pl.when((k <= z) & (z < 3))(lambda k=k, h=half, p=p: self.line(k, h, p, 0).wait_send())
                        pl.when((k >= z) & (z > 0))(lambda k=k, h=half, p=p: self.line(k, h, p, 1).wait_send())
                        self.last(k, half, p).wait_send()
            if self.share:
                for b in range(16):
                    for half in range(2):
                        self.twin(b, half).wait_send()

    groups = []
    for at in range(n):
        height = ins[at].shape[1]
        group = [Cross(at, pl.ds(0, cuts[at]))] if cuts[at] > 0 else []
        if cuts[at] < height:
            group.append(Part(at, pl.ds(cuts[at], height - cuts[at])))
        groups.append(group)
    parts = [p for g in groups for p in g]
    for p in parts:
        p.copy.start()
    pl.semaphore_wait(bar, 3 + (z < 3).astype(jnp.int32) + (z > 0).astype(jnp.int32))
    for p in parts:
        p.copy.wait()
    turns = [(p, k) for k in range(4) for p in parts]
    lag = len(parts)
    for t in range(len(turns) + lag):
        if t < len(turns):
            turns[t][0].first(turns[t][1])
        if t >= lag:
            turns[t - lag][0].second(turns[t - lag][1])
    for p, k in turns:
        p.third(k)
        if not p.share:
            p.fourth(k)
    for p, k in turns:
        if p.share:
            p.fourth(k)
    for p in parts:
        p.end()


def ag16(arrays, kinds, cid, cuts=None):
    S = pltpu.SemaphoreType.DMA
    any_ = pl.BlockSpec(memory_space=pl.ANY)
    cuts = cuts or tuple(v.shape[1] // 2 for v in arrays)
    counts = (
        ((2,), (2,), (2, 4, 2, 2), (4, 2, 2), (4, 2, 2), (4, 2, 2), (16, 2), (16, 2), (), (4,))
        + ((8,), (4,), (4, 3), (4, 3), (4, 3), (4, 3), (16,), (16,), (), (4,))
    )
    shapes = [(16, 2 if share else 1) + v.shape for v, share in zip(arrays, kinds)]
    return pl.pallas_call(
        functools.partial(ag_kernel, kinds, cuts),
        out_shape=[jax.ShapeDtypeStruct(s, v.dtype) for s, v in zip(shapes, arrays)],
        in_specs=[any_] * len(arrays),
        out_specs=[any_] * len(arrays),
        scratch_shapes=[pltpu.VMEM(s, v.dtype) for s, v in zip(shapes, arrays)]
        + [S(s) for _ in arrays for s in counts],
        compiler_params=pltpu.CompilerParams(collective_id=cid, has_side_effects=True, vmem_limit_bytes=60 << 20),
    )(*arrays)


def add_into(dst, src):
    def step(i, _):
        r = pl.ds(pl.multiple_of(i * 16, 16), 16)
        dst[r] = dst[r] + src[r]
        return 0

    lax.fori_loop(0, dst.shape[0] // 16, step, 0)


def rs_kernel(a_ref, b_ref, o_ref, own, fr, zr, lr, yr, xr, z2r, lsem, fs, frs, zs, zrs, ls, lrs, xs, xrs, ys, yrs, z2s, z2rs):
    me = lax.axis_index("dp")
    core = lax.axis_index("tensor")
    z = me // 4
    y = (me // 2) % 2
    x = me % 2
    xn = z * 4 + y * 2 + (1 - x)
    yn = z * 4 + (1 - y) * 2 + x
    up = jnp.minimum(z + 1, 3) * 4 + y * 2 + x
    dn = jnp.maximum(z - 1, 0) * 4 + y * 2 + x
    wide = a_ref.shape[3]
    cut = fr.shape[3]
    crossing, rest = pl.ds(0, cut), pl.ds(cut, own.shape[2] - cut)

    def rc(src, dst, ss, rs, dev):
        return pltpu.make_async_remote_copy(
            src_ref=src, dst_ref=dst, send_sem=ss, recv_sem=rs, device_id=(dev, core), device_id_type=MESH
        )

    def loads(zp):
        at = pl.ds(zp * 4, 4)
        return [
            pltpu.make_async_copy(a_ref.at[at], own.at[at, :, :, 0:wide], lsem.at[zp, 0]),
            pltpu.make_async_copy(b_ref.at[at], own.at[at, :, :, wide:], lsem.at[zp, 1]),
        ]

    for k in range(4):
        for c in loads(plane_at(z, 3 - k)):
            c.start()
    bar = pltpu.get_barrier_semaphore()

    def sig(d):
        pl.semaphore_signal(bar, inc=1, device_id=(d, core), device_id_type=MESH)

    sig(xn)
    sig(yn)
    pl.when(z < 3)(lambda: sig(up))
    pl.when(z > 0)(lambda: sig(dn))
    pl.semaphore_wait(bar, 2 + (z < 3).astype(jnp.int32) + (z > 0).astype(jnp.int32))

    def blk(zp, yy, xx):
        return zp * 4 + yy * 2 + xx

    def place(zp, half, p):
        if half == 0:
            return blk(zp, y, x if p == 0 else 1 - x)
        return blk(zp, y if p == 0 else 1 - y, x)

    def hop(zp, half, p):
        b = blk(zp, 1 - y, x if p == 0 else 1 - x) if half == 0 else blk(zp, y if p == 0 else 1 - y, 1 - x)
        return rc(
            own.at[b, half, crossing], fr.at[zp, half, p], fs.at[zp, half, p], frs.at[zp, half, p], yn if half == 0 else xn
        )

    def line(zp, half, p, dev, slot):
        b = place(zp, half, p)
        return rc(own.at[b, half, crossing], zr.at[slot, half, p], zs.at[zp, half, p], zrs.at[slot, half, p], dev)

    def last(half):
        b = place(z, half, 1)
        return rc(own.at[b, half, crossing], lr.at[half], ls.at[half], lrs.at[half], xn if half == 0 else yn)

    def y_(j, b, half, zp):
        return rc(own.at[b, half, rest], yr.at[zp, j], ys.at[zp, j], yrs.at[zp, j], yn)

    def x_(j, b, half, zp):
        return rc(own.at[b, half, rest], xr.at[zp, j], xs.at[zp, j], xrs.at[zp, j], xn)

    def zc(zp, dev, d):
        return rc(own.at[zp * 4 + y * 2 + x, :, rest], z2r.at[d, zp], z2s.at[zp], z2rs.at[d, zp], dev)

    def s1(k):
        zp = plane_at(z, 3 - k)
        for c in loads(zp):
            c.wait()
        for p in range(2):
            for half in range(2):
                hop(zp, half, 1 - p).start()
        y_(0, blk(zp, 1 - y, 1 - x), 0, zp).start()
        x_(0, blk(zp, 1 - y, 1 - x), 1, zp).start()
        y_(1, blk(zp, 1 - y, x), 0, zp).start()
        x_(1, blk(zp, y, 1 - x), 1, zp).start()

    def arrive(zp, half, p, slot):
        line(zp, half, p, me, slot).wait_recv()
        add_into(own.at[place(zp, half, p), half, crossing], zr.at[slot, half, p])

    def s2(k):
        zp = plane_at(z, 3 - k)
        for p in (1, 0):
            for half in range(2):
                hop(zp, half, p).wait_recv()
                add_into(own.at[place(zp, half, p), half, crossing], fr.at[zp, half, p])
                pl.when((zp <= z) & (z < 3))(lambda h=half, p=p: arrive(zp, h, p, jnp.where(zp == z, 4, zp)))
                pl.when((zp >= z) & (z > 0))(lambda h=half, p=p: arrive(zp, h, p, zp))
                pl.when(zp < z)(lambda h=half, p=p: line(zp, h, p, dn, jnp.where(zp == z - 1, 4, zp)).start())
                pl.when(zp > z)(lambda h=half, p=p: line(zp, h, p, up, zp).start())
                if k == 3 and p == 1:
                    last(half).start()
        mine = blk(zp, y, x)
        y_(0, blk(zp, 1 - y, 1 - x), 0, zp).wait_recv()
        add_into(own.at[blk(zp, y, 1 - x), 0, rest], yr.at[zp, 0])
        x_(2, blk(zp, y, 1 - x), 0, zp).start()
        x_(0, blk(zp, 1 - y, 1 - x), 1, zp).wait_recv()
        add_into(own.at[blk(zp, 1 - y, x), 1, rest], xr.at[zp, 0])
        y_(2, blk(zp, 1 - y, x), 1, zp).start()
        y_(1, blk(zp, 1 - y, x), 0, zp).wait_recv()
        add_into(own.at[mine, 0, rest], yr.at[zp, 1])
        x_(1, blk(zp, y, 1 - x), 1, zp).wait_recv()
        add_into(own.at[mine, 1, rest], xr.at[zp, 1])

    def s3(k):
        zp = plane_at(z, 3 - k)
        mine = blk(zp, y, x)
        x_(2, blk(zp, y, 1 - x), 0, zp).wait_recv()
        add_into(own.at[mine, 0, rest], xr.at[zp, 2])
        y_(2, blk(zp, 1 - y, x), 1, zp).wait_recv()
        add_into(own.at[mine, 1, rest], yr.at[zp, 2])

        def arrived(d):
            zc(zp, me, d).wait_recv()
            add_into(own.at[mine, 0, rest], z2r.at[d, zp, 0])
            add_into(own.at[mine, 1, rest], z2r.at[d, zp, 1])

        pl.when((zp <= z) & (z < 3))(lambda: arrived(1))
        pl.when((zp >= z) & (z > 0))(lambda: arrived(0))
        pl.when(zp < z)(lambda: zc(zp, dn, 1).start())
        pl.when(zp > z)(lambda: zc(zp, up, 0).start())

    s1(0)
    s1(1)
    s2(0)
    s1(2)
    s2(1)
    s3(0)
    s1(3)
    s2(2)
    s3(1)
    s2(3)
    s3(2)
    s3(3)
    for half in range(2):
        last(half).wait_recv()
        add_into(own.at[me, half, crossing], lr.at[half])
    for a in range(2):

        def row(i, _):
            r = pl.ds(pl.multiple_of(i * 16, 16), 16)
            o_ref[a, r] = own[me, a, r].astype(jnp.float32)
            return 0

        lax.fori_loop(0, o_ref.shape[1] // 16, row, 0)
    for half in range(2):
        last(half).wait_send()
    for k in range(4):
        for half in range(2):
            for p in range(2):
                hop(k, half, p).wait_send()
                pl.when(k != z)(lambda k=k, h=half, p=p: line(k, h, p, me, 0).wait_send())
        for j in range(3):
            x_(j, 0, 0, k).wait_send()
            y_(j, 0, 0, k).wait_send()
        pl.when(k != z)(lambda k=k: zc(k, up, 0).wait_send())


def rs16(a, b, cid):
    S = pltpu.SemaphoreType.DMA
    high, total = a.shape[2], a.shape[3] + b.shape[3]
    blkshape = (2, high, total)
    cross, half = (high // 2, total), (high - high // 2, total)
    V = lambda s: pltpu.VMEM(s, a.dtype)
    return pl.pallas_call(
        rs_kernel,
        out_shape=jax.ShapeDtypeStruct(blkshape, jnp.float32),
        in_specs=[pl.BlockSpec(memory_space=pl.ANY)] * 2,
        out_specs=pl.BlockSpec(memory_space=pltpu.VMEM),
        scratch_shapes=[
            V((16,) + blkshape), V((4, 2, 2) + cross), V((5, 2, 2) + cross), V((2,) + cross),
            V((4, 3) + half), V((4, 3) + half), V((2, 4, 2) + half),
            S((4, 2)), S((4, 2, 2)), S((4, 2, 2)), S((4, 2, 2)), S((5, 2, 2)), S((2,)), S((2,)),
            S((4, 3)), S((4, 3)), S((4, 3)), S((4, 3)), S((4,)), S((2, 4)),
        ],
        compiler_params=pltpu.CompilerParams(collective_id=cid, has_side_effects=True, vmem_limit_bytes=60 << 20),
    )(a, b)


def nt(a, b):
    return lax.dot_general(a, b, (((1,), (1,)), ((), ())), preferred_element_type=jnp.float32)


def tn(a, b):
    return lax.dot_general(a, b, (((0,), (0,)), ((), ())), preferred_element_type=jnp.float32)


def mm(a, b):
    return jnp.dot(a, b, preferred_element_type=jnp.float32)


def gate_parts(a, b, dc):
    s = 1.0 / (1.0 + jnp.exp(-a))
    act = a * s
    return act * b, dc * b * (s * (1.0 + a * (1.0 - s))), dc * act


def moe_kernel(
    moe, grd, pick, pick_t, wg_in, wu_in, wd_in, wr, sgu, sdn,
    o_out, r_out, rg_out, act_out, da_out, db_out, sg_out, yr, xr, zr,
    wg, wu, wd, own, sib, sibr, stage, xb, gb, pk, pt, rr, rg, ly, ld, ry, rd, acts, das, dbs, dgs,
    w_sem, in_sem, out_sem, st_sem, free, cs, cr, xs, xrs, ys, yrs, zs, zrs, fs, fr,
):
    me = lax.axis_index("dp")
    core = lax.axis_index("tensor")
    other = 1 - core
    z = me // 4
    y = (me // 2) % 2
    x = me % 2
    xn = z * 4 + y * 2 + (1 - x)
    yn = z * 4 + (1 - y) * 2 + x
    up = jnp.minimum(z + 1, 3) * 4 + y * 2 + x
    dn = jnp.maximum(z - 1, 0) * 4 + y * 2 + x
    width = moe.shape[2]
    hid = 128
    cut = 512

    def rc(src, dst, ss, rs, dev, c):
        return pltpu.make_async_remote_copy(
            src_ref=src, dst_ref=dst, send_sem=ss, recv_sem=rs, device_id=(dev, c), device_id_type=MESH
        )

    def loads(i):
        k, half = i // 2, i % 2
        b = plane_at(z, 3 - k) * 4 + jnp.where(half == 0, 1 - y, y) * 2
        at = pl.ds(b, 2)
        return [
            pltpu.make_async_copy(moe.at[at], xb, in_sem.at[0]),
            pltpu.make_async_copy(grd.at[at], gb, in_sem.at[1]),
            pltpu.make_async_copy(pick.at[at], pk, in_sem.at[2]),
            pltpu.make_async_copy(pick_t.at[at], pt, in_sem.at[3]),
        ]

    for c in loads(0):
        c.start()
    weights = [
        pltpu.make_async_copy(src, dst, w_sem.at[n]) for n, (src, dst) in enumerate(((wd_in, wd), (wg_in, wg), (wu_in, wu)))
    ]
    for c in weights:
        c.start()
    bar = pltpu.get_barrier_semaphore()

    def sig(d, c):
        pl.semaphore_signal(bar, inc=1, device_id=(d, c), device_id_type=MESH)

    sig(xn, core)
    sig(yn, core)
    sig(me, other)
    pl.when(z < 3)(lambda: sig(up, core))
    pl.when(z > 0)(lambda: sig(dn, core))
    pl.semaphore_wait(bar, 3 + (z < 3).astype(jnp.int32) + (z > 0).astype(jnp.int32))

    for q in range(2):
        ry[q, hid:] = sdn[...]
        rd[q, hid:] = sgu[...]
    sg_out[...] = jnp.zeros_like(sg_out)

    def y_(j, b, half, zp):
        return rc(own.at[b, half], yr.at[zp, j], ys.at[zp, j], yrs.at[zp, j], yn, core)

    def x_(j, b, half, zp):
        return rc(own.at[b, half], xr.at[zp, j], xs.at[zp, j], xrs.at[zp, j], xn, core)

    def zc(zp, dev, d):
        b = zp * 4 + y * 2 + x
        return rc(own.at[b], zr.at[d, zp], zs.at[zp], zrs.at[d, zp], dev, core)

    def sib_send(i):
        return rc(sib, sibr, cs, cr, me, other)

    def outs(i):
        at = pl.ds(pl.multiple_of(i * 256, 256), 256)
        return [
            pltpu.make_async_copy(rr, r_out.at[at], out_sem.at[0]),
            pltpu.make_async_copy(rg, rg_out.at[at], out_sem.at[1]),
            pltpu.make_async_copy(acts, act_out.at[at], out_sem.at[2]),
            pltpu.make_async_copy(das, da_out.at[at], out_sem.at[3]),
            pltpu.make_async_copy(dbs, db_out.at[at], out_sem.at[4]),
        ]

    def columns(step):
        def one(n, _):
            step(pl.ds(pl.multiple_of(n * cut, cut), cut))
            return 0

        lax.fori_loop(0, width // cut, one, 0)

    def first_part(i):
        for c in loads(i):
            c.wait()

        @pl.when(i > 0)
        def _():
            for c in outs(i - 1):
                c.wait()

        def pick_rows(n):
            for q in range(2):
                rr[q * hid : (q + 1) * hid, n] = mm(pk[q], xb[q, :, n]).astype(jnp.bfloat16)
                rg[q * hid : (q + 1) * hid, n] = mm(pk[q], gb[q, :, n]).astype(jnp.bfloat16)

        columns(pick_rows)
        for q in range(2):
            ab = nt(xb[q], sgu[...])
            act, d_a, d_b = gate_parts(ab[:, :hid], ab[:, hid:], nt(gb[q], sdn[...]))
            ly[q, :, :hid] = pt[q]
            ly[q, :, hid:] = act.astype(jnp.bfloat16)
            ld[q, :, :hid] = pt[q]
            ld[q, :, hid : 2 * hid] = d_a.astype(jnp.bfloat16)
            ld[q, :, 2 * hid :] = d_b.astype(jnp.bfloat16)

        def shared_grads(n):
            sg_out[: 2 * hid, n] += tn(ld[0, :, hid:], xb[0, :, n]) + tn(ld[1, :, hid:], xb[1, :, n])
            sg_out[2 * hid :, n] += tn(ly[0, :, hid:], gb[0, :, n]) + tn(ly[1, :, hid:], gb[1, :, n])

        columns(shared_grads)

        @pl.when(i < 7)
        def _():
            for c in loads(i + 1):
                c.start()

    def second_part(i):
        @pl.when(i == 0)
        def _():
            for c in weights:
                c.wait()

        logits = mm(rr[...], wr[...])
        lane = lax.broadcasted_iota(jnp.int32, logits.shape, 1)
        logits = jnp.where(lane < 16, logits, -jnp.inf)
        e = jnp.exp(logits - jnp.max(logits, axis=1, keepdims=True))
        gate = jnp.sum(jnp.where(lane == me, e, 0.0), axis=1, keepdims=True) / jnp.sum(
            e, axis=1, keepdims=True
        )
        pre = nt(rg[...], wd[...])
        act, d_a, d_b = gate_parts(nt(rr[...], wg[...]), nt(rr[...], wu[...]), gate * pre)
        low = act.astype(jnp.bfloat16)
        back = low.astype(jnp.float32)
        d_gate = jnp.sum(back * pre, axis=1, keepdims=True)
        acts[...] = (gate * back).astype(jnp.bfloat16)
        das[...] = d_a.astype(jnp.bfloat16)
        dbs[...] = d_b.astype(jnp.bfloat16)

        def spread(n):
            o = (gate * mm(low, wd[:, n])).astype(jnp.bfloat16)
            s = (mm(das[...], wg[:, n]) + mm(dbs[...], wu[:, n])).astype(jnp.bfloat16)
            for q in range(2):
                ry[q, :hid, n] = o[q * hid : (q + 1) * hid]
                rd[q, :hid, n] = s[q * hid : (q + 1) * hid]

        columns(spread)
        for c in outs(i):
            c.start()
        dgs[...] = jnp.where(lane == me, d_gate, 0.0).astype(jnp.bfloat16)

    def third_part(i):
        k, half = i // 2, i % 2
        b = plane_at(z, 3 - k) * 4 + jnp.where(half == 0, 1 - y, y) * 2

        @pl.when(i > 0)
        def _():
            sib_send(i - 1).wait_send()

        def store(q, n, v):
            v = v.astype(jnp.bfloat16)
            mine = jnp.where(core == 0, v[:128], v[128:])
            theirs = jnp.where(core == 0, v[128:], v[:128])
            own[b + q, 0, :, n] = mine[:64]
            own[b + q, 1, :, n] = mine[64:]
            sib[q, 0, :, n] = theirs[:64]
            sib[q, 1, :, n] = theirs[64:]

        def put(m, _):
            n = pl.ds(pl.multiple_of(m * cut, cut), cut)
            n2 = pl.ds(pl.multiple_of(width + m * cut, cut), cut)
            for q in range(2):
                store(q, n, mm(ly[q], ry[q, :, n]))
                store(q, n2, mm(ld[q], rd[q, :, n]))
            return 0

        lax.fori_loop(0, width // cut, put, 0)
        for q in range(2):
            store(q, pl.ds(2 * width, 128), mm(pt_of(q), dgs[q * hid : (q + 1) * hid]))

        @pl.when(i > 0)
        def _():
            pl.semaphore_wait(free, 1)

        sib_send(i).start()

    def pt_of(q):
        return ly[q, :, :hid]

    def staged(src, dst, sem):
        return pltpu.make_async_copy(src, dst, sem)

    def blk(zp, yy, xx):
        return zp * 4 + yy * 2 + xx

    def pair_sum(i):
        k, half = i // 2, i % 2
        zp = plane_at(z, 3 - k)
        b = zp * 4 + jnp.where(half == 0, 1 - y, y) * 2
        sib_send(i).wait_recv()

        def one(q, _):
            add_into(own.at[b + q, 0], sibr.at[q, 0])
            add_into(own.at[b + q, 1], sibr.at[q, 1])
            return 0

        lax.fori_loop(0, 2, one, 0)

        @pl.when(i < 7)
        def _():
            pl.semaphore_signal(free, inc=1, device_id=(me, other), device_id_type=MESH)

        @pl.when(half == 0)
        def _():
            y_(0, blk(zp, 1 - y, 1 - x), 0, zp).start()
            x_(0, blk(zp, 1 - y, 1 - x), 1, zp).start()
            y_(1, blk(zp, 1 - y, x), 0, zp).start()

        @pl.when(half == 1)
        def _():
            x_(1, blk(zp, y, 1 - x), 1, zp).start()

    def second_staging(k):
        zp = plane_at(z, 3 - k)
        return [
            staged(yr.at[zp, 0], stage.at[0, 0], st_sem.at[0]),
            staged(xr.at[zp, 0], stage.at[0, 1], st_sem.at[1]),
            staged(yr.at[zp, 1], stage.at[1, 0], st_sem.at[2]),
            staged(xr.at[zp, 1], stage.at[1, 1], st_sem.at[3]),
        ]

    def second_fetch(k):
        zp = plane_at(z, 3 - k)
        c = second_staging(k)
        y_(0, blk(zp, 1 - y, 1 - x), 0, zp).wait_recv()
        c[0].start()
        x_(0, blk(zp, 1 - y, 1 - x), 1, zp).wait_recv()
        c[1].start()
        y_(1, blk(zp, 1 - y, x), 0, zp).wait_recv()
        c[2].start()
        x_(1, blk(zp, y, 1 - x), 1, zp).wait_recv()
        c[3].start()

    def second_hop(k):
        zp = plane_at(z, 3 - k)
        mine = blk(zp, y, x)
        c = second_staging(k)
        c[0].wait()
        add_into(own.at[blk(zp, y, 1 - x), 0], stage.at[0, 0])
        x_(2, blk(zp, y, 1 - x), 0, zp).start()
        c[1].wait()
        add_into(own.at[blk(zp, 1 - y, x), 1], stage.at[0, 1])
        y_(2, blk(zp, 1 - y, x), 1, zp).start()
        c[2].wait()
        add_into(own.at[mine, 0], stage.at[1, 0])
        c[3].wait()
        add_into(own.at[mine, 1], stage.at[1, 1])

    def last_staging(k):
        zp = plane_at(z, 3 - k)
        return [
            staged(xr.at[zp, 2], stage.at[0, 0], st_sem.at[0]),
            staged(yr.at[zp, 2], stage.at[0, 1], st_sem.at[1]),
            staged(zr.at[1, zp], stage.at[1], st_sem.at[2]),
            staged(zr.at[0, zp], stage.at[2], st_sem.at[3]),
        ]

    def last_fetch(k):
        zp = plane_at(z, 3 - k)
        c = last_staging(k)
        x_(2, blk(zp, y, 1 - x), 0, zp).wait_recv()
        c[0].start()
        y_(2, blk(zp, 1 - y, x), 1, zp).wait_recv()
        c[1].start()

        @pl.when((zp <= z) & (z < 3))
        def _():
            zc(zp, me, 1).wait_recv()
            c[2].start()

        @pl.when((zp >= z) & (z > 0))
        def _():
            zc(zp, me, 0).wait_recv()
            c[3].start()

    def last_hop(k):
        zp = plane_at(z, 3 - k)
        mine = blk(zp, y, x)
        c = last_staging(k)
        c[0].wait()
        add_into(own.at[mine, 0], stage.at[0, 0])
        c[1].wait()
        add_into(own.at[mine, 1], stage.at[0, 1])

        def arrived(d):
            c[3 - d].wait()
            add_into(own.at[mine, 0], stage.at[2 - d, 0])
            add_into(own.at[mine, 1], stage.at[2 - d, 1])

        pl.when((zp <= z) & (z < 3))(lambda: arrived(1))
        pl.when((zp >= z) & (z > 0))(lambda: arrived(0))
        pl.when(zp < z)(lambda: zc(zp, dn, 1).start())
        pl.when(zp > z)(lambda: zc(zp, up, 0).start())

    lag = jnp.where((z == 0) | (z == 3), 5, 7)

    def step(i, _):
        pl.when(i < 8)(lambda: first_part(i))
        pl.when((i >= 1) & (i <= 8))(lambda: pair_sum(i - 1))
        seconds = (i % 2 == 0) & (i >= 4) & (i <= 10)
        lasts = (i % 2 == 1) & (i >= lag) & (i <= lag + 6)
        pl.when(seconds)(lambda: second_fetch((i - 4) // 2))
        pl.when(lasts)(lambda: last_fetch((i - lag) // 2))
        pl.when(i < 8)(lambda: second_part(i))
        pl.when(seconds)(lambda: second_hop((i - 4) // 2))
        pl.when(lasts)(lambda: last_hop((i - lag) // 2))
        pl.when(i < 8)(lambda: third_part(i))
        return 0

    lax.fori_loop(0, 14, step, 0)
    for a in range(2):

        def row(n, _):
            r = pl.ds(pl.multiple_of(n * 16, 16), 16)
            o_out[core, a, r] = own[me, a, r]
            return 0

        lax.fori_loop(0, 4, row, 0)
    f = rc(o_out.at[core], o_out.at[core], fs, fr, me, other)
    f.start()
    for c in outs(7):
        c.wait()
    sib_send(7).wait_send()
    for k in range(4):
        for j in range(3):
            x_(j, 0, 0, k).wait_send()
            y_(j, 0, 0, k).wait_send()

        @pl.when(k != z)
        def _():
            zc(k, up, 0).wait_send()

    rc(o_out.at[core], o_out.at[other], fs, fr, me, other).wait_recv()
    f.wait_send()


def moe_call(moe, grd, pick, pick_t, wg, wu, wd, wr, sgu, sdn, cid):
    ffe, width = wg.shape
    total = 2 * width + 128
    slots = pick.shape[0] * pick.shape[1]
    low, S, V = jnp.bfloat16, pltpu.SemaphoreType.DMA, pltpu.VMEM
    any_, vmem = pl.BlockSpec(memory_space=pl.ANY), pl.BlockSpec(memory_space=pltpu.VMEM)
    shape = lambda *s: jax.ShapeDtypeStruct(s, low)
    blk = (2, 64, total)
    return pl.pallas_call(
        moe_kernel,
        out_shape=[
            shape(2, *blk), shape(slots, width), shape(slots, width), shape(slots, ffe), shape(slots, ffe),
            shape(slots, ffe), jax.ShapeDtypeStruct((384, width), jnp.float32),
            shape(4, 3, 64, total), shape(4, 3, 64, total), shape(2, 4, *blk),
        ],
        in_specs=[any_] * 7 + [vmem] * 3,
        out_specs=[vmem] + [any_] * 5 + [vmem] + [any_] * 3,
        scratch_shapes=[
            V(wg.shape, low), V(wu.shape, low), V(wd.shape, low),
            V((16,) + blk, low), V((2,) + blk, low), V((2,) + blk, low), V((3,) + blk, low),
            V((2, 256, width), low), V((2, 256, width), low), V((2, 128, 256), low), V((2, 256, 128), low),
            V((256, width), low), V((256, width), low), V((2, 256, 256), low), V((2, 256, 384), low),
            V((2, 256, width), low), V((2, 384, width), low),
            V((256, ffe), low), V((256, ffe), low), V((256, ffe), low), V((256, 128), low),
            S((3,)), S((4,)), S((5,)), S((4,)), pltpu.SemaphoreType.REGULAR, S, S, S((4, 3)), S((4, 3)), S((4, 3)), S((4, 3)), S((4,)), S((2, 4)), S, S,
        ],
        compiler_params=pltpu.CompilerParams(collective_id=cid, has_side_effects=True, vmem_limit_bytes=60 << 20),
        cost_estimate=pl.CostEstimate(flops=65 * 10**9, bytes_accessed=80 * 10**6, transcendentals=0),
    )(moe, grd, pick, pick_t, wg, wu, wd, wr, sgu, sdn)


SLOTS = 5
KEYS = SLOTS * 256


def turned(v, cos, sin):
    n = v.shape[1]
    lane = lax.broadcasted_iota(jnp.int32, v.shape, 1) % 64
    swap = jnp.where(lane < 32, -pltpu.roll(v, n - 32, 1), pltpu.roll(v, 32, 1))
    return v * cos + swap * sin


def root(v):
    return lax.rsqrt(jnp.mean(v * v, axis=1, keepdims=True) + eps_norm)


def neighbours(me, core, bar):
    count = jnp.int32(1)
    pl.semaphore_signal(bar, inc=1, device_id=(me, 1 - core), device_id_type=MESH)
    for d in range(1, SLOTS):

        @pl.when(me + d < 16)
        def _():
            pl.semaphore_signal(bar, inc=1, device_id=(jnp.minimum(me + d, 15), core), device_id_type=MESH)

        @pl.when(me >= d)
        def _():
            pl.semaphore_signal(bar, inc=1, device_id=(jnp.maximum(me - d, 0), core), device_id_type=MESH)

        count = count + (me + d < 16).astype(jnp.int32) + (me >= d).astype(jnp.int32)
    return count


def slab_copies(w4, w2, wq, wo, wkv, wlat, sem):
    pairs = [
        (w2.at[:, 2560:3200], wlat, sem.at[0]),
        (w2.at[:, 0:1536], wq, sem.at[1]),
        (w2.at[:, 1536:2560], wo, sem.at[2]),
    ]
    for c in range(4):
        pairs.append((w4.at[:, c, :, w4.shape[3] - 512 :], wkv.at[:, :, c * 512 : (c + 1) * 512], sem.at[3 + c]))
    return pairs


def att_fwd_kernel(
    tok, w4, w2, g_att, g_moe, g_lat, cos, sin, bias,
    middle, moe_low, normed, lat_raw, qcat, keys, kv_out, lse, att,
    kv, wq, wo, wkv, wlat, part, arrived, w_sem, kv_sem, ks, kr, ts, tr, cs, cr,
):
    me = lax.axis_index("dp")
    core = lax.axis_index("tensor")
    loads = [pltpu.make_async_copy(h, v, s) for h, v, s in slab_copies(w4, w2, wq, wo, wkv, wlat, w_sem)]
    for c in loads:
        c.start()
    bar = pltpu.get_barrier_semaphore()
    pl.semaphore_wait(bar, neighbours(me, core, bar))
    t = tok[...].astype(jnp.float32)
    normed[...] = (t * root(t) * g_att[...]).astype(jnp.bfloat16)
    loads[0].wait()
    lat = mm(normed[...], wlat[...])
    lat_raw[...] = lat
    first = lat[:, :RANK]
    rot = turned(lat[:, RANK:], cos[:, :128], sin[:, :128])
    rot = jnp.where(lax.broadcasted_iota(jnp.int32, rot.shape, 1) < 64, rot, 0.0)
    keys[SLOTS - 1, :, :RANK] = (first * root(first) * g_lat[...]).astype(jnp.bfloat16)
    keys[SLOTS - 1, :, RANK:] = (rot + pltpu.roll(rot, 64, 1)).astype(jnp.bfloat16)

    mine = pl.ds(pl.multiple_of(core * 128, 128), 128)

    def send(d):
        return pltpu.make_async_remote_copy(
            src_ref=keys.at[SLOTS - 1, mine], dst_ref=keys.at[SLOTS - 1 - d, mine], send_sem=ks.at[d - 1],
            recv_sem=kr.at[d - 1], device_id=(jnp.minimum(me + d, 15), core), device_id_type=MESH,
        )

    def hand(d):
        return pltpu.make_async_remote_copy(
            src_ref=keys.at[SLOTS - 1 - d, mine], dst_ref=keys.at[SLOTS - 1 - d, mine], send_sem=ts.at[d - 1],
            recv_sem=tr.at[d - 1], device_id=(me, 1 - core), device_id_type=MESH,
        )

    def handed(d):
        other = keys.at[SLOTS - 1 - d, pl.ds(pl.multiple_of((1 - core) * 128, 128), 128)]
        return pltpu.make_async_remote_copy(
            src_ref=other, dst_ref=other, send_sem=ts.at[d - 1], recv_sem=tr.at[d - 1],
            device_id=(me, 1 - core), device_id_type=MESH,
        )

    for d in range(1, SLOTS):
        pl.when(me + d < 16)(lambda d=d: send(d).start())

        @pl.when(me < d)
        def _():
            keys[SLOTS - 1 - d] = jnp.zeros((256, 640), jnp.bfloat16)

    loads[1].wait()
    half = lax.broadcasted_iota(jnp.int32, (256, 128), 1) < 64
    q_nope = mm(normed[...], wq[:, :1024])
    q_rope = turned(mm(normed[...], wq[:, 1024:]), cos[...], sin[...])
    for h in range(8):
        qcat[h, :, :128] = q_nope[:, h * 128 : (h + 1) * 128].astype(jnp.bfloat16)
        pair = q_rope[:, h // 2 * 128 : (h // 2 + 1) * 128]
        qcat[h, :, 128:] = jnp.where(half == (h % 2 == 0), pair, 0.0).astype(jnp.bfloat16)
    for c in loads[3:]:
        c.wait()
    def project(s):
        kv[s * 256 : (s + 1) * 256] = mm(keys[s, :, :RANK], wkv[...].reshape(RANK, 2048)).astype(jnp.bfloat16)

    project(SLOTS - 1)
    for d in range(1, SLOTS + 1):
        if d < SLOTS:

            @pl.when(me >= d)
            def _(d=d):
                send(d).wait_recv()
                hand(d).start()

        if d > 1:
            pl.when(me >= d - 1)(lambda d=d: handed(d - 1).wait_recv())
            project(SLOTS - d)
    save = pltpu.make_async_copy(kv, kv_out, kv_sem)
    save.start()

    def head(h, _):
        kn = kv[:, pl.ds(pl.multiple_of(h * 256, 256), 128)]
        v = kv[:, pl.ds(pl.multiple_of(h * 256 + 128, 128), 128)]
        rope = keys[:, :, RANK:].reshape(KEYS, 128)
        s = nt(qcat[h], jnp.concatenate([kn, rope], 1)) * ((NOPE + ROPE) ** -0.5) + bias[...]
        top = jnp.max(s, axis=1, keepdims=True)
        e = jnp.exp(s - top)
        den = jnp.sum(e, axis=1, keepdims=True)
        lse[h] = top + jnp.log(den)
        p = (e * (1.0 / den)).astype(jnp.bfloat16)
        att[:, pl.ds(pl.multiple_of(h * 128, 128), 128)] = mm(p, v).astype(jnp.bfloat16)
        return 0

    lax.fori_loop(0, 8, head, 0)
    loads[2].wait()

    def out(n, _):
        r = pl.ds(pl.multiple_of(n * 512, 512), 512)
        part[:, r] = nt(att[...], wo[r]).astype(jnp.bfloat16)
        return 0

    lax.fori_loop(0, 4, out, 0)
    swap = pltpu.make_async_remote_copy(
        src_ref=part, dst_ref=arrived, send_sem=cs, recv_sem=cr, device_id=(me, 1 - core), device_id_type=MESH
    )
    swap.start()
    swap.wait()
    m = tok[...].astype(jnp.float32) + (part[...].astype(jnp.float32) + arrived[...].astype(jnp.float32))
    middle[...] = m
    moe_low[...] = (m * root(m) * g_moe[...]).astype(jnp.bfloat16)
    save.wait()
    for d in range(1, SLOTS):
        pl.when(me + d < 16)(lambda d=d: send(d).wait_send())
        pl.when(me >= d)(lambda d=d: hand(d).wait_send())


def att_fwd(tok, weights, g_att, g_moe, g_lat, cos, sin, bias, cid):
    low, f32, S, V = jnp.bfloat16, jnp.float32, pltpu.SemaphoreType.DMA, pltpu.VMEM
    any_, vmem = pl.BlockSpec(memory_space=pl.ANY), pl.BlockSpec(memory_space=pltpu.VMEM)
    shape = lambda kind, *s: jax.ShapeDtypeStruct(s, kind)
    rows, width = tok.shape
    pack = weights.shape[1]
    return pl.pallas_call(
        att_fwd_kernel,
        out_shape=[
            shape(f32, rows, width), shape(low, rows, width), shape(low, rows, width), shape(f32, rows, 640),
            shape(low, 8, rows, 256), shape(low, SLOTS, rows, 640), shape(low, KEYS, 2048), shape(f32, 8, rows, 1),
            shape(low, rows, 1024),
        ],
        in_specs=[vmem, any_, any_] + [vmem] * 6,
        out_specs=[vmem] * 6 + [any_] + [vmem] * 2,
        scratch_shapes=[
            V((KEYS, 2048), low), V((width, 1536), low), V((width, 1024), low), V((16, 32, 2048), low), V((width, 640), low),
            V((rows, width), low), V((rows, width), low), S((7,)), S, S((4,)), S((4,)), S((4,)), S((4,)), S, S,
        ],
        compiler_params=pltpu.CompilerParams(collective_id=cid, has_side_effects=True, vmem_limit_bytes=60 << 20),
        cost_estimate=pl.CostEstimate(flops=10**10, bytes_accessed=40 * 10**6, transcendentals=0),
    )(tok, weights.reshape(16, 4, 32, pack), weights, g_att, g_moe, g_lat, cos, sin, bias)


def att_bwd_kernel(
    w4, w2, home, grad, middle, moe_low, wr, g_att, g_moe, g_lat, kv_in,
    tok_in, normed_in, lat_raw_in, qcat_in, keys_in, lse_in, att_in, cos_in, sin_in, bias_in,
    tok_grad, packed, p4,
    tok, normed, lat_raw, qcat, keys, lse, att, cos, sin, bias,
    kv, wq, wo, wkv, wlat, dmid, dnorm, dmid_low, d_att, dq, dqr, dkr, dk_out, dk_pair, dk_in, own_dk, part, arrived, d_keys,
    late_sem, w_sem, kv_sem, ks, kr, cs, cr, ps, pr, hs, hr, o_sem,
):
    me = lax.axis_index("dp")
    core = lax.axis_index("tensor")
    width = grad.shape[1]
    scale = (NOPE + ROPE) ** -0.5
    loads = [pltpu.make_async_copy(h, v, s) for h, v, s in slab_copies(w4, w2, wq, wo, wkv, wlat, w_sem)]
    stores = [pltpu.make_async_copy(v, h, s) for h, v, s in slab_copies(p4, packed, wq, wo, wkv, wlat, o_sem)]
    kv_load = pltpu.make_async_copy(kv_in, kv, kv_sem)
    late = [
        pltpu.make_async_copy(src, dst, late_sem.at[n])
        for n, (src, dst) in enumerate(
            (
                (att_in, att), (qcat_in, qcat), (keys_in, keys), (bias_in, bias), (lse_in, lse), (cos_in, cos),
                (sin_in, sin), (normed_in, normed), (lat_raw_in, lat_raw), (tok_in, tok),
            )
        )
    ]
    loads[2].start()
    kv_load.start()
    for c in late:
        c.start()
    for n in (1, 3, 4, 5, 6, 0):
        loads[n].start()
    bar = pltpu.get_barrier_semaphore()
    pl.semaphore_wait(bar, neighbours(me, core, bar))
    lane = lax.broadcasted_iota(jnp.int32, (256, 128), 1)

    logits = jnp.where(lane < 16, mm(moe_low[...], wr[...]), -jnp.inf)
    e = jnp.exp(logits - jnp.max(logits, axis=1, keepdims=True))
    router = e / jnp.sum(e, axis=1, keepdims=True)
    d_router = jnp.where(lane < 16, home[:, width:].astype(jnp.float32), 0.0)
    d_logits = (router * (d_router - jnp.sum(router * d_router, axis=1, keepdims=True))).astype(jnp.bfloat16)

    def norm_back(v, gain, dy):
        r = root(v)
        hat = v * r
        up = dy * gain
        return r * (up - hat * jnp.mean(up * hat, axis=1, keepdims=True)), dy * hat

    def one_lane(n):
        return (lane == n).astype(jnp.bfloat16)

    d_moe = home[:, :width].astype(jnp.float32) + nt(d_logits, wr[...])
    d_norm2, gain_rows = norm_back(middle[...], g_moe[...], d_moe)
    d_middle = grad[...].astype(jnp.float32) + d_norm2
    dmid[...] = d_middle
    dmid_low[...] = d_middle.astype(jnp.bfloat16)
    gains = gain_rows.astype(jnp.bfloat16)
    moved = pltpu.roll(d_logits.astype(jnp.float32), 64, 1).astype(jnp.bfloat16)
    small = tn(moe_low[...], moved) + tn(gains, one_lane(81))

    loads[2].wait()
    for c in late:
        c.wait()
    d_att[...] = mm(dmid_low[...], wo[...]).astype(jnp.bfloat16)

    def wo_rows(n, _):
        r = pl.ds(pl.multiple_of(n * 256, 256), 256)
        wo[r] = tn(dmid_low[:, r], att[...]).astype(jnp.bfloat16)
        return 0

    lax.fori_loop(0, width // 256, wo_rows, 0)
    stores[2].start()
    kv_load.wait()
    dkr[...] = jnp.zeros_like(dkr)
    dqr[...] = jnp.zeros_like(dqr)

    def head(h, _):
        cols = pl.ds(pl.multiple_of(h * 128, 128), 128)
        nope_at = pl.ds(pl.multiple_of(h * 256, 256), 128)
        value_at = pl.ds(pl.multiple_of(h * 256 + 128, 128), 128)
        pair = pl.ds(pl.multiple_of(h // 2 * 128, 128), 128)
        kc = jnp.concatenate([kv[:, nope_at], keys[:, :, RANK:].reshape(KEYS, 128)], 1)
        p = jnp.exp(nt(qcat[h], kc) * scale + bias[...] - lse[h])
        dv = tn(p.astype(jnp.bfloat16), d_att[:, cols])
        dp = nt(d_att[:, cols], kv[:, value_at])
        ds = (p * (dp - jnp.sum(p * dp, axis=1, keepdims=True))).astype(jnp.bfloat16)
        dqc = mm(ds, kc) * scale
        dkc = tn(ds, qcat[h]) * scale
        dq[:, cols] = dqc[:, :128].astype(jnp.bfloat16)
        dqr[:, pair] += jnp.where((lane < 64) == (h % 2 == 0), dqc[:, 128:], 0.0)
        kv[:, nope_at] = dkc[:, :128].astype(jnp.bfloat16)
        kv[:, value_at] = dv.astype(jnp.bfloat16)
        dkr[...] += dkc[:, 128:]
        return 0

    lax.fori_loop(0, 8, head, 0)
    for n in (3, 4, 5, 6):
        loads[n].wait()

    mine = pl.ds(pl.multiple_of(core * 128, 128), 128)
    others = pl.ds(pl.multiple_of((1 - core) * 128, 128), 128)

    def send(d, to):
        return pltpu.make_async_remote_copy(
            src_ref=dk_out.at[d - 1, mine], dst_ref=dk_in.at[d - 1], send_sem=ks.at[d - 1], recv_sem=kr.at[d - 1],
            device_id=(jnp.clip(to, 0, 15), core), device_id_type=MESH,
        )

    pair = pltpu.make_async_remote_copy(
        src_ref=dk_out.at[:, others], dst_ref=dk_pair, send_sem=ps, recv_sem=pr, device_id=(me, 1 - core), device_id_type=MESH
    )
    for s in range(SLOTS):
        r = slice(s * 256, (s + 1) * 256)
        d = SLOTS - 1 - s if s < SLOTS - 1 else SLOTS
        dk_out[d - 1, :, :RANK] = nt(kv[r], wkv[...].reshape(RANK, 2048)).astype(jnp.bfloat16)
        dk_out[d - 1, :, RANK:] = (dkr[r] + pltpu.roll(dkr[r], 64, 1)).astype(jnp.bfloat16)
    pair.start()
    dq[:, 1024:] = turned(dqr[...], cos[...], -sin[...]).astype(jnp.bfloat16)
    loads[1].wait()

    def normed_cols(n, _):
        r = pl.ds(pl.multiple_of(n * 512, 512), 512)
        v = nt(dq[...], wq[r])
        part[:, r] = v.astype(jnp.bfloat16)
        wq[r] = tn(normed[:, r], dq[...]).astype(jnp.bfloat16)
        return 0

    normed_cols(0, 0)
    pair.wait_recv()
    for d in range(1, SLOTS):
        dk_out[d - 1, mine] = dk_out[d - 1, mine] + dk_pair[d - 1]
        pl.when(me >= d)(lambda d=d: send(d, me - d).start())
    own_dk[...] = dk_out[SLOTS - 1, mine].astype(jnp.float32) + dk_pair[SLOTS - 1].astype(jnp.float32)
    lax.fori_loop(1, 4, normed_cols, 0)
    swap = pltpu.make_async_remote_copy(
        src_ref=part, dst_ref=arrived, send_sem=cs, recv_sem=cr, device_id=(me, 1 - core), device_id_type=MESH
    )
    swap.start()
    stores[1].start()
    latent_all = keys[:, :, :RANK].reshape(KEYS, RANK)
    for c in range(4):
        g = tn(latent_all, kv[:, c * 512 : (c + 1) * 512]).astype(jnp.bfloat16)
        wkv[:, :, c * 512 : (c + 1) * 512] = g.reshape(16, 32, 512)
        stores[3 + c].start()
    for d in range(1, SLOTS):

        @pl.when(me + d < 16)
        def _():
            send(d, me + d).wait_recv()
            own_dk[...] += dk_in[d - 1].astype(jnp.float32)

    d_keys[mine] = own_dk[...].astype(jnp.bfloat16)

    def half(rows):
        return pltpu.make_async_remote_copy(
            src_ref=d_keys.at[rows], dst_ref=d_keys.at[rows], send_sem=hs, recv_sem=hr,
            device_id=(me, 1 - core), device_id_type=MESH,
        )

    half(mine).start()
    swap.wait_recv()
    dnorm[...] = part[...].astype(jnp.float32) + arrived[...].astype(jnp.float32)
    half(others).wait_recv()

    d_first, lat_gain_rows = norm_back(lat_raw[:, :RANK], g_lat[...], d_keys[:, :RANK].astype(jnp.float32))
    d_second = turned(d_keys[:, RANK:].astype(jnp.float32), cos[:, :128], -sin[:, :128])
    d_second = jnp.where(lane < 64, d_second, 0.0)
    d_lat_low = jnp.concatenate([d_first, d_second], 1).astype(jnp.bfloat16)
    loads[0].wait()
    d_normed = dnorm[...] + nt(d_lat_low, wlat[...])
    d_norm1, att_gain_rows = norm_back(tok[...].astype(jnp.float32), g_att[...], d_normed)
    tok_grad[...] = dmid[...] + d_norm1
    small = small + tn(normed[...], d_lat_low[:, RANK:]) + tn(att_gain_rows.astype(jnp.bfloat16), one_lane(80))
    wlat[:, :RANK] = tn(normed[...], d_lat_low[:, :RANK]).astype(jnp.bfloat16)
    wlat[:, RANK:] = small.astype(jnp.bfloat16)
    lat_col = tn(lat_gain_rows.astype(jnp.bfloat16), one_lane(82))
    for b in range(16):
        r = slice(b * 128, b * 128 + 32)
        wlat[r, RANK:] = (small[r] + lat_col[b * 32 : (b + 1) * 32]).astype(jnp.bfloat16)
    stores[0].start()
    for c in stores:
        c.wait()
    for d in range(1, SLOTS):
        pl.when(me >= d)(lambda d=d: send(d, me - d).wait_send())
    pair.wait_send()
    swap.wait_send()
    half(mine).wait_send()


def att_bwd(weights, home, grad, middle, moe_low, tok, normed, lat_raw, qcat, keys, kv, lse, att, wr, g_att, g_moe, g_lat, cos, sin, bias, cid):
    low, f32, S, V = jnp.bfloat16, jnp.float32, pltpu.SemaphoreType.DMA, pltpu.VMEM
    any_, vmem = pl.BlockSpec(memory_space=pl.ANY), pl.BlockSpec(memory_space=pltpu.VMEM)
    shape = lambda kind, *s: jax.ShapeDtypeStruct(s, kind)
    rows, width = tok.shape
    pack = weights.shape[1]
    return pl.pallas_call(
        att_bwd_kernel,
        out_shape=[shape(f32, rows, width), shape(low, width, pack - 512), shape(low, 16, 4, 32, 512)],
        in_specs=[any_, any_] + [vmem] * 8 + [any_] * 11,
        out_specs=[vmem, any_, any_],
        scratch_shapes=[
            V((rows, width), low), V((rows, width), low), V((rows, 640), f32), V((8, rows, 256), low), V((SLOTS, rows, 640), low),
            V((8, rows, 1), f32), V((rows, 1024), low), V((rows, 512), f32), V((rows, 512), f32), V((rows, KEYS), f32),
            V((KEYS, 2048), low), V((width, 1536), low), V((width, 1024), low), V((16, 32, 2048), low),
            V((width, 640), low), V((rows, width), f32), V((rows, width), f32), V((rows, width), low), V((rows, 1024), low),
            V((rows, 1536), low), V((rows, 512), f32), V((KEYS, 128), f32), V((SLOTS, rows, 640), low), V((SLOTS, rows // 2, 640), low),
            V((4, rows // 2, 640), low), V((rows // 2, 640), f32), V((rows, width), low), V((rows, width), low), V((rows, 640), low),
            S((10,)), S((7,)), S, S((4,)), S((4,)), S, S, S, S, S, S, S((7,)),
        ],
        compiler_params=pltpu.CompilerParams(collective_id=cid, has_side_effects=True, vmem_limit_bytes=60 << 20),
        cost_estimate=pl.CostEstimate(flops=25 * 10**9, bytes_accessed=70 * 10**6, transcendentals=0),
    )(
        weights.reshape(16, 4, 32, pack), weights, home, grad, middle, moe_low, wr, g_att, g_moe, g_lat, kv,
        tok, normed, lat_raw, qcat, keys, lse, att, cos, sin, bias,
    )


def swapped(v):
    return lax.ppermute(v, "tensor", [(0, 1), (1, 0)])


def my_half(v, rows):
    return lax.dynamic_slice_in_dim(v, lax.axis_index("tensor") * rows, rows, 0)


def row_halves(v):
    rows = v.shape[0] // 2
    return my_half(v, rows).reshape(2, rows // 2, v.shape[1])


def exchange(parts):
    return lax.all_to_all(parts, "dp", split_axis=0, concat_axis=0, tiled=True)


def nope_first(w):
    heads = w.reshape(w.shape[0], -1, NOPE + ROPE)
    return jnp.concatenate(
        [heads[:, :, :NOPE].reshape(w.shape[0], -1), heads[:, :, NOPE:].reshape(w.shape[0], -1)], 1
    )


def heads_first(w):
    heads = w.shape[1] // (NOPE + ROPE)
    nope = w[:, : heads * NOPE].reshape(w.shape[0], heads, NOPE)
    rope = w[:, heads * NOPE :].reshape(w.shape[0], heads, ROPE)
    return jnp.concatenate([nope, rope], 2).reshape(w.shape[0], -1)


def shards_sixteen(
    tokens,
    out_grad,
    segments,
    routes,
    attn_gain,
    w_query,
    w_latent,
    latent_gain,
    w_keyval,
    w_out,
    moe_gain,
    w_router,
    shared_gate,
    shared_up,
    shared_down,
    expert_gate,
    routed_up_weight,
    expert_down,
):
    n_rows, width = tokens.shape
    dp_count = lax.axis_size("dp")
    dp_index = lax.axis_index("dp")
    seq_len = segments.shape[1]
    total = n_rows * dp_count
    hop_count = (WINDOW - 1) // n_rows + 1
    n_keys = (hop_count + 1) * n_rows
    experts = w_router.shape[1]
    capacity = 4 * n_rows * TOPK // (3 * experts)
    row_start = dp_index * n_rows
    seg_row = segments[0]
    depth = w_query.shape[0]
    q_width, o_width, kv_width = w_query.shape[1], w_out.shape[0], w_keyval.shape[1]
    kv_rows = w_keyval.shape[0]
    kv_cuts = depth // kv_rows
    kv_part = kv_width // kv_cuts
    lat_width = w_latent.shape[1]
    route_width = n_rows * TOPK // depth
    small = (lat_width + experts + 3 + route_width + 127) // 128 * 128

    gains = jnp.stack(
        [attn_gain, moe_gain, jnp.pad(latent_gain, (0, depth - kv_rows))], 1
    )
    packed = jnp.concatenate(
        [
            nope_first(w_query),
            w_out.T,
            w_latent,
            w_router,
            gains,
            routes.reshape(depth, route_width).astype(jnp.bfloat16),
            jnp.zeros((depth, small - lat_width - experts - 3 - route_width), jnp.bfloat16),
            w_keyval.reshape(kv_rows, kv_cuts, kv_part).transpose(1, 0, 2).reshape(depth, kv_part),
        ],
        1,
    )
    pack_width = packed.shape[1]
    weights, grad_all = ag16(
        [packed.reshape(2, depth // 2, pack_width), row_halves(out_grad)], (False, True), 1
    )
    weights = weights.reshape(width, pack_width)
    shared_part = shared_gate.shape[1] // dp_count
    shared_send = jnp.stack(
        [
            shared_gate.reshape(depth, dp_count, shared_part).transpose(1, 2, 0),
            shared_up.reshape(depth, dp_count, shared_part).transpose(1, 2, 0),
            shared_down.reshape(dp_count, shared_part, depth),
        ],
        1,
    )
    shared_send, weights = lax.optimization_barrier((shared_send, weights))
    shared_all = exchange(shared_send).transpose(1, 2, 0, 3).reshape(3, shared_part, width)
    lead = jnp.pad(shared_all, ((0, 0), (0, 128 - shared_part), (0, 0)))
    shared_in, shared_out = lead[:2].reshape(256, width), lead[2]

    at = q_width + o_width + lat_width
    wr_full = weights[:, at : at + experts]
    at += experts
    gain_attn = weights[:, at].astype(jnp.float32)
    gain_moe = weights[:, at + 1].astype(jnp.float32)
    gain_latent = (
        weights[:, at + 2].reshape(dp_count, depth)[:, :kv_rows].reshape(-1).astype(jnp.float32)
    )

    all_routes = (
        weights[:, at + 3 : at + 3 + route_width].reshape(total, TOPK).astype(jnp.int32)
    )

    local_heads = q_width // (NOPE + ROPE)
    positions = (row_start + jnp.arange(n_rows, dtype=jnp.int32)).astype(jnp.float32)
    cos_tab, sin_tab = rope_tables(positions)
    cos_lanes, sin_lanes = jnp.tile(cos_tab, (1, 2 * local_heads)), jnp.tile(sin_tab, (1, 2 * local_heads))
    key_pos = row_start - hop_count * n_rows + jnp.arange(n_keys, dtype=jnp.int32)
    query_pos = row_start + jnp.arange(n_rows, dtype=jnp.int32)
    padded_seg = jnp.concatenate([jnp.full((hop_count * n_rows,), -1, jnp.int32), seg_row])
    key_seg = lax.dynamic_slice_in_dim(padded_seg, row_start, n_keys, 0)
    query_seg = lax.dynamic_slice_in_dim(seg_row, row_start, n_rows, 0)
    allowed = (key_pos[None, :] >= 0) & (key_pos[None, :] <= query_pos[:, None])
    allowed = (
        allowed
        & (query_pos[:, None] - key_pos[None, :] < WINDOW)
        & (query_seg[:, None] == key_seg[None, :])
    )

    bias = jnp.where(allowed, 0.0, -jnp.inf)
    middle, moe_low, normed_low, lat_raw, qcat, keys, kv, lse, attended_low = att_fwd(
        tokens, weights, gain_attn[None], gain_moe[None], gain_latent[None], cos_lanes, sin_lanes, bias, 7
    )
    moe_low, shared_in, shared_out = lax.optimization_barrier((moe_low, shared_in, shared_out))
    (moe_all,) = ag16([row_halves(moe_low)], (True,), 3)
    chosen = jnp.any(all_routes == dp_index, axis=1).reshape(dp_count, n_rows)
    earlier = jnp.arange(n_rows)[:, None] < jnp.arange(n_rows)[None, :]
    rank = matmul(chosen.astype(jnp.bfloat16), earlier.astype(jnp.bfloat16)).astype(jnp.int32)
    pick = (
        (rank[:, None, :] == jnp.arange(capacity, dtype=jnp.int32)[None, :, None])
        & chosen[:, None, :]
    ).astype(jnp.bfloat16)

    slot_rows = dp_count * capacity
    moe_wr = jnp.pad(wr_full, ((0, 0), (0, 128 - experts)))
    home, rows_in, rows_grad, scaled_act, d_ea_low, d_eb_low, shared_grads = moe_call(
        moe_all.reshape(dp_count, n_rows, width),
        grad_all.reshape(dp_count, n_rows, width),
        pick,
        pick.transpose(0, 2, 1),
        expert_gate[0].T,
        routed_up_weight[0].T,
        expert_down[0],
        moe_wr,
        shared_in,
        shared_out,
        4,
    )[:7]
    home = home.reshape(n_rows, 2 * width + 128)
    result = (middle + home[:, :width].astype(jnp.float32)).astype(jnp.bfloat16)
    grad_down = matmul_tn(scaled_act, rows_grad)[None]
    grad_gate = matmul_tn(rows_in, d_ea_low)[None]
    grad_up = matmul_tn(rows_in, d_eb_low)[None]
    shared_home = exchange(
        shared_grads.astype(jnp.bfloat16)
        .reshape(3, 128, dp_count, depth)[:, :shared_part]
        .transpose(2, 0, 1, 3)
    ).astype(jnp.float32)
    shared_home = shared_home.transpose(1, 0, 2, 3).reshape(3, dp_count * shared_part, depth)

    token_input_gradient, packed_grads, kv_grads = att_bwd(
        weights, home[:, width:], out_grad, middle, moe_low, tokens, normed_low, lat_raw, qcat, keys, kv, lse,
        attended_low, moe_wr, gain_attn[None], gain_moe[None], gain_latent[None], cos_lanes, sin_lanes, bias, 8
    )
    packed_grads, shared_home = lax.optimization_barrier((packed_grads, shared_home))
    mine = rs16(
        packed_grads.reshape(dp_count, 2, depth // 2, pack_width - kv_part),
        kv_grads.reshape(dp_count, 2, depth // 2, kv_part),
        6,
    ).reshape(depth, pack_width)
    grad_sgate, grad_sup, grad_sdown = shared_home[0].T, shared_home[1].T, shared_home[2]
    out_wq = heads_first(mine[:, :q_width])
    at = q_width
    out_wo = mine[:, at : at + o_width].T
    at += o_width
    out_wlat = mine[:, at : at + lat_width]
    at += lat_width
    out_router = mine[:, at : at + experts]
    at += experts
    out_wkv = (
        mine[:, pack_width - kv_part :]
        .reshape(kv_cuts, kv_rows, kv_part)
        .transpose(1, 0, 2)
        .reshape(kv_rows, kv_width)
    )
    return (
        result,
        token_input_gradient,
        mine[:, at],
        out_wq,
        out_wlat,
        mine[:kv_rows, at + 2],
        out_wkv,
        out_wo,
        mine[:, at + 1],
        out_router,
        grad_sgate,
        grad_sup,
        grad_sdown,
        grad_gate,
        grad_up,
        grad_down,
    )


def shards_general(
    tokens,
    out_grad,
    segments,
    routes,
    attn_gain,
    w_query,
    w_latent,
    latent_gain,
    w_keyval,
    w_out,
    moe_gain,
    w_router,
    shared_gate,
    shared_up,
    shared_down,
    expert_gate,
    routed_up_weight,
    expert_down,
):
    n_rows = tokens.shape[0]
    model_width = tokens.shape[1]
    dp_count = lax.axis_size("dp")
    dp_index = lax.axis_index("dp")
    seq_len = segments.shape[1]
    seq_devs = seq_len // n_rows
    hop_count = (WINDOW - 1) // n_rows + 1
    n_keys = (hop_count + 1) * n_rows
    experts = w_router.shape[1]
    local_experts = expert_gate.shape[0]
    capacity = 4 * n_rows * TOPK // (3 * experts)
    slot_total = experts * capacity
    score_scale = (NOPE + ROPE) ** (-0.5)
    row_start = dp_index % seq_devs * n_rows
    seg_row = lax.dynamic_index_in_dim(segments, dp_index // seq_devs, 0, keepdims=False)
    gathered = (
        lax.all_gather(attn_gain, "dp", axis=0, tiled=True),
        lax.all_gather(w_query, "dp", axis=0, tiled=True),
        lax.all_gather(w_latent, "dp", axis=0, tiled=True),
        lax.all_gather(latent_gain, "dp", axis=0, tiled=True),
        lax.all_gather(w_keyval, "dp", axis=0, tiled=True),
        lax.all_gather(w_out, "dp", axis=1, tiled=True),
        lax.all_gather(moe_gain, "dp", axis=0, tiled=True),
        lax.all_gather(w_router, "dp", axis=0, tiled=True),
        lax.all_gather(shared_gate, "dp", axis=0, tiled=True),
        lax.all_gather(shared_up, "dp", axis=0, tiled=True),
        lax.all_gather(shared_down, "dp", axis=1, tiled=True),
    )
    (
        gain_attn,
        wq_full,
        wlat_full,
        gain_latent,
        wkv_full,
        wo_full,
        gain_moe,
        wr_full,
        sgate_full,
        sup_full,
        sdown_full,
    ) = gathered
    local_heads = wq_full.shape[1] // (NOPE + ROPE)
    positions = (row_start + jnp.arange(n_rows, dtype=jnp.int32)).astype(jnp.float32)
    cos_tab, sin_tab = rope_tables(positions)
    resid_in = tokens.astype(jnp.float32)
    normed, attn_norm_back = jax.vjp(rms_scale, resid_in, gain_attn.astype(jnp.float32))
    normed_low = normed.astype(jnp.bfloat16)

    def rope_queries(q_flat):
        shaped = q_flat.reshape(n_rows, local_heads, NOPE + ROPE)
        return jnp.concatenate(
            [shaped[..., :NOPE], rotate(shaped[..., NOPE:], cos_tab[:, None], sin_tab[:, None])], -1
        )

    queries, query_back = jax.vjp(rope_queries, matmul(normed_low, wq_full))
    query_low = queries.astype(jnp.bfloat16)

    def latent_piece(latent_raw, gain_vec):
        return (
            rms_scale(latent_raw[:, :RANK], gain_vec),
            rotate(latent_raw[:, RANK:], cos_tab, sin_tab),
        )

    (latent, key_rope), latent_back = jax.vjp(
        latent_piece, matmul(normed_low, wlat_full), gain_latent.astype(jnp.float32)
    )
    latent_low = latent.astype(jnp.bfloat16)
    rope_low = key_rope.astype(jnp.bfloat16)
    latent_parts = []
    rope_parts = []
    for distance in range(hop_count, 0, -1):
        moved_latent, moved_rope = passed_along((latent_low, rope_low), "dp", distance)
        latent_parts.append(moved_latent)
        rope_parts.append(moved_rope)
    keys_latent = jnp.concatenate(latent_parts + [latent_low], 0)
    keys_rope = jnp.concatenate(rope_parts + [rope_low], 0)
    keyval = (
        matmul(keys_latent, wkv_full).astype(jnp.bfloat16).reshape(n_keys, local_heads, NOPE + VDIM)
    )
    key_nope = keyval[..., :NOPE]
    values = keyval[..., NOPE:]
    key_pos = row_start - hop_count * n_rows + jnp.arange(n_keys, dtype=jnp.int32)
    query_pos = row_start + jnp.arange(n_rows, dtype=jnp.int32)
    padded_seg = jnp.concatenate([jnp.full((hop_count * n_rows,), -1, jnp.int32), seg_row])
    key_seg = lax.dynamic_slice_in_dim(padded_seg, row_start, n_keys, 0)
    query_seg = lax.dynamic_slice_in_dim(seg_row, row_start, n_rows, 0)
    allowed = (key_pos[None, :] >= 0) & (key_pos[None, :] <= query_pos[:, None])
    allowed = (
        allowed
        & (query_pos[:, None] - key_pos[None, :] < WINDOW)
        & (query_seg[:, None] == key_seg[None, :])
    )

    def masked_scores():
        nope_part = jnp.einsum(
            "qhd,khd->hqk", query_low[..., :NOPE], key_nope, preferred_element_type=jnp.float32
        )
        rope_part = jnp.einsum(
            "qhr,kr->hqk", query_low[..., NOPE:], keys_rope, preferred_element_type=jnp.float32
        )
        return jnp.where(allowed[None], score_scale * (nope_part + rope_part), -jnp.inf)

    scores = masked_scores()
    top_score = jnp.max(scores, axis=-1, keepdims=True)
    exp_scores = jnp.exp(scores - top_score)
    denom = jnp.sum(exp_scores, axis=-1, keepdims=True)
    attn_probs = exp_scores / denom
    log_total = top_score + jnp.log(denom)
    attended = jnp.einsum(
        "hqk,khv->qhv", attn_probs.astype(jnp.bfloat16), values, preferred_element_type=jnp.float32
    )
    attended_low = attended.astype(jnp.bfloat16).reshape(n_rows, local_heads * VDIM)
    attn_out = lax.psum(matmul(attended_low, wo_full).astype(jnp.bfloat16), "tensor").astype(
        jnp.float32
    )
    middle = resid_in + attn_out
    moe_normed, moe_norm_back = jax.vjp(rms_scale, middle, gain_moe.astype(jnp.float32))
    moe_low = moe_normed.astype(jnp.bfloat16)
    router, router_back = jax.vjp(
        lambda logit_vals: jax.nn.softmax(logit_vals, axis=-1), matmul(moe_low, wr_full)
    )
    expert_ids = jnp.arange(experts, dtype=jnp.int32)
    route_hot = (routes[:, :, None] == expert_ids[None, None, :]).astype(jnp.float32)
    gate_w = jnp.einsum("te,tke->tk", router, route_hot, precision=highest)
    flat_routes = routes.reshape(-1)
    assign_count = flat_routes.shape[0]
    flat_hot = (flat_routes[:, None] == expert_ids[None, :]).astype(jnp.int32)
    earlier = ranks_before(flat_hot)
    slot_in = jnp.sum(earlier * flat_hot, axis=1)
    target = flat_routes * capacity + slot_in
    assign_ids = jnp.arange(assign_count, dtype=jnp.int32)
    assign_of_slot = jnp.zeros((slot_total,), jnp.int32).at[target].set(assign_ids)
    slot_live = (
        jnp.zeros((slot_total,), jnp.bfloat16)
        .at[target]
        .set(jnp.ones((assign_count,), jnp.bfloat16))
    )
    send_rows = moe_low[assign_of_slot // TOPK] * slot_live[:, None]
    recv_rows = lax.all_to_all(
        send_rows.reshape(dp_count, local_experts * capacity, model_width),
        "dp",
        split_axis=0,
        concat_axis=0,
        tiled=True,
    )
    received_four_parts = recv_rows.reshape(dp_count, local_experts, capacity, model_width)
    exp_gate = jnp.einsum(
        "sjcd,jdf->sjcf", received_four_parts, expert_gate, preferred_element_type=jnp.float32
    )
    exp_up = jnp.einsum(
        "sjcd,jdf->sjcf", received_four_parts, routed_up_weight, preferred_element_type=jnp.float32
    )
    exp_act, exp_act_back = jax.vjp(gated_act, exp_gate, exp_up)
    exp_act_low = exp_act.astype(jnp.bfloat16)
    exp_result = jnp.einsum(
        "sjcf,jfd->sjcd", exp_act_low, expert_down, preferred_element_type=jnp.float32
    )
    returned = lax.all_to_all(
        exp_result.reshape(dp_count, local_experts * capacity, model_width).astype(jnp.bfloat16),
        "dp",
        split_axis=0,
        concat_axis=0,
        tiled=True,
    ).astype(jnp.float32)
    per_assign = returned.reshape(slot_total, model_width)[target].reshape(
        n_rows, TOPK, model_width
    )
    routed = jnp.einsum("tk,tkd->td", gate_w, per_assign, precision=highest)
    shared_a = matmul(moe_low, sgate_full)
    shared_b = matmul(moe_low, sup_full)
    shared_act, shared_back = jax.vjp(gated_act, shared_a, shared_b)
    shared_low = shared_act.astype(jnp.bfloat16)
    moe_out = lax.psum(
        (routed + matmul(shared_low, sdown_full)).astype(jnp.bfloat16), "tensor"
    ).astype(jnp.float32)
    result = (middle + moe_out).astype(jnp.bfloat16)
    grad_y = out_grad.astype(jnp.float32)
    grad_sdown = matmul_tn(shared_low, out_grad)
    d_shared_a, d_shared_b = shared_back(matmul_nt(out_grad, sdown_full))
    d_sa_low = d_shared_a.astype(jnp.bfloat16)
    d_sb_low = d_shared_b.astype(jnp.bfloat16)
    grad_sgate = matmul_tn(moe_low, d_sa_low)
    grad_sup = matmul_tn(moe_low, d_sb_low)
    d_moe = matmul_nt(d_sa_low, sgate_full) + matmul_nt(d_sb_low, sup_full)
    d_gate_part = jnp.einsum("td,tkd->tk", grad_y, per_assign, precision=highest)
    d_assign = (
        (gate_w[:, :, None] * grad_y[:, None, :])
        .astype(jnp.bfloat16)
        .reshape(assign_count, model_width)
    )
    send_grads = d_assign[assign_of_slot] * slot_live[:, None]
    recv_grads = lax.all_to_all(
        send_grads.reshape(dp_count, local_experts * capacity, model_width),
        "dp",
        split_axis=0,
        concat_axis=0,
        tiled=True,
    )
    recv_grads = recv_grads.reshape(dp_count, local_experts, capacity, model_width)
    expert_down_weight_gradient = jnp.einsum(
        "sjcf,sjcd->jfd", exp_act_low, recv_grads, preferred_element_type=jnp.float32
    )
    d_exp_act = jnp.einsum(
        "sjcd,jfd->sjcf", recv_grads, expert_down, preferred_element_type=jnp.float32
    )
    d_exp_gate, expert_up_act_gradient = exp_act_back(d_exp_act)
    d_egate_low = d_exp_gate.astype(jnp.bfloat16)
    expert_up_gradient_lowp = expert_up_act_gradient.astype(jnp.bfloat16)
    expert_gate_weight_gradient = jnp.einsum(
        "bmky,bmkx->myx", received_four_parts, d_egate_low, preferred_element_type=jnp.float32
    )
    expert_up_weight_gradient = jnp.einsum(
        "bmky,bmkx->myx",
        received_four_parts,
        expert_up_gradient_lowp,
        preferred_element_type=jnp.float32,
    )
    d_slots = jnp.einsum(
        "hteg,tmg->htem", d_egate_low, expert_gate, preferred_element_type=jnp.float32
    )
    d_slots = d_slots + jnp.einsum(
        "hteg,tmg->htem",
        expert_up_gradient_lowp,
        routed_up_weight,
        preferred_element_type=jnp.float32,
    )
    back_grads = lax.all_to_all(
        d_slots.reshape(dp_count, local_experts * capacity, model_width).astype(jnp.bfloat16),
        "dp",
        split_axis=0,
        concat_axis=0,
        tiled=True,
    ).astype(jnp.float32)
    d_moe = d_moe + jnp.sum(
        back_grads.reshape(slot_total, model_width)[target].reshape(n_rows, TOPK, model_width),
        axis=1,
    )
    d_moe, d_gate = (
        lax.psum(d_moe.astype(jnp.bfloat16), "tensor").astype(jnp.float32),
        lax.psum(d_gate_part.astype(jnp.bfloat16), "tensor").astype(jnp.float32),
    )
    d_router = jnp.einsum("tk,tke->te", d_gate, route_hot, precision=highest)
    (d_logits,) = router_back(d_router)
    d_logits_low = d_logits.astype(jnp.bfloat16)
    grad_router = matmul_tn(moe_low, d_logits_low)
    d_moe = d_moe + matmul_nt(d_logits_low, wr_full)
    d_mid_norm, grad_gain_moe = moe_norm_back(d_moe)
    d_middle = grad_y + d_mid_norm
    d_middle_low = d_middle.astype(jnp.bfloat16)
    grad_wout = matmul_tn(attended_low, d_middle_low)
    d_att_low = (
        matmul_nt(d_middle_low, wo_full).astype(jnp.bfloat16).reshape(n_rows, local_heads, VDIM)
    )
    again_probs = jnp.exp(masked_scores() - log_total)
    d_values = jnp.einsum(
        "hqk,qhv->khv",
        again_probs.astype(jnp.bfloat16),
        d_att_low,
        preferred_element_type=jnp.float32,
    )
    d_probs = jnp.einsum("qhv,khv->hqk", d_att_low, values, preferred_element_type=jnp.float32)
    d_scores = (
        again_probs * (d_probs - jnp.sum(d_probs * again_probs, axis=-1, keepdims=True))
    ).astype(jnp.bfloat16)
    d_query_nope = score_scale * jnp.einsum(
        "hqk,khd->qhd", d_scores, key_nope, preferred_element_type=jnp.float32
    )
    d_query_rope = score_scale * jnp.einsum(
        "hqk,kr->qhr", d_scores, keys_rope, preferred_element_type=jnp.float32
    )
    d_key_nope = score_scale * jnp.einsum(
        "hqk,qhd->khd", d_scores, query_low[..., :NOPE], preferred_element_type=jnp.float32
    )
    d_key_rope = score_scale * jnp.einsum(
        "hqk,qhr->kr", d_scores, query_low[..., NOPE:], preferred_element_type=jnp.float32
    )
    (d_q_raw,) = query_back(jnp.concatenate([d_query_nope, d_query_rope], -1))
    d_q_low = d_q_raw.astype(jnp.bfloat16)
    grad_wq = matmul_tn(normed_low, d_q_low)
    d_normed = matmul_nt(d_q_low, wq_full)
    d_kv_low = (
        jnp.concatenate([d_key_nope, d_values], -1)
        .astype(jnp.bfloat16)
        .reshape(n_keys, local_heads * (NOPE + VDIM))
    )
    grad_wkv = matmul_tn(keys_latent, d_kv_low)
    d_keys_latent = matmul_nt(d_kv_low, wkv_full)
    own_latent = d_keys_latent[hop_count * n_rows :]
    own_rope = d_key_rope[hop_count * n_rows :]
    for distance in range(hop_count, 0, -1):
        block_index = hop_count - distance
        lower = block_index * n_rows
        home_latent, home_rope = (
            passed_along(
                d_keys_latent[lower : lower + n_rows].astype(jnp.bfloat16), "dp", -distance
            ).astype(jnp.float32),
            passed_along(
                d_key_rope[lower : lower + n_rows].astype(jnp.bfloat16), "dp", -distance
            ).astype(jnp.float32),
        )
        own_latent = own_latent + home_latent
        own_rope = own_rope + home_rope
    d_normed, own_latent, own_rope = (
        lax.psum(d_normed.astype(jnp.bfloat16), "tensor").astype(jnp.float32),
        lax.psum(own_latent.astype(jnp.bfloat16), "tensor").astype(jnp.float32),
        lax.psum(own_rope.astype(jnp.bfloat16), "tensor").astype(jnp.float32),
    )
    d_latent_raw, grad_gain_latent = latent_back((own_latent, own_rope))
    d_latent_low = d_latent_raw.astype(jnp.bfloat16)
    grad_wlat = matmul_tn(normed_low, d_latent_low)
    d_normed = d_normed + matmul_nt(d_latent_low, wlat_full)
    d_tokens_norm, grad_gain_attn = attn_norm_back(d_normed)
    token_input_gradient = d_middle + d_tokens_norm
    reduced_result = tuple(
        (
            lax.psum_scatter(grad_gain_attn, "dp", scatter_dimension=0, tiled=True),
            lax.psum_scatter(grad_wq, "dp", scatter_dimension=0, tiled=True),
            lax.psum_scatter(grad_wlat, "dp", scatter_dimension=0, tiled=True),
            lax.psum_scatter(grad_gain_latent, "dp", scatter_dimension=0, tiled=True),
            lax.psum_scatter(grad_wkv, "dp", scatter_dimension=0, tiled=True),
            lax.psum_scatter(grad_wout, "dp", scatter_dimension=1, tiled=True),
            lax.psum_scatter(grad_gain_moe, "dp", scatter_dimension=0, tiled=True),
            lax.psum_scatter(grad_router, "dp", scatter_dimension=0, tiled=True),
            lax.psum_scatter(grad_sgate, "dp", scatter_dimension=0, tiled=True),
            lax.psum_scatter(grad_sup, "dp", scatter_dimension=0, tiled=True),
            lax.psum_scatter(grad_sdown, "dp", scatter_dimension=1, tiled=True),
        )
    )
    return (
        (result, token_input_gradient)
        + reduced_result
        + (expert_gate_weight_gradient, expert_up_weight_gradient, expert_down_weight_gradient)
    )


def solution(mesh):
    placed = (
        P("dp", None),
        P("dp", None),
        P(),
        P("dp", None),
        P("dp"),
        P("dp", "tensor"),
        P("dp", None),
        P("dp"),
        P("dp", "tensor"),
        P("tensor", "dp"),
        P("dp"),
        P("dp", None),
        P("dp", "tensor"),
        P("dp", "tensor"),
        P("tensor", "dp"),
        P("dp", None, "tensor"),
        P("dp", None, "tensor"),
        P("dp", "tensor", None),
    )
    sixteen = mesh.shape["dp"] == 16 and mesh.shape["tensor"] == 2

    def body(*args):
        fits_sixteen = sixteen and args[2].shape[0] == 1 and args[15].shape[0] == 1 and args[0].shape[0] == 256
        return (shards_sixteen if fits_sixteen else shards_general)(*args)

    return jax.shard_map(
        body,
        mesh=mesh,
        in_specs=placed,
        out_specs=(
            P("dp", None),
            P("dp", None),
            P("dp"),
            P("dp", "tensor"),
            P("dp", None),
            P("dp"),
            P("dp", "tensor"),
            P("tensor", "dp"),
            P("dp"),
            P("dp", None),
            P("dp", "tensor"),
            P("dp", "tensor"),
            P("tensor", "dp"),
            P("dp", None, "tensor"),
            P("dp", None, "tensor"),
            P("dp", "tensor", None),
        ),
        check_vma=False,
    )
```

```python
import functools
import math

import jax
import jax.numpy as jnp
from jax import lax
from jax.experimental import pallas as pl
from jax.experimental.pallas import tpu as pltpu
from jax.sharding import PartitionSpec as P

NOPE = 128
ROPE = 64
VDIM = 128
RANK = 512
TOPK = 6
WINDOW = 1024


eps_norm = 1e-06
highest = lax.Precision.HIGHEST


def passed_along(value, axis, steps):
    count = lax.axis_size(axis)
    leading, last = (max(0, -steps), min(count, count - steps))
    return lax.ppermute(value, axis, [(source, source + steps) for source in range(leading, last)])


def rms_scale(values, gain_vec):
    inv_root = lax.rsqrt(jnp.mean(values * values, axis=-1, keepdims=True) + eps_norm)
    return values * inv_root * gain_vec


def rope_tables(positions):
    half_width = ROPE // 2
    frequency = jnp.exp(
        -jnp.arange(half_width, dtype=jnp.float32) * (2.0 * math.log(10000.0) / ROPE)
    )
    angles = positions[:, None] * frequency[None, :]
    return (jnp.cos(angles), jnp.sin(angles))


def rotate(values, cos_tab, sin_tab):
    half_width = values.shape[-1] // 2
    first_half = values[..., :half_width]
    second = values[..., half_width:]
    return jnp.concatenate(
        [first_half * cos_tab - second * sin_tab, second * cos_tab + first_half * sin_tab], axis=-1
    )


def gated_act(gate_a, up_b):
    return jax.nn.silu(gate_a) * up_b


def matmul(left_mat, right_mat):
    return jnp.dot(left_mat, right_mat, preferred_element_type=jnp.float32)


def matmul_nt(left_mat, right_mat):
    return lax.dot_general(
        left_mat, right_mat, (((1,), (1,)), ((), ())), preferred_element_type=jnp.float32
    )


def matmul_tn(left_mat, right_mat):
    return lax.dot_general(
        left_mat, right_mat, (((0,), (0,)), ((), ())), preferred_element_type=jnp.float32
    )


def ranks_before(hot):
    count = hot.shape[0]
    below = jnp.arange(count)[:, None] > jnp.arange(count)[None, :]
    return matmul(below.astype(jnp.bfloat16), hot.astype(jnp.bfloat16)).astype(jnp.int32)


MESH = pl.DeviceIdType.MESH


def plane_at(z, k):
    edge = jnp.where(z >= 2, 3 - z, z)
    near = jnp.where(k == 0, edge, jnp.where(k == 1, 1 - edge, k))
    return jnp.where(z >= 2, 3 - near, near)


def ag_kernel(kinds, cuts, *refs):
    n = len(kinds)
    ins, outs, lands, sems = refs[:n], refs[n : 2 * n], refs[2 * n : 3 * n], refs[3 * n :]
    me = lax.axis_index("dp")
    core = lax.axis_index("tensor")
    z = me // 4
    y = (me // 2) % 2
    x = me % 2
    xn = z * 4 + y * 2 + (1 - x)
    yn = z * 4 + (1 - y) * 2 + x
    up = jnp.minimum(z + 1, 3) * 4 + y * 2 + x
    dn = jnp.maximum(z - 1, 0) * 4 + y * 2 + x
    bar = pltpu.get_barrier_semaphore()

    def sig(d, c):
        pl.semaphore_signal(bar, inc=1, device_id=(d, c), device_id_type=MESH)

    sig(xn, core)
    sig(yn, core)
    sig(me, 1 - core)
    pl.when(z < 3)(lambda: sig(up, core))
    pl.when(z > 0)(lambda: sig(dn, core))

    def rc(src, dst, ss, rs, dev, c):
        return pltpu.make_async_remote_copy(
            src_ref=src, dst_ref=dst, send_sem=ss, recv_sem=rs, device_id=(dev, c), device_id_type=MESH
        )

    class Part:
        def __init__(self, at, rows):
            self.share = kinds[at]
            self.x, self.o, self.hbm = ins[at], lands[at], outs[at]
            self.rows = rows
            self.zs, self.zr, self.xs, self.xr, self.ys, self.yr, self.cs, self.cr, self.own, self.out = sems[20 * at + 10 : 20 * at + 20]
            self.slot = core if self.share else 0
            self.copy = pltpu.make_async_copy(self.x.at[:, self.rows], self.whole(me), self.own)

        def whole(self, b):
            return self.o.at[b, self.slot, :, self.rows]

        def z_(self, zp, dev, s):
            b = zp * 4 + y * 2 + x
            return rc(self.whole(b), self.whole(b), self.zs.at[s], self.zr.at[zp], dev, core)

        def x_(self, j, b, half, zp):
            r = self.o.at[b, self.slot, half, self.rows]
            return rc(r, r, self.xs.at[zp, j], self.xr.at[zp, j], xn, core)

        def y_(self, j, b, half, zp):
            r = self.o.at[b, self.slot, half, self.rows]
            return rc(r, r, self.ys.at[zp, j], self.yr.at[zp, j], yn, core)

        def twin(self, b):
            return rc(self.whole(b), self.whole(b), self.cs.at[b], self.cr.at[b], me, 1 - core)

        def first(self, k):
            zp = plane_at(z, k)
            b = zp * 4 + y * 2 + x
            if k > 0:
                self.z_(zp, up, 0).wait_recv()
            pl.when((zp <= z) & (z < 3))(lambda: self.z_(zp, up, zp).start())
            pl.when((zp >= z) & (z > 0))(lambda: self.z_(zp, dn, 4 + zp).start())
            self.x_(0, b, 0, zp).start()
            self.y_(0, b, 1, zp).start()
            self.y_(1, b, 0, zp).start()
            self.x_(1, b, 1, zp).start()
            if self.share:
                self.twin(b).start()

        def second(self, k):
            zp = plane_at(z, k)
            bx = zp * 4 + y * 2 + (1 - x)
            by = zp * 4 + (1 - y) * 2 + x
            self.x_(0, bx, 0, zp).wait_recv()
            self.y_(2, bx, 0, zp).start()
            self.y_(0, by, 1, zp).wait_recv()
            self.x_(2, by, 1, zp).start()
            self.x_(1, bx, 1, zp).wait_recv()
            self.y_(1, by, 0, zp).wait_recv()
            if self.share:
                self.twin(bx).start()
                self.twin(by).start()

        def third(self, k):
            zp = plane_at(z, k)
            bd = zp * 4 + (1 - y) * 2 + (1 - x)
            self.y_(2, bd, 0, zp).wait_recv()
            self.x_(2, bd, 1, zp).wait_recv()
            if self.share:
                self.twin(bd).start()

        def save(self, k):
            at = pl.ds(plane_at(z, k) * 4, 4)
            return pltpu.make_async_copy(
                self.o.at[at, :, :, self.rows], self.hbm.at[at, :, :, self.rows], self.out.at[k]
            )

        def fourth(self, k):
            if self.share:
                for q in range(4):
                    b = plane_at(z, k) * 4 + q
                    src, dst = self.o.at[b, core, :, self.rows], self.o.at[b, 1 - core, :, self.rows]
                    rc(src, dst, self.cs.at[b], self.cr.at[b], me, 1 - core).wait_recv()
            self.save(k).start()

        def end(self):
            for k in range(4):
                self.save(k).wait()
                pl.when((k <= z) & (z < 3))(lambda k=k: self.z_(k, up, k).wait_send())
                pl.when((k >= z) & (z > 0))(lambda k=k: self.z_(k, dn, 4 + k).wait_send())
                for j in range(3):
                    self.x_(j, 0, 0, k).wait_send()
                    self.y_(j, 0, 0, k).wait_send()
            if self.share:
                for b in range(16):
                    self.twin(b).wait_send()

    class Cross:
        def __init__(self, at, rows):
            self.share = kinds[at]
            self.x, self.o, self.hbm = ins[at], lands[at], outs[at]
            self.rows = rows
            self.fs, self.fr, self.zs, self.zr, self.ls, self.lr, self.cs, self.cr, self.own, self.out = sems[20 * at : 20 * at + 10]
            self.slot = core if self.share else 0
            self.copy = pltpu.make_async_copy(self.x.at[:, rows], self.o.at[me, self.slot, :, rows], self.own)

        def ref(self, b, half):
            return self.o.at[b, self.slot, half, self.rows]

        def block(self, zp, half, p):
            if half == 0:
                return zp * 4 + y * 2 + (x if p == 0 else 1 - x)
            return zp * 4 + (y if p == 0 else 1 - y) * 2 + x

        def hop(self, half):
            r = self.ref(me, half)
            return rc(r, r, self.fs.at[half], self.fr.at[half], xn if half == 0 else yn, core)

        def line(self, zp, half, p, d):
            r = self.ref(self.block(zp, half, p), half)
            return rc(r, r, self.zs.at[d, zp, half, p], self.zr.at[zp, half, p], up if d == 0 else dn, core)

        def last(self, zp, half, p):
            r = self.ref(self.block(zp, half, p), half)
            return rc(r, r, self.ls.at[zp, half, p], self.lr.at[zp, half, p], yn if half == 0 else xn, core)

        def twin(self, b, half):
            r = self.ref(b, half)
            return rc(r, r, self.cs.at[b, half], self.cr.at[b, half], me, 1 - core)

        def pass_on(self, zp, half, p):
            pl.when((zp <= z) & (z < 3))(lambda: self.line(zp, half, p, 0).start())
            pl.when((zp >= z) & (z > 0))(lambda: self.line(zp, half, p, 1).start())
            self.last(zp, half, p).start()
            if self.share:
                self.twin(self.block(zp, half, p), half).start()

        def first(self, k):
            zp = plane_at(z, k)
            if k == 0:
                for half in range(2):
                    self.hop(half).start()
                for half in range(2):
                    self.pass_on(zp, half, 0)
                for half in range(2):
                    self.hop(half).wait_recv()
                    self.pass_on(zp, half, 1)
            else:
                for p in range(2):
                    for half in range(2):
                        self.line(zp, half, p, 0).wait_recv()
                        self.pass_on(zp, half, p)

        def second(self, k):
            pass

        def third(self, k):
            zp = plane_at(z, k)
            for p in range(2):
                for half in range(2):
                    self.last(zp, half, p).wait_recv()
                    if self.share:
                        far = zp * 4 + (1 - y) * 2 + (x if p == 0 else 1 - x)
                        if half == 1:
                            far = zp * 4 + (y if p == 0 else 1 - y) * 2 + (1 - x)
                        self.twin(far, half).start()

        def save(self, k):
            at = pl.ds(plane_at(z, k) * 4, 4)
            return pltpu.make_async_copy(
                self.o.at[at, :, :, self.rows], self.hbm.at[at, :, :, self.rows], self.out.at[k]
            )

        def fourth(self, k):
            if self.share:
                for q in range(4):
                    b = plane_at(z, k) * 4 + q
                    for half in range(2):
                        src, dst = self.o.at[b, core, half, self.rows], self.o.at[b, 1 - core, half, self.rows]
                        rc(src, dst, self.cs.at[b, half], self.cr.at[b, half], me, 1 - core).wait_recv()
            self.save(k).start()

        def end(self):
            for half in range(2):
                self.hop(half).wait_send()
            for k in range(4):
                self.save(k).wait()
                for half in range(2):
                    for p in range(2):
                        pl.when((k <= z) & (z < 3))(lambda k=k, h=half, p=p: self.line(k, h, p, 0).wait_send())
                        pl.when((k >= z) & (z > 0))(lambda k=k, h=half, p=p: self.line(k, h, p, 1).wait_send())
                        self.last(k, half, p).wait_send()
            if self.share:
                for b in range(16):
                    for half in range(2):
                        self.twin(b, half).wait_send()

    groups = []
    for at in range(n):
        height = ins[at].shape[1]
        group = [Cross(at, pl.ds(0, cuts[at]))] if cuts[at] > 0 else []
        if cuts[at] < height:
            group.append(Part(at, pl.ds(cuts[at], height - cuts[at])))
        groups.append(group)
    parts = [p for g in groups for p in g]
    for p in parts:
        p.copy.start()
    pl.semaphore_wait(bar, 3 + (z < 3).astype(jnp.int32) + (z > 0).astype(jnp.int32))
    for p in parts:
        p.copy.wait()
    turns = [(p, k) for k in range(4) for p in parts]
    lag = len(parts)
    for t in range(len(turns) + lag):
        if t < len(turns):
            turns[t][0].first(turns[t][1])
        if t >= lag:
            turns[t - lag][0].second(turns[t - lag][1])
    for p, k in turns:
        p.third(k)
        if not p.share:
            p.fourth(k)
    for p, k in turns:
        if p.share:
            p.fourth(k)
    for p in parts:
        p.end()


def ag16(arrays, kinds, cid, cuts=None):
    S = pltpu.SemaphoreType.DMA
    any_ = pl.BlockSpec(memory_space=pl.ANY)
    cuts = cuts or tuple(v.shape[1] // 2 for v in arrays)
    counts = (
        ((2,), (2,), (2, 4, 2, 2), (4, 2, 2), (4, 2, 2), (4, 2, 2), (16, 2), (16, 2), (), (4,))
        + ((8,), (4,), (4, 3), (4, 3), (4, 3), (4, 3), (16,), (16,), (), (4,))
    )
    shapes = [(16, 2 if share else 1) + v.shape for v, share in zip(arrays, kinds)]
    return pl.pallas_call(
        functools.partial(ag_kernel, kinds, cuts),
        out_shape=[jax.ShapeDtypeStruct(s, v.dtype) for s, v in zip(shapes, arrays)],
        in_specs=[any_] * len(arrays),
        out_specs=[any_] * len(arrays),
        scratch_shapes=[pltpu.VMEM(s, v.dtype) for s, v in zip(shapes, arrays)]
        + [S(s) for _ in arrays for s in counts],
        compiler_params=pltpu.CompilerParams(collective_id=cid, has_side_effects=True, vmem_limit_bytes=60 << 20),
    )(*arrays)


def add_into(dst, src):
    def step(i, _):
        r = pl.ds(pl.multiple_of(i * 16, 16), 16)
        dst[r] = dst[r] + src[r]
        return 0

    lax.fori_loop(0, dst.shape[0] // 16, step, 0)


def rs_kernel(a_ref, b_ref, o_ref, own, fr, zr, lr, yr, xr, z2r, lsem, fs, frs, zs, zrs, ls, lrs, xs, xrs, ys, yrs, z2s, z2rs):
    me = lax.axis_index("dp")
    core = lax.axis_index("tensor")
    z = me // 4
    y = (me // 2) % 2
    x = me % 2
    xn = z * 4 + y * 2 + (1 - x)
    yn = z * 4 + (1 - y) * 2 + x
    up = jnp.minimum(z + 1, 3) * 4 + y * 2 + x
    dn = jnp.maximum(z - 1, 0) * 4 + y * 2 + x
    wide = a_ref.shape[3]
    cut = fr.shape[3]
    crossing, rest = pl.ds(0, cut), pl.ds(cut, own.shape[2] - cut)

    def rc(src, dst, ss, rs, dev):
        return pltpu.make_async_remote_copy(
            src_ref=src, dst_ref=dst, send_sem=ss, recv_sem=rs, device_id=(dev, core), device_id_type=MESH
        )

    def loads(zp):
        at = pl.ds(zp * 4, 4)
        return [
            pltpu.make_async_copy(a_ref.at[at], own.at[at, :, :, 0:wide], lsem.at[zp, 0]),
            pltpu.make_async_copy(b_ref.at[at], own.at[at, :, :, wide:], lsem.at[zp, 1]),
        ]

    for k in range(4):
        for c in loads(plane_at(z, 3 - k)):
            c.start()
    bar = pltpu.get_barrier_semaphore()

    def sig(d):
        pl.semaphore_signal(bar, inc=1, device_id=(d, core), device_id_type=MESH)

    sig(xn)
    sig(yn)
    pl.when(z < 3)(lambda: sig(up))
    pl.when(z > 0)(lambda: sig(dn))
    pl.semaphore_wait(bar, 2 + (z < 3).astype(jnp.int32) + (z > 0).astype(jnp.int32))

    def blk(zp, yy, xx):
        return zp * 4 + yy * 2 + xx

    def place(zp, half, p):
        if half == 0:
            return blk(zp, y, x if p == 0 else 1 - x)
        return blk(zp, y if p == 0 else 1 - y, x)

    def hop(zp, half, p):
        b = blk(zp, 1 - y, x if p == 0 else 1 - x) if half == 0 else blk(zp, y if p == 0 else 1 - y, 1 - x)
        return rc(
            own.at[b, half, crossing], fr.at[zp, half, p], fs.at[zp, half, p], frs.at[zp, half, p], yn if half == 0 else xn
        )

    def line(zp, half, p, dev, slot):
        b = place(zp, half, p)
        return rc(own.at[b, half, crossing], zr.at[slot, half, p], zs.at[zp, half, p], zrs.at[slot, half, p], dev)

    def last(half):
        b = place(z, half, 1)
        return rc(own.at[b, half, crossing], lr.at[half], ls.at[half], lrs.at[half], xn if half == 0 else yn)

    def y_(j, b, half, zp):
        return rc(own.at[b, half, rest], yr.at[zp, j], ys.at[zp, j], yrs.at[zp, j], yn)

    def x_(j, b, half, zp):
        return rc(own.at[b, half, rest], xr.at[zp, j], xs.at[zp, j], xrs.at[zp, j], xn)

    def zc(zp, dev, d):
        return rc(own.at[zp * 4 + y * 2 + x, :, rest], z2r.at[d, zp], z2s.at[zp], z2rs.at[d, zp], dev)

    def s1(k):
        zp = plane_at(z, 3 - k)
        for c in loads(zp):
            c.wait()
        for p in range(2):
            for half in range(2):
                hop(zp, half, 1 - p).start()
        y_(0, blk(zp, 1 - y, 1 - x), 0, zp).start()
        x_(0, blk(zp, 1 - y, 1 - x), 1, zp).start()
        y_(1, blk(zp, 1 - y, x), 0, zp).start()
        x_(1, blk(zp, y, 1 - x), 1, zp).start()

    def arrive(zp, half, p, slot):
        line(zp, half, p, me, slot).wait_recv()
        add_into(own.at[place(zp, half, p), half, crossing], zr.at[slot, half, p])

    def s2(k):
        zp = plane_at(z, 3 - k)
        for p in (1, 0):
            for half in range(2):
                hop(zp, half, p).wait_recv()
                add_into(own.at[place(zp, half, p), half, crossing], fr.at[zp, half, p])
                pl.when((zp <= z) & (z < 3))(lambda h=half, p=p: arrive(zp, h, p, jnp.where(zp == z, 4, zp)))
                pl.when((zp >= z) & (z > 0))(lambda h=half, p=p: arrive(zp, h, p, zp))
                pl.when(zp < z)(lambda h=half, p=p: line(zp, h, p, dn, jnp.where(zp == z - 1, 4, zp)).start())
                pl.when(zp > z)(lambda h=half, p=p: line(zp, h, p, up, zp).start())
                if k == 3 and p == 1:
                    last(half).start()
        mine = blk(zp, y, x)
        y_(0, blk(zp, 1 - y, 1 - x), 0, zp).wait_recv()
        add_into(own.at[blk(zp, y, 1 - x), 0, rest], yr.at[zp, 0])
        x_(2, blk(zp, y, 1 - x), 0, zp).start()
        x_(0, blk(zp, 1 - y, 1 - x), 1, zp).wait_recv()
        add_into(own.at[blk(zp, 1 - y, x), 1, rest], xr.at[zp, 0])
        y_(2, blk(zp, 1 - y, x), 1, zp).start()
        y_(1, blk(zp, 1 - y, x), 0, zp).wait_recv()
        add_into(own.at[mine, 0, rest], yr.at[zp, 1])
        x_(1, blk(zp, y, 1 - x), 1, zp).wait_recv()
        add_into(own.at[mine, 1, rest], xr.at[zp, 1])

    def s3(k):
        zp = plane_at(z, 3 - k)
        mine = blk(zp, y, x)
        x_(2, blk(zp, y, 1 - x), 0, zp).wait_recv()
        add_into(own.at[mine, 0, rest], xr.at[zp, 2])
        y_(2, blk(zp, 1 - y, x), 1, zp).wait_recv()
        add_into(own.at[mine, 1, rest], yr.at[zp, 2])

        def arrived(d):
            zc(zp, me, d).wait_recv()
            add_into(own.at[mine, 0, rest], z2r.at[d, zp, 0])
            add_into(own.at[mine, 1, rest], z2r.at[d, zp, 1])

        pl.when((zp <= z) & (z < 3))(lambda: arrived(1))
        pl.when((zp >= z) & (z > 0))(lambda: arrived(0))
        pl.when(zp < z)(lambda: zc(zp, dn, 1).start())
        pl.when(zp > z)(lambda: zc(zp, up, 0).start())

    s1(0)
    s1(1)
    s2(0)
    s1(2)
    s2(1)
    s3(0)
    s1(3)
    s2(2)
    s3(1)
    s2(3)
    s3(2)
    s3(3)
    for half in range(2):
        last(half).wait_recv()
        add_into(own.at[me, half, crossing], lr.at[half])
    for a in range(2):

        def row(i, _):
            r = pl.ds(pl.multiple_of(i * 16, 16), 16)
            o_ref[a, r] = own[me, a, r].astype(jnp.float32)
            return 0

        lax.fori_loop(0, o_ref.shape[1] // 16, row, 0)
    for half in range(2):
        last(half).wait_send()
    for k in range(4):
        for half in range(2):
            for p in range(2):
                hop(k, half, p).wait_send()
                pl.when(k != z)(lambda k=k, h=half, p=p: line(k, h, p, me, 0).wait_send())
        for j in range(3):
            x_(j, 0, 0, k).wait_send()
            y_(j, 0, 0, k).wait_send()
        pl.when(k != z)(lambda k=k: zc(k, up, 0).wait_send())


def rs16(a, b, cid):
    S = pltpu.SemaphoreType.DMA
    high, total = a.shape[2], a.shape[3] + b.shape[3]
    blkshape = (2, high, total)
    cross, half = (high // 2, total), (high - high // 2, total)
    V = lambda s: pltpu.VMEM(s, a.dtype)
    return pl.pallas_call(
        rs_kernel,
        out_shape=jax.ShapeDtypeStruct(blkshape, jnp.float32),
        in_specs=[pl.BlockSpec(memory_space=pl.ANY)] * 2,
        out_specs=pl.BlockSpec(memory_space=pltpu.VMEM),
        scratch_shapes=[
            V((16,) + blkshape), V((4, 2, 2) + cross), V((5, 2, 2) + cross), V((2,) + cross),
            V((4, 3) + half), V((4, 3) + half), V((2, 4, 2) + half),
            S((4, 2)), S((4, 2, 2)), S((4, 2, 2)), S((4, 2, 2)), S((5, 2, 2)), S((2,)), S((2,)),
            S((4, 3)), S((4, 3)), S((4, 3)), S((4, 3)), S((4,)), S((2, 4)),
        ],
        compiler_params=pltpu.CompilerParams(collective_id=cid, has_side_effects=True, vmem_limit_bytes=60 << 20),
    )(a, b)


def nt(a, b):
    return lax.dot_general(a, b, (((1,), (1,)), ((), ())), preferred_element_type=jnp.float32)


def tn(a, b):
    return lax.dot_general(a, b, (((0,), (0,)), ((), ())), preferred_element_type=jnp.float32)


def mm(a, b):
    return jnp.dot(a, b, preferred_element_type=jnp.float32)


def gate_parts(a, b, dc):
    s = 1.0 / (1.0 + jnp.exp(-a))
    act = a * s
    return act * b, dc * b * (s * (1.0 + a * (1.0 - s))), dc * act


def moe_kernel(
    moe, grd, pick, pick_t, wg_in, wu_in, wd_in, wr, sgu, sdn,
    o_out, r_out, rg_out, act_out, da_out, db_out, sg_out, yr, xr, zr,
    sg_sum, wg, wu, wd, own, sib, sibr, stage, xb, gb, pk, pt, rr, rg, ly, ld, ry, rd, acts, das, dbs, dgs,
    w_sem, in_sem, out_sem, st_sem, free, cs, cr, xs, xrs, ys, yrs, zs, zrs, fs, fr,
):
    me = lax.axis_index("dp")
    core = lax.axis_index("tensor")
    other = 1 - core
    z = me // 4
    y = (me // 2) % 2
    x = me % 2
    xn = z * 4 + y * 2 + (1 - x)
    yn = z * 4 + (1 - y) * 2 + x
    up = jnp.minimum(z + 1, 3) * 4 + y * 2 + x
    dn = jnp.maximum(z - 1, 0) * 4 + y * 2 + x
    width = moe.shape[2]
    hid = 128
    cut = 512

    def rc(src, dst, ss, rs, dev, c):
        return pltpu.make_async_remote_copy(
            src_ref=src, dst_ref=dst, send_sem=ss, recv_sem=rs, device_id=(dev, c), device_id_type=MESH
        )

    def loads(i):
        k, half = i // 2, i % 2
        b = plane_at(z, 3 - k) * 4 + jnp.where(half == 0, 1 - y, y) * 2
        at = pl.ds(b, 2)
        return [
            pltpu.make_async_copy(moe.at[at], xb, in_sem.at[0]),
            pltpu.make_async_copy(grd.at[at], gb, in_sem.at[1]),
            pltpu.make_async_copy(pick.at[at], pk, in_sem.at[2]),
            pltpu.make_async_copy(pick_t.at[at], pt, in_sem.at[3]),
        ]

    for c in loads(0):
        c.start()
    weights = [
        pltpu.make_async_copy(src, dst, w_sem.at[n]) for n, (src, dst) in enumerate(((wd_in, wd), (wg_in, wg), (wu_in, wu)))
    ]
    for c in weights:
        c.start()
    bar = pltpu.get_barrier_semaphore()

    def sig(d, c):
        pl.semaphore_signal(bar, inc=1, device_id=(d, c), device_id_type=MESH)

    sig(xn, core)
    sig(yn, core)
    sig(me, other)
    pl.when(z < 3)(lambda: sig(up, core))
    pl.when(z > 0)(lambda: sig(dn, core))
    pl.semaphore_wait(bar, 3 + (z < 3).astype(jnp.int32) + (z > 0).astype(jnp.int32))

    for q in range(2):
        ry[q, hid:] = sdn[...]
        rd[q, hid:] = sgu[...]
    sg_sum[...] = jnp.zeros_like(sg_sum)

    def y_(j, b, half, zp):
        return rc(own.at[b, half], yr.at[zp, j], ys.at[zp, j], yrs.at[zp, j], yn, core)

    def x_(j, b, half, zp):
        return rc(own.at[b, half], xr.at[zp, j], xs.at[zp, j], xrs.at[zp, j], xn, core)

    def zc(zp, dev, d):
        b = zp * 4 + y * 2 + x
        return rc(own.at[b], zr.at[d, zp], zs.at[zp], zrs.at[d, zp], dev, core)

    def sib_send(i):
        return rc(sib, sibr, cs, cr, me, other)

    def outs(i):
        at = pl.ds(pl.multiple_of(i * 256, 256), 256)
        return [
            pltpu.make_async_copy(rr, r_out.at[at], out_sem.at[0]),
            pltpu.make_async_copy(rg, rg_out.at[at], out_sem.at[1]),
            pltpu.make_async_copy(acts, act_out.at[at], out_sem.at[2]),
            pltpu.make_async_copy(das, da_out.at[at], out_sem.at[3]),
            pltpu.make_async_copy(dbs, db_out.at[at], out_sem.at[4]),
        ]

    def columns(step):
        def one(n, _):
            step(pl.ds(pl.multiple_of(n * cut, cut), cut))
            return 0

        lax.fori_loop(0, width // cut, one, 0)

    def first_part(i):
        for c in loads(i):
            c.wait()

        @pl.when(i > 0)
        def _():
            for c in outs(i - 1):
                c.wait()

        def pick_rows(n):
            for q in range(2):
                rr[q * hid : (q + 1) * hid, n] = mm(pk[q], xb[q, :, n]).astype(jnp.bfloat16)
                rg[q * hid : (q + 1) * hid, n] = mm(pk[q], gb[q, :, n]).astype(jnp.bfloat16)

        columns(pick_rows)
        for q in range(2):
            ab = nt(xb[q], sgu[...])
            act, d_a, d_b = gate_parts(ab[:, :hid], ab[:, hid:], nt(gb[q], sdn[...]))
            ly[q, :, :hid] = pt[q]
            ly[q, :, hid:] = act.astype(jnp.bfloat16)
            ld[q, :, :hid] = pt[q]
            ld[q, :, hid : 2 * hid] = d_a.astype(jnp.bfloat16)
            ld[q, :, 2 * hid :] = d_b.astype(jnp.bfloat16)

        def shared_grads(n):
            sg_sum[: 2 * hid, n] += tn(ld[0, :, hid:], xb[0, :, n]) + tn(ld[1, :, hid:], xb[1, :, n])
            sg_sum[2 * hid :, n] += tn(ly[0, :, hid:], gb[0, :, n]) + tn(ly[1, :, hid:], gb[1, :, n])

        columns(shared_grads)

        @pl.when(i < 7)
        def _():
            for c in loads(i + 1):
                c.start()

    def second_part(i):
        @pl.when(i == 0)
        def _():
            for c in weights:
                c.wait()

        logits = mm(rr[...], wr[...])
        lane = lax.broadcasted_iota(jnp.int32, logits.shape, 1)
        logits = jnp.where(lane < 16, logits, -jnp.inf)
        e = jnp.exp(logits - jnp.max(logits, axis=1, keepdims=True))
        gate = jnp.sum(jnp.where(lane == me, e, 0.0), axis=1, keepdims=True) / jnp.sum(
            e, axis=1, keepdims=True
        )
        pre = nt(rg[...], wd[...])
        act, d_a, d_b = gate_parts(nt(rr[...], wg[...]), nt(rr[...], wu[...]), gate * pre)
        low = act.astype(jnp.bfloat16)
        back = low.astype(jnp.float32)
        d_gate = jnp.sum(back * pre, axis=1, keepdims=True)
        acts[...] = (gate * back).astype(jnp.bfloat16)
        das[...] = d_a.astype(jnp.bfloat16)
        dbs[...] = d_b.astype(jnp.bfloat16)

        def spread(n):
            o = (gate * mm(low, wd[:, n])).astype(jnp.bfloat16)
            s = (mm(das[...], wg[:, n]) + mm(dbs[...], wu[:, n])).astype(jnp.bfloat16)
            for q in range(2):
                ry[q, :hid, n] = o[q * hid : (q + 1) * hid]
                rd[q, :hid, n] = s[q * hid : (q + 1) * hid]

        columns(spread)
        for c in outs(i):
            c.start()
        dgs[...] = jnp.where(lane == me, d_gate, 0.0).astype(jnp.bfloat16)

    def third_part(i):
        k, half = i // 2, i % 2
        b = plane_at(z, 3 - k) * 4 + jnp.where(half == 0, 1 - y, y) * 2

        @pl.when(i > 0)
        def _():
            sib_send(i - 1).wait_send()

        def store(q, n, v):
            v = v.astype(jnp.bfloat16)
            mine = jnp.where(core == 0, v[:128], v[128:])
            theirs = jnp.where(core == 0, v[128:], v[:128])
            own[b + q, 0, :, n] = mine[:64]
            own[b + q, 1, :, n] = mine[64:]
            sib[q, 0, :, n] = theirs[:64]
            sib[q, 1, :, n] = theirs[64:]

        def put(m, _):
            n = pl.ds(pl.multiple_of(m * cut, cut), cut)
            n2 = pl.ds(pl.multiple_of(width + m * cut, cut), cut)
            for q in range(2):
                store(q, n, mm(ly[q], ry[q, :, n]))
                store(q, n2, mm(ld[q], rd[q, :, n]))
            return 0

        lax.fori_loop(0, width // cut, put, 0)
        for q in range(2):
            store(q, pl.ds(2 * width, 128), mm(pt_of(q), dgs[q * hid : (q + 1) * hid]))

        @pl.when(i > 0)
        def _():
            pl.semaphore_wait(free, 1)

        sib_send(i).start()

    def pt_of(q):
        return ly[q, :, :hid]

    def staged(src, dst, sem):
        return pltpu.make_async_copy(src, dst, sem)

    def blk(zp, yy, xx):
        return zp * 4 + yy * 2 + xx

    def pair_sum(i):
        k, half = i // 2, i % 2
        zp = plane_at(z, 3 - k)
        b = zp * 4 + jnp.where(half == 0, 1 - y, y) * 2
        sib_send(i).wait_recv()

        def one(q, _):
            add_into(own.at[b + q, 0], sibr.at[q, 0])
            add_into(own.at[b + q, 1], sibr.at[q, 1])
            return 0

        lax.fori_loop(0, 2, one, 0)

        @pl.when(i < 7)
        def _():
            pl.semaphore_signal(free, inc=1, device_id=(me, other), device_id_type=MESH)

        @pl.when(half == 0)
        def _():
            y_(0, blk(zp, 1 - y, 1 - x), 0, zp).start()
            x_(0, blk(zp, 1 - y, 1 - x), 1, zp).start()
            y_(1, blk(zp, 1 - y, x), 0, zp).start()

        @pl.when(half == 1)
        def _():
            x_(1, blk(zp, y, 1 - x), 1, zp).start()

    def second_staging(k):
        zp = plane_at(z, 3 - k)
        return [
            staged(yr.at[zp, 0], stage.at[0, 0], st_sem.at[0]),
            staged(xr.at[zp, 0], stage.at[0, 1], st_sem.at[1]),
            staged(yr.at[zp, 1], stage.at[1, 0], st_sem.at[2]),
            staged(xr.at[zp, 1], stage.at[1, 1], st_sem.at[3]),
        ]

    def second_fetch(k):
        zp = plane_at(z, 3 - k)
        c = second_staging(k)
        y_(0, blk(zp, 1 - y, 1 - x), 0, zp).wait_recv()
        c[0].start()
        x_(0, blk(zp, 1 - y, 1 - x), 1, zp).wait_recv()
        c[1].start()
        y_(1, blk(zp, 1 - y, x), 0, zp).wait_recv()
        c[2].start()
        x_(1, blk(zp, y, 1 - x), 1, zp).wait_recv()
        c[3].start()

    def second_hop(k):
        zp = plane_at(z, 3 - k)
        mine = blk(zp, y, x)
        c = second_staging(k)
        c[0].wait()
        add_into(own.at[blk(zp, y, 1 - x), 0], stage.at[0, 0])
        x_(2, blk(zp, y, 1 - x), 0, zp).start()
        c[1].wait()
        add_into(own.at[blk(zp, 1 - y, x), 1], stage.at[0, 1])
        y_(2, blk(zp, 1 - y, x), 1, zp).start()
        c[2].wait()
        add_into(own.at[mine, 0], stage.at[1, 0])
        c[3].wait()
        add_into(own.at[mine, 1], stage.at[1, 1])

    def last_staging(k):
        zp = plane_at(z, 3 - k)
        return [
            staged(xr.at[zp, 2], stage.at[0, 0], st_sem.at[0]),
            staged(yr.at[zp, 2], stage.at[0, 1], st_sem.at[1]),
            staged(zr.at[1, zp], stage.at[1], st_sem.at[2]),
            staged(zr.at[0, zp], stage.at[2], st_sem.at[3]),
        ]

    def last_fetch(k):
        zp = plane_at(z, 3 - k)
        c = last_staging(k)
        x_(2, blk(zp, y, 1 - x), 0, zp).wait_recv()
        c[0].start()
        y_(2, blk(zp, 1 - y, x), 1, zp).wait_recv()
        c[1].start()

        @pl.when((zp <= z) & (z < 3))
        def _():
            zc(zp, me, 1).wait_recv()
            c[2].start()

        @pl.when((zp >= z) & (z > 0))
        def _():
            zc(zp, me, 0).wait_recv()
            c[3].start()

    def last_hop(k):
        zp = plane_at(z, 3 - k)
        mine = blk(zp, y, x)
        c = last_staging(k)
        c[0].wait()
        add_into(own.at[mine, 0], stage.at[0, 0])
        c[1].wait()
        add_into(own.at[mine, 1], stage.at[0, 1])

        def arrived(d):
            c[3 - d].wait()
            add_into(own.at[mine, 0], stage.at[2 - d, 0])
            add_into(own.at[mine, 1], stage.at[2 - d, 1])

        pl.when((zp <= z) & (z < 3))(lambda: arrived(1))
        pl.when((zp >= z) & (z > 0))(lambda: arrived(0))
        pl.when(zp < z)(lambda: zc(zp, dn, 1).start())
        pl.when(zp > z)(lambda: zc(zp, up, 0).start())

    lag = jnp.where((z == 0) | (z == 3), 5, 7)

    def step(i, _):
        pl.when(i < 8)(lambda: first_part(i))
        pl.when((i >= 1) & (i <= 8))(lambda: pair_sum(i - 1))
        seconds = (i % 2 == 0) & (i >= 4) & (i <= 10)
        lasts = (i % 2 == 1) & (i >= lag) & (i <= lag + 6)
        pl.when(seconds)(lambda: second_fetch((i - 4) // 2))
        pl.when(lasts)(lambda: last_fetch((i - lag) // 2))
        pl.when(i < 8)(lambda: second_part(i))
        pl.when(seconds)(lambda: second_hop((i - 4) // 2))
        pl.when(lasts)(lambda: last_hop((i - lag) // 2))
        pl.when(i < 8)(lambda: third_part(i))
        return 0

    lax.fori_loop(0, 14, step, 0)

    def give(n):
        sg_out[:, n] = sg_sum[:, n].astype(jnp.bfloat16)

    columns(give)
    for a in range(2):

        def row(n, _):
            r = pl.ds(pl.multiple_of(n * 16, 16), 16)
            o_out[core, a, r] = own[me, a, r]
            return 0

        lax.fori_loop(0, 4, row, 0)
    f = rc(o_out.at[core], o_out.at[core], fs, fr, me, other)
    f.start()
    for c in outs(7):
        c.wait()
    sib_send(7).wait_send()
    for k in range(4):
        for j in range(3):
            x_(j, 0, 0, k).wait_send()
            y_(j, 0, 0, k).wait_send()

        @pl.when(k != z)
        def _():
            zc(k, up, 0).wait_send()

    rc(o_out.at[core], o_out.at[other], fs, fr, me, other).wait_recv()
    f.wait_send()


def moe_call(moe, grd, pick, pick_t, wg, wu, wd, wr, sgu, sdn, cid):
    ffe, width = wg.shape
    total = 2 * width + 128
    slots = pick.shape[0] * pick.shape[1]
    low, S, V = jnp.bfloat16, pltpu.SemaphoreType.DMA, pltpu.VMEM
    any_, vmem = pl.BlockSpec(memory_space=pl.ANY), pl.BlockSpec(memory_space=pltpu.VMEM)
    shape = lambda *s: jax.ShapeDtypeStruct(s, low)
    blk = (2, 64, total)
    return pl.pallas_call(
        moe_kernel,
        out_shape=[
            shape(2, *blk), shape(slots, width), shape(slots, width), shape(slots, ffe), shape(slots, ffe),
            shape(slots, ffe), shape(384, width),
            shape(4, 3, 64, total), shape(4, 3, 64, total), shape(2, 4, *blk),
        ],
        in_specs=[any_] * 7 + [vmem] * 3,
        out_specs=[vmem] + [any_] * 5 + [vmem] + [any_] * 3,
        scratch_shapes=[
            V((384, width), jnp.float32), V(wg.shape, low), V(wu.shape, low), V(wd.shape, low),
            V((16,) + blk, low), V((2,) + blk, low), V((2,) + blk, low), V((3,) + blk, low),
            V((2, 256, width), low), V((2, 256, width), low), V((2, 128, 256), low), V((2, 256, 128), low),
            V((256, width), low), V((256, width), low), V((2, 256, 256), low), V((2, 256, 384), low),
            V((2, 256, width), low), V((2, 384, width), low),
            V((256, ffe), low), V((256, ffe), low), V((256, ffe), low), V((256, 128), low),
            S((3,)), S((4,)), S((5,)), S((4,)), pltpu.SemaphoreType.REGULAR, S, S, S((4, 3)), S((4, 3)), S((4, 3)), S((4, 3)), S((4,)), S((2, 4)), S, S,
        ],
        compiler_params=pltpu.CompilerParams(collective_id=cid, has_side_effects=True, vmem_limit_bytes=60 << 20),
        cost_estimate=pl.CostEstimate(flops=65 * 10**9, bytes_accessed=80 * 10**6, transcendentals=0),
    )(moe, grd, pick, pick_t, wg, wu, wd, wr, sgu, sdn)


SLOTS = 5
KEYS = SLOTS * 256


def turned(v, cos, sin):
    n = v.shape[1]
    lane = lax.broadcasted_iota(jnp.int32, v.shape, 1) % 64
    swap = jnp.where(lane < 32, -pltpu.roll(v, n - 32, 1), pltpu.roll(v, 32, 1))
    return v * cos + swap * sin


def root(v):
    return lax.rsqrt(jnp.mean(v * v, axis=1, keepdims=True) + eps_norm)


def greet_all(me, core, bar):
    pl.semaphore_signal(bar, inc=1, device_id=(me, 1 - core), device_id_type=MESH)
    for j in range(1, 16):
        pl.semaphore_signal(bar, inc=1, device_id=((me + j) % 16, core), device_id_type=MESH)
    pl.semaphore_wait(bar, 16)


class Trade:
    def __init__(self, source, land, me, core, send_sem, recv_sem, own_sem):
        def copy(j, to, to_slot):
            return pltpu.make_async_remote_copy(
                src_ref=source(to), dst_ref=land.at[to_slot], send_sem=send_sem.at[j - 1], recv_sem=recv_sem.at[j - 1],
                device_id=(to, core), device_id_type=MESH,
            )

        self.out = [copy(j, (me + j) % 16, me) for j in range(1, 16)]
        self.back = [copy(j, (me + 16 - j) % 16, (me + 16 - j) % 16) for j in range(1, 16)]
        self.own = pltpu.make_async_copy(source(me), land.at[me], own_sem)

    def start(self):
        self.own.start()
        for c in self.out:
            c.start()

    def wait(self):
        self.own.wait()
        for c in self.back:
            c.wait_recv()
        for c in self.out:
            c.wait_send()


def read_gains(wlat):
    lane = lax.broadcasted_iota(jnp.int32, (16, 128), 1)
    row = lax.broadcasted_iota(jnp.int32, (16, 128), 0)
    rows = nt((lane == row + 80).astype(jnp.bfloat16), wlat[:, RANK:])
    return rows[0:1], rows[1:2]


def slab_copies(w4, w2, wq, wo, wkv, wlat, sem):
    pairs = [
        (w2.at[:, 2560:3200], wlat, sem.at[0]),
        (w2.at[:, 0:1536], wq, sem.at[1]),
        (w2.at[:, 1536:2560], wo, sem.at[2]),
    ]
    for c in range(4):
        pairs.append((w4.at[:, c, :, w4.shape[3] - 512 :], wkv.at[:, :, c * 512 : (c + 1) * 512], sem.at[3 + c]))
    return pairs


def att_fwd_kernel(
    tok, w4, w2, trade_in, g_lat, cos, sin, bias,
    middle, moe_low, normed, lat_raw, qcat, keys, kv_out, lse, att, trade_out,
    kv, wq, wo, wkv, wlat, part, arrived, w_sem, kv_sem, ks, kr, ts, tr, cs, cr, as_, ar, ao,
):
    me = lax.axis_index("dp")
    core = lax.axis_index("tensor")
    loads = [pltpu.make_async_copy(h, v, s) for h, v, s in slab_copies(w4, w2, wq, wo, wkv, wlat, w_sem)]
    for c in loads:
        c.start()
    bar = pltpu.get_barrier_semaphore()
    greet_all(me, core, bar)
    trade = Trade(lambda i: trade_in.at[i], trade_out, me, core, as_, ar, ao)
    t = tok[...].astype(jnp.float32)
    loads[0].wait()
    g_att, g_moe = read_gains(wlat)
    normed[...] = (t * root(t) * g_att).astype(jnp.bfloat16)
    lat = mm(normed[...], wlat[...])
    lat_raw[...] = lat
    first = lat[:, :RANK]
    rot = turned(lat[:, RANK:], cos[:, :128], sin[:, :128])
    rot = jnp.where(lax.broadcasted_iota(jnp.int32, rot.shape, 1) < 64, rot, 0.0)
    keys[SLOTS - 1, :, :RANK] = (first * root(first) * g_lat[...]).astype(jnp.bfloat16)
    keys[SLOTS - 1, :, RANK:] = (rot + pltpu.roll(rot, 64, 1)).astype(jnp.bfloat16)

    mine = pl.ds(pl.multiple_of(core * 128, 128), 128)

    def send(d):
        return pltpu.make_async_remote_copy(
            src_ref=keys.at[SLOTS - 1, mine], dst_ref=keys.at[SLOTS - 1 - d, mine], send_sem=ks.at[d - 1],
            recv_sem=kr.at[d - 1], device_id=(jnp.minimum(me + d, 15), core), device_id_type=MESH,
        )

    def hand(d):
        return pltpu.make_async_remote_copy(
            src_ref=keys.at[SLOTS - 1 - d, mine], dst_ref=keys.at[SLOTS - 1 - d, mine], send_sem=ts.at[d - 1],
            recv_sem=tr.at[d - 1], device_id=(me, 1 - core), device_id_type=MESH,
        )

    def handed(d):
        other = keys.at[SLOTS - 1 - d, pl.ds(pl.multiple_of((1 - core) * 128, 128), 128)]
        return pltpu.make_async_remote_copy(
            src_ref=other, dst_ref=other, send_sem=ts.at[d - 1], recv_sem=tr.at[d - 1],
            device_id=(me, 1 - core), device_id_type=MESH,
        )

    for d in range(1, SLOTS):
        pl.when(me + d < 16)(lambda d=d: send(d).start())

        @pl.when(me < d)
        def _():
            keys[SLOTS - 1 - d] = jnp.zeros((256, 640), jnp.bfloat16)

    trade.start()

    loads[1].wait()
    half = lax.broadcasted_iota(jnp.int32, (256, 128), 1) < 64
    q_nope = mm(normed[...], wq[:, :1024])
    q_rope = turned(mm(normed[...], wq[:, 1024:]), cos[...], sin[...])
    for h in range(8):
        qcat[h, :, :128] = q_nope[:, h * 128 : (h + 1) * 128].astype(jnp.bfloat16)
        pair = q_rope[:, h // 2 * 128 : (h // 2 + 1) * 128]
        qcat[h, :, 128:] = jnp.where(half == (h % 2 == 0), pair, 0.0).astype(jnp.bfloat16)
    for c in loads[3:]:
        c.wait()
    def project(s):
        kv[s * 256 : (s + 1) * 256] = mm(keys[s, :, :RANK], wkv[...].reshape(RANK, 2048)).astype(jnp.bfloat16)

    project(SLOTS - 1)
    for d in range(1, SLOTS + 1):
        if d < SLOTS:

            @pl.when(me >= d)
            def _(d=d):
                send(d).wait_recv()
                hand(d).start()

        if d > 1:
            pl.when(me >= d - 1)(lambda d=d: handed(d - 1).wait_recv())
            project(SLOTS - d)
    save = pltpu.make_async_copy(kv, kv_out, kv_sem)
    save.start()

    def head(h, _):
        kn = kv[:, pl.ds(pl.multiple_of(h * 256, 256), 128)]
        v = kv[:, pl.ds(pl.multiple_of(h * 256 + 128, 128), 128)]
        rope = keys[:, :, RANK:].reshape(KEYS, 128)
        s = nt(qcat[h], jnp.concatenate([kn, rope], 1)) * ((NOPE + ROPE) ** -0.5) + bias[...]
        top = jnp.max(s, axis=1, keepdims=True)
        e = jnp.exp(s - top)
        den = jnp.sum(e, axis=1, keepdims=True)
        lse[h] = top + jnp.log(den)
        p = (e * (1.0 / den)).astype(jnp.bfloat16)
        att[:, pl.ds(pl.multiple_of(h * 128, 128), 128)] = mm(p, v).astype(jnp.bfloat16)
        return 0

    lax.fori_loop(0, 8, head, 0)
    loads[2].wait()

    def out(n, _):
        r = pl.ds(pl.multiple_of(n * 512, 512), 512)
        part[:, r] = nt(att[...], wo[r]).astype(jnp.bfloat16)
        return 0

    lax.fori_loop(0, 4, out, 0)
    swap = pltpu.make_async_remote_copy(
        src_ref=part, dst_ref=arrived, send_sem=cs, recv_sem=cr, device_id=(me, 1 - core), device_id_type=MESH
    )
    swap.start()
    swap.wait()
    m = tok[...].astype(jnp.float32) + (part[...].astype(jnp.float32) + arrived[...].astype(jnp.float32))
    middle[...] = m
    moe_low[...] = (m * root(m) * g_moe).astype(jnp.bfloat16)
    save.wait()
    trade.wait()
    for d in range(1, SLOTS):
        pl.when(me + d < 16)(lambda d=d: send(d).wait_send())
        pl.when(me >= d)(lambda d=d: hand(d).wait_send())


def att_fwd(tok, weights, trade, g_lat, cos, sin, bias, cid):
    low, f32, S, V = jnp.bfloat16, jnp.float32, pltpu.SemaphoreType.DMA, pltpu.VMEM
    any_, vmem = pl.BlockSpec(memory_space=pl.ANY), pl.BlockSpec(memory_space=pltpu.VMEM)
    shape = lambda kind, *s: jax.ShapeDtypeStruct(s, kind)
    rows, width = tok.shape
    pack = weights.shape[1]
    return pl.pallas_call(
        att_fwd_kernel,
        out_shape=[
            shape(f32, rows, width), shape(low, rows, width), shape(low, rows, width), shape(f32, rows, 640),
            shape(low, 8, rows, 256), shape(low, SLOTS, rows, 640), shape(low, KEYS, 2048), shape(f32, 8, rows, 1),
            shape(low, rows, 1024), shape(low, *trade.shape),
        ],
        in_specs=[vmem, any_, any_, any_] + [vmem] * 4,
        out_specs=[vmem] * 6 + [any_] + [vmem] * 2 + [any_],
        scratch_shapes=[
            V((KEYS, 2048), low), V((width, 1536), low), V((width, 1024), low), V((16, 32, 2048), low), V((width, 640), low),
            V((rows, width), low), V((rows, width), low), S((7,)), S, S((4,)), S((4,)), S((4,)), S((4,)), S, S,
            S((15,)), S((15,)), S,
        ],
        compiler_params=pltpu.CompilerParams(collective_id=cid, has_side_effects=True, vmem_limit_bytes=60 << 20),
        cost_estimate=pl.CostEstimate(flops=10**10, bytes_accessed=40 * 10**6, transcendentals=0),
    )(tok, weights.reshape(16, 4, 32, pack), weights, trade, g_lat, cos, sin, bias)


def att_bwd_kernel(
    w4, w2, home_in, trade_in, grad, middle, moe_low, wr, g_lat, kv_in,
    tok_in, normed_in, lat_raw_in, qcat_in, keys_in, lse_in, att_in, cos_in, sin_in, bias_in,
    tok_grad, packed, p4, trade_out,
    home,
    tok, normed, lat_raw, qcat, keys, lse, att, cos, sin, bias,
    kv, wq, wo, wkv, wlat, dmid, dnorm, dmid_low, d_att, dq, dqr, dkr, dk_out, dk_pair, dk_in, own_dk, part, arrived, d_keys,
    home_sem, as_, ar, ao, late_sem, w_sem, kv_sem, ks, kr, cs, cr, ps, pr, hs, hr, o_sem,
):
    me = lax.axis_index("dp")
    core = lax.axis_index("tensor")
    width = grad.shape[1]
    scale = (NOPE + ROPE) ** -0.5
    loads = [pltpu.make_async_copy(h, v, s) for h, v, s in slab_copies(w4, w2, wq, wo, wkv, wlat, w_sem)]
    stores = [pltpu.make_async_copy(v, h, s) for h, v, s in slab_copies(p4, packed, wq, wo, wkv, wlat, o_sem)]
    kv_load = pltpu.make_async_copy(kv_in, kv, kv_sem)
    late = [
        pltpu.make_async_copy(src, dst, late_sem.at[n])
        for n, (src, dst) in enumerate(
            (
                (att_in, att), (qcat_in, qcat), (keys_in, keys), (bias_in, bias), (lse_in, lse), (cos_in, cos),
                (sin_in, sin), (normed_in, normed), (lat_raw_in, lat_raw), (tok_in, tok),
            )
        )
    ]
    home_load = pltpu.make_async_copy(home_in.at[:, width:], home, home_sem)
    home_load.start()
    loads[0].start()
    loads[2].start()
    kv_load.start()
    for c in late:
        c.start()
    for n in (1, 3, 4, 5, 6):
        loads[n].start()
    bar = pltpu.get_barrier_semaphore()
    greet_all(me, core, bar)
    trade = Trade(
        lambda i: trade_in.at[:, pl.ds(pl.multiple_of(i * 128, 128), 128)], trade_out, me, core, as_, ar, ao
    )
    trade.start()
    loads[0].wait()
    g_att, g_moe = read_gains(wlat)
    home_load.wait()
    lane = lax.broadcasted_iota(jnp.int32, (256, 128), 1)

    logits = jnp.where(lane < 16, mm(moe_low[...], wr[...]), -jnp.inf)
    e = jnp.exp(logits - jnp.max(logits, axis=1, keepdims=True))
    router = e / jnp.sum(e, axis=1, keepdims=True)
    d_router = jnp.where(lane < 16, home[:, width:].astype(jnp.float32), 0.0)
    d_logits = (router * (d_router - jnp.sum(router * d_router, axis=1, keepdims=True))).astype(jnp.bfloat16)

    def norm_back(v, gain, dy):
        r = root(v)
        hat = v * r
        up = dy * gain
        return r * (up - hat * jnp.mean(up * hat, axis=1, keepdims=True)), dy * hat

    def one_lane(n):
        return (lane == n).astype(jnp.bfloat16)

    d_moe = home[:, :width].astype(jnp.float32) + nt(d_logits, wr[...])
    d_norm2, gain_rows = norm_back(middle[...], g_moe, d_moe)
    d_middle = grad[...].astype(jnp.float32) + d_norm2
    dmid[...] = d_middle
    dmid_low[...] = d_middle.astype(jnp.bfloat16)
    gains = gain_rows.astype(jnp.bfloat16)
    moved = pltpu.roll(d_logits.astype(jnp.float32), 64, 1).astype(jnp.bfloat16)
    small = tn(moe_low[...], moved) + tn(gains, one_lane(81))

    loads[2].wait()
    for c in late:
        c.wait()
    d_att[...] = mm(dmid_low[...], wo[...]).astype(jnp.bfloat16)

    def wo_rows(n, _):
        r = pl.ds(pl.multiple_of(n * 256, 256), 256)
        wo[r] = tn(dmid_low[:, r], att[...]).astype(jnp.bfloat16)
        return 0

    lax.fori_loop(0, width // 256, wo_rows, 0)
    stores[2].start()
    kv_load.wait()
    dkr[...] = jnp.zeros_like(dkr)
    dqr[...] = jnp.zeros_like(dqr)

    def head(h, _):
        cols = pl.ds(pl.multiple_of(h * 128, 128), 128)
        nope_at = pl.ds(pl.multiple_of(h * 256, 256), 128)
        value_at = pl.ds(pl.multiple_of(h * 256 + 128, 128), 128)
        pair = pl.ds(pl.multiple_of(h // 2 * 128, 128), 128)
        kc = jnp.concatenate([kv[:, nope_at], keys[:, :, RANK:].reshape(KEYS, 128)], 1)
        p = jnp.exp(nt(qcat[h], kc) * scale + bias[...] - lse[h])
        dv = tn(p.astype(jnp.bfloat16), d_att[:, cols])
        dp = nt(d_att[:, cols], kv[:, value_at])
        ds = (p * (dp - jnp.sum(p * dp, axis=1, keepdims=True))).astype(jnp.bfloat16)
        dqc = mm(ds, kc) * scale
        dkc = tn(ds, qcat[h]) * scale
        dq[:, cols] = dqc[:, :128].astype(jnp.bfloat16)
        dqr[:, pair] += jnp.where((lane < 64) == (h % 2 == 0), dqc[:, 128:], 0.0)
        kv[:, nope_at] = dkc[:, :128].astype(jnp.bfloat16)
        kv[:, value_at] = dv.astype(jnp.bfloat16)
        dkr[...] += dkc[:, 128:]
        return 0

    lax.fori_loop(0, 8, head, 0)
    for n in (3, 4, 5, 6):
        loads[n].wait()

    mine = pl.ds(pl.multiple_of(core * 128, 128), 128)
    others = pl.ds(pl.multiple_of((1 - core) * 128, 128), 128)

    def send(d, to):
        return pltpu.make_async_remote_copy(
            src_ref=dk_out.at[d - 1, mine], dst_ref=dk_in.at[d - 1], send_sem=ks.at[d - 1], recv_sem=kr.at[d - 1],
            device_id=(jnp.clip(to, 0, 15), core), device_id_type=MESH,
        )

    pair = pltpu.make_async_remote_copy(
        src_ref=dk_out.at[:, others], dst_ref=dk_pair, send_sem=ps, recv_sem=pr, device_id=(me, 1 - core), device_id_type=MESH
    )
    for s in range(SLOTS):
        r = slice(s * 256, (s + 1) * 256)
        d = SLOTS - 1 - s if s < SLOTS - 1 else SLOTS
        dk_out[d - 1, :, :RANK] = nt(kv[r], wkv[...].reshape(RANK, 2048)).astype(jnp.bfloat16)
        dk_out[d - 1, :, RANK:] = (dkr[r] + pltpu.roll(dkr[r], 64, 1)).astype(jnp.bfloat16)
    pair.start()
    dq[:, 1024:] = turned(dqr[...], cos[...], -sin[...]).astype(jnp.bfloat16)
    loads[1].wait()

    def normed_cols(n, _):
        r = pl.ds(pl.multiple_of(n * 512, 512), 512)
        v = nt(dq[...], wq[r])
        part[:, r] = v.astype(jnp.bfloat16)
        wq[r] = tn(normed[:, r], dq[...]).astype(jnp.bfloat16)
        return 0

    normed_cols(0, 0)
    pair.wait_recv()
    for d in range(1, SLOTS):
        dk_out[d - 1, mine] = dk_out[d - 1, mine] + dk_pair[d - 1]
        pl.when(me >= d)(lambda d=d: send(d, me - d).start())
    own_dk[...] = dk_out[SLOTS - 1, mine].astype(jnp.float32) + dk_pair[SLOTS - 1].astype(jnp.float32)
    lax.fori_loop(1, 4, normed_cols, 0)
    swap = pltpu.make_async_remote_copy(
        src_ref=part, dst_ref=arrived, send_sem=cs, recv_sem=cr, device_id=(me, 1 - core), device_id_type=MESH
    )
    swap.start()
    stores[1].start()
    latent_all = keys[:, :, :RANK].reshape(KEYS, RANK)
    for c in range(4):
        g = tn(latent_all, kv[:, c * 512 : (c + 1) * 512]).astype(jnp.bfloat16)
        wkv[:, :, c * 512 : (c + 1) * 512] = g.reshape(16, 32, 512)
        stores[3 + c].start()
    for d in range(1, SLOTS):

        @pl.when(me + d < 16)
        def _():
            send(d, me + d).wait_recv()
            own_dk[...] += dk_in[d - 1].astype(jnp.float32)

    d_keys[mine] = own_dk[...].astype(jnp.bfloat16)

    def half(rows):
        return pltpu.make_async_remote_copy(
            src_ref=d_keys.at[rows], dst_ref=d_keys.at[rows], send_sem=hs, recv_sem=hr,
            device_id=(me, 1 - core), device_id_type=MESH,
        )

    half(mine).start()
    swap.wait_recv()
    dnorm[...] = part[...].astype(jnp.float32) + arrived[...].astype(jnp.float32)
    half(others).wait_recv()

    d_first, lat_gain_rows = norm_back(lat_raw[:, :RANK], g_lat[...], d_keys[:, :RANK].astype(jnp.float32))
    d_second = turned(d_keys[:, RANK:].astype(jnp.float32), cos[:, :128], -sin[:, :128])
    d_second = jnp.where(lane < 64, d_second, 0.0)
    d_lat_low = jnp.concatenate([d_first, d_second], 1).astype(jnp.bfloat16)
    d_normed = dnorm[...] + nt(d_lat_low, wlat[...])
    d_norm1, att_gain_rows = norm_back(tok[...].astype(jnp.float32), g_att, d_normed)
    tok_grad[...] = dmid[...] + d_norm1
    small = small + tn(normed[...], d_lat_low[:, RANK:]) + tn(att_gain_rows.astype(jnp.bfloat16), one_lane(80))
    wlat[:, :RANK] = tn(normed[...], d_lat_low[:, :RANK]).astype(jnp.bfloat16)
    wlat[:, RANK:] = small.astype(jnp.bfloat16)
    lat_col = tn(lat_gain_rows.astype(jnp.bfloat16), one_lane(82))
    for b in range(16):
        r = slice(b * 128, b * 128 + 32)
        wlat[r, RANK:] = (small[r] + lat_col[b * 32 : (b + 1) * 32]).astype(jnp.bfloat16)
    stores[0].start()
    for c in stores:
        c.wait()
    trade.wait()
    for d in range(1, SLOTS):
        pl.when(me >= d)(lambda d=d: send(d, me - d).wait_send())
    pair.wait_send()
    swap.wait_send()
    half(mine).wait_send()


def att_bwd(
    weights, home, trade, grad, middle, moe_low, tok, normed, lat_raw, qcat, keys, kv, lse, att, wr, g_lat, cos, sin, bias, cid
):
    low, f32, S, V = jnp.bfloat16, jnp.float32, pltpu.SemaphoreType.DMA, pltpu.VMEM
    any_, vmem = pl.BlockSpec(memory_space=pl.ANY), pl.BlockSpec(memory_space=pltpu.VMEM)
    shape = lambda kind, *s: jax.ShapeDtypeStruct(s, kind)
    rows, width = tok.shape
    pack = weights.shape[1]
    return pl.pallas_call(
        att_bwd_kernel,
        out_shape=[shape(f32, rows, width), shape(low, width, pack - 512), shape(low, 16, 4, 32, 512), shape(low, 16, 384, 128)],
        in_specs=[any_] * 4 + [vmem] * 5 + [any_] * 11,
        out_specs=[vmem, any_, any_, any_],
        scratch_shapes=[
            V((rows, width + 128), low),
            V((rows, width), low), V((rows, width), low), V((rows, 640), f32), V((8, rows, 256), low), V((SLOTS, rows, 640), low),
            V((8, rows, 1), f32), V((rows, 1024), low), V((rows, 512), f32), V((rows, 512), f32), V((rows, KEYS), f32),
            V((KEYS, 2048), low), V((width, 1536), low), V((width, 1024), low), V((16, 32, 2048), low),
            V((width, 640), low), V((rows, width), f32), V((rows, width), f32), V((rows, width), low), V((rows, 1024), low),
            V((rows, 1536), low), V((rows, 512), f32), V((KEYS, 128), f32), V((SLOTS, rows, 640), low), V((SLOTS, rows // 2, 640), low),
            V((4, rows // 2, 640), low), V((rows // 2, 640), f32), V((rows, width), low), V((rows, width), low), V((rows, 640), low),
            S, S((15,)), S((15,)), S, S((10,)), S((7,)), S, S((4,)), S((4,)), S, S, S, S, S, S, S((7,)),
        ],
        compiler_params=pltpu.CompilerParams(collective_id=cid, has_side_effects=True, vmem_limit_bytes=60 << 20),
        cost_estimate=pl.CostEstimate(flops=25 * 10**9, bytes_accessed=70 * 10**6, transcendentals=0),
    )(
        weights.reshape(16, 4, 32, pack), weights, home, trade, grad, middle, moe_low, wr, g_lat, kv,
        tok, normed, lat_raw, qcat, keys, lse, att, cos, sin, bias,
    )


def my_half(v, rows):
    return lax.dynamic_slice_in_dim(v, lax.axis_index("tensor") * rows, rows, 0)


def row_halves(v):
    rows = v.shape[0] // 2
    return my_half(v, rows).reshape(2, rows // 2, v.shape[1])


def nope_first(w):
    heads = w.reshape(w.shape[0], -1, NOPE + ROPE)
    return jnp.concatenate(
        [heads[:, :, :NOPE].reshape(w.shape[0], -1), heads[:, :, NOPE:].reshape(w.shape[0], -1)], 1
    )


def heads_first(w):
    heads = w.shape[1] // (NOPE + ROPE)
    nope = w[:, : heads * NOPE].reshape(w.shape[0], heads, NOPE)
    rope = w[:, heads * NOPE :].reshape(w.shape[0], heads, ROPE)
    return jnp.concatenate([nope, rope], 2).reshape(w.shape[0], -1)


def shards_sixteen(
    tokens,
    out_grad,
    segments,
    routes,
    attn_gain,
    w_query,
    w_latent,
    latent_gain,
    w_keyval,
    w_out,
    moe_gain,
    w_router,
    shared_gate,
    shared_up,
    shared_down,
    expert_gate,
    routed_up_weight,
    expert_down,
):
    n_rows, width = tokens.shape
    dp_count = lax.axis_size("dp")
    dp_index = lax.axis_index("dp")
    seq_len = segments.shape[1]
    total = n_rows * dp_count
    hop_count = (WINDOW - 1) // n_rows + 1
    n_keys = (hop_count + 1) * n_rows
    experts = w_router.shape[1]
    capacity = 4 * n_rows * TOPK // (3 * experts)
    row_start = dp_index * n_rows
    seg_row = segments[0]
    depth = w_query.shape[0]
    q_width, o_width, kv_width = w_query.shape[1], w_out.shape[0], w_keyval.shape[1]
    kv_rows = w_keyval.shape[0]
    kv_cuts = depth // kv_rows
    kv_part = kv_width // kv_cuts
    lat_width = w_latent.shape[1]
    route_width = n_rows * TOPK // depth
    small = (lat_width + experts + 3 + route_width + 127) // 128 * 128

    gains = jnp.stack(
        [attn_gain, moe_gain, jnp.pad(latent_gain, (0, depth - kv_rows))], 1
    )
    packed = jnp.concatenate(
        [
            nope_first(w_query),
            w_out.T,
            w_latent,
            w_router,
            gains,
            routes.reshape(depth, route_width).astype(jnp.bfloat16),
            jnp.zeros((depth, small - lat_width - experts - 3 - route_width), jnp.bfloat16),
            w_keyval.reshape(kv_rows, kv_cuts, kv_part).transpose(1, 0, 2).reshape(depth, kv_part),
        ],
        1,
    )
    pack_width = packed.shape[1]
    weights, grad_all = ag16(
        [packed.reshape(2, depth // 2, pack_width), row_halves(out_grad)], (False, True), 1
    )
    weights = weights.reshape(width, pack_width)
    shared_part = shared_gate.shape[1] // dp_count
    shared_send = jnp.stack(
        [
            shared_gate.reshape(depth, dp_count, shared_part).transpose(1, 2, 0),
            shared_up.reshape(depth, dp_count, shared_part).transpose(1, 2, 0),
            shared_down.reshape(dp_count, shared_part, depth),
        ],
        1,
    )
    shared_send = jnp.pad(shared_send, ((0, 0), (0, 0), (0, 96 - shared_part), (0, 0)))
    at = q_width + o_width + lat_width
    wr_full = weights[:, at : at + experts]
    at += experts
    gain_latent = (
        weights[:, at + 2].reshape(dp_count, depth)[:, :kv_rows].reshape(-1).astype(jnp.float32)
    )

    all_routes = (
        weights[:, at + 3 : at + 3 + route_width].reshape(total, TOPK).astype(jnp.int32)
    )

    local_heads = q_width // (NOPE + ROPE)
    positions = (row_start + jnp.arange(n_rows, dtype=jnp.int32)).astype(jnp.float32)
    cos_tab, sin_tab = rope_tables(positions)
    cos_lanes, sin_lanes = jnp.tile(cos_tab, (1, 2 * local_heads)), jnp.tile(sin_tab, (1, 2 * local_heads))
    key_pos = row_start - hop_count * n_rows + jnp.arange(n_keys, dtype=jnp.int32)
    query_pos = row_start + jnp.arange(n_rows, dtype=jnp.int32)
    padded_seg = jnp.concatenate([jnp.full((hop_count * n_rows,), -1, jnp.int32), seg_row])
    key_seg = lax.dynamic_slice_in_dim(padded_seg, row_start, n_keys, 0)
    query_seg = lax.dynamic_slice_in_dim(seg_row, row_start, n_rows, 0)
    allowed = (key_pos[None, :] >= 0) & (key_pos[None, :] <= query_pos[:, None])
    allowed = (
        allowed
        & (query_pos[:, None] - key_pos[None, :] < WINDOW)
        & (query_seg[:, None] == key_seg[None, :])
    )

    bias = jnp.where(allowed, 0.0, -jnp.inf)
    middle, moe_low, normed_low, lat_raw, qcat, keys, kv, lse, attended_low, shared_all = att_fwd(
        tokens, weights, shared_send.reshape(dp_count, 3 * 96, depth), gain_latent[None], cos_lanes, sin_lanes, bias, 7
    )
    shared_all = shared_all.reshape(dp_count, 3, 96, depth)[:, :, :shared_part].transpose(1, 2, 0, 3)
    lead = jnp.pad(shared_all.reshape(3, shared_part, width), ((0, 0), (0, 128 - shared_part), (0, 0)))
    shared_in, shared_out = lead[:2].reshape(256, width), lead[2]
    (moe_all,) = ag16([row_halves(moe_low)], (True,), 3)
    chosen = jnp.any(all_routes == dp_index, axis=1).reshape(dp_count, n_rows)
    earlier = jnp.arange(n_rows)[:, None] < jnp.arange(n_rows)[None, :]
    rank = matmul(chosen.astype(jnp.bfloat16), earlier.astype(jnp.bfloat16)).astype(jnp.int32)
    pick = (
        (rank[:, None, :] == jnp.arange(capacity, dtype=jnp.int32)[None, :, None])
        & chosen[:, None, :]
    ).astype(jnp.bfloat16)

    slot_rows = dp_count * capacity
    moe_wr = jnp.pad(wr_full, ((0, 0), (0, 128 - experts)))
    home, rows_in, rows_grad, scaled_act, d_ea_low, d_eb_low, shared_grads = moe_call(
        moe_all.reshape(dp_count, n_rows, width),
        grad_all.reshape(dp_count, n_rows, width),
        pick,
        pick.transpose(0, 2, 1),
        expert_gate[0].T,
        routed_up_weight[0].T,
        expert_down[0],
        moe_wr,
        shared_in,
        shared_out,
        4,
    )[:7]
    home = home.reshape(n_rows, 2 * width + 128)
    result = (middle + home[:, :width].astype(jnp.float32)).astype(jnp.bfloat16)
    grad_down = matmul_tn(scaled_act, rows_grad)[None]
    grad_gate = matmul_tn(rows_in, d_ea_low)[None]
    grad_up = matmul_tn(rows_in, d_eb_low)[None]
    token_input_gradient, packed_grads, kv_grads, shared_home = att_bwd(
        weights, home, shared_grads, out_grad, middle, moe_low, tokens, normed_low, lat_raw, qcat, keys, kv, lse,
        attended_low, moe_wr, gain_latent[None], cos_lanes, sin_lanes, bias, 8
    )
    mine = rs16(
        packed_grads.reshape(dp_count, 2, depth // 2, pack_width - kv_part),
        kv_grads.reshape(dp_count, 2, depth // 2, kv_part),
        6,
    ).reshape(depth, pack_width)
    shared_home = shared_home.reshape(dp_count, 3, 128, depth)[:, :, :shared_part].astype(jnp.float32)
    grad_sgate = shared_home[:, 0].transpose(2, 0, 1).reshape(depth, -1)
    grad_sup = shared_home[:, 1].transpose(2, 0, 1).reshape(depth, -1)
    grad_sdown = shared_home[:, 2].reshape(-1, depth)
    out_wq = heads_first(mine[:, :q_width])
    at = q_width
    out_wo = mine[:, at : at + o_width].T
    at += o_width
    out_wlat = mine[:, at : at + lat_width]
    at += lat_width
    out_router = mine[:, at : at + experts]
    at += experts
    out_wkv = (
        mine[:, pack_width - kv_part :]
        .reshape(kv_cuts, kv_rows, kv_part)
        .transpose(1, 0, 2)
        .reshape(kv_rows, kv_width)
    )
    return (
        result,
        token_input_gradient,
        mine[:, at],
        out_wq,
        out_wlat,
        mine[:kv_rows, at + 2],
        out_wkv,
        out_wo,
        mine[:, at + 1],
        out_router,
        grad_sgate,
        grad_sup,
        grad_sdown,
        grad_gate,
        grad_up,
        grad_down,
    )


def shards_general(
    tokens,
    out_grad,
    segments,
    routes,
    attn_gain,
    w_query,
    w_latent,
    latent_gain,
    w_keyval,
    w_out,
    moe_gain,
    w_router,
    shared_gate,
    shared_up,
    shared_down,
    expert_gate,
    routed_up_weight,
    expert_down,
):
    n_rows = tokens.shape[0]
    model_width = tokens.shape[1]
    dp_count = lax.axis_size("dp")
    dp_index = lax.axis_index("dp")
    seq_len = segments.shape[1]
    seq_devs = seq_len // n_rows
    hop_count = (WINDOW - 1) // n_rows + 1
    n_keys = (hop_count + 1) * n_rows
    experts = w_router.shape[1]
    local_experts = expert_gate.shape[0]
    capacity = 4 * n_rows * TOPK // (3 * experts)
    slot_total = experts * capacity
    score_scale = (NOPE + ROPE) ** (-0.5)
    row_start = dp_index % seq_devs * n_rows
    seg_row = lax.dynamic_index_in_dim(segments, dp_index // seq_devs, 0, keepdims=False)
    gathered = (
        lax.all_gather(attn_gain, "dp", axis=0, tiled=True),
        lax.all_gather(w_query, "dp", axis=0, tiled=True),
        lax.all_gather(w_latent, "dp", axis=0, tiled=True),
        lax.all_gather(latent_gain, "dp", axis=0, tiled=True),
        lax.all_gather(w_keyval, "dp", axis=0, tiled=True),
        lax.all_gather(w_out, "dp", axis=1, tiled=True),
        lax.all_gather(moe_gain, "dp", axis=0, tiled=True),
        lax.all_gather(w_router, "dp", axis=0, tiled=True),
        lax.all_gather(shared_gate, "dp", axis=0, tiled=True),
        lax.all_gather(shared_up, "dp", axis=0, tiled=True),
        lax.all_gather(shared_down, "dp", axis=1, tiled=True),
    )
    (
        gain_attn,
        wq_full,
        wlat_full,
        gain_latent,
        wkv_full,
        wo_full,
        gain_moe,
        wr_full,
        sgate_full,
        sup_full,
        sdown_full,
    ) = gathered
    local_heads = wq_full.shape[1] // (NOPE + ROPE)
    positions = (row_start + jnp.arange(n_rows, dtype=jnp.int32)).astype(jnp.float32)
    cos_tab, sin_tab = rope_tables(positions)
    resid_in = tokens.astype(jnp.float32)
    normed, attn_norm_back = jax.vjp(rms_scale, resid_in, gain_attn.astype(jnp.float32))
    normed_low = normed.astype(jnp.bfloat16)

    def rope_queries(q_flat):
        shaped = q_flat.reshape(n_rows, local_heads, NOPE + ROPE)
        return jnp.concatenate(
            [shaped[..., :NOPE], rotate(shaped[..., NOPE:], cos_tab[:, None], sin_tab[:, None])], -1
        )

    queries, query_back = jax.vjp(rope_queries, matmul(normed_low, wq_full))
    query_low = queries.astype(jnp.bfloat16)

    def latent_piece(latent_raw, gain_vec):
        return (
            rms_scale(latent_raw[:, :RANK], gain_vec),
            rotate(latent_raw[:, RANK:], cos_tab, sin_tab),
        )

    (latent, key_rope), latent_back = jax.vjp(
        latent_piece, matmul(normed_low, wlat_full), gain_latent.astype(jnp.float32)
    )
    latent_low = latent.astype(jnp.bfloat16)
    rope_low = key_rope.astype(jnp.bfloat16)
    latent_parts = []
    rope_parts = []
    for distance in range(hop_count, 0, -1):
        moved_latent, moved_rope = passed_along((latent_low, rope_low), "dp", distance)
        latent_parts.append(moved_latent)
        rope_parts.append(moved_rope)
    keys_latent = jnp.concatenate(latent_parts + [latent_low], 0)
    keys_rope = jnp.concatenate(rope_parts + [rope_low], 0)
    keyval = (
        matmul(keys_latent, wkv_full).astype(jnp.bfloat16).reshape(n_keys, local_heads, NOPE + VDIM)
    )
    key_nope = keyval[..., :NOPE]
    values = keyval[..., NOPE:]
    key_pos = row_start - hop_count * n_rows + jnp.arange(n_keys, dtype=jnp.int32)
    query_pos = row_start + jnp.arange(n_rows, dtype=jnp.int32)
    padded_seg = jnp.concatenate([jnp.full((hop_count * n_rows,), -1, jnp.int32), seg_row])
    key_seg = lax.dynamic_slice_in_dim(padded_seg, row_start, n_keys, 0)
    query_seg = lax.dynamic_slice_in_dim(seg_row, row_start, n_rows, 0)
    allowed = (key_pos[None, :] >= 0) & (key_pos[None, :] <= query_pos[:, None])
    allowed = (
        allowed
        & (query_pos[:, None] - key_pos[None, :] < WINDOW)
        & (query_seg[:, None] == key_seg[None, :])
    )

    def masked_scores():
        nope_part = jnp.einsum(
            "qhd,khd->hqk", query_low[..., :NOPE], key_nope, preferred_element_type=jnp.float32
        )
        rope_part = jnp.einsum(
            "qhr,kr->hqk", query_low[..., NOPE:], keys_rope, preferred_element_type=jnp.float32
        )
        return jnp.where(allowed[None], score_scale * (nope_part + rope_part), -jnp.inf)

    scores = masked_scores()
    top_score = jnp.max(scores, axis=-1, keepdims=True)
    exp_scores = jnp.exp(scores - top_score)
    denom = jnp.sum(exp_scores, axis=-1, keepdims=True)
    attn_probs = exp_scores / denom
    log_total = top_score + jnp.log(denom)
    attended = jnp.einsum(
        "hqk,khv->qhv", attn_probs.astype(jnp.bfloat16), values, preferred_element_type=jnp.float32
    )
    attended_low = attended.astype(jnp.bfloat16).reshape(n_rows, local_heads * VDIM)
    attn_out = lax.psum(matmul(attended_low, wo_full).astype(jnp.bfloat16), "tensor").astype(
        jnp.float32
    )
    middle = resid_in + attn_out
    moe_normed, moe_norm_back = jax.vjp(rms_scale, middle, gain_moe.astype(jnp.float32))
    moe_low = moe_normed.astype(jnp.bfloat16)
    router, router_back = jax.vjp(
        lambda logit_vals: jax.nn.softmax(logit_vals, axis=-1), matmul(moe_low, wr_full)
    )
    expert_ids = jnp.arange(experts, dtype=jnp.int32)
    route_hot = (routes[:, :, None] == expert_ids[None, None, :]).astype(jnp.float32)
    gate_w = jnp.einsum("te,tke->tk", router, route_hot, precision=highest)
    flat_routes = routes.reshape(-1)
    assign_count = flat_routes.shape[0]
    flat_hot = (flat_routes[:, None] == expert_ids[None, :]).astype(jnp.int32)
    earlier = ranks_before(flat_hot)
    slot_in = jnp.sum(earlier * flat_hot, axis=1)
    target = flat_routes * capacity + slot_in
    assign_ids = jnp.arange(assign_count, dtype=jnp.int32)
    assign_of_slot = jnp.zeros((slot_total,), jnp.int32).at[target].set(assign_ids)
    slot_live = (
        jnp.zeros((slot_total,), jnp.bfloat16)
        .at[target]
        .set(jnp.ones((assign_count,), jnp.bfloat16))
    )
    send_rows = moe_low[assign_of_slot // TOPK] * slot_live[:, None]
    recv_rows = lax.all_to_all(
        send_rows.reshape(dp_count, local_experts * capacity, model_width),
        "dp",
        split_axis=0,
        concat_axis=0,
        tiled=True,
    )
    received_four_parts = recv_rows.reshape(dp_count, local_experts, capacity, model_width)
    exp_gate = jnp.einsum(
        "sjcd,jdf->sjcf", received_four_parts, expert_gate, preferred_element_type=jnp.float32
    )
    exp_up = jnp.einsum(
        "sjcd,jdf->sjcf", received_four_parts, routed_up_weight, preferred_element_type=jnp.float32
    )
    exp_act, exp_act_back = jax.vjp(gated_act, exp_gate, exp_up)
    exp_act_low = exp_act.astype(jnp.bfloat16)
    exp_result = jnp.einsum(
        "sjcf,jfd->sjcd", exp_act_low, expert_down, preferred_element_type=jnp.float32
    )
    returned = lax.all_to_all(
        exp_result.reshape(dp_count, local_experts * capacity, model_width).astype(jnp.bfloat16),
        "dp",
        split_axis=0,
        concat_axis=0,
        tiled=True,
    ).astype(jnp.float32)
    per_assign = returned.reshape(slot_total, model_width)[target].reshape(
        n_rows, TOPK, model_width
    )
    routed = jnp.einsum("tk,tkd->td", gate_w, per_assign, precision=highest)
    shared_a = matmul(moe_low, sgate_full)
    shared_b = matmul(moe_low, sup_full)
    shared_act, shared_back = jax.vjp(gated_act, shared_a, shared_b)
    shared_low = shared_act.astype(jnp.bfloat16)
    moe_out = lax.psum(
        (routed + matmul(shared_low, sdown_full)).astype(jnp.bfloat16), "tensor"
    ).astype(jnp.float32)
    result = (middle + moe_out).astype(jnp.bfloat16)
    grad_y = out_grad.astype(jnp.float32)
    grad_sdown = matmul_tn(shared_low, out_grad)
    d_shared_a, d_shared_b = shared_back(matmul_nt(out_grad, sdown_full))
    d_sa_low = d_shared_a.astype(jnp.bfloat16)
    d_sb_low = d_shared_b.astype(jnp.bfloat16)
    grad_sgate = matmul_tn(moe_low, d_sa_low)
    grad_sup = matmul_tn(moe_low, d_sb_low)
    d_moe = matmul_nt(d_sa_low, sgate_full) + matmul_nt(d_sb_low, sup_full)
    d_gate_part = jnp.einsum("td,tkd->tk", grad_y, per_assign, precision=highest)
    d_assign = (
        (gate_w[:, :, None] * grad_y[:, None, :])
        .astype(jnp.bfloat16)
        .reshape(assign_count, model_width)
    )
    send_grads = d_assign[assign_of_slot] * slot_live[:, None]
    recv_grads = lax.all_to_all(
        send_grads.reshape(dp_count, local_experts * capacity, model_width),
        "dp",
        split_axis=0,
        concat_axis=0,
        tiled=True,
    )
    recv_grads = recv_grads.reshape(dp_count, local_experts, capacity, model_width)
    expert_down_weight_gradient = jnp.einsum(
        "sjcf,sjcd->jfd", exp_act_low, recv_grads, preferred_element_type=jnp.float32
    )
    d_exp_act = jnp.einsum(
        "sjcd,jfd->sjcf", recv_grads, expert_down, preferred_element_type=jnp.float32
    )
    d_exp_gate, expert_up_act_gradient = exp_act_back(d_exp_act)
    d_egate_low = d_exp_gate.astype(jnp.bfloat16)
    expert_up_gradient_lowp = expert_up_act_gradient.astype(jnp.bfloat16)
    expert_gate_weight_gradient = jnp.einsum(
        "bmky,bmkx->myx", received_four_parts, d_egate_low, preferred_element_type=jnp.float32
    )
    expert_up_weight_gradient = jnp.einsum(
        "bmky,bmkx->myx",
        received_four_parts,
        expert_up_gradient_lowp,
        preferred_element_type=jnp.float32,
    )
    d_slots = jnp.einsum(
        "hteg,tmg->htem", d_egate_low, expert_gate, preferred_element_type=jnp.float32
    )
    d_slots = d_slots + jnp.einsum(
        "hteg,tmg->htem",
        expert_up_gradient_lowp,
        routed_up_weight,
        preferred_element_type=jnp.float32,
    )
    back_grads = lax.all_to_all(
        d_slots.reshape(dp_count, local_experts * capacity, model_width).astype(jnp.bfloat16),
        "dp",
        split_axis=0,
        concat_axis=0,
        tiled=True,
    ).astype(jnp.float32)
    d_moe = d_moe + jnp.sum(
        back_grads.reshape(slot_total, model_width)[target].reshape(n_rows, TOPK, model_width),
        axis=1,
    )
    d_moe, d_gate = (
        lax.psum(d_moe.astype(jnp.bfloat16), "tensor").astype(jnp.float32),
        lax.psum(d_gate_part.astype(jnp.bfloat16), "tensor").astype(jnp.float32),
    )
    d_router = jnp.einsum("tk,tke->te", d_gate, route_hot, precision=highest)
    (d_logits,) = router_back(d_router)
    d_logits_low = d_logits.astype(jnp.bfloat16)
    grad_router = matmul_tn(moe_low, d_logits_low)
    d_moe = d_moe + matmul_nt(d_logits_low, wr_full)
    d_mid_norm, grad_gain_moe = moe_norm_back(d_moe)
    d_middle = grad_y + d_mid_norm
    d_middle_low = d_middle.astype(jnp.bfloat16)
    grad_wout = matmul_tn(attended_low, d_middle_low)
    d_att_low = (
        matmul_nt(d_middle_low, wo_full).astype(jnp.bfloat16).reshape(n_rows, local_heads, VDIM)
    )
    again_probs = jnp.exp(masked_scores() - log_total)
    d_values = jnp.einsum(
        "hqk,qhv->khv",
        again_probs.astype(jnp.bfloat16),
        d_att_low,
        preferred_element_type=jnp.float32,
    )
    d_probs = jnp.einsum("qhv,khv->hqk", d_att_low, values, preferred_element_type=jnp.float32)
    d_scores = (
        again_probs * (d_probs - jnp.sum(d_probs * again_probs, axis=-1, keepdims=True))
    ).astype(jnp.bfloat16)
    d_query_nope = score_scale * jnp.einsum(
        "hqk,khd->qhd", d_scores, key_nope, preferred_element_type=jnp.float32
    )
    d_query_rope = score_scale * jnp.einsum(
        "hqk,kr->qhr", d_scores, keys_rope, preferred_element_type=jnp.float32
    )
    d_key_nope = score_scale * jnp.einsum(
        "hqk,qhd->khd", d_scores, query_low[..., :NOPE], preferred_element_type=jnp.float32
    )
    d_key_rope = score_scale * jnp.einsum(
        "hqk,qhr->kr", d_scores, query_low[..., NOPE:], preferred_element_type=jnp.float32
    )
    (d_q_raw,) = query_back(jnp.concatenate([d_query_nope, d_query_rope], -1))
    d_q_low = d_q_raw.astype(jnp.bfloat16)
    grad_wq = matmul_tn(normed_low, d_q_low)
    d_normed = matmul_nt(d_q_low, wq_full)
    d_kv_low = (
        jnp.concatenate([d_key_nope, d_values], -1)
        .astype(jnp.bfloat16)
        .reshape(n_keys, local_heads * (NOPE + VDIM))
    )
    grad_wkv = matmul_tn(keys_latent, d_kv_low)
    d_keys_latent = matmul_nt(d_kv_low, wkv_full)
    own_latent = d_keys_latent[hop_count * n_rows :]
    own_rope = d_key_rope[hop_count * n_rows :]
    for distance in range(hop_count, 0, -1):
        block_index = hop_count - distance
        lower = block_index * n_rows
        home_latent, home_rope = (
            passed_along(
                d_keys_latent[lower : lower + n_rows].astype(jnp.bfloat16), "dp", -distance
            ).astype(jnp.float32),
            passed_along(
                d_key_rope[lower : lower + n_rows].astype(jnp.bfloat16), "dp", -distance
            ).astype(jnp.float32),
        )
        own_latent = own_latent + home_latent
        own_rope = own_rope + home_rope
    d_normed, own_latent, own_rope = (
        lax.psum(d_normed.astype(jnp.bfloat16), "tensor").astype(jnp.float32),
        lax.psum(own_latent.astype(jnp.bfloat16), "tensor").astype(jnp.float32),
        lax.psum(own_rope.astype(jnp.bfloat16), "tensor").astype(jnp.float32),
    )
    d_latent_raw, grad_gain_latent = latent_back((own_latent, own_rope))
    d_latent_low = d_latent_raw.astype(jnp.bfloat16)
    grad_wlat = matmul_tn(normed_low, d_latent_low)
    d_normed = d_normed + matmul_nt(d_latent_low, wlat_full)
    d_tokens_norm, grad_gain_attn = attn_norm_back(d_normed)
    token_input_gradient = d_middle + d_tokens_norm
    reduced_result = tuple(
        (
            lax.psum_scatter(grad_gain_attn, "dp", scatter_dimension=0, tiled=True),
            lax.psum_scatter(grad_wq, "dp", scatter_dimension=0, tiled=True),
            lax.psum_scatter(grad_wlat, "dp", scatter_dimension=0, tiled=True),
            lax.psum_scatter(grad_gain_latent, "dp", scatter_dimension=0, tiled=True),
            lax.psum_scatter(grad_wkv, "dp", scatter_dimension=0, tiled=True),
            lax.psum_scatter(grad_wout, "dp", scatter_dimension=1, tiled=True),
            lax.psum_scatter(grad_gain_moe, "dp", scatter_dimension=0, tiled=True),
            lax.psum_scatter(grad_router, "dp", scatter_dimension=0, tiled=True),
            lax.psum_scatter(grad_sgate, "dp", scatter_dimension=0, tiled=True),
            lax.psum_scatter(grad_sup, "dp", scatter_dimension=0, tiled=True),
            lax.psum_scatter(grad_sdown, "dp", scatter_dimension=1, tiled=True),
        )
    )
    return (
        (result, token_input_gradient)
        + reduced_result
        + (expert_gate_weight_gradient, expert_up_weight_gradient, expert_down_weight_gradient)
    )


def solution(mesh):
    placed = (
        P("dp", None),
        P("dp", None),
        P(),
        P("dp", None),
        P("dp"),
        P("dp", "tensor"),
        P("dp", None),
        P("dp"),
        P("dp", "tensor"),
        P("tensor", "dp"),
        P("dp"),
        P("dp", None),
        P("dp", "tensor"),
        P("dp", "tensor"),
        P("tensor", "dp"),
        P("dp", None, "tensor"),
        P("dp", None, "tensor"),
        P("dp", "tensor", None),
    )
    sixteen = mesh.shape["dp"] == 16 and mesh.shape["tensor"] == 2

    def body(*args):
        fits_sixteen = sixteen and args[2].shape[0] == 1 and args[15].shape[0] == 1 and args[0].shape[0] == 256
        return (shards_sixteen if fits_sixteen else shards_general)(*args)

    return jax.shard_map(
        body,
        mesh=mesh,
        in_specs=placed,
        out_specs=(
            P("dp", None),
            P("dp", None),
            P("dp"),
            P("dp", "tensor"),
            P("dp", None),
            P("dp"),
            P("dp", "tensor"),
            P("tensor", "dp"),
            P("dp"),
            P("dp", None),
            P("dp", "tensor"),
            P("dp", "tensor"),
            P("tensor", "dp"),
            P("dp", None, "tensor"),
            P("dp", None, "tensor"),
            P("dp", "tensor", None),
        ),
        check_vma=False,
    )
```

```python
import functools
import math

import jax
import jax.numpy as jnp
from jax import lax
from jax.experimental import pallas as pl
from jax.experimental.pallas import tpu as pltpu
from jax.sharding import PartitionSpec as P

NOPE = 128
ROPE = 64
VDIM = 128
RANK = 512
TOPK = 6
WINDOW = 1024


eps_norm = 1e-06
highest = lax.Precision.HIGHEST


def passed_along(value, axis, steps):
    count = lax.axis_size(axis)
    leading, last = (max(0, -steps), min(count, count - steps))
    return lax.ppermute(value, axis, [(source, source + steps) for source in range(leading, last)])


def rms_scale(values, gain_vec):
    inv_root = lax.rsqrt(jnp.mean(values * values, axis=-1, keepdims=True) + eps_norm)
    return values * inv_root * gain_vec


def rope_tables(positions):
    half_width = ROPE // 2
    frequency = jnp.exp(
        -jnp.arange(half_width, dtype=jnp.float32) * (2.0 * math.log(10000.0) / ROPE)
    )
    angles = positions[:, None] * frequency[None, :]
    return (jnp.cos(angles), jnp.sin(angles))


def rotate(values, cos_tab, sin_tab):
    half_width = values.shape[-1] // 2
    first_half = values[..., :half_width]
    second = values[..., half_width:]
    return jnp.concatenate(
        [first_half * cos_tab - second * sin_tab, second * cos_tab + first_half * sin_tab], axis=-1
    )


def gated_act(gate_a, up_b):
    return jax.nn.silu(gate_a) * up_b


def matmul(left_mat, right_mat):
    return jnp.dot(left_mat, right_mat, preferred_element_type=jnp.float32)


def matmul_nt(left_mat, right_mat):
    return lax.dot_general(
        left_mat, right_mat, (((1,), (1,)), ((), ())), preferred_element_type=jnp.float32
    )


def matmul_tn(left_mat, right_mat):
    return lax.dot_general(
        left_mat, right_mat, (((0,), (0,)), ((), ())), preferred_element_type=jnp.float32
    )


def ranks_before(hot):
    count = hot.shape[0]
    below = jnp.arange(count)[:, None] > jnp.arange(count)[None, :]
    return matmul(below.astype(jnp.bfloat16), hot.astype(jnp.bfloat16)).astype(jnp.int32)


MESH = pl.DeviceIdType.MESH


def plane_at(z, k):
    edge = jnp.where(z >= 2, 3 - z, z)
    near = jnp.where(k == 0, edge, jnp.where(k == 1, 1 - edge, k))
    return jnp.where(z >= 2, 3 - near, near)


def ag_kernel(kinds, cuts, *refs):
    n = len(kinds)
    ins, outs, lands, sems = refs[:n], refs[n : 2 * n], refs[2 * n : 3 * n], refs[3 * n :]
    me = lax.axis_index("dp")
    core = lax.axis_index("tensor")
    z = me // 4
    y = (me // 2) % 2
    x = me % 2
    xn = z * 4 + y * 2 + (1 - x)
    yn = z * 4 + (1 - y) * 2 + x
    up = jnp.minimum(z + 1, 3) * 4 + y * 2 + x
    dn = jnp.maximum(z - 1, 0) * 4 + y * 2 + x
    bar = pltpu.get_barrier_semaphore()

    def sig(d, c):
        pl.semaphore_signal(bar, inc=1, device_id=(d, c), device_id_type=MESH)

    sig(xn, core)
    sig(yn, core)
    sig(me, 1 - core)
    pl.when(z < 3)(lambda: sig(up, core))
    pl.when(z > 0)(lambda: sig(dn, core))

    def rc(src, dst, ss, rs, dev, c):
        return pltpu.make_async_remote_copy(
            src_ref=src, dst_ref=dst, send_sem=ss, recv_sem=rs, device_id=(dev, c), device_id_type=MESH
        )

    class Part:
        def __init__(self, at, rows):
            self.share = kinds[at]
            self.x, self.o, self.hbm = ins[at], lands[at], outs[at]
            self.rows = rows
            self.zs, self.zr, self.xs, self.xr, self.ys, self.yr, self.cs, self.cr, self.own, self.out = sems[20 * at + 10 : 20 * at + 20]
            self.slot = core if self.share else 0
            self.copy = pltpu.make_async_copy(self.x.at[:, self.rows], self.whole(me), self.own)

        def whole(self, b):
            return self.o.at[b, self.slot, :, self.rows]

        def z_(self, zp, dev, s):
            b = zp * 4 + y * 2 + x
            return rc(self.whole(b), self.whole(b), self.zs.at[s], self.zr.at[zp], dev, core)

        def x_(self, j, b, half, zp):
            r = self.o.at[b, self.slot, half, self.rows]
            return rc(r, r, self.xs.at[zp, j], self.xr.at[zp, j], xn, core)

        def y_(self, j, b, half, zp):
            r = self.o.at[b, self.slot, half, self.rows]
            return rc(r, r, self.ys.at[zp, j], self.yr.at[zp, j], yn, core)

        def twin(self, b):
            return rc(self.whole(b), self.whole(b), self.cs.at[b], self.cr.at[b], me, 1 - core)

        def first(self, k):
            zp = plane_at(z, k)
            b = zp * 4 + y * 2 + x
            if k > 0:
                self.z_(zp, up, 0).wait_recv()
            pl.when((zp <= z) & (z < 3))(lambda: self.z_(zp, up, zp).start())
            pl.when((zp >= z) & (z > 0))(lambda: self.z_(zp, dn, 4 + zp).start())
            self.x_(0, b, 0, zp).start()
            self.y_(0, b, 1, zp).start()
            self.y_(1, b, 0, zp).start()
            self.x_(1, b, 1, zp).start()
            if self.share:
                self.twin(b).start()

        def second(self, k):
            zp = plane_at(z, k)
            bx = zp * 4 + y * 2 + (1 - x)
            by = zp * 4 + (1 - y) * 2 + x
            self.x_(0, bx, 0, zp).wait_recv()
            self.y_(2, bx, 0, zp).start()
            self.y_(0, by, 1, zp).wait_recv()
            self.x_(2, by, 1, zp).start()
            self.x_(1, bx, 1, zp).wait_recv()
            self.y_(1, by, 0, zp).wait_recv()
            if self.share:
                self.twin(bx).start()
                self.twin(by).start()

        def third(self, k):
            zp = plane_at(z, k)
            bd = zp * 4 + (1 - y) * 2 + (1 - x)
            self.y_(2, bd, 0, zp).wait_recv()
            self.x_(2, bd, 1, zp).wait_recv()
            if self.share:
                self.twin(bd).start()

        def save(self, k):
            at = pl.ds(plane_at(z, k) * 4, 4)
            return pltpu.make_async_copy(
                self.o.at[at, :, :, self.rows], self.hbm.at[at, :, :, self.rows], self.out.at[k]
            )

        def fourth(self, k):
            if self.share:
                for q in range(4):
                    b = plane_at(z, k) * 4 + q
                    src, dst = self.o.at[b, core, :, self.rows], self.o.at[b, 1 - core, :, self.rows]
                    rc(src, dst, self.cs.at[b], self.cr.at[b], me, 1 - core).wait_recv()
            self.save(k).start()

        def end(self):
            for k in range(4):
                self.save(k).wait()
                pl.when((k <= z) & (z < 3))(lambda k=k: self.z_(k, up, k).wait_send())
                pl.when((k >= z) & (z > 0))(lambda k=k: self.z_(k, dn, 4 + k).wait_send())
                for j in range(3):
                    self.x_(j, 0, 0, k).wait_send()
                    self.y_(j, 0, 0, k).wait_send()
            if self.share:
                for b in range(16):
                    self.twin(b).wait_send()

    class Cross:
        def __init__(self, at, rows):
            self.share = kinds[at]
            self.x, self.o, self.hbm = ins[at], lands[at], outs[at]
            self.rows = rows
            self.fs, self.fr, self.zs, self.zr, self.ls, self.lr, self.cs, self.cr, self.own, self.out = sems[20 * at : 20 * at + 10]
            self.slot = core if self.share else 0
            self.copy = pltpu.make_async_copy(self.x.at[:, rows], self.o.at[me, self.slot, :, rows], self.own)

        def ref(self, b, half):
            return self.o.at[b, self.slot, half, self.rows]

        def block(self, zp, half, p):
            if half == 0:
                return zp * 4 + y * 2 + (x if p == 0 else 1 - x)
            return zp * 4 + (y if p == 0 else 1 - y) * 2 + x

        def hop(self, half):
            r = self.ref(me, half)
            return rc(r, r, self.fs.at[half], self.fr.at[half], xn if half == 0 else yn, core)

        def line(self, zp, half, p, d):
            r = self.ref(self.block(zp, half, p), half)
            return rc(r, r, self.zs.at[d, zp, half, p], self.zr.at[zp, half, p], up if d == 0 else dn, core)

        def last(self, zp, half, p):
            r = self.ref(self.block(zp, half, p), half)
            return rc(r, r, self.ls.at[zp, half, p], self.lr.at[zp, half, p], yn if half == 0 else xn, core)

        def twin(self, b, half):
            r = self.ref(b, half)
            return rc(r, r, self.cs.at[b, half], self.cr.at[b, half], me, 1 - core)

        def pass_on(self, zp, half, p):
            pl.when((zp <= z) & (z < 3))(lambda: self.line(zp, half, p, 0).start())
            pl.when((zp >= z) & (z > 0))(lambda: self.line(zp, half, p, 1).start())
            self.last(zp, half, p).start()
            if self.share:
                self.twin(self.block(zp, half, p), half).start()

        def first(self, k):
            zp = plane_at(z, k)
            if k == 0:
                for half in range(2):
                    self.hop(half).start()
                for half in range(2):
                    self.pass_on(zp, half, 0)
                for half in range(2):
                    self.hop(half).wait_recv()
                    self.pass_on(zp, half, 1)
            else:
                for p in range(2):
                    for half in range(2):
                        self.line(zp, half, p, 0).wait_recv()
                        self.pass_on(zp, half, p)

        def second(self, k):
            pass

        def third(self, k):
            zp = plane_at(z, k)
            for p in range(2):
                for half in range(2):
                    self.last(zp, half, p).wait_recv()
                    if self.share:
                        far = zp * 4 + (1 - y) * 2 + (x if p == 0 else 1 - x)
                        if half == 1:
                            far = zp * 4 + (y if p == 0 else 1 - y) * 2 + (1 - x)
                        self.twin(far, half).start()

        def save(self, k):
            at = pl.ds(plane_at(z, k) * 4, 4)
            return pltpu.make_async_copy(
                self.o.at[at, :, :, self.rows], self.hbm.at[at, :, :, self.rows], self.out.at[k]
            )

        def fourth(self, k):
            if self.share:
                for q in range(4):
                    b = plane_at(z, k) * 4 + q
                    for half in range(2):
                        src, dst = self.o.at[b, core, half, self.rows], self.o.at[b, 1 - core, half, self.rows]
                        rc(src, dst, self.cs.at[b, half], self.cr.at[b, half], me, 1 - core).wait_recv()
            self.save(k).start()

        def end(self):
            for half in range(2):
                self.hop(half).wait_send()
            for k in range(4):
                self.save(k).wait()
                for half in range(2):
                    for p in range(2):
                        pl.when((k <= z) & (z < 3))(lambda k=k, h=half, p=p: self.line(k, h, p, 0).wait_send())
                        pl.when((k >= z) & (z > 0))(lambda k=k, h=half, p=p: self.line(k, h, p, 1).wait_send())
                        self.last(k, half, p).wait_send()
            if self.share:
                for b in range(16):
                    for half in range(2):
                        self.twin(b, half).wait_send()

    groups = []
    for at in range(n):
        height = ins[at].shape[1]
        group = [Cross(at, pl.ds(0, cuts[at]))] if cuts[at] > 0 else []
        if cuts[at] < height:
            group.append(Part(at, pl.ds(cuts[at], height - cuts[at])))
        groups.append(group)
    parts = [p for g in groups for p in g]
    for p in parts:
        p.copy.start()
    pl.semaphore_wait(bar, 3 + (z < 3).astype(jnp.int32) + (z > 0).astype(jnp.int32))
    for p in parts:
        p.copy.wait()
    turns = [(p, k) for k in range(4) for p in parts]
    lag = len(parts)
    for t in range(len(turns) + lag):
        if t < len(turns):
            turns[t][0].first(turns[t][1])
        if t >= lag:
            turns[t - lag][0].second(turns[t - lag][1])
    for p, k in turns:
        p.third(k)
        if not p.share:
            p.fourth(k)
    for p, k in turns:
        if p.share:
            p.fourth(k)
    for p in parts:
        p.end()


def ag16(arrays, kinds, cid, cuts=None):
    S = pltpu.SemaphoreType.DMA
    any_ = pl.BlockSpec(memory_space=pl.ANY)
    cuts = cuts or tuple(v.shape[1] // 2 for v in arrays)
    counts = (
        ((2,), (2,), (2, 4, 2, 2), (4, 2, 2), (4, 2, 2), (4, 2, 2), (16, 2), (16, 2), (), (4,))
        + ((8,), (4,), (4, 3), (4, 3), (4, 3), (4, 3), (16,), (16,), (), (4,))
    )
    shapes = [(16, 2 if share else 1) + v.shape for v, share in zip(arrays, kinds)]
    return pl.pallas_call(
        functools.partial(ag_kernel, kinds, cuts),
        out_shape=[jax.ShapeDtypeStruct(s, v.dtype) for s, v in zip(shapes, arrays)],
        in_specs=[any_] * len(arrays),
        out_specs=[any_] * len(arrays),
        scratch_shapes=[pltpu.VMEM(s, v.dtype) for s, v in zip(shapes, arrays)]
        + [S(s) for _ in arrays for s in counts],
        compiler_params=pltpu.CompilerParams(collective_id=cid, has_side_effects=True, vmem_limit_bytes=60 << 20),
    )(*arrays)


def add_into(dst, src):
    def step(i, _):
        r = pl.ds(pl.multiple_of(i * 16, 16), 16)
        dst[r] = dst[r] + src[r]
        return 0

    lax.fori_loop(0, dst.shape[0] // 16, step, 0)


def rs_kernel(a_ref, b_ref, o_ref, own, fr, zr, lr, yr, xr, z2r, lsem, fs, frs, zs, zrs, ls, lrs, xs, xrs, ys, yrs, z2s, z2rs):
    me = lax.axis_index("dp")
    core = lax.axis_index("tensor")
    z = me // 4
    y = (me // 2) % 2
    x = me % 2
    xn = z * 4 + y * 2 + (1 - x)
    yn = z * 4 + (1 - y) * 2 + x
    up = jnp.minimum(z + 1, 3) * 4 + y * 2 + x
    dn = jnp.maximum(z - 1, 0) * 4 + y * 2 + x
    wide = a_ref.shape[3]
    cut = fr.shape[3]
    crossing, rest = pl.ds(0, cut), pl.ds(cut, own.shape[2] - cut)

    def rc(src, dst, ss, rs, dev):
        return pltpu.make_async_remote_copy(
            src_ref=src, dst_ref=dst, send_sem=ss, recv_sem=rs, device_id=(dev, core), device_id_type=MESH
        )

    def loads(zp):
        at = pl.ds(zp * 4, 4)
        return [
            pltpu.make_async_copy(a_ref.at[at], own.at[at, :, :, 0:wide], lsem.at[zp, 0]),
            pltpu.make_async_copy(b_ref.at[at], own.at[at, :, :, wide:], lsem.at[zp, 1]),
        ]

    for k in range(4):
        for c in loads(plane_at(z, 3 - k)):
            c.start()
    bar = pltpu.get_barrier_semaphore()

    def sig(d):
        pl.semaphore_signal(bar, inc=1, device_id=(d, core), device_id_type=MESH)

    sig(xn)
    sig(yn)
    pl.when(z < 3)(lambda: sig(up))
    pl.when(z > 0)(lambda: sig(dn))
    pl.semaphore_wait(bar, 2 + (z < 3).astype(jnp.int32) + (z > 0).astype(jnp.int32))

    def blk(zp, yy, xx):
        return zp * 4 + yy * 2 + xx

    def place(zp, half, p):
        if half == 0:
            return blk(zp, y, x if p == 0 else 1 - x)
        return blk(zp, y if p == 0 else 1 - y, x)

    def hop(zp, half, p):
        b = blk(zp, 1 - y, x if p == 0 else 1 - x) if half == 0 else blk(zp, y if p == 0 else 1 - y, 1 - x)
        return rc(
            own.at[b, half, crossing], fr.at[zp, half, p], fs.at[zp, half, p], frs.at[zp, half, p], yn if half == 0 else xn
        )

    def line(zp, half, p, dev, slot):
        b = place(zp, half, p)
        return rc(own.at[b, half, crossing], zr.at[slot, half, p], zs.at[zp, half, p], zrs.at[slot, half, p], dev)

    def last(half):
        b = place(z, half, 1)
        return rc(own.at[b, half, crossing], lr.at[half], ls.at[half], lrs.at[half], xn if half == 0 else yn)

    def y_(j, b, half, zp):
        return rc(own.at[b, half, rest], yr.at[zp, j], ys.at[zp, j], yrs.at[zp, j], yn)

    def x_(j, b, half, zp):
        return rc(own.at[b, half, rest], xr.at[zp, j], xs.at[zp, j], xrs.at[zp, j], xn)

    def zc(zp, dev, d):
        return rc(own.at[zp * 4 + y * 2 + x, :, rest], z2r.at[d, zp], z2s.at[zp], z2rs.at[d, zp], dev)

    def s1(k):
        zp = plane_at(z, 3 - k)
        for c in loads(zp):
            c.wait()
        for p in range(2):
            for half in range(2):
                hop(zp, half, 1 - p).start()
        y_(0, blk(zp, 1 - y, 1 - x), 0, zp).start()
        x_(0, blk(zp, 1 - y, 1 - x), 1, zp).start()
        y_(1, blk(zp, 1 - y, x), 0, zp).start()
        x_(1, blk(zp, y, 1 - x), 1, zp).start()

    def arrive(zp, half, p, slot):
        line(zp, half, p, me, slot).wait_recv()
        add_into(own.at[place(zp, half, p), half, crossing], zr.at[slot, half, p])

    def s2(k):
        zp = plane_at(z, 3 - k)
        for p in (1, 0):
            for half in range(2):
                hop(zp, half, p).wait_recv()
                add_into(own.at[place(zp, half, p), half, crossing], fr.at[zp, half, p])
                pl.when((zp <= z) & (z < 3))(lambda h=half, p=p: arrive(zp, h, p, jnp.where(zp == z, 4, zp)))
                pl.when((zp >= z) & (z > 0))(lambda h=half, p=p: arrive(zp, h, p, zp))
                pl.when(zp < z)(lambda h=half, p=p: line(zp, h, p, dn, jnp.where(zp == z - 1, 4, zp)).start())
                pl.when(zp > z)(lambda h=half, p=p: line(zp, h, p, up, zp).start())
                if k == 3 and p == 1:
                    last(half).start()
        mine = blk(zp, y, x)
        y_(0, blk(zp, 1 - y, 1 - x), 0, zp).wait_recv()
        add_into(own.at[blk(zp, y, 1 - x), 0, rest], yr.at[zp, 0])
        x_(2, blk(zp, y, 1 - x), 0, zp).start()
        x_(0, blk(zp, 1 - y, 1 - x), 1, zp).wait_recv()
        add_into(own.at[blk(zp, 1 - y, x), 1, rest], xr.at[zp, 0])
        y_(2, blk(zp, 1 - y, x), 1, zp).start()
        y_(1, blk(zp, 1 - y, x), 0, zp).wait_recv()
        add_into(own.at[mine, 0, rest], yr.at[zp, 1])
        x_(1, blk(zp, y, 1 - x), 1, zp).wait_recv()
        add_into(own.at[mine, 1, rest], xr.at[zp, 1])

    def s3(k):
        zp = plane_at(z, 3 - k)
        mine = blk(zp, y, x)
        x_(2, blk(zp, y, 1 - x), 0, zp).wait_recv()
        add_into(own.at[mine, 0, rest], xr.at[zp, 2])
        y_(2, blk(zp, 1 - y, x), 1, zp).wait_recv()
        add_into(own.at[mine, 1, rest], yr.at[zp, 2])

        def arrived(d):
            zc(zp, me, d).wait_recv()
            add_into(own.at[mine, 0, rest], z2r.at[d, zp, 0])
            add_into(own.at[mine, 1, rest], z2r.at[d, zp, 1])

        pl.when((zp <= z) & (z < 3))(lambda: arrived(1))
        pl.when((zp >= z) & (z > 0))(lambda: arrived(0))
        pl.when(zp < z)(lambda: zc(zp, dn, 1).start())
        pl.when(zp > z)(lambda: zc(zp, up, 0).start())

    s1(0)
    s1(1)
    s2(0)
    s1(2)
    s2(1)
    s3(0)
    s1(3)
    s2(2)
    s3(1)
    s2(3)
    s3(2)
    s3(3)
    for half in range(2):
        last(half).wait_recv()
        add_into(own.at[me, half, crossing], lr.at[half])
    for a in range(2):

        def row(i, _):
            r = pl.ds(pl.multiple_of(i * 16, 16), 16)
            o_ref[a, r] = own[me, a, r].astype(jnp.float32)
            return 0

        lax.fori_loop(0, o_ref.shape[1] // 16, row, 0)
    for half in range(2):
        last(half).wait_send()
    for k in range(4):
        for half in range(2):
            for p in range(2):
                hop(k, half, p).wait_send()
                pl.when(k != z)(lambda k=k, h=half, p=p: line(k, h, p, me, 0).wait_send())
        for j in range(3):
            x_(j, 0, 0, k).wait_send()
            y_(j, 0, 0, k).wait_send()
        pl.when(k != z)(lambda k=k: zc(k, up, 0).wait_send())


def rs16(a, b, cid):
    S = pltpu.SemaphoreType.DMA
    high, total = a.shape[2], a.shape[3] + b.shape[3]
    blkshape = (2, high, total)
    cross, half = (high // 2, total), (high - high // 2, total)
    V = lambda s: pltpu.VMEM(s, a.dtype)
    return pl.pallas_call(
        rs_kernel,
        out_shape=jax.ShapeDtypeStruct(blkshape, jnp.float32),
        in_specs=[pl.BlockSpec(memory_space=pl.ANY)] * 2,
        out_specs=pl.BlockSpec(memory_space=pltpu.VMEM),
        scratch_shapes=[
            V((16,) + blkshape), V((4, 2, 2) + cross), V((5, 2, 2) + cross), V((2,) + cross),
            V((4, 3) + half), V((4, 3) + half), V((2, 4, 2) + half),
            S((4, 2)), S((4, 2, 2)), S((4, 2, 2)), S((4, 2, 2)), S((5, 2, 2)), S((2,)), S((2,)),
            S((4, 3)), S((4, 3)), S((4, 3)), S((4, 3)), S((4,)), S((2, 4)),
        ],
        compiler_params=pltpu.CompilerParams(collective_id=cid, has_side_effects=True, vmem_limit_bytes=60 << 20),
    )(a, b)


def nt(a, b):
    return lax.dot_general(a, b, (((1,), (1,)), ((), ())), preferred_element_type=jnp.float32)


def tn(a, b):
    return lax.dot_general(a, b, (((0,), (0,)), ((), ())), preferred_element_type=jnp.float32)


def mm(a, b):
    return jnp.dot(a, b, preferred_element_type=jnp.float32)


def gate_parts(a, b, dc):
    s = 1.0 / (1.0 + jnp.exp(-a))
    act = a * s
    return act * b, dc * b * (s * (1.0 + a * (1.0 - s))), dc * act


def moe_kernel(
    moe, grd, pick, pick_t, wg_in, wu_in, wd_in, wr, sgu, sdn,
    o_out, r_out, rg_out, act_out, da_out, db_out, sg_out, yr, xr, zr,
    sg_sum, wg, wu, wd, own, sib, sibr, stage, xb, gb, pk, pt, rr, rg, ly, ld, ry, rd, acts, das, dbs, dgs,
    w_sem, in_sem, out_sem, st_sem, free, cs, cr, xs, xrs, ys, yrs, zs, zrs, fs, fr,
):
    me = lax.axis_index("dp")
    core = lax.axis_index("tensor")
    other = 1 - core
    z = me // 4
    y = (me // 2) % 2
    x = me % 2
    xn = z * 4 + y * 2 + (1 - x)
    yn = z * 4 + (1 - y) * 2 + x
    up = jnp.minimum(z + 1, 3) * 4 + y * 2 + x
    dn = jnp.maximum(z - 1, 0) * 4 + y * 2 + x
    width = moe.shape[2]
    hid = 128
    cut = 512

    def rc(src, dst, ss, rs, dev, c):
        return pltpu.make_async_remote_copy(
            src_ref=src, dst_ref=dst, send_sem=ss, recv_sem=rs, device_id=(dev, c), device_id_type=MESH
        )

    def loads(i):
        k, half = i // 2, i % 2
        b = plane_at(z, 3 - k) * 4 + jnp.where(half == 0, 1 - y, y) * 2
        at = pl.ds(b, 2)
        return [
            pltpu.make_async_copy(moe.at[at], xb, in_sem.at[0]),
            pltpu.make_async_copy(grd.at[at], gb, in_sem.at[1]),
            pltpu.make_async_copy(pick.at[at], pk, in_sem.at[2]),
            pltpu.make_async_copy(pick_t.at[at], pt, in_sem.at[3]),
        ]

    for c in loads(0):
        c.start()
    weights = [
        pltpu.make_async_copy(src, dst, w_sem.at[n]) for n, (src, dst) in enumerate(((wd_in, wd), (wg_in, wg), (wu_in, wu)))
    ]
    for c in weights:
        c.start()
    bar = pltpu.get_barrier_semaphore()

    def sig(d, c):
        pl.semaphore_signal(bar, inc=1, device_id=(d, c), device_id_type=MESH)

    sig(xn, core)
    sig(yn, core)
    sig(me, other)
    pl.when(z < 3)(lambda: sig(up, core))
    pl.when(z > 0)(lambda: sig(dn, core))
    pl.semaphore_wait(bar, 3 + (z < 3).astype(jnp.int32) + (z > 0).astype(jnp.int32))

    for q in range(2):
        ry[q, hid:] = sdn[...]
        rd[q, hid:] = sgu[...]
    sg_sum[...] = jnp.zeros_like(sg_sum)

    def y_(j, b, half, zp):
        return rc(own.at[b, half], yr.at[zp, j], ys.at[zp, j], yrs.at[zp, j], yn, core)

    def x_(j, b, half, zp):
        return rc(own.at[b, half], xr.at[zp, j], xs.at[zp, j], xrs.at[zp, j], xn, core)

    def zc(zp, dev, d):
        b = zp * 4 + y * 2 + x
        return rc(own.at[b], zr.at[d, zp], zs.at[zp], zrs.at[d, zp], dev, core)

    def sib_send(i):
        return rc(sib, sibr, cs, cr, me, other)

    def outs(i):
        at = pl.ds(pl.multiple_of(i * 256, 256), 256)
        return [
            pltpu.make_async_copy(rr, r_out.at[at], out_sem.at[0]),
            pltpu.make_async_copy(rg, rg_out.at[at], out_sem.at[1]),
            pltpu.make_async_copy(acts, act_out.at[at], out_sem.at[2]),
            pltpu.make_async_copy(das, da_out.at[at], out_sem.at[3]),
            pltpu.make_async_copy(dbs, db_out.at[at], out_sem.at[4]),
        ]

    def columns(step):
        def one(n, _):
            step(pl.ds(pl.multiple_of(n * cut, cut), cut))
            return 0

        lax.fori_loop(0, width // cut, one, 0)

    def first_part(i):
        for c in loads(i):
            c.wait()

        @pl.when(i > 0)
        def _():
            for c in outs(i - 1):
                c.wait()

        def pick_rows(n):
            for q in range(2):
                rr[q * hid : (q + 1) * hid, n] = mm(pk[q], xb[q, :, n]).astype(jnp.bfloat16)
                rg[q * hid : (q + 1) * hid, n] = mm(pk[q], gb[q, :, n]).astype(jnp.bfloat16)

        columns(pick_rows)
        for q in range(2):
            ab = nt(xb[q], sgu[...])
            act, d_a, d_b = gate_parts(ab[:, :hid], ab[:, hid:], nt(gb[q], sdn[...]))
            ly[q, :, :hid] = pt[q]
            ly[q, :, hid:] = act.astype(jnp.bfloat16)
            ld[q, :, :hid] = pt[q]
            ld[q, :, hid : 2 * hid] = d_a.astype(jnp.bfloat16)
            ld[q, :, 2 * hid :] = d_b.astype(jnp.bfloat16)

        def shared_grads(n):
            sg_sum[: 2 * hid, n] += tn(ld[0, :, hid:], xb[0, :, n]) + tn(ld[1, :, hid:], xb[1, :, n])
            sg_sum[2 * hid :, n] += tn(ly[0, :, hid:], gb[0, :, n]) + tn(ly[1, :, hid:], gb[1, :, n])

        columns(shared_grads)

        @pl.when(i < 7)
        def _():
            for c in loads(i + 1):
                c.start()

    def second_part(i):
        @pl.when(i == 0)
        def _():
            for c in weights:
                c.wait()

        logits = mm(rr[...], wr[...])
        lane = lax.broadcasted_iota(jnp.int32, logits.shape, 1)
        logits = jnp.where(lane < 16, logits, -jnp.inf)
        e = jnp.exp(logits - jnp.max(logits, axis=1, keepdims=True))
        gate = jnp.sum(jnp.where(lane == me, e, 0.0), axis=1, keepdims=True) / jnp.sum(
            e, axis=1, keepdims=True
        )
        pre = nt(rg[...], wd[...])
        act, d_a, d_b = gate_parts(nt(rr[...], wg[...]), nt(rr[...], wu[...]), gate * pre)
        low = act.astype(jnp.bfloat16)
        back = low.astype(jnp.float32)
        d_gate = jnp.sum(back * pre, axis=1, keepdims=True)
        acts[...] = (gate * back).astype(jnp.bfloat16)
        das[...] = d_a.astype(jnp.bfloat16)
        dbs[...] = d_b.astype(jnp.bfloat16)

        def spread(n):
            o = (gate * mm(low, wd[:, n])).astype(jnp.bfloat16)
            s = (mm(das[...], wg[:, n]) + mm(dbs[...], wu[:, n])).astype(jnp.bfloat16)
            for q in range(2):
                ry[q, :hid, n] = o[q * hid : (q + 1) * hid]
                rd[q, :hid, n] = s[q * hid : (q + 1) * hid]

        columns(spread)
        for c in outs(i):
            c.start()
        dgs[...] = jnp.where(lane == me, d_gate, 0.0).astype(jnp.bfloat16)

    def third_part(i):
        k, half = i // 2, i % 2
        b = plane_at(z, 3 - k) * 4 + jnp.where(half == 0, 1 - y, y) * 2

        @pl.when(i > 0)
        def _():
            sib_send(i - 1).wait_send()

        def store(q, n, v):
            v = v.astype(jnp.bfloat16)
            mine = jnp.where(core == 0, v[:128], v[128:])
            theirs = jnp.where(core == 0, v[128:], v[:128])
            own[b + q, 0, :, n] = mine[:64]
            own[b + q, 1, :, n] = mine[64:]
            sib[q, 0, :, n] = theirs[:64]
            sib[q, 1, :, n] = theirs[64:]

        def put(m, _):
            n = pl.ds(pl.multiple_of(m * cut, cut), cut)
            n2 = pl.ds(pl.multiple_of(width + m * cut, cut), cut)
            for q in range(2):
                store(q, n, mm(ly[q], ry[q, :, n]))
                store(q, n2, mm(ld[q], rd[q, :, n]))
            return 0

        lax.fori_loop(0, width // cut, put, 0)
        for q in range(2):
            store(q, pl.ds(2 * width, 128), mm(pt_of(q), dgs[q * hid : (q + 1) * hid]))

        @pl.when(i > 0)
        def _():
            pl.semaphore_wait(free, 1)

        sib_send(i).start()

    def pt_of(q):
        return ly[q, :, :hid]

    def staged(src, dst, sem):
        return pltpu.make_async_copy(src, dst, sem)

    def blk(zp, yy, xx):
        return zp * 4 + yy * 2 + xx

    def pair_sum(i):
        k, half = i // 2, i % 2
        zp = plane_at(z, 3 - k)
        b = zp * 4 + jnp.where(half == 0, 1 - y, y) * 2
        sib_send(i).wait_recv()

        def one(q, _):
            add_into(own.at[b + q, 0], sibr.at[q, 0])
            add_into(own.at[b + q, 1], sibr.at[q, 1])
            return 0

        lax.fori_loop(0, 2, one, 0)

        @pl.when(i < 7)
        def _():
            pl.semaphore_signal(free, inc=1, device_id=(me, other), device_id_type=MESH)

        @pl.when(half == 0)
        def _():
            y_(0, blk(zp, 1 - y, 1 - x), 0, zp).start()
            x_(0, blk(zp, 1 - y, 1 - x), 1, zp).start()
            y_(1, blk(zp, 1 - y, x), 0, zp).start()

        @pl.when(half == 1)
        def _():
            x_(1, blk(zp, y, 1 - x), 1, zp).start()

    def second_staging(k):
        zp = plane_at(z, 3 - k)
        return [
            staged(yr.at[zp, 0], stage.at[0, 0], st_sem.at[0]),
            staged(xr.at[zp, 0], stage.at[0, 1], st_sem.at[1]),
            staged(yr.at[zp, 1], stage.at[1, 0], st_sem.at[2]),
            staged(xr.at[zp, 1], stage.at[1, 1], st_sem.at[3]),
        ]

    def second_fetch(k):
        zp = plane_at(z, 3 - k)
        c = second_staging(k)
        y_(0, blk(zp, 1 - y, 1 - x), 0, zp).wait_recv()
        c[0].start()
        x_(0, blk(zp, 1 - y, 1 - x), 1, zp).wait_recv()
        c[1].start()
        y_(1, blk(zp, 1 - y, x), 0, zp).wait_recv()
        c[2].start()
        x_(1, blk(zp, y, 1 - x), 1, zp).wait_recv()
        c[3].start()

    def second_hop(k):
        zp = plane_at(z, 3 - k)
        mine = blk(zp, y, x)
        c = second_staging(k)
        c[0].wait()
        add_into(own.at[blk(zp, y, 1 - x), 0], stage.at[0, 0])
        x_(2, blk(zp, y, 1 - x), 0, zp).start()
        c[1].wait()
        add_into(own.at[blk(zp, 1 - y, x), 1], stage.at[0, 1])
        y_(2, blk(zp, 1 - y, x), 1, zp).start()
        c[2].wait()
        add_into(own.at[mine, 0], stage.at[1, 0])
        c[3].wait()
        add_into(own.at[mine, 1], stage.at[1, 1])

    def last_staging(k):
        zp = plane_at(z, 3 - k)
        return [
            staged(xr.at[zp, 2], stage.at[0, 0], st_sem.at[0]),
            staged(yr.at[zp, 2], stage.at[0, 1], st_sem.at[1]),
            staged(zr.at[1, zp], stage.at[1], st_sem.at[2]),
            staged(zr.at[0, zp], stage.at[2], st_sem.at[3]),
        ]

    def last_fetch(k):
        zp = plane_at(z, 3 - k)
        c = last_staging(k)
        x_(2, blk(zp, y, 1 - x), 0, zp).wait_recv()
        c[0].start()
        y_(2, blk(zp, 1 - y, x), 1, zp).wait_recv()
        c[1].start()

        @pl.when((zp <= z) & (z < 3))
        def _():
            zc(zp, me, 1).wait_recv()
            c[2].start()

        @pl.when((zp >= z) & (z > 0))
        def _():
            zc(zp, me, 0).wait_recv()
            c[3].start()

    def last_hop(k):
        zp = plane_at(z, 3 - k)
        mine = blk(zp, y, x)
        c = last_staging(k)
        c[0].wait()
        add_into(own.at[mine, 0], stage.at[0, 0])
        c[1].wait()
        add_into(own.at[mine, 1], stage.at[0, 1])

        def arrived(d):
            c[3 - d].wait()
            add_into(own.at[mine, 0], stage.at[2 - d, 0])
            add_into(own.at[mine, 1], stage.at[2 - d, 1])

        pl.when((zp <= z) & (z < 3))(lambda: arrived(1))
        pl.when((zp >= z) & (z > 0))(lambda: arrived(0))
        pl.when(zp < z)(lambda: zc(zp, dn, 1).start())
        pl.when(zp > z)(lambda: zc(zp, up, 0).start())

    lag = jnp.where((z == 0) | (z == 3), 5, 7)

    def step(i, _):
        pl.when(i < 8)(lambda: first_part(i))
        pl.when((i >= 1) & (i <= 8))(lambda: pair_sum(i - 1))
        seconds = (i % 2 == 0) & (i >= 4) & (i <= 10)
        lasts = (i % 2 == 1) & (i >= lag) & (i <= lag + 6)
        pl.when(seconds)(lambda: second_fetch((i - 4) // 2))
        pl.when(lasts)(lambda: last_fetch((i - lag) // 2))
        pl.when(i < 8)(lambda: second_part(i))
        pl.when(seconds)(lambda: second_hop((i - 4) // 2))
        pl.when(lasts)(lambda: last_hop((i - lag) // 2))
        pl.when(i < 8)(lambda: third_part(i))
        return 0

    lax.fori_loop(0, 14, step, 0)

    def give(n):
        for part in range(3):
            kept = sg_sum[part * hid : part * hid + 96, n]
            sg_out[part * 96 : (part + 1) * 96, n] = kept.astype(jnp.bfloat16)

    columns(give)
    for a in range(2):

        def row(n, _):
            r = pl.ds(pl.multiple_of(n * 16, 16), 16)
            o_out[core, a, r] = own[me, a, r]
            return 0

        lax.fori_loop(0, 4, row, 0)
    f = rc(o_out.at[core], o_out.at[core], fs, fr, me, other)
    f.start()
    for c in outs(7):
        c.wait()
    sib_send(7).wait_send()
    for k in range(4):
        for j in range(3):
            x_(j, 0, 0, k).wait_send()
            y_(j, 0, 0, k).wait_send()

        @pl.when(k != z)
        def _():
            zc(k, up, 0).wait_send()

    rc(o_out.at[core], o_out.at[other], fs, fr, me, other).wait_recv()
    f.wait_send()


def moe_call(moe, grd, pick, pick_t, wg, wu, wd, wr, sgu, sdn, cid):
    ffe, width = wg.shape
    total = 2 * width + 128
    slots = pick.shape[0] * pick.shape[1]
    low, S, V = jnp.bfloat16, pltpu.SemaphoreType.DMA, pltpu.VMEM
    any_, vmem = pl.BlockSpec(memory_space=pl.ANY), pl.BlockSpec(memory_space=pltpu.VMEM)
    shape = lambda *s: jax.ShapeDtypeStruct(s, low)
    blk = (2, 64, total)
    return pl.pallas_call(
        moe_kernel,
        out_shape=[
            shape(2, *blk), shape(slots, width), shape(slots, width), shape(slots, ffe), shape(slots, ffe),
            shape(slots, ffe), shape(288, width),
            shape(4, 3, 64, total), shape(4, 3, 64, total), shape(2, 4, *blk),
        ],
        in_specs=[any_] * 7 + [vmem] * 3,
        out_specs=[vmem] + [any_] * 5 + [vmem] + [any_] * 3,
        scratch_shapes=[
            V((384, width), jnp.float32), V(wg.shape, low), V(wu.shape, low), V(wd.shape, low),
            V((16,) + blk, low), V((2,) + blk, low), V((2,) + blk, low), V((3,) + blk, low),
            V((2, 256, width), low), V((2, 256, width), low), V((2, 128, 256), low), V((2, 256, 128), low),
            V((256, width), low), V((256, width), low), V((2, 256, 256), low), V((2, 256, 384), low),
            V((2, 256, width), low), V((2, 384, width), low),
            V((256, ffe), low), V((256, ffe), low), V((256, ffe), low), V((256, 128), low),
            S((3,)), S((4,)), S((5,)), S((4,)), pltpu.SemaphoreType.REGULAR, S, S, S((4, 3)), S((4, 3)), S((4, 3)), S((4, 3)), S((4,)), S((2, 4)), S, S,
        ],
        compiler_params=pltpu.CompilerParams(collective_id=cid, has_side_effects=True, vmem_limit_bytes=60 << 20),
        cost_estimate=pl.CostEstimate(flops=65 * 10**9, bytes_accessed=80 * 10**6, transcendentals=0),
    )(moe, grd, pick, pick_t, wg, wu, wd, wr, sgu, sdn)


SLOTS = 5
KEYS = SLOTS * 256


def turned(v, cos, sin):
    n = v.shape[1]
    lane = lax.broadcasted_iota(jnp.int32, v.shape, 1) % 64
    swap = jnp.where(lane < 32, -pltpu.roll(v, n - 32, 1), pltpu.roll(v, 32, 1))
    return v * cos + swap * sin


def root(v):
    return lax.rsqrt(jnp.mean(v * v, axis=1, keepdims=True) + eps_norm)


def greet_all(me, core, bar):
    pl.semaphore_signal(bar, inc=1, device_id=(me, 1 - core), device_id_type=MESH)
    for j in range(1, 16):
        pl.semaphore_signal(bar, inc=1, device_id=((me + j) % 16, core), device_id_type=MESH)
    pl.semaphore_wait(bar, 16)


class Trade:
    def __init__(self, source, land, me, core, send_sem, recv_sem, own_sem):
        def copy(j, to, to_slot):
            return pltpu.make_async_remote_copy(
                src_ref=source(to), dst_ref=land.at[to_slot], send_sem=send_sem.at[j - 1], recv_sem=recv_sem.at[j - 1],
                device_id=(to, core), device_id_type=MESH,
            )

        self.out = [copy(j, (me + j) % 16, me) for j in range(1, 16)]
        self.back = [copy(j, (me + 16 - j) % 16, (me + 16 - j) % 16) for j in range(1, 16)]
        self.own = pltpu.make_async_copy(source(me), land.at[me], own_sem)

    def start(self):
        self.own.start()
        for c in self.out:
            c.start()

    def wait(self):
        self.own.wait()
        for c in self.back:
            c.wait_recv()
        for c in self.out:
            c.wait_send()


def read_gains(wlat):
    lane = lax.broadcasted_iota(jnp.int32, (16, 128), 1)
    row = lax.broadcasted_iota(jnp.int32, (16, 128), 0)
    rows = nt((lane == row + 80).astype(jnp.bfloat16), wlat[:, RANK:])
    return rows[0:1], rows[1:2]


def slab_copies(w4, w2, wq, wo, wkv, wlat, sem):
    pairs = [
        (w2.at[:, 2560:3200], wlat, sem.at[0]),
        (w2.at[:, 0:1536], wq, sem.at[1]),
        (w2.at[:, 1536:2560], wo, sem.at[2]),
    ]
    for c in range(4):
        pairs.append((w4.at[:, c, :, w4.shape[3] - 512 :], wkv.at[:, :, c * 512 : (c + 1) * 512], sem.at[3 + c]))
    return pairs


def att_fwd_kernel(
    tok, w4, w2, trade_in, g_lat, cos, sin, bias,
    middle, moe_low, normed, lat_raw, qcat, keys, kv_out, lse, att, trade_out,
    kv, wq, wo, wkv, wlat, part, arrived, w_sem, kv_sem, ks, kr, ts, tr, cs, cr, as_, ar, ao,
):
    me = lax.axis_index("dp")
    core = lax.axis_index("tensor")
    loads = [pltpu.make_async_copy(h, v, s) for h, v, s in slab_copies(w4, w2, wq, wo, wkv, wlat, w_sem)]
    for c in loads:
        c.start()
    bar = pltpu.get_barrier_semaphore()
    greet_all(me, core, bar)
    trade = Trade(lambda i: trade_in.at[i], trade_out, me, core, as_, ar, ao)
    t = tok[...].astype(jnp.float32)
    loads[0].wait()
    g_att, g_moe = read_gains(wlat)
    normed[...] = (t * root(t) * g_att).astype(jnp.bfloat16)
    lat = mm(normed[...], wlat[...])
    lat_raw[...] = lat
    first = lat[:, :RANK]
    rot = turned(lat[:, RANK:], cos[:, :128], sin[:, :128])
    rot = jnp.where(lax.broadcasted_iota(jnp.int32, rot.shape, 1) < 64, rot, 0.0)
    keys[SLOTS - 1, :, :RANK] = (first * root(first) * g_lat[...]).astype(jnp.bfloat16)
    keys[SLOTS - 1, :, RANK:] = (rot + pltpu.roll(rot, 64, 1)).astype(jnp.bfloat16)

    mine = pl.ds(pl.multiple_of(core * 128, 128), 128)

    def send(d):
        return pltpu.make_async_remote_copy(
            src_ref=keys.at[SLOTS - 1, mine], dst_ref=keys.at[SLOTS - 1 - d, mine], send_sem=ks.at[d - 1],
            recv_sem=kr.at[d - 1], device_id=(jnp.minimum(me + d, 15), core), device_id_type=MESH,
        )

    def hand(d):
        return pltpu.make_async_remote_copy(
            src_ref=keys.at[SLOTS - 1 - d, mine], dst_ref=keys.at[SLOTS - 1 - d, mine], send_sem=ts.at[d - 1],
            recv_sem=tr.at[d - 1], device_id=(me, 1 - core), device_id_type=MESH,
        )

    def handed(d):
        other = keys.at[SLOTS - 1 - d, pl.ds(pl.multiple_of((1 - core) * 128, 128), 128)]
        return pltpu.make_async_remote_copy(
            src_ref=other, dst_ref=other, send_sem=ts.at[d - 1], recv_sem=tr.at[d - 1],
            device_id=(me, 1 - core), device_id_type=MESH,
        )

    for d in range(1, SLOTS):
        pl.when(me + d < 16)(lambda d=d: send(d).start())

        @pl.when(me < d)
        def _():
            keys[SLOTS - 1 - d] = jnp.zeros((256, 640), jnp.bfloat16)

    trade.start()

    loads[1].wait()
    half = lax.broadcasted_iota(jnp.int32, (256, 128), 1) < 64
    q_nope = mm(normed[...], wq[:, :1024])
    q_rope = turned(mm(normed[...], wq[:, 1024:]), cos[...], sin[...])
    for h in range(8):
        qcat[h, :, :128] = q_nope[:, h * 128 : (h + 1) * 128].astype(jnp.bfloat16)
        pair = q_rope[:, h // 2 * 128 : (h // 2 + 1) * 128]
        qcat[h, :, 128:] = jnp.where(half == (h % 2 == 0), pair, 0.0).astype(jnp.bfloat16)
    for c in loads[3:]:
        c.wait()
    def project(s):
        kv[s * 256 : (s + 1) * 256] = mm(keys[s, :, :RANK], wkv[...].reshape(RANK, 2048)).astype(jnp.bfloat16)

    project(SLOTS - 1)
    for d in range(1, SLOTS + 1):
        if d < SLOTS:

            @pl.when(me >= d)
            def _(d=d):
                send(d).wait_recv()
                hand(d).start()

        if d > 1:
            pl.when(me >= d - 1)(lambda d=d: handed(d - 1).wait_recv())
            project(SLOTS - d)
    save = pltpu.make_async_copy(kv, kv_out, kv_sem)
    save.start()

    def head(h, _):
        kn = kv[:, pl.ds(pl.multiple_of(h * 256, 256), 128)]
        v = kv[:, pl.ds(pl.multiple_of(h * 256 + 128, 128), 128)]
        rope = keys[:, :, RANK:].reshape(KEYS, 128)
        s = nt(qcat[h], jnp.concatenate([kn, rope], 1)) * ((NOPE + ROPE) ** -0.5) + bias[...]
        top = jnp.max(s, axis=1, keepdims=True)
        e = jnp.exp(s - top)
        den = jnp.sum(e, axis=1, keepdims=True)
        lse[h] = top + jnp.log(den)
        p = (e * (1.0 / den)).astype(jnp.bfloat16)
        att[:, pl.ds(pl.multiple_of(h * 128, 128), 128)] = mm(p, v).astype(jnp.bfloat16)
        return 0

    lax.fori_loop(0, 8, head, 0)
    loads[2].wait()

    def out(n, _):
        r = pl.ds(pl.multiple_of(n * 512, 512), 512)
        part[:, r] = nt(att[...], wo[r]).astype(jnp.bfloat16)
        return 0

    lax.fori_loop(0, 4, out, 0)
    swap = pltpu.make_async_remote_copy(
        src_ref=part, dst_ref=arrived, send_sem=cs, recv_sem=cr, device_id=(me, 1 - core), device_id_type=MESH
    )
    swap.start()
    swap.wait()
    m = tok[...].astype(jnp.float32) + (part[...].astype(jnp.float32) + arrived[...].astype(jnp.float32))
    middle[...] = m
    moe_low[...] = (m * root(m) * g_moe).astype(jnp.bfloat16)
    save.wait()
    trade.wait()
    for d in range(1, SLOTS):
        pl.when(me + d < 16)(lambda d=d: send(d).wait_send())
        pl.when(me >= d)(lambda d=d: hand(d).wait_send())


def att_fwd(tok, weights, trade, g_lat, cos, sin, bias, cid):
    low, f32, S, V = jnp.bfloat16, jnp.float32, pltpu.SemaphoreType.DMA, pltpu.VMEM
    any_, vmem = pl.BlockSpec(memory_space=pl.ANY), pl.BlockSpec(memory_space=pltpu.VMEM)
    shape = lambda kind, *s: jax.ShapeDtypeStruct(s, kind)
    rows, width = tok.shape
    pack = weights.shape[1]
    return pl.pallas_call(
        att_fwd_kernel,
        out_shape=[
            shape(f32, rows, width), shape(low, rows, width), shape(low, rows, width), shape(f32, rows, 640),
            shape(low, 8, rows, 256), shape(low, SLOTS, rows, 640), shape(low, KEYS, 2048), shape(f32, 8, rows, 1),
            shape(low, rows, 1024), shape(low, *trade.shape),
        ],
        in_specs=[vmem, any_, any_, any_] + [vmem] * 4,
        out_specs=[vmem] * 6 + [any_] + [vmem] * 2 + [any_],
        scratch_shapes=[
            V((KEYS, 2048), low), V((width, 1536), low), V((width, 1024), low), V((16, 32, 2048), low), V((width, 640), low),
            V((rows, width), low), V((rows, width), low), S((7,)), S, S((4,)), S((4,)), S((4,)), S((4,)), S, S,
            S((15,)), S((15,)), S,
        ],
        compiler_params=pltpu.CompilerParams(collective_id=cid, has_side_effects=True, vmem_limit_bytes=60 << 20),
        cost_estimate=pl.CostEstimate(flops=10**10, bytes_accessed=40 * 10**6, transcendentals=0),
    )(tok, weights.reshape(16, 4, 32, pack), weights, trade, g_lat, cos, sin, bias)


def att_bwd_kernel(
    w4, w2, home_in, trade_in, grad, middle, moe_low, wr, g_lat, kv_in,
    tok_in, normed_in, lat_raw_in, qcat_in, keys_in, lse_in, att_in, cos_in, sin_in, bias_in,
    tok_grad, packed, p4, trade_out,
    home,
    tok, normed, lat_raw, qcat, keys, lse, att, cos, sin, bias,
    kv, wq, wo, wkv, wlat, dmid, dnorm, dmid_low, d_att, dq, dqr, dkr, dk_out, dk_pair, dk_in, own_dk, part, arrived, d_keys,
    home_sem, as_, ar, ao, late_sem, w_sem, kv_sem, ks, kr, cs, cr, ps, pr, hs, hr, o_sem,
):
    me = lax.axis_index("dp")
    core = lax.axis_index("tensor")
    width = grad.shape[1]
    scale = (NOPE + ROPE) ** -0.5
    loads = [pltpu.make_async_copy(h, v, s) for h, v, s in slab_copies(w4, w2, wq, wo, wkv, wlat, w_sem)]
    stores = [pltpu.make_async_copy(v, h, s) for h, v, s in slab_copies(p4, packed, wq, wo, wkv, wlat, o_sem)]
    kv_load = pltpu.make_async_copy(kv_in, kv, kv_sem)
    late = [
        pltpu.make_async_copy(src, dst, late_sem.at[n])
        for n, (src, dst) in enumerate(
            (
                (att_in, att), (qcat_in, qcat), (keys_in, keys), (bias_in, bias), (lse_in, lse), (cos_in, cos),
                (sin_in, sin), (normed_in, normed), (lat_raw_in, lat_raw), (tok_in, tok),
            )
        )
    ]
    home_load = pltpu.make_async_copy(home_in.at[:, width:], home, home_sem)
    home_load.start()
    loads[0].start()
    loads[2].start()
    kv_load.start()
    for c in late:
        c.start()
    for n in (1, 3, 4, 5, 6):
        loads[n].start()
    bar = pltpu.get_barrier_semaphore()
    greet_all(me, core, bar)
    trade = Trade(
        lambda i: trade_in.at[:, pl.ds(pl.multiple_of(i * 128, 128), 128)], trade_out, me, core, as_, ar, ao
    )
    trade.start()
    loads[0].wait()
    g_att, g_moe = read_gains(wlat)
    home_load.wait()
    lane = lax.broadcasted_iota(jnp.int32, (256, 128), 1)

    logits = jnp.where(lane < 16, mm(moe_low[...], wr[...]), -jnp.inf)
    e = jnp.exp(logits - jnp.max(logits, axis=1, keepdims=True))
    router = e / jnp.sum(e, axis=1, keepdims=True)
    d_router = jnp.where(lane < 16, home[:, width:].astype(jnp.float32), 0.0)
    d_logits = (router * (d_router - jnp.sum(router * d_router, axis=1, keepdims=True))).astype(jnp.bfloat16)

    def norm_back(v, gain, dy):
        r = root(v)
        hat = v * r
        up = dy * gain
        return r * (up - hat * jnp.mean(up * hat, axis=1, keepdims=True)), dy * hat

    def one_lane(n):
        return (lane == n).astype(jnp.bfloat16)

    d_moe = home[:, :width].astype(jnp.float32) + nt(d_logits, wr[...])
    d_norm2, gain_rows = norm_back(middle[...], g_moe, d_moe)
    d_middle = grad[...].astype(jnp.float32) + d_norm2
    dmid[...] = d_middle
    dmid_low[...] = d_middle.astype(jnp.bfloat16)
    gains = gain_rows.astype(jnp.bfloat16)
    moved = pltpu.roll(d_logits.astype(jnp.float32), 64, 1).astype(jnp.bfloat16)
    small = tn(moe_low[...], moved) + tn(gains, one_lane(81))

    loads[2].wait()
    for c in late:
        c.wait()
    d_att[...] = mm(dmid_low[...], wo[...]).astype(jnp.bfloat16)

    def wo_rows(n, _):
        r = pl.ds(pl.multiple_of(n * 256, 256), 256)
        wo[r] = tn(dmid_low[:, r], att[...]).astype(jnp.bfloat16)
        return 0

    lax.fori_loop(0, width // 256, wo_rows, 0)
    stores[2].start()
    kv_load.wait()
    dkr[...] = jnp.zeros_like(dkr)
    dqr[...] = jnp.zeros_like(dqr)

    def head(h, _):
        cols = pl.ds(pl.multiple_of(h * 128, 128), 128)
        nope_at = pl.ds(pl.multiple_of(h * 256, 256), 128)
        value_at = pl.ds(pl.multiple_of(h * 256 + 128, 128), 128)
        pair = pl.ds(pl.multiple_of(h // 2 * 128, 128), 128)
        kc = jnp.concatenate([kv[:, nope_at], keys[:, :, RANK:].reshape(KEYS, 128)], 1)
        p = jnp.exp(nt(qcat[h], kc) * scale + bias[...] - lse[h])
        dv = tn(p.astype(jnp.bfloat16), d_att[:, cols])
        dp = nt(d_att[:, cols], kv[:, value_at])
        ds = (p * (dp - jnp.sum(p * dp, axis=1, keepdims=True))).astype(jnp.bfloat16)
        dqc = mm(ds, kc) * scale
        dkc = tn(ds, qcat[h]) * scale
        dq[:, cols] = dqc[:, :128].astype(jnp.bfloat16)
        dqr[:, pair] += jnp.where((lane < 64) == (h % 2 == 0), dqc[:, 128:], 0.0)
        kv[:, nope_at] = dkc[:, :128].astype(jnp.bfloat16)
        kv[:, value_at] = dv.astype(jnp.bfloat16)
        dkr[...] += dkc[:, 128:]
        return 0

    lax.fori_loop(0, 8, head, 0)
    for n in (3, 4, 5, 6):
        loads[n].wait()

    mine = pl.ds(pl.multiple_of(core * 128, 128), 128)
    others = pl.ds(pl.multiple_of((1 - core) * 128, 128), 128)

    def send(d, to):
        return pltpu.make_async_remote_copy(
            src_ref=dk_out.at[d - 1, mine], dst_ref=dk_in.at[d - 1], send_sem=ks.at[d - 1], recv_sem=kr.at[d - 1],
            device_id=(jnp.clip(to, 0, 15), core), device_id_type=MESH,
        )

    pair = pltpu.make_async_remote_copy(
        src_ref=dk_out.at[:, others], dst_ref=dk_pair, send_sem=ps, recv_sem=pr, device_id=(me, 1 - core), device_id_type=MESH
    )
    for s in range(SLOTS):
        r = slice(s * 256, (s + 1) * 256)
        d = SLOTS - 1 - s if s < SLOTS - 1 else SLOTS
        dk_out[d - 1, :, :RANK] = nt(kv[r], wkv[...].reshape(RANK, 2048)).astype(jnp.bfloat16)
        dk_out[d - 1, :, RANK:] = (dkr[r] + pltpu.roll(dkr[r], 64, 1)).astype(jnp.bfloat16)
    pair.start()
    dq[:, 1024:] = turned(dqr[...], cos[...], -sin[...]).astype(jnp.bfloat16)
    loads[1].wait()

    def normed_cols(n, _):
        r = pl.ds(pl.multiple_of(n * 512, 512), 512)
        v = nt(dq[...], wq[r])
        part[:, r] = v.astype(jnp.bfloat16)
        wq[r] = tn(normed[:, r], dq[...]).astype(jnp.bfloat16)
        return 0

    normed_cols(0, 0)
    pair.wait_recv()
    for d in range(1, SLOTS):
        dk_out[d - 1, mine] = dk_out[d - 1, mine] + dk_pair[d - 1]
        pl.when(me >= d)(lambda d=d: send(d, me - d).start())
    own_dk[...] = dk_out[SLOTS - 1, mine].astype(jnp.float32) + dk_pair[SLOTS - 1].astype(jnp.float32)
    lax.fori_loop(1, 4, normed_cols, 0)
    swap = pltpu.make_async_remote_copy(
        src_ref=part, dst_ref=arrived, send_sem=cs, recv_sem=cr, device_id=(me, 1 - core), device_id_type=MESH
    )
    swap.start()
    stores[1].start()
    latent_all = keys[:, :, :RANK].reshape(KEYS, RANK)
    for c in range(4):
        g = tn(latent_all, kv[:, c * 512 : (c + 1) * 512]).astype(jnp.bfloat16)
        wkv[:, :, c * 512 : (c + 1) * 512] = g.reshape(16, 32, 512)
        stores[3 + c].start()
    for d in range(1, SLOTS):

        @pl.when(me + d < 16)
        def _():
            send(d, me + d).wait_recv()
            own_dk[...] += dk_in[d - 1].astype(jnp.float32)

    d_keys[mine] = own_dk[...].astype(jnp.bfloat16)

    def half(rows):
        return pltpu.make_async_remote_copy(
            src_ref=d_keys.at[rows], dst_ref=d_keys.at[rows], send_sem=hs, recv_sem=hr,
            device_id=(me, 1 - core), device_id_type=MESH,
        )

    half(mine).start()
    swap.wait_recv()
    dnorm[...] = part[...].astype(jnp.float32) + arrived[...].astype(jnp.float32)
    half(others).wait_recv()

    d_first, lat_gain_rows = norm_back(lat_raw[:, :RANK], g_lat[...], d_keys[:, :RANK].astype(jnp.float32))
    d_second = turned(d_keys[:, RANK:].astype(jnp.float32), cos[:, :128], -sin[:, :128])
    d_second = jnp.where(lane < 64, d_second, 0.0)
    d_lat_low = jnp.concatenate([d_first, d_second], 1).astype(jnp.bfloat16)
    d_normed = dnorm[...] + nt(d_lat_low, wlat[...])
    d_norm1, att_gain_rows = norm_back(tok[...].astype(jnp.float32), g_att, d_normed)
    tok_grad[...] = dmid[...] + d_norm1
    small = small + tn(normed[...], d_lat_low[:, RANK:]) + tn(att_gain_rows.astype(jnp.bfloat16), one_lane(80))
    wlat[:, :RANK] = tn(normed[...], d_lat_low[:, :RANK]).astype(jnp.bfloat16)
    wlat[:, RANK:] = small.astype(jnp.bfloat16)
    lat_col = tn(lat_gain_rows.astype(jnp.bfloat16), one_lane(82))
    for b in range(16):
        r = slice(b * 128, b * 128 + 32)
        wlat[r, RANK:] = (small[r] + lat_col[b * 32 : (b + 1) * 32]).astype(jnp.bfloat16)
    stores[0].start()
    for c in stores:
        c.wait()
    trade.wait()
    for d in range(1, SLOTS):
        pl.when(me >= d)(lambda d=d: send(d, me - d).wait_send())
    pair.wait_send()
    swap.wait_send()
    half(mine).wait_send()


def att_bwd(
    weights, home, trade, grad, middle, moe_low, tok, normed, lat_raw, qcat, keys, kv, lse, att, wr, g_lat, cos, sin, bias, cid
):
    low, f32, S, V = jnp.bfloat16, jnp.float32, pltpu.SemaphoreType.DMA, pltpu.VMEM
    any_, vmem = pl.BlockSpec(memory_space=pl.ANY), pl.BlockSpec(memory_space=pltpu.VMEM)
    shape = lambda kind, *s: jax.ShapeDtypeStruct(s, kind)
    rows, width = tok.shape
    pack = weights.shape[1]
    return pl.pallas_call(
        att_bwd_kernel,
        out_shape=[shape(f32, rows, width), shape(low, width, pack - 512), shape(low, 16, 4, 32, 512), shape(low, 16, 288, 128)],
        in_specs=[any_] * 4 + [vmem] * 5 + [any_] * 11,
        out_specs=[vmem, any_, any_, any_],
        scratch_shapes=[
            V((rows, width + 128), low),
            V((rows, width), low), V((rows, width), low), V((rows, 640), f32), V((8, rows, 256), low), V((SLOTS, rows, 640), low),
            V((8, rows, 1), f32), V((rows, 1024), low), V((rows, 512), f32), V((rows, 512), f32), V((rows, KEYS), f32),
            V((KEYS, 2048), low), V((width, 1536), low), V((width, 1024), low), V((16, 32, 2048), low),
            V((width, 640), low), V((rows, width), f32), V((rows, width), f32), V((rows, width), low), V((rows, 1024), low),
            V((rows, 1536), low), V((rows, 512), f32), V((KEYS, 128), f32), V((SLOTS, rows, 640), low), V((SLOTS, rows // 2, 640), low),
            V((4, rows // 2, 640), low), V((rows // 2, 640), f32), V((rows, width), low), V((rows, width), low), V((rows, 640), low),
            S, S((15,)), S((15,)), S, S((10,)), S((7,)), S, S((4,)), S((4,)), S, S, S, S, S, S, S((7,)),
        ],
        compiler_params=pltpu.CompilerParams(collective_id=cid, has_side_effects=True, vmem_limit_bytes=60 << 20),
        cost_estimate=pl.CostEstimate(flops=25 * 10**9, bytes_accessed=70 * 10**6, transcendentals=0),
    )(
        weights.reshape(16, 4, 32, pack), weights, home, trade, grad, middle, moe_low, wr, g_lat, kv,
        tok, normed, lat_raw, qcat, keys, lse, att, cos, sin, bias,
    )


def my_half(v, rows):
    return lax.dynamic_slice_in_dim(v, lax.axis_index("tensor") * rows, rows, 0)


def row_halves(v):
    rows = v.shape[0] // 2
    return my_half(v, rows).reshape(2, rows // 2, v.shape[1])


def nope_first(w):
    heads = w.reshape(w.shape[0], -1, NOPE + ROPE)
    return jnp.concatenate(
        [heads[:, :, :NOPE].reshape(w.shape[0], -1), heads[:, :, NOPE:].reshape(w.shape[0], -1)], 1
    )


def heads_first(w):
    heads = w.shape[1] // (NOPE + ROPE)
    nope = w[:, : heads * NOPE].reshape(w.shape[0], heads, NOPE)
    rope = w[:, heads * NOPE :].reshape(w.shape[0], heads, ROPE)
    return jnp.concatenate([nope, rope], 2).reshape(w.shape[0], -1)


def shards_sixteen(
    tokens,
    out_grad,
    segments,
    routes,
    attn_gain,
    w_query,
    w_latent,
    latent_gain,
    w_keyval,
    w_out,
    moe_gain,
    w_router,
    shared_gate,
    shared_up,
    shared_down,
    expert_gate,
    routed_up_weight,
    expert_down,
):
    n_rows, width = tokens.shape
    dp_count = lax.axis_size("dp")
    dp_index = lax.axis_index("dp")
    seq_len = segments.shape[1]
    total = n_rows * dp_count
    hop_count = (WINDOW - 1) // n_rows + 1
    n_keys = (hop_count + 1) * n_rows
    experts = w_router.shape[1]
    capacity = 4 * n_rows * TOPK // (3 * experts)
    row_start = dp_index * n_rows
    seg_row = segments[0]
    depth = w_query.shape[0]
    q_width, o_width, kv_width = w_query.shape[1], w_out.shape[0], w_keyval.shape[1]
    kv_rows = w_keyval.shape[0]
    kv_cuts = depth // kv_rows
    kv_part = kv_width // kv_cuts
    lat_width = w_latent.shape[1]
    route_width = n_rows * TOPK // depth
    small = (lat_width + experts + 3 + route_width + 127) // 128 * 128

    gains = jnp.stack(
        [attn_gain, moe_gain, jnp.pad(latent_gain, (0, depth - kv_rows))], 1
    )
    packed = jnp.concatenate(
        [
            nope_first(w_query),
            w_out.T,
            w_latent,
            w_router,
            gains,
            routes.reshape(depth, route_width).astype(jnp.bfloat16),
            jnp.zeros((depth, small - lat_width - experts - 3 - route_width), jnp.bfloat16),
            w_keyval.reshape(kv_rows, kv_cuts, kv_part).transpose(1, 0, 2).reshape(depth, kv_part),
        ],
        1,
    )
    pack_width = packed.shape[1]
    weights, grad_all = ag16(
        [packed.reshape(2, depth // 2, pack_width), row_halves(out_grad)], (False, True), 1
    )
    weights = weights.reshape(width, pack_width)
    shared_part = shared_gate.shape[1] // dp_count
    shared_send = jnp.stack(
        [
            shared_gate.reshape(depth, dp_count, shared_part).transpose(1, 2, 0),
            shared_up.reshape(depth, dp_count, shared_part).transpose(1, 2, 0),
            shared_down.reshape(dp_count, shared_part, depth),
        ],
        1,
    )
    shared_send = jnp.pad(shared_send, ((0, 0), (0, 0), (0, 96 - shared_part), (0, 0)))
    at = q_width + o_width + lat_width
    wr_full = weights[:, at : at + experts]
    at += experts
    gain_latent = (
        weights[:, at + 2].reshape(dp_count, depth)[:, :kv_rows].reshape(-1).astype(jnp.float32)
    )

    all_routes = (
        weights[:, at + 3 : at + 3 + route_width].reshape(total, TOPK).astype(jnp.int32)
    )

    local_heads = q_width // (NOPE + ROPE)
    positions = (row_start + jnp.arange(n_rows, dtype=jnp.int32)).astype(jnp.float32)
    cos_tab, sin_tab = rope_tables(positions)
    cos_lanes, sin_lanes = jnp.tile(cos_tab, (1, 2 * local_heads)), jnp.tile(sin_tab, (1, 2 * local_heads))
    key_pos = row_start - hop_count * n_rows + jnp.arange(n_keys, dtype=jnp.int32)
    query_pos = row_start + jnp.arange(n_rows, dtype=jnp.int32)
    padded_seg = jnp.concatenate([jnp.full((hop_count * n_rows,), -1, jnp.int32), seg_row])
    key_seg = lax.dynamic_slice_in_dim(padded_seg, row_start, n_keys, 0)
    query_seg = lax.dynamic_slice_in_dim(seg_row, row_start, n_rows, 0)
    allowed = (key_pos[None, :] >= 0) & (key_pos[None, :] <= query_pos[:, None])
    allowed = (
        allowed
        & (query_pos[:, None] - key_pos[None, :] < WINDOW)
        & (query_seg[:, None] == key_seg[None, :])
    )

    bias = jnp.where(allowed, 0.0, -jnp.inf)
    middle, moe_low, normed_low, lat_raw, qcat, keys, kv, lse, attended_low, shared_all = att_fwd(
        tokens, weights, shared_send.reshape(dp_count, 3 * 96, depth), gain_latent[None], cos_lanes, sin_lanes, bias, 7
    )
    shared_all = shared_all.reshape(dp_count, 3, 96, depth)[:, :, :shared_part].transpose(1, 2, 0, 3)
    lead = jnp.pad(shared_all.reshape(3, shared_part, width), ((0, 0), (0, 128 - shared_part), (0, 0)))
    shared_in, shared_out = lead[:2].reshape(256, width), lead[2]
    (moe_all,) = ag16([row_halves(moe_low)], (True,), 3)
    chosen = jnp.any(all_routes == dp_index, axis=1).reshape(dp_count, n_rows)
    earlier = jnp.arange(n_rows)[:, None] < jnp.arange(n_rows)[None, :]
    rank = matmul(chosen.astype(jnp.bfloat16), earlier.astype(jnp.bfloat16)).astype(jnp.int32)
    pick = (
        (rank[:, None, :] == jnp.arange(capacity, dtype=jnp.int32)[None, :, None])
        & chosen[:, None, :]
    ).astype(jnp.bfloat16)

    slot_rows = dp_count * capacity
    moe_wr = jnp.pad(wr_full, ((0, 0), (0, 128 - experts)))
    home, rows_in, rows_grad, scaled_act, d_ea_low, d_eb_low, shared_grads = moe_call(
        moe_all.reshape(dp_count, n_rows, width),
        grad_all.reshape(dp_count, n_rows, width),
        pick,
        pick.transpose(0, 2, 1),
        expert_gate[0].T,
        routed_up_weight[0].T,
        expert_down[0],
        moe_wr,
        shared_in,
        shared_out,
        4,
    )[:7]
    home = home.reshape(n_rows, 2 * width + 128)
    result = (middle + home[:, :width].astype(jnp.float32)).astype(jnp.bfloat16)
    grad_down = matmul_tn(scaled_act, rows_grad)[None]
    grad_gate = matmul_tn(rows_in, d_ea_low)[None]
    grad_up = matmul_tn(rows_in, d_eb_low)[None]
    token_input_gradient, packed_grads, kv_grads, shared_home = att_bwd(
        weights, home, shared_grads, out_grad, middle, moe_low, tokens, normed_low, lat_raw, qcat, keys, kv, lse,
        attended_low, moe_wr, gain_latent[None], cos_lanes, sin_lanes, bias, 8
    )
    mine = rs16(
        packed_grads.reshape(dp_count, 2, depth // 2, pack_width - kv_part),
        kv_grads.reshape(dp_count, 2, depth // 2, kv_part),
        6,
    ).reshape(depth, pack_width)
    shared_home = shared_home.reshape(dp_count, 3, 96, depth)[:, :, :shared_part].astype(jnp.float32)
    grad_sgate = shared_home[:, 0].transpose(2, 0, 1).reshape(depth, -1)
    grad_sup = shared_home[:, 1].transpose(2, 0, 1).reshape(depth, -1)
    grad_sdown = shared_home[:, 2].reshape(-1, depth)
    out_wq = heads_first(mine[:, :q_width])
    at = q_width
    out_wo = mine[:, at : at + o_width].T
    at += o_width
    out_wlat = mine[:, at : at + lat_width]
    at += lat_width
    out_router = mine[:, at : at + experts]
    at += experts
    out_wkv = (
        mine[:, pack_width - kv_part :]
        .reshape(kv_cuts, kv_rows, kv_part)
        .transpose(1, 0, 2)
        .reshape(kv_rows, kv_width)
    )
    return (
        result,
        token_input_gradient,
        mine[:, at],
        out_wq,
        out_wlat,
        mine[:kv_rows, at + 2],
        out_wkv,
        out_wo,
        mine[:, at + 1],
        out_router,
        grad_sgate,
        grad_sup,
        grad_sdown,
        grad_gate,
        grad_up,
        grad_down,
    )


def shards_general(
    tokens,
    out_grad,
    segments,
    routes,
    attn_gain,
    w_query,
    w_latent,
    latent_gain,
    w_keyval,
    w_out,
    moe_gain,
    w_router,
    shared_gate,
    shared_up,
    shared_down,
    expert_gate,
    routed_up_weight,
    expert_down,
):
    n_rows = tokens.shape[0]
    model_width = tokens.shape[1]
    dp_count = lax.axis_size("dp")
    dp_index = lax.axis_index("dp")
    seq_len = segments.shape[1]
    seq_devs = seq_len // n_rows
    hop_count = (WINDOW - 1) // n_rows + 1
    n_keys = (hop_count + 1) * n_rows
    experts = w_router.shape[1]
    local_experts = expert_gate.shape[0]
    capacity = 4 * n_rows * TOPK // (3 * experts)
    slot_total = experts * capacity
    score_scale = (NOPE + ROPE) ** (-0.5)
    row_start = dp_index % seq_devs * n_rows
    seg_row = lax.dynamic_index_in_dim(segments, dp_index // seq_devs, 0, keepdims=False)
    gathered = (
        lax.all_gather(attn_gain, "dp", axis=0, tiled=True),
        lax.all_gather(w_query, "dp", axis=0, tiled=True),
        lax.all_gather(w_latent, "dp", axis=0, tiled=True),
        lax.all_gather(latent_gain, "dp", axis=0, tiled=True),
        lax.all_gather(w_keyval, "dp", axis=0, tiled=True),
        lax.all_gather(w_out, "dp", axis=1, tiled=True),
        lax.all_gather(moe_gain, "dp", axis=0, tiled=True),
        lax.all_gather(w_router, "dp", axis=0, tiled=True),
        lax.all_gather(shared_gate, "dp", axis=0, tiled=True),
        lax.all_gather(shared_up, "dp", axis=0, tiled=True),
        lax.all_gather(shared_down, "dp", axis=1, tiled=True),
    )
    (
        gain_attn,
        wq_full,
        wlat_full,
        gain_latent,
        wkv_full,
        wo_full,
        gain_moe,
        wr_full,
        sgate_full,
        sup_full,
        sdown_full,
    ) = gathered
    local_heads = wq_full.shape[1] // (NOPE + ROPE)
    positions = (row_start + jnp.arange(n_rows, dtype=jnp.int32)).astype(jnp.float32)
    cos_tab, sin_tab = rope_tables(positions)
    resid_in = tokens.astype(jnp.float32)
    normed, attn_norm_back = jax.vjp(rms_scale, resid_in, gain_attn.astype(jnp.float32))
    normed_low = normed.astype(jnp.bfloat16)

    def rope_queries(q_flat):
        shaped = q_flat.reshape(n_rows, local_heads, NOPE + ROPE)
        return jnp.concatenate(
            [shaped[..., :NOPE], rotate(shaped[..., NOPE:], cos_tab[:, None], sin_tab[:, None])], -1
        )

    queries, query_back = jax.vjp(rope_queries, matmul(normed_low, wq_full))
    query_low = queries.astype(jnp.bfloat16)

    def latent_piece(latent_raw, gain_vec):
        return (
            rms_scale(latent_raw[:, :RANK], gain_vec),
            rotate(latent_raw[:, RANK:], cos_tab, sin_tab),
        )

    (latent, key_rope), latent_back = jax.vjp(
        latent_piece, matmul(normed_low, wlat_full), gain_latent.astype(jnp.float32)
    )
    latent_low = latent.astype(jnp.bfloat16)
    rope_low = key_rope.astype(jnp.bfloat16)
    latent_parts = []
    rope_parts = []
    for distance in range(hop_count, 0, -1):
        moved_latent, moved_rope = passed_along((latent_low, rope_low), "dp", distance)
        latent_parts.append(moved_latent)
        rope_parts.append(moved_rope)
    keys_latent = jnp.concatenate(latent_parts + [latent_low], 0)
    keys_rope = jnp.concatenate(rope_parts + [rope_low], 0)
    keyval = (
        matmul(keys_latent, wkv_full).astype(jnp.bfloat16).reshape(n_keys, local_heads, NOPE + VDIM)
    )
    key_nope = keyval[..., :NOPE]
    values = keyval[..., NOPE:]
    key_pos = row_start - hop_count * n_rows + jnp.arange(n_keys, dtype=jnp.int32)
    query_pos = row_start + jnp.arange(n_rows, dtype=jnp.int32)
    padded_seg = jnp.concatenate([jnp.full((hop_count * n_rows,), -1, jnp.int32), seg_row])
    key_seg = lax.dynamic_slice_in_dim(padded_seg, row_start, n_keys, 0)
    query_seg = lax.dynamic_slice_in_dim(seg_row, row_start, n_rows, 0)
    allowed = (key_pos[None, :] >= 0) & (key_pos[None, :] <= query_pos[:, None])
    allowed = (
        allowed
        & (query_pos[:, None] - key_pos[None, :] < WINDOW)
        & (query_seg[:, None] == key_seg[None, :])
    )

    def masked_scores():
        nope_part = jnp.einsum(
            "qhd,khd->hqk", query_low[..., :NOPE], key_nope, preferred_element_type=jnp.float32
        )
        rope_part = jnp.einsum(
            "qhr,kr->hqk", query_low[..., NOPE:], keys_rope, preferred_element_type=jnp.float32
        )
        return jnp.where(allowed[None], score_scale * (nope_part + rope_part), -jnp.inf)

    scores = masked_scores()
    top_score = jnp.max(scores, axis=-1, keepdims=True)
    exp_scores = jnp.exp(scores - top_score)
    denom = jnp.sum(exp_scores, axis=-1, keepdims=True)
    attn_probs = exp_scores / denom
    log_total = top_score + jnp.log(denom)
    attended = jnp.einsum(
        "hqk,khv->qhv", attn_probs.astype(jnp.bfloat16), values, preferred_element_type=jnp.float32
    )
    attended_low = attended.astype(jnp.bfloat16).reshape(n_rows, local_heads * VDIM)
    attn_out = lax.psum(matmul(attended_low, wo_full).astype(jnp.bfloat16), "tensor").astype(
        jnp.float32
    )
    middle = resid_in + attn_out
    moe_normed, moe_norm_back = jax.vjp(rms_scale, middle, gain_moe.astype(jnp.float32))
    moe_low = moe_normed.astype(jnp.bfloat16)
    router, router_back = jax.vjp(
        lambda logit_vals: jax.nn.softmax(logit_vals, axis=-1), matmul(moe_low, wr_full)
    )
    expert_ids = jnp.arange(experts, dtype=jnp.int32)
    route_hot = (routes[:, :, None] == expert_ids[None, None, :]).astype(jnp.float32)
    gate_w = jnp.einsum("te,tke->tk", router, route_hot, precision=highest)
    flat_routes = routes.reshape(-1)
    assign_count = flat_routes.shape[0]
    flat_hot = (flat_routes[:, None] == expert_ids[None, :]).astype(jnp.int32)
    earlier = ranks_before(flat_hot)
    slot_in = jnp.sum(earlier * flat_hot, axis=1)
    target = flat_routes * capacity + slot_in
    assign_ids = jnp.arange(assign_count, dtype=jnp.int32)
    assign_of_slot = jnp.zeros((slot_total,), jnp.int32).at[target].set(assign_ids)
    slot_live = (
        jnp.zeros((slot_total,), jnp.bfloat16)
        .at[target]
        .set(jnp.ones((assign_count,), jnp.bfloat16))
    )
    send_rows = moe_low[assign_of_slot // TOPK] * slot_live[:, None]
    recv_rows = lax.all_to_all(
        send_rows.reshape(dp_count, local_experts * capacity, model_width),
        "dp",
        split_axis=0,
        concat_axis=0,
        tiled=True,
    )
    received_four_parts = recv_rows.reshape(dp_count, local_experts, capacity, model_width)
    exp_gate = jnp.einsum(
        "sjcd,jdf->sjcf", received_four_parts, expert_gate, preferred_element_type=jnp.float32
    )
    exp_up = jnp.einsum(
        "sjcd,jdf->sjcf", received_four_parts, routed_up_weight, preferred_element_type=jnp.float32
    )
    exp_act, exp_act_back = jax.vjp(gated_act, exp_gate, exp_up)
    exp_act_low = exp_act.astype(jnp.bfloat16)
    exp_result = jnp.einsum(
        "sjcf,jfd->sjcd", exp_act_low, expert_down, preferred_element_type=jnp.float32
    )
    returned = lax.all_to_all(
        exp_result.reshape(dp_count, local_experts * capacity, model_width).astype(jnp.bfloat16),
        "dp",
        split_axis=0,
        concat_axis=0,
        tiled=True,
    ).astype(jnp.float32)
    per_assign = returned.reshape(slot_total, model_width)[target].reshape(
        n_rows, TOPK, model_width
    )
    routed = jnp.einsum("tk,tkd->td", gate_w, per_assign, precision=highest)
    shared_a = matmul(moe_low, sgate_full)
    shared_b = matmul(moe_low, sup_full)
    shared_act, shared_back = jax.vjp(gated_act, shared_a, shared_b)
    shared_low = shared_act.astype(jnp.bfloat16)
    moe_out = lax.psum(
        (routed + matmul(shared_low, sdown_full)).astype(jnp.bfloat16), "tensor"
    ).astype(jnp.float32)
    result = (middle + moe_out).astype(jnp.bfloat16)
    grad_y = out_grad.astype(jnp.float32)
    grad_sdown = matmul_tn(shared_low, out_grad)
    d_shared_a, d_shared_b = shared_back(matmul_nt(out_grad, sdown_full))
    d_sa_low = d_shared_a.astype(jnp.bfloat16)
    d_sb_low = d_shared_b.astype(jnp.bfloat16)
    grad_sgate = matmul_tn(moe_low, d_sa_low)
    grad_sup = matmul_tn(moe_low, d_sb_low)
    d_moe = matmul_nt(d_sa_low, sgate_full) + matmul_nt(d_sb_low, sup_full)
    d_gate_part = jnp.einsum("td,tkd->tk", grad_y, per_assign, precision=highest)
    d_assign = (
        (gate_w[:, :, None] * grad_y[:, None, :])
        .astype(jnp.bfloat16)
        .reshape(assign_count, model_width)
    )
    send_grads = d_assign[assign_of_slot] * slot_live[:, None]
    recv_grads = lax.all_to_all(
        send_grads.reshape(dp_count, local_experts * capacity, model_width),
        "dp",
        split_axis=0,
        concat_axis=0,
        tiled=True,
    )
    recv_grads = recv_grads.reshape(dp_count, local_experts, capacity, model_width)
    expert_down_weight_gradient = jnp.einsum(
        "sjcf,sjcd->jfd", exp_act_low, recv_grads, preferred_element_type=jnp.float32
    )
    d_exp_act = jnp.einsum(
        "sjcd,jfd->sjcf", recv_grads, expert_down, preferred_element_type=jnp.float32
    )
    d_exp_gate, expert_up_act_gradient = exp_act_back(d_exp_act)
    d_egate_low = d_exp_gate.astype(jnp.bfloat16)
    expert_up_gradient_lowp = expert_up_act_gradient.astype(jnp.bfloat16)
    expert_gate_weight_gradient = jnp.einsum(
        "bmky,bmkx->myx", received_four_parts, d_egate_low, preferred_element_type=jnp.float32
    )
    expert_up_weight_gradient = jnp.einsum(
        "bmky,bmkx->myx",
        received_four_parts,
        expert_up_gradient_lowp,
        preferred_element_type=jnp.float32,
    )
    d_slots = jnp.einsum(
        "hteg,tmg->htem", d_egate_low, expert_gate, preferred_element_type=jnp.float32
    )
    d_slots = d_slots + jnp.einsum(
        "hteg,tmg->htem",
        expert_up_gradient_lowp,
        routed_up_weight,
        preferred_element_type=jnp.float32,
    )
    back_grads = lax.all_to_all(
        d_slots.reshape(dp_count, local_experts * capacity, model_width).astype(jnp.bfloat16),
        "dp",
        split_axis=0,
        concat_axis=0,
        tiled=True,
    ).astype(jnp.float32)
    d_moe = d_moe + jnp.sum(
        back_grads.reshape(slot_total, model_width)[target].reshape(n_rows, TOPK, model_width),
        axis=1,
    )
    d_moe, d_gate = (
        lax.psum(d_moe.astype(jnp.bfloat16), "tensor").astype(jnp.float32),
        lax.psum(d_gate_part.astype(jnp.bfloat16), "tensor").astype(jnp.float32),
    )
    d_router = jnp.einsum("tk,tke->te", d_gate, route_hot, precision=highest)
    (d_logits,) = router_back(d_router)
    d_logits_low = d_logits.astype(jnp.bfloat16)
    grad_router = matmul_tn(moe_low, d_logits_low)
    d_moe = d_moe + matmul_nt(d_logits_low, wr_full)
    d_mid_norm, grad_gain_moe = moe_norm_back(d_moe)
    d_middle = grad_y + d_mid_norm
    d_middle_low = d_middle.astype(jnp.bfloat16)
    grad_wout = matmul_tn(attended_low, d_middle_low)
    d_att_low = (
        matmul_nt(d_middle_low, wo_full).astype(jnp.bfloat16).reshape(n_rows, local_heads, VDIM)
    )
    again_probs = jnp.exp(masked_scores() - log_total)
    d_values = jnp.einsum(
        "hqk,qhv->khv",
        again_probs.astype(jnp.bfloat16),
        d_att_low,
        preferred_element_type=jnp.float32,
    )
    d_probs = jnp.einsum("qhv,khv->hqk", d_att_low, values, preferred_element_type=jnp.float32)
    d_scores = (
        again_probs * (d_probs - jnp.sum(d_probs * again_probs, axis=-1, keepdims=True))
    ).astype(jnp.bfloat16)
    d_query_nope = score_scale * jnp.einsum(
        "hqk,khd->qhd", d_scores, key_nope, preferred_element_type=jnp.float32
    )
    d_query_rope = score_scale * jnp.einsum(
        "hqk,kr->qhr", d_scores, keys_rope, preferred_element_type=jnp.float32
    )
    d_key_nope = score_scale * jnp.einsum(
        "hqk,qhd->khd", d_scores, query_low[..., :NOPE], preferred_element_type=jnp.float32
    )
    d_key_rope = score_scale * jnp.einsum(
        "hqk,qhr->kr", d_scores, query_low[..., NOPE:], preferred_element_type=jnp.float32
    )
    (d_q_raw,) = query_back(jnp.concatenate([d_query_nope, d_query_rope], -1))
    d_q_low = d_q_raw.astype(jnp.bfloat16)
    grad_wq = matmul_tn(normed_low, d_q_low)
    d_normed = matmul_nt(d_q_low, wq_full)
    d_kv_low = (
        jnp.concatenate([d_key_nope, d_values], -1)
        .astype(jnp.bfloat16)
        .reshape(n_keys, local_heads * (NOPE + VDIM))
    )
    grad_wkv = matmul_tn(keys_latent, d_kv_low)
    d_keys_latent = matmul_nt(d_kv_low, wkv_full)
    own_latent = d_keys_latent[hop_count * n_rows :]
    own_rope = d_key_rope[hop_count * n_rows :]
    for distance in range(hop_count, 0, -1):
        block_index = hop_count - distance
        lower = block_index * n_rows
        home_latent, home_rope = (
            passed_along(
                d_keys_latent[lower : lower + n_rows].astype(jnp.bfloat16), "dp", -distance
            ).astype(jnp.float32),
            passed_along(
                d_key_rope[lower : lower + n_rows].astype(jnp.bfloat16), "dp", -distance
            ).astype(jnp.float32),
        )
        own_latent = own_latent + home_latent
        own_rope = own_rope + home_rope
    d_normed, own_latent, own_rope = (
        lax.psum(d_normed.astype(jnp.bfloat16), "tensor").astype(jnp.float32),
        lax.psum(own_latent.astype(jnp.bfloat16), "tensor").astype(jnp.float32),
        lax.psum(own_rope.astype(jnp.bfloat16), "tensor").astype(jnp.float32),
    )
    d_latent_raw, grad_gain_latent = latent_back((own_latent, own_rope))
    d_latent_low = d_latent_raw.astype(jnp.bfloat16)
    grad_wlat = matmul_tn(normed_low, d_latent_low)
    d_normed = d_normed + matmul_nt(d_latent_low, wlat_full)
    d_tokens_norm, grad_gain_attn = attn_norm_back(d_normed)
    token_input_gradient = d_middle + d_tokens_norm
    reduced_result = tuple(
        (
            lax.psum_scatter(grad_gain_attn, "dp", scatter_dimension=0, tiled=True),
            lax.psum_scatter(grad_wq, "dp", scatter_dimension=0, tiled=True),
            lax.psum_scatter(grad_wlat, "dp", scatter_dimension=0, tiled=True),
            lax.psum_scatter(grad_gain_latent, "dp", scatter_dimension=0, tiled=True),
            lax.psum_scatter(grad_wkv, "dp", scatter_dimension=0, tiled=True),
            lax.psum_scatter(grad_wout, "dp", scatter_dimension=1, tiled=True),
            lax.psum_scatter(grad_gain_moe, "dp", scatter_dimension=0, tiled=True),
            lax.psum_scatter(grad_router, "dp", scatter_dimension=0, tiled=True),
            lax.psum_scatter(grad_sgate, "dp", scatter_dimension=0, tiled=True),
            lax.psum_scatter(grad_sup, "dp", scatter_dimension=0, tiled=True),
            lax.psum_scatter(grad_sdown, "dp", scatter_dimension=1, tiled=True),
        )
    )
    return (
        (result, token_input_gradient)
        + reduced_result
        + (expert_gate_weight_gradient, expert_up_weight_gradient, expert_down_weight_gradient)
    )


def solution(mesh):
    placed = (
        P("dp", None),
        P("dp", None),
        P(),
        P("dp", None),
        P("dp"),
        P("dp", "tensor"),
        P("dp", None),
        P("dp"),
        P("dp", "tensor"),
        P("tensor", "dp"),
        P("dp"),
        P("dp", None),
        P("dp", "tensor"),
        P("dp", "tensor"),
        P("tensor", "dp"),
        P("dp", None, "tensor"),
        P("dp", None, "tensor"),
        P("dp", "tensor", None),
    )
    sixteen = mesh.shape["dp"] == 16 and mesh.shape["tensor"] == 2

    def body(*args):
        fits_sixteen = sixteen and args[2].shape[0] == 1 and args[15].shape[0] == 1 and args[0].shape[0] == 256
        return (shards_sixteen if fits_sixteen else shards_general)(*args)

    return jax.shard_map(
        body,
        mesh=mesh,
        in_specs=placed,
        out_specs=(
            P("dp", None),
            P("dp", None),
            P("dp"),
            P("dp", "tensor"),
            P("dp", None),
            P("dp"),
            P("dp", "tensor"),
            P("tensor", "dp"),
            P("dp"),
            P("dp", None),
            P("dp", "tensor"),
            P("dp", "tensor"),
            P("tensor", "dp"),
            P("dp", None, "tensor"),
            P("dp", None, "tensor"),
            P("dp", "tensor", None),
        ),
        check_vma=False,
    )
```

```python
import functools
import math

import jax
import jax.numpy as jnp
from jax import lax
from jax.experimental import pallas as pl
from jax.experimental.pallas import tpu as pltpu
from jax.sharding import PartitionSpec as P

NOPE = 128
ROPE = 64
VDIM = 128
RANK = 512
TOPK = 6
WINDOW = 1024


eps_norm = 1e-06
highest = lax.Precision.HIGHEST


def passed_along(value, axis, steps):
    count = lax.axis_size(axis)
    leading, last = (max(0, -steps), min(count, count - steps))
    return lax.ppermute(value, axis, [(source, source + steps) for source in range(leading, last)])


def rms_scale(values, gain_vec):
    inv_root = lax.rsqrt(jnp.mean(values * values, axis=-1, keepdims=True) + eps_norm)
    return values * inv_root * gain_vec


def rope_tables(positions):
    half_width = ROPE // 2
    frequency = jnp.exp(
        -jnp.arange(half_width, dtype=jnp.float32) * (2.0 * math.log(10000.0) / ROPE)
    )
    angles = positions[:, None] * frequency[None, :]
    return (jnp.cos(angles), jnp.sin(angles))


def rotate(values, cos_tab, sin_tab):
    half_width = values.shape[-1] // 2
    first_half = values[..., :half_width]
    second = values[..., half_width:]
    return jnp.concatenate(
        [first_half * cos_tab - second * sin_tab, second * cos_tab + first_half * sin_tab], axis=-1
    )


def gated_act(gate_a, up_b):
    return jax.nn.silu(gate_a) * up_b


def matmul(left_mat, right_mat):
    return jnp.dot(left_mat, right_mat, preferred_element_type=jnp.float32)


def matmul_nt(left_mat, right_mat):
    return lax.dot_general(
        left_mat, right_mat, (((1,), (1,)), ((), ())), preferred_element_type=jnp.float32
    )


def matmul_tn(left_mat, right_mat):
    return lax.dot_general(
        left_mat, right_mat, (((0,), (0,)), ((), ())), preferred_element_type=jnp.float32
    )


def ranks_before(hot):
    count = hot.shape[0]
    below = jnp.arange(count)[:, None] > jnp.arange(count)[None, :]
    return matmul(below.astype(jnp.bfloat16), hot.astype(jnp.bfloat16)).astype(jnp.int32)


MESH = pl.DeviceIdType.MESH


def plane_at(z, k):
    edge = jnp.where(z >= 2, 3 - z, z)
    near = jnp.where(k == 0, edge, jnp.where(k == 1, 1 - edge, k))
    return jnp.where(z >= 2, 3 - near, near)


def ag_kernel(kinds, cuts, *refs):
    n = len(kinds)
    ins, outs, lands, sems = refs[:n], refs[n : 2 * n], refs[2 * n : 3 * n], refs[3 * n :]
    me = lax.axis_index("dp")
    core = lax.axis_index("tensor")
    z = me // 4
    y = (me // 2) % 2
    x = me % 2
    xn = z * 4 + y * 2 + (1 - x)
    yn = z * 4 + (1 - y) * 2 + x
    up = jnp.minimum(z + 1, 3) * 4 + y * 2 + x
    dn = jnp.maximum(z - 1, 0) * 4 + y * 2 + x
    bar = pltpu.get_barrier_semaphore()

    def sig(d, c):
        pl.semaphore_signal(bar, inc=1, device_id=(d, c), device_id_type=MESH)

    sig(xn, core)
    sig(yn, core)
    sig(me, 1 - core)
    pl.when(z < 3)(lambda: sig(up, core))
    pl.when(z > 0)(lambda: sig(dn, core))

    def rc(src, dst, ss, rs, dev, c):
        return pltpu.make_async_remote_copy(
            src_ref=src, dst_ref=dst, send_sem=ss, recv_sem=rs, device_id=(dev, c), device_id_type=MESH
        )

    class Part:
        def __init__(self, at, rows):
            self.share = kinds[at]
            self.x, self.o, self.hbm = ins[at], lands[at], outs[at]
            self.rows = rows
            self.zs, self.zr, self.xs, self.xr, self.ys, self.yr, self.cs, self.cr, self.own, self.out = sems[20 * at + 10 : 20 * at + 20]
            self.slot = core if self.share else 0
            self.copy = pltpu.make_async_copy(self.x.at[:, self.rows], self.whole(me), self.own)

        def whole(self, b):
            return self.o.at[b, self.slot, :, self.rows]

        def z_(self, zp, dev, s):
            b = zp * 4 + y * 2 + x
            return rc(self.whole(b), self.whole(b), self.zs.at[s], self.zr.at[zp], dev, core)

        def x_(self, j, b, half, zp):
            r = self.o.at[b, self.slot, half, self.rows]
            return rc(r, r, self.xs.at[zp, j], self.xr.at[zp, j], xn, core)

        def y_(self, j, b, half, zp):
            r = self.o.at[b, self.slot, half, self.rows]
            return rc(r, r, self.ys.at[zp, j], self.yr.at[zp, j], yn, core)

        def twin(self, b):
            return rc(self.whole(b), self.whole(b), self.cs.at[b], self.cr.at[b], me, 1 - core)

        def first(self, k):
            zp = plane_at(z, k)
            b = zp * 4 + y * 2 + x
            if k > 0:
                self.z_(zp, up, 0).wait_recv()
            pl.when((zp <= z) & (z < 3))(lambda: self.z_(zp, up, zp).start())
            pl.when((zp >= z) & (z > 0))(lambda: self.z_(zp, dn, 4 + zp).start())
            self.x_(0, b, 0, zp).start()
            self.y_(0, b, 1, zp).start()
            self.y_(1, b, 0, zp).start()
            self.x_(1, b, 1, zp).start()
            if self.share:
                self.twin(b).start()

        def second(self, k):
            zp = plane_at(z, k)
            bx = zp * 4 + y * 2 + (1 - x)
            by = zp * 4 + (1 - y) * 2 + x
            self.x_(0, bx, 0, zp).wait_recv()
            self.y_(2, bx, 0, zp).start()
            self.y_(0, by, 1, zp).wait_recv()
            self.x_(2, by, 1, zp).start()
            self.x_(1, bx, 1, zp).wait_recv()
            self.y_(1, by, 0, zp).wait_recv()
            if self.share:
                self.twin(bx).start()
                self.twin(by).start()

        def third(self, k):
            zp = plane_at(z, k)
            bd = zp * 4 + (1 - y) * 2 + (1 - x)
            self.y_(2, bd, 0, zp).wait_recv()
            self.x_(2, bd, 1, zp).wait_recv()
            if self.share:
                self.twin(bd).start()

        def save(self, k):
            at = pl.ds(plane_at(z, k) * 4, 4)
            return pltpu.make_async_copy(
                self.o.at[at, :, :, self.rows], self.hbm.at[at, :, :, self.rows], self.out.at[k]
            )

        def fourth(self, k):
            if self.share:
                for q in range(4):
                    b = plane_at(z, k) * 4 + q
                    src, dst = self.o.at[b, core, :, self.rows], self.o.at[b, 1 - core, :, self.rows]
                    rc(src, dst, self.cs.at[b], self.cr.at[b], me, 1 - core).wait_recv()
            self.save(k).start()

        def end(self):
            for k in range(4):
                self.save(k).wait()
                pl.when((k <= z) & (z < 3))(lambda k=k: self.z_(k, up, k).wait_send())
                pl.when((k >= z) & (z > 0))(lambda k=k: self.z_(k, dn, 4 + k).wait_send())
                for j in range(3):
                    self.x_(j, 0, 0, k).wait_send()
                    self.y_(j, 0, 0, k).wait_send()
            if self.share:
                for b in range(16):
                    self.twin(b).wait_send()

    class Cross:
        def __init__(self, at, rows):
            self.share = kinds[at]
            self.x, self.o, self.hbm = ins[at], lands[at], outs[at]
            self.rows = rows
            self.fs, self.fr, self.zs, self.zr, self.ls, self.lr, self.cs, self.cr, self.own, self.out = sems[20 * at : 20 * at + 10]
            self.slot = core if self.share else 0
            self.copy = pltpu.make_async_copy(self.x.at[:, rows], self.o.at[me, self.slot, :, rows], self.own)

        def ref(self, b, half):
            return self.o.at[b, self.slot, half, self.rows]

        def block(self, zp, half, p):
            if half == 0:
                return zp * 4 + y * 2 + (x if p == 0 else 1 - x)
            return zp * 4 + (y if p == 0 else 1 - y) * 2 + x

        def hop(self, half):
            r = self.ref(me, half)
            return rc(r, r, self.fs.at[half], self.fr.at[half], xn if half == 0 else yn, core)

        def line(self, zp, half, p, d):
            r = self.ref(self.block(zp, half, p), half)
            return rc(r, r, self.zs.at[d, zp, half, p], self.zr.at[zp, half, p], up if d == 0 else dn, core)

        def last(self, zp, half, p):
            r = self.ref(self.block(zp, half, p), half)
            return rc(r, r, self.ls.at[zp, half, p], self.lr.at[zp, half, p], yn if half == 0 else xn, core)

        def twin(self, b, half):
            r = self.ref(b, half)
            return rc(r, r, self.cs.at[b, half], self.cr.at[b, half], me, 1 - core)

        def pass_on(self, zp, half, p):
            pl.when((zp <= z) & (z < 3))(lambda: self.line(zp, half, p, 0).start())
            pl.when((zp >= z) & (z > 0))(lambda: self.line(zp, half, p, 1).start())
            self.last(zp, half, p).start()
            if self.share:
                self.twin(self.block(zp, half, p), half).start()

        def first(self, k):
            zp = plane_at(z, k)
            if k == 0:
                for half in range(2):
                    self.hop(half).start()
                for half in range(2):
                    self.pass_on(zp, half, 0)
                for half in range(2):
                    self.hop(half).wait_recv()
                    self.pass_on(zp, half, 1)
            else:
                for p in range(2):
                    for half in range(2):
                        self.line(zp, half, p, 0).wait_recv()
                        self.pass_on(zp, half, p)

        def second(self, k):
            pass

        def third(self, k):
            zp = plane_at(z, k)
            for p in range(2):
                for half in range(2):
                    self.last(zp, half, p).wait_recv()
                    if self.share:
                        far = zp * 4 + (1 - y) * 2 + (x if p == 0 else 1 - x)
                        if half == 1:
                            far = zp * 4 + (y if p == 0 else 1 - y) * 2 + (1 - x)
                        self.twin(far, half).start()

        def save(self, k):
            at = pl.ds(plane_at(z, k) * 4, 4)
            return pltpu.make_async_copy(
                self.o.at[at, :, :, self.rows], self.hbm.at[at, :, :, self.rows], self.out.at[k]
            )

        def fourth(self, k):
            if self.share:
                for q in range(4):
                    b = plane_at(z, k) * 4 + q
                    for half in range(2):
                        src, dst = self.o.at[b, core, half, self.rows], self.o.at[b, 1 - core, half, self.rows]
                        rc(src, dst, self.cs.at[b, half], self.cr.at[b, half], me, 1 - core).wait_recv()
            self.save(k).start()

        def end(self):
            for half in range(2):
                self.hop(half).wait_send()
            for k in range(4):
                self.save(k).wait()
                for half in range(2):
                    for p in range(2):
                        pl.when((k <= z) & (z < 3))(lambda k=k, h=half, p=p: self.line(k, h, p, 0).wait_send())
                        pl.when((k >= z) & (z > 0))(lambda k=k, h=half, p=p: self.line(k, h, p, 1).wait_send())
                        self.last(k, half, p).wait_send()
            if self.share:
                for b in range(16):
                    for half in range(2):
                        self.twin(b, half).wait_send()

    groups = []
    for at in range(n):
        height = ins[at].shape[1]
        group = [Cross(at, pl.ds(0, cuts[at]))] if cuts[at] > 0 else []
        if cuts[at] < height:
            group.append(Part(at, pl.ds(cuts[at], height - cuts[at])))
        groups.append(group)
    parts = [p for g in groups for p in g]
    for p in parts:
        p.copy.start()
    pl.semaphore_wait(bar, 3 + (z < 3).astype(jnp.int32) + (z > 0).astype(jnp.int32))
    for p in parts:
        p.copy.wait()
    turns = [(p, k) for k in range(4) for p in parts]
    lag = len(parts)
    for t in range(len(turns) + lag):
        if t < len(turns):
            turns[t][0].first(turns[t][1])
        if t >= lag:
            turns[t - lag][0].second(turns[t - lag][1])
    for p, k in turns:
        p.third(k)
        if not p.share:
            p.fourth(k)
    for p, k in turns:
        if p.share:
            p.fourth(k)
    for p in parts:
        p.end()


def ag16(arrays, kinds, cid, cuts=None):
    S = pltpu.SemaphoreType.DMA
    any_ = pl.BlockSpec(memory_space=pl.ANY)
    cuts = cuts or tuple(v.shape[1] // 2 for v in arrays)
    counts = (
        ((2,), (2,), (2, 4, 2, 2), (4, 2, 2), (4, 2, 2), (4, 2, 2), (16, 2), (16, 2), (), (4,))
        + ((8,), (4,), (4, 3), (4, 3), (4, 3), (4, 3), (16,), (16,), (), (4,))
    )
    shapes = [(16, 2 if share else 1) + v.shape for v, share in zip(arrays, kinds)]
    return pl.pallas_call(
        functools.partial(ag_kernel, kinds, cuts),
        out_shape=[jax.ShapeDtypeStruct(s, v.dtype) for s, v in zip(shapes, arrays)],
        in_specs=[any_] * len(arrays),
        out_specs=[any_] * len(arrays),
        scratch_shapes=[pltpu.VMEM(s, v.dtype) for s, v in zip(shapes, arrays)]
        + [S(s) for _ in arrays for s in counts],
        compiler_params=pltpu.CompilerParams(collective_id=cid, has_side_effects=True, vmem_limit_bytes=60 << 20),
    )(*arrays)


def add_into(dst, src):
    def step(i, _):
        r = pl.ds(pl.multiple_of(i * 16, 16), 16)
        dst[r] = dst[r] + src[r]
        return 0

    lax.fori_loop(0, dst.shape[0] // 16, step, 0)


def rs_kernel(a_ref, b_ref, o_ref, own, fr, zr, lr, yr, xr, z2r, lsem, fs, frs, zs, zrs, ls, lrs, xs, xrs, ys, yrs, z2s, z2rs):
    me = lax.axis_index("dp")
    core = lax.axis_index("tensor")
    z = me // 4
    y = (me // 2) % 2
    x = me % 2
    xn = z * 4 + y * 2 + (1 - x)
    yn = z * 4 + (1 - y) * 2 + x
    up = jnp.minimum(z + 1, 3) * 4 + y * 2 + x
    dn = jnp.maximum(z - 1, 0) * 4 + y * 2 + x
    wide = a_ref.shape[3]
    cut = fr.shape[3]
    crossing, rest = pl.ds(0, cut), pl.ds(cut, own.shape[2] - cut)

    def rc(src, dst, ss, rs, dev):
        return pltpu.make_async_remote_copy(
            src_ref=src, dst_ref=dst, send_sem=ss, recv_sem=rs, device_id=(dev, core), device_id_type=MESH
        )

    def loads(zp):
        at = pl.ds(zp * 4, 4)
        return [
            pltpu.make_async_copy(a_ref.at[at], own.at[at, :, :, 0:wide], lsem.at[zp, 0]),
            pltpu.make_async_copy(b_ref.at[at], own.at[at, :, :, wide:], lsem.at[zp, 1]),
        ]

    for k in range(4):
        for c in loads(plane_at(z, 3 - k)):
            c.start()
    bar = pltpu.get_barrier_semaphore()

    def sig(d):
        pl.semaphore_signal(bar, inc=1, device_id=(d, core), device_id_type=MESH)

    sig(xn)
    sig(yn)
    pl.when(z < 3)(lambda: sig(up))
    pl.when(z > 0)(lambda: sig(dn))
    pl.semaphore_wait(bar, 2 + (z < 3).astype(jnp.int32) + (z > 0).astype(jnp.int32))

    def blk(zp, yy, xx):
        return zp * 4 + yy * 2 + xx

    def place(zp, half, p):
        if half == 0:
            return blk(zp, y, x if p == 0 else 1 - x)
        return blk(zp, y if p == 0 else 1 - y, x)

    def hop(zp, half, p):
        b = blk(zp, 1 - y, x if p == 0 else 1 - x) if half == 0 else blk(zp, y if p == 0 else 1 - y, 1 - x)
        return rc(
            own.at[b, half, crossing], fr.at[zp, half, p], fs.at[zp, half, p], frs.at[zp, half, p], yn if half == 0 else xn
        )

    def line(zp, half, p, dev, slot):
        b = place(zp, half, p)
        return rc(own.at[b, half, crossing], zr.at[slot, half, p], zs.at[zp, half, p], zrs.at[slot, half, p], dev)

    def last(half):
        b = place(z, half, 1)
        return rc(own.at[b, half, crossing], lr.at[half], ls.at[half], lrs.at[half], xn if half == 0 else yn)

    def y_(j, b, half, zp):
        return rc(own.at[b, half, rest], yr.at[zp, j], ys.at[zp, j], yrs.at[zp, j], yn)

    def x_(j, b, half, zp):
        return rc(own.at[b, half, rest], xr.at[zp, j], xs.at[zp, j], xrs.at[zp, j], xn)

    def zc(zp, dev, d):
        return rc(own.at[zp * 4 + y * 2 + x, :, rest], z2r.at[d, zp], z2s.at[zp], z2rs.at[d, zp], dev)

    def s1(k):
        zp = plane_at(z, 3 - k)
        for c in loads(zp):
            c.wait()
        for p in range(2):
            for half in range(2):
                hop(zp, half, 1 - p).start()
        y_(0, blk(zp, 1 - y, 1 - x), 0, zp).start()
        x_(0, blk(zp, 1 - y, 1 - x), 1, zp).start()
        y_(1, blk(zp, 1 - y, x), 0, zp).start()
        x_(1, blk(zp, y, 1 - x), 1, zp).start()

    def arrive(zp, half, p, slot):
        line(zp, half, p, me, slot).wait_recv()
        add_into(own.at[place(zp, half, p), half, crossing], zr.at[slot, half, p])

    def s2(k):
        zp = plane_at(z, 3 - k)
        for p in (1, 0):
            for half in range(2):
                hop(zp, half, p).wait_recv()
                add_into(own.at[place(zp, half, p), half, crossing], fr.at[zp, half, p])
                pl.when((zp <= z) & (z < 3))(lambda h=half, p=p: arrive(zp, h, p, jnp.where(zp == z, 4, zp)))
                pl.when((zp >= z) & (z > 0))(lambda h=half, p=p: arrive(zp, h, p, zp))
                pl.when(zp < z)(lambda h=half, p=p: line(zp, h, p, dn, jnp.where(zp == z - 1, 4, zp)).start())
                pl.when(zp > z)(lambda h=half, p=p: line(zp, h, p, up, zp).start())
                if k == 3 and p == 1:
                    last(half).start()
        mine = blk(zp, y, x)
        y_(0, blk(zp, 1 - y, 1 - x), 0, zp).wait_recv()
        add_into(own.at[blk(zp, y, 1 - x), 0, rest], yr.at[zp, 0])
        x_(2, blk(zp, y, 1 - x), 0, zp).start()
        x_(0, blk(zp, 1 - y, 1 - x), 1, zp).wait_recv()
        add_into(own.at[blk(zp, 1 - y, x), 1, rest], xr.at[zp, 0])
        y_(2, blk(zp, 1 - y, x), 1, zp).start()
        y_(1, blk(zp, 1 - y, x), 0, zp).wait_recv()
        add_into(own.at[mine, 0, rest], yr.at[zp, 1])
        x_(1, blk(zp, y, 1 - x), 1, zp).wait_recv()
        add_into(own.at[mine, 1, rest], xr.at[zp, 1])

    def s3(k):
        zp = plane_at(z, 3 - k)
        mine = blk(zp, y, x)
        x_(2, blk(zp, y, 1 - x), 0, zp).wait_recv()
        add_into(own.at[mine, 0, rest], xr.at[zp, 2])
        y_(2, blk(zp, 1 - y, x), 1, zp).wait_recv()
        add_into(own.at[mine, 1, rest], yr.at[zp, 2])

        def arrived(d):
            zc(zp, me, d).wait_recv()
            add_into(own.at[mine, 0, rest], z2r.at[d, zp, 0])
            add_into(own.at[mine, 1, rest], z2r.at[d, zp, 1])

        pl.when((zp <= z) & (z < 3))(lambda: arrived(1))
        pl.when((zp >= z) & (z > 0))(lambda: arrived(0))
        pl.when(zp < z)(lambda: zc(zp, dn, 1).start())
        pl.when(zp > z)(lambda: zc(zp, up, 0).start())

    s1(0)
    s1(1)
    s2(0)
    s1(2)
    s2(1)
    s3(0)
    s1(3)
    s2(2)
    s3(1)
    s2(3)
    s3(2)
    s3(3)
    for half in range(2):
        last(half).wait_recv()
        add_into(own.at[me, half, crossing], lr.at[half])
    for a in range(2):

        def row(i, _):
            r = pl.ds(pl.multiple_of(i * 16, 16), 16)
            o_ref[a, r] = own[me, a, r].astype(jnp.float32)
            return 0

        lax.fori_loop(0, o_ref.shape[1] // 16, row, 0)
    for half in range(2):
        last(half).wait_send()
    for k in range(4):
        for half in range(2):
            for p in range(2):
                hop(k, half, p).wait_send()
                pl.when(k != z)(lambda k=k, h=half, p=p: line(k, h, p, me, 0).wait_send())
        for j in range(3):
            x_(j, 0, 0, k).wait_send()
            y_(j, 0, 0, k).wait_send()
        pl.when(k != z)(lambda k=k: zc(k, up, 0).wait_send())


def rs16(a, b, cid):
    S = pltpu.SemaphoreType.DMA
    high, total = a.shape[2], a.shape[3] + b.shape[3]
    blkshape = (2, high, total)
    cross, half = (high // 2, total), (high - high // 2, total)
    V = lambda s: pltpu.VMEM(s, a.dtype)
    return pl.pallas_call(
        rs_kernel,
        out_shape=jax.ShapeDtypeStruct(blkshape, jnp.float32),
        in_specs=[pl.BlockSpec(memory_space=pl.ANY)] * 2,
        out_specs=pl.BlockSpec(memory_space=pltpu.VMEM),
        scratch_shapes=[
            V((16,) + blkshape), V((4, 2, 2) + cross), V((5, 2, 2) + cross), V((2,) + cross),
            V((4, 3) + half), V((4, 3) + half), V((2, 4, 2) + half),
            S((4, 2)), S((4, 2, 2)), S((4, 2, 2)), S((4, 2, 2)), S((5, 2, 2)), S((2,)), S((2,)),
            S((4, 3)), S((4, 3)), S((4, 3)), S((4, 3)), S((4,)), S((2, 4)),
        ],
        compiler_params=pltpu.CompilerParams(collective_id=cid, has_side_effects=True, vmem_limit_bytes=60 << 20),
    )(a, b)


def nt(a, b):
    return lax.dot_general(a, b, (((1,), (1,)), ((), ())), preferred_element_type=jnp.float32)


def tn(a, b):
    return lax.dot_general(a, b, (((0,), (0,)), ((), ())), preferred_element_type=jnp.float32)


def mm(a, b):
    return jnp.dot(a, b, preferred_element_type=jnp.float32)


def gate_parts(a, b, dc):
    s = 1.0 / (1.0 + jnp.exp(-a))
    act = a * s
    return act * b, dc * b * (s * (1.0 + a * (1.0 - s))), dc * act


def moe_kernel(
    moe, grd, pick, pick_t, wg_in, wu_in, wd_in, wr, sgu, sdn,
    o_out, r_out, rg_out, act_out, da_out, db_out, sg_out, yr, xr, zr,
    sg_sum, wg, wu, wd, own, sib, sibr, stage, xb, gb, pk, pt, rr, rg, ly, ld, ry, rd, acts, das, dbs, dgs,
    w_sem, in_sem, out_sem, st_sem, free, cs, cr, xs, xrs, ys, yrs, zs, zrs, fs, fr,
):
    me = lax.axis_index("dp")
    core = lax.axis_index("tensor")
    other = 1 - core
    z = me // 4
    y = (me // 2) % 2
    x = me % 2
    xn = z * 4 + y * 2 + (1 - x)
    yn = z * 4 + (1 - y) * 2 + x
    up = jnp.minimum(z + 1, 3) * 4 + y * 2 + x
    dn = jnp.maximum(z - 1, 0) * 4 + y * 2 + x
    width = moe.shape[2]
    hid = 128
    cut = 512

    def rc(src, dst, ss, rs, dev, c):
        return pltpu.make_async_remote_copy(
            src_ref=src, dst_ref=dst, send_sem=ss, recv_sem=rs, device_id=(dev, c), device_id_type=MESH
        )

    def loads(i):
        k, half = i // 2, i % 2
        b = plane_at(z, 3 - k) * 4 + jnp.where(half == 0, 1 - y, y) * 2
        at = pl.ds(b, 2)
        return [
            pltpu.make_async_copy(moe.at[at], xb, in_sem.at[0]),
            pltpu.make_async_copy(grd.at[at], gb, in_sem.at[1]),
            pltpu.make_async_copy(pick.at[at], pk, in_sem.at[2]),
            pltpu.make_async_copy(pick_t.at[at], pt, in_sem.at[3]),
        ]

    for c in loads(0):
        c.start()
    weights = [
        pltpu.make_async_copy(src, dst, w_sem.at[n]) for n, (src, dst) in enumerate(((wd_in, wd), (wg_in, wg), (wu_in, wu)))
    ]
    for c in weights:
        c.start()
    bar = pltpu.get_barrier_semaphore()

    def sig(d, c):
        pl.semaphore_signal(bar, inc=1, device_id=(d, c), device_id_type=MESH)

    sig(xn, core)
    sig(yn, core)
    sig(me, other)
    pl.when(z < 3)(lambda: sig(up, core))
    pl.when(z > 0)(lambda: sig(dn, core))
    pl.semaphore_wait(bar, 3 + (z < 3).astype(jnp.int32) + (z > 0).astype(jnp.int32))

    for q in range(2):
        ry[q, hid:] = sdn[...]
        rd[q, hid:] = sgu[...]
    sg_sum[...] = jnp.zeros_like(sg_sum)

    def y_(j, b, half, zp):
        return rc(own.at[b, half], yr.at[zp, j], ys.at[zp, j], yrs.at[zp, j], yn, core)

    def x_(j, b, half, zp):
        return rc(own.at[b, half], xr.at[zp, j], xs.at[zp, j], xrs.at[zp, j], xn, core)

    def zc(zp, dev, d):
        b = zp * 4 + y * 2 + x
        return rc(own.at[b], zr.at[d, zp], zs.at[zp], zrs.at[d, zp], dev, core)

    def sib_send(i):
        return rc(sib, sibr, cs, cr, me, other)

    def outs(i):
        at = pl.ds(pl.multiple_of(i * 256, 256), 256)
        return [
            pltpu.make_async_copy(rr, r_out.at[at], out_sem.at[0]),
            pltpu.make_async_copy(rg, rg_out.at[at], out_sem.at[1]),
            pltpu.make_async_copy(acts, act_out.at[at], out_sem.at[2]),
            pltpu.make_async_copy(das, da_out.at[at], out_sem.at[3]),
            pltpu.make_async_copy(dbs, db_out.at[at], out_sem.at[4]),
        ]

    def columns(step):
        def one(n, _):
            step(pl.ds(pl.multiple_of(n * cut, cut), cut))
            return 0

        lax.fori_loop(0, width // cut, one, 0)

    def first_part(i):
        for c in loads(i):
            c.wait()

        @pl.when(i > 0)
        def _():
            for c in outs(i - 1):
                c.wait()

        def pick_rows(n):
            for q in range(2):
                rr[q * hid : (q + 1) * hid, n] = mm(pk[q], xb[q, :, n]).astype(jnp.bfloat16)
                rg[q * hid : (q + 1) * hid, n] = mm(pk[q], gb[q, :, n]).astype(jnp.bfloat16)

        columns(pick_rows)
        for q in range(2):
            ab = nt(xb[q], sgu[...])
            act, d_a, d_b = gate_parts(ab[:, :hid], ab[:, hid:], nt(gb[q], sdn[...]))
            ly[q, :, :hid] = pt[q]
            ly[q, :, hid:] = act.astype(jnp.bfloat16)
            ld[q, :, :hid] = pt[q]
            ld[q, :, hid : 2 * hid] = d_a.astype(jnp.bfloat16)
            ld[q, :, 2 * hid :] = d_b.astype(jnp.bfloat16)

        def shared_grads(n):
            sg_sum[: 2 * hid, n] += tn(ld[0, :, hid:], xb[0, :, n]) + tn(ld[1, :, hid:], xb[1, :, n])
            sg_sum[2 * hid :, n] += tn(ly[0, :, hid:], gb[0, :, n]) + tn(ly[1, :, hid:], gb[1, :, n])

        columns(shared_grads)

        @pl.when(i < 7)
        def _():
            for c in loads(i + 1):
                c.start()

    def second_part(i):
        @pl.when(i == 0)
        def _():
            for c in weights:
                c.wait()

        logits = mm(rr[...], wr[...])
        lane = lax.broadcasted_iota(jnp.int32, logits.shape, 1)
        logits = jnp.where((lane >= ROPE) & (lane < ROPE + 16), logits, -jnp.inf)
        e = jnp.exp(logits - jnp.max(logits, axis=1, keepdims=True))
        gate = jnp.sum(jnp.where(lane == ROPE + me, e, 0.0), axis=1, keepdims=True) / jnp.sum(
            e, axis=1, keepdims=True
        )
        pre = nt(rg[...], wd[...])
        act, d_a, d_b = gate_parts(nt(rr[...], wg[...]), nt(rr[...], wu[...]), gate * pre)
        low = act.astype(jnp.bfloat16)
        back = low.astype(jnp.float32)
        d_gate = jnp.sum(back * pre, axis=1, keepdims=True)
        acts[...] = (gate * back).astype(jnp.bfloat16)
        das[...] = d_a.astype(jnp.bfloat16)
        dbs[...] = d_b.astype(jnp.bfloat16)

        def spread(n):
            o = (gate * mm(low, wd[:, n])).astype(jnp.bfloat16)
            s = (mm(das[...], wg[:, n]) + mm(dbs[...], wu[:, n])).astype(jnp.bfloat16)
            for q in range(2):
                ry[q, :hid, n] = o[q * hid : (q + 1) * hid]
                rd[q, :hid, n] = s[q * hid : (q + 1) * hid]

        columns(spread)
        for c in outs(i):
            c.start()
        dgs[...] = jnp.where(lane == ROPE + me, d_gate, 0.0).astype(jnp.bfloat16)

    def third_part(i):
        k, half = i // 2, i % 2
        b = plane_at(z, 3 - k) * 4 + jnp.where(half == 0, 1 - y, y) * 2

        @pl.when(i > 0)
        def _():
            sib_send(i - 1).wait_send()

        def store(q, n, v):
            v = v.astype(jnp.bfloat16)
            mine = jnp.where(core == 0, v[:128], v[128:])
            theirs = jnp.where(core == 0, v[128:], v[:128])
            own[b + q, 0, :, n] = mine[:64]
            own[b + q, 1, :, n] = mine[64:]
            sib[q, 0, :, n] = theirs[:64]
            sib[q, 1, :, n] = theirs[64:]

        def put(m, _):
            n = pl.ds(pl.multiple_of(m * cut, cut), cut)
            n2 = pl.ds(pl.multiple_of(width + m * cut, cut), cut)
            for q in range(2):
                store(q, n, mm(ly[q], ry[q, :, n]))
                store(q, n2, mm(ld[q], rd[q, :, n]))
            return 0

        lax.fori_loop(0, width // cut, put, 0)
        for q in range(2):
            store(q, pl.ds(2 * width, 128), mm(pt_of(q), dgs[q * hid : (q + 1) * hid]))

        @pl.when(i > 0)
        def _():
            pl.semaphore_wait(free, 1)

        sib_send(i).start()

    def pt_of(q):
        return ly[q, :, :hid]

    def staged(src, dst, sem):
        return pltpu.make_async_copy(src, dst, sem)

    def blk(zp, yy, xx):
        return zp * 4 + yy * 2 + xx

    def pair_sum(i):
        k, half = i // 2, i % 2
        zp = plane_at(z, 3 - k)
        b = zp * 4 + jnp.where(half == 0, 1 - y, y) * 2
        sib_send(i).wait_recv()

        def one(q, _):
            add_into(own.at[b + q, 0], sibr.at[q, 0])
            add_into(own.at[b + q, 1], sibr.at[q, 1])
            return 0

        lax.fori_loop(0, 2, one, 0)

        @pl.when(i < 7)
        def _():
            pl.semaphore_signal(free, inc=1, device_id=(me, other), device_id_type=MESH)

        @pl.when(half == 0)
        def _():
            y_(0, blk(zp, 1 - y, 1 - x), 0, zp).start()
            x_(0, blk(zp, 1 - y, 1 - x), 1, zp).start()
            y_(1, blk(zp, 1 - y, x), 0, zp).start()

        @pl.when(half == 1)
        def _():
            x_(1, blk(zp, y, 1 - x), 1, zp).start()

    def second_staging(k):
        zp = plane_at(z, 3 - k)
        return [
            staged(yr.at[zp, 0], stage.at[0, 0], st_sem.at[0]),
            staged(xr.at[zp, 0], stage.at[0, 1], st_sem.at[1]),
            staged(yr.at[zp, 1], stage.at[1, 0], st_sem.at[2]),
            staged(xr.at[zp, 1], stage.at[1, 1], st_sem.at[3]),
        ]

    def second_fetch(k):
        zp = plane_at(z, 3 - k)
        c = second_staging(k)
        y_(0, blk(zp, 1 - y, 1 - x), 0, zp).wait_recv()
        c[0].start()
        x_(0, blk(zp, 1 - y, 1 - x), 1, zp).wait_recv()
        c[1].start()
        y_(1, blk(zp, 1 - y, x), 0, zp).wait_recv()
        c[2].start()
        x_(1, blk(zp, y, 1 - x), 1, zp).wait_recv()
        c[3].start()

    def second_hop(k):
        zp = plane_at(z, 3 - k)
        mine = blk(zp, y, x)
        c = second_staging(k)
        c[0].wait()
        add_into(own.at[blk(zp, y, 1 - x), 0], stage.at[0, 0])
        x_(2, blk(zp, y, 1 - x), 0, zp).start()
        c[1].wait()
        add_into(own.at[blk(zp, 1 - y, x), 1], stage.at[0, 1])
        y_(2, blk(zp, 1 - y, x), 1, zp).start()
        c[2].wait()
        add_into(own.at[mine, 0], stage.at[1, 0])
        c[3].wait()
        add_into(own.at[mine, 1], stage.at[1, 1])

    def last_staging(k):
        zp = plane_at(z, 3 - k)
        return [
            staged(xr.at[zp, 2], stage.at[0, 0], st_sem.at[0]),
            staged(yr.at[zp, 2], stage.at[0, 1], st_sem.at[1]),
            staged(zr.at[1, zp], stage.at[1], st_sem.at[2]),
            staged(zr.at[0, zp], stage.at[2], st_sem.at[3]),
        ]

    def last_fetch(k):
        zp = plane_at(z, 3 - k)
        c = last_staging(k)
        x_(2, blk(zp, y, 1 - x), 0, zp).wait_recv()
        c[0].start()
        y_(2, blk(zp, 1 - y, x), 1, zp).wait_recv()
        c[1].start()

        @pl.when((zp <= z) & (z < 3))
        def _():
            zc(zp, me, 1).wait_recv()
            c[2].start()

        @pl.when((zp >= z) & (z > 0))
        def _():
            zc(zp, me, 0).wait_recv()
            c[3].start()

    def last_hop(k):
        zp = plane_at(z, 3 - k)
        mine = blk(zp, y, x)
        c = last_staging(k)
        c[0].wait()
        add_into(own.at[mine, 0], stage.at[0, 0])
        c[1].wait()
        add_into(own.at[mine, 1], stage.at[0, 1])

        def arrived(d):
            c[3 - d].wait()
            add_into(own.at[mine, 0], stage.at[2 - d, 0])
            add_into(own.at[mine, 1], stage.at[2 - d, 1])

        pl.when((zp <= z) & (z < 3))(lambda: arrived(1))
        pl.when((zp >= z) & (z > 0))(lambda: arrived(0))
        pl.when(zp < z)(lambda: zc(zp, dn, 1).start())
        pl.when(zp > z)(lambda: zc(zp, up, 0).start())

    lag = jnp.where((z == 0) | (z == 3), 5, 7)

    def step(i, _):
        pl.when(i < 8)(lambda: first_part(i))
        pl.when((i >= 1) & (i <= 8))(lambda: pair_sum(i - 1))
        seconds = (i % 2 == 0) & (i >= 4) & (i <= 10)
        lasts = (i % 2 == 1) & (i >= lag) & (i <= lag + 6)
        pl.when(seconds)(lambda: second_fetch((i - 4) // 2))
        pl.when(lasts)(lambda: last_fetch((i - lag) // 2))
        pl.when(i < 8)(lambda: second_part(i))
        pl.when(seconds)(lambda: second_hop((i - 4) // 2))
        pl.when(lasts)(lambda: last_hop((i - lag) // 2))
        pl.when(i < 8)(lambda: third_part(i))
        return 0

    lax.fori_loop(0, 14, step, 0)

    def give(n):
        for part in range(3):
            kept = sg_sum[part * hid : part * hid + 96, n]
            sg_out[part * 96 : (part + 1) * 96, n] = kept.astype(jnp.bfloat16)

    columns(give)
    for a in range(2):

        def row(n, _):
            r = pl.ds(pl.multiple_of(n * 16, 16), 16)
            o_out[core, a, r] = own[me, a, r]
            return 0

        lax.fori_loop(0, 4, row, 0)
    f = rc(o_out.at[core], o_out.at[core], fs, fr, me, other)
    f.start()
    for c in outs(7):
        c.wait()
    sib_send(7).wait_send()
    for k in range(4):
        for j in range(3):
            x_(j, 0, 0, k).wait_send()
            y_(j, 0, 0, k).wait_send()

        @pl.when(k != z)
        def _():
            zc(k, up, 0).wait_send()

    rc(o_out.at[core], o_out.at[other], fs, fr, me, other).wait_recv()
    f.wait_send()


def moe_call(moe, grd, pick, pick_t, wg, wu, wd, wr, sgu, sdn, cid):
    ffe, width = wg.shape
    total = 2 * width + 128
    slots = pick.shape[0] * pick.shape[1]
    low, S, V = jnp.bfloat16, pltpu.SemaphoreType.DMA, pltpu.VMEM
    any_, vmem = pl.BlockSpec(memory_space=pl.ANY), pl.BlockSpec(memory_space=pltpu.VMEM)
    shape = lambda *s: jax.ShapeDtypeStruct(s, low)
    blk = (2, 64, total)
    return pl.pallas_call(
        moe_kernel,
        out_shape=[
            shape(2, *blk), shape(slots, width), shape(slots, width), shape(slots, ffe), shape(slots, ffe),
            shape(slots, ffe), shape(288, width),
            shape(4, 3, 64, total), shape(4, 3, 64, total), shape(2, 4, *blk),
        ],
        in_specs=[any_] * 7 + [vmem] * 3,
        out_specs=[vmem] + [any_] * 5 + [vmem] + [any_] * 3,
        scratch_shapes=[
            V((384, width), jnp.float32), V(wg.shape, low), V(wu.shape, low), V(wd.shape, low),
            V((16,) + blk, low), V((2,) + blk, low), V((2,) + blk, low), V((3,) + blk, low),
            V((2, 256, width), low), V((2, 256, width), low), V((2, 128, 256), low), V((2, 256, 128), low),
            V((256, width), low), V((256, width), low), V((2, 256, 256), low), V((2, 256, 384), low),
            V((2, 256, width), low), V((2, 384, width), low),
            V((256, ffe), low), V((256, ffe), low), V((256, ffe), low), V((256, 128), low),
            S((3,)), S((4,)), S((5,)), S((4,)), pltpu.SemaphoreType.REGULAR, S, S, S((4, 3)), S((4, 3)), S((4, 3)), S((4, 3)), S((4,)), S((2, 4)), S, S,
        ],
        compiler_params=pltpu.CompilerParams(collective_id=cid, has_side_effects=True, vmem_limit_bytes=60 << 20),
        cost_estimate=pl.CostEstimate(flops=65 * 10**9, bytes_accessed=80 * 10**6, transcendentals=0),
    )(moe, grd, pick, pick_t, wg, wu, wd, wr, sgu, sdn)


SLOTS = 5
KEYS = SLOTS * 256


def turned(v, cos, sin):
    n = v.shape[1]
    lane = lax.broadcasted_iota(jnp.int32, v.shape, 1) % 64
    swap = jnp.where(lane < 32, -pltpu.roll(v, n - 32, 1), pltpu.roll(v, 32, 1))
    return v * cos + swap * sin


def root(v):
    return lax.rsqrt(jnp.mean(v * v, axis=1, keepdims=True) + eps_norm)


def greet_all(me, core, bar):
    pl.semaphore_signal(bar, inc=1, device_id=(me, 1 - core), device_id_type=MESH)
    for j in range(1, 16):
        pl.semaphore_signal(bar, inc=1, device_id=((me + j) % 16, core), device_id_type=MESH)
    pl.semaphore_wait(bar, 16)


class Trade:
    def __init__(self, source, land, me, core, send_sem, recv_sem, own_sem):
        def copy(j, to, to_slot):
            return pltpu.make_async_remote_copy(
                src_ref=source(to), dst_ref=land.at[to_slot], send_sem=send_sem.at[j - 1], recv_sem=recv_sem.at[j - 1],
                device_id=(to, core), device_id_type=MESH,
            )

        self.out = [copy(j, (me + j) % 16, me) for j in range(1, 16)]
        self.back = [copy(j, (me + 16 - j) % 16, (me + 16 - j) % 16) for j in range(1, 16)]
        self.own = pltpu.make_async_copy(source(me), land.at[me], own_sem)

    def start(self):
        self.own.start()
        for c in self.out:
            c.start()

    def wait(self):
        self.own.wait()
        for c in self.back:
            c.wait_recv()
        for c in self.out:
            c.wait_send()


def read_gains(wlat):
    lane = lax.broadcasted_iota(jnp.int32, (16, 128), 1)
    row = lax.broadcasted_iota(jnp.int32, (16, 128), 0)
    rows = nt((lane == row + 80).astype(jnp.bfloat16), wlat[:, RANK:])
    return rows[0:1], rows[1:2]


def slab_copies(w4, w2, wq, wo, wkv, wlat, sem):
    pairs = [
        (w2.at[:, 2560:3200], wlat, sem.at[0]),
        (w2.at[:, 0:1536], wq, sem.at[1]),
        (w2.at[:, 1536:2560], wo, sem.at[2]),
    ]
    for c in range(4):
        pairs.append((w4.at[:, c, :, w4.shape[3] - 512 :], wkv.at[:, :, c * 512 : (c + 1) * 512], sem.at[3 + c]))
    return pairs


def att_fwd_kernel(
    tok, w4, w2, trade_in, g_lat, cos, sin, bias,
    middle, moe_low, normed, lat_raw, qcat, keys, kv_out, lse, att, trade_out,
    kv, wq, wo, wkv, wlat, part, arrived, w_sem, kv_sem, ks, kr, ts, tr, cs, cr, as_, ar, ao,
):
    me = lax.axis_index("dp")
    core = lax.axis_index("tensor")
    loads = [pltpu.make_async_copy(h, v, s) for h, v, s in slab_copies(w4, w2, wq, wo, wkv, wlat, w_sem)]
    for c in loads:
        c.start()
    bar = pltpu.get_barrier_semaphore()
    greet_all(me, core, bar)
    trade = Trade(lambda i: trade_in.at[i], trade_out, me, core, as_, ar, ao)
    t = tok[...].astype(jnp.float32)
    loads[0].wait()
    g_att, g_moe = read_gains(wlat)
    normed[...] = (t * root(t) * g_att).astype(jnp.bfloat16)
    lat = mm(normed[...], wlat[...])
    lat_raw[...] = lat
    first = lat[:, :RANK]
    rot = turned(lat[:, RANK:], cos[:, :128], sin[:, :128])
    rot = jnp.where(lax.broadcasted_iota(jnp.int32, rot.shape, 1) < 64, rot, 0.0)
    keys[SLOTS - 1, :, :RANK] = (first * root(first) * g_lat[...]).astype(jnp.bfloat16)
    keys[SLOTS - 1, :, RANK:] = (rot + pltpu.roll(rot, 64, 1)).astype(jnp.bfloat16)

    mine = pl.ds(pl.multiple_of(core * 128, 128), 128)

    def send(d):
        return pltpu.make_async_remote_copy(
            src_ref=keys.at[SLOTS - 1, mine], dst_ref=keys.at[SLOTS - 1 - d, mine], send_sem=ks.at[d - 1],
            recv_sem=kr.at[d - 1], device_id=(jnp.minimum(me + d, 15), core), device_id_type=MESH,
        )

    def hand(d):
        return pltpu.make_async_remote_copy(
            src_ref=keys.at[SLOTS - 1 - d, mine], dst_ref=keys.at[SLOTS - 1 - d, mine], send_sem=ts.at[d - 1],
            recv_sem=tr.at[d - 1], device_id=(me, 1 - core), device_id_type=MESH,
        )

    def handed(d):
        other = keys.at[SLOTS - 1 - d, pl.ds(pl.multiple_of((1 - core) * 128, 128), 128)]
        return pltpu.make_async_remote_copy(
            src_ref=other, dst_ref=other, send_sem=ts.at[d - 1], recv_sem=tr.at[d - 1],
            device_id=(me, 1 - core), device_id_type=MESH,
        )

    for d in range(1, SLOTS):
        pl.when(me + d < 16)(lambda d=d: send(d).start())

        @pl.when(me < d)
        def _():
            keys[SLOTS - 1 - d] = jnp.zeros((256, 640), jnp.bfloat16)

    trade.start()

    loads[1].wait()
    half = lax.broadcasted_iota(jnp.int32, (256, 128), 1) < 64
    q_nope = mm(normed[...], wq[:, :1024])
    q_rope = turned(mm(normed[...], wq[:, 1024:]), cos[...], sin[...])
    for h in range(8):
        qcat[h, :, :128] = q_nope[:, h * 128 : (h + 1) * 128].astype(jnp.bfloat16)
        pair = q_rope[:, h // 2 * 128 : (h // 2 + 1) * 128]
        qcat[h, :, 128:] = jnp.where(half == (h % 2 == 0), pair, 0.0).astype(jnp.bfloat16)
    for c in loads[3:]:
        c.wait()
    def project(s):
        kv[s * 256 : (s + 1) * 256] = mm(keys[s, :, :RANK], wkv[...].reshape(RANK, 2048)).astype(jnp.bfloat16)

    project(SLOTS - 1)
    for d in range(1, SLOTS + 1):
        if d < SLOTS:

            @pl.when(me >= d)
            def _(d=d):
                send(d).wait_recv()
                hand(d).start()

        if d > 1:
            pl.when(me >= d - 1)(lambda d=d: handed(d - 1).wait_recv())
            project(SLOTS - d)
    save = pltpu.make_async_copy(kv, kv_out, kv_sem)
    save.start()

    def head(h, _):
        kn = kv[:, pl.ds(pl.multiple_of(h * 256, 256), 128)]
        v = kv[:, pl.ds(pl.multiple_of(h * 256 + 128, 128), 128)]
        rope = keys[:, :, RANK:].reshape(KEYS, 128)
        s = nt(qcat[h], jnp.concatenate([kn, rope], 1)) * ((NOPE + ROPE) ** -0.5) + bias[...]
        top = jnp.max(s, axis=1, keepdims=True)
        e = jnp.exp(s - top)
        den = jnp.sum(e, axis=1, keepdims=True)
        lse[h] = top + jnp.log(den)
        p = (e * (1.0 / den)).astype(jnp.bfloat16)
        att[:, pl.ds(pl.multiple_of(h * 128, 128), 128)] = mm(p, v).astype(jnp.bfloat16)
        return 0

    lax.fori_loop(0, 8, head, 0)
    loads[2].wait()

    def out(n, _):
        r = pl.ds(pl.multiple_of(n * 512, 512), 512)
        part[:, r] = nt(att[...], wo[r]).astype(jnp.bfloat16)
        return 0

    lax.fori_loop(0, 4, out, 0)
    swap = pltpu.make_async_remote_copy(
        src_ref=part, dst_ref=arrived, send_sem=cs, recv_sem=cr, device_id=(me, 1 - core), device_id_type=MESH
    )
    swap.start()
    swap.wait()
    m = tok[...].astype(jnp.float32) + (part[...].astype(jnp.float32) + arrived[...].astype(jnp.float32))
    middle[...] = m
    moe_low[...] = (m * root(m) * g_moe).astype(jnp.bfloat16)
    save.wait()
    trade.wait()
    for d in range(1, SLOTS):
        pl.when(me + d < 16)(lambda d=d: send(d).wait_send())
        pl.when(me >= d)(lambda d=d: hand(d).wait_send())


def att_fwd(tok, weights, trade, g_lat, cos, sin, bias, cid):
    low, f32, S, V = jnp.bfloat16, jnp.float32, pltpu.SemaphoreType.DMA, pltpu.VMEM
    any_, vmem = pl.BlockSpec(memory_space=pl.ANY), pl.BlockSpec(memory_space=pltpu.VMEM)
    shape = lambda kind, *s: jax.ShapeDtypeStruct(s, kind)
    rows, width = tok.shape
    pack = weights.shape[1]
    return pl.pallas_call(
        att_fwd_kernel,
        out_shape=[
            shape(f32, rows, width), shape(low, rows, width), shape(low, rows, width), shape(f32, rows, 640),
            shape(low, 8, rows, 256), shape(low, SLOTS, rows, 640), shape(low, KEYS, 2048), shape(f32, 8, rows, 1),
            shape(low, rows, 1024), shape(low, *trade.shape),
        ],
        in_specs=[vmem, any_, any_, any_] + [vmem] * 4,
        out_specs=[vmem] * 6 + [any_] + [vmem] * 2 + [any_],
        scratch_shapes=[
            V((KEYS, 2048), low), V((width, 1536), low), V((width, 1024), low), V((16, 32, 2048), low), V((width, 640), low),
            V((rows, width), low), V((rows, width), low), S((7,)), S, S((4,)), S((4,)), S((4,)), S((4,)), S, S,
            S((15,)), S((15,)), S,
        ],
        compiler_params=pltpu.CompilerParams(collective_id=cid, has_side_effects=True, vmem_limit_bytes=60 << 20),
        cost_estimate=pl.CostEstimate(flops=10**10, bytes_accessed=40 * 10**6, transcendentals=0),
    )(tok, weights.reshape(16, 4, 32, pack), weights, trade, g_lat, cos, sin, bias)


def att_bwd_kernel(
    w4, w2, home_in, trade_in, grad, middle, moe_low, wr, g_lat, kv_in,
    tok_in, normed_in, lat_raw_in, qcat_in, keys_in, lse_in, att_in, cos_in, sin_in, bias_in,
    tok_grad, packed, p4, trade_out,
    home,
    tok, normed, lat_raw, qcat, keys, lse, att, cos, sin, bias,
    kv, wq, wo, wkv, wlat, dmid, dnorm, dmid_low, d_att, dq, dqr, dkr, dk_out, dk_pair, dk_in, own_dk, part, arrived, d_keys,
    home_sem, as_, ar, ao, late_sem, w_sem, kv_sem, ks, kr, cs, cr, ps, pr, hs, hr, o_sem,
):
    me = lax.axis_index("dp")
    core = lax.axis_index("tensor")
    width = grad.shape[1]
    scale = (NOPE + ROPE) ** -0.5
    loads = [pltpu.make_async_copy(h, v, s) for h, v, s in slab_copies(w4, w2, wq, wo, wkv, wlat, w_sem)]
    stores = [pltpu.make_async_copy(v, h, s) for h, v, s in slab_copies(p4, packed, wq, wo, wkv, wlat, o_sem)]
    kv_load = pltpu.make_async_copy(kv_in, kv, kv_sem)
    late = [
        pltpu.make_async_copy(src, dst, late_sem.at[n])
        for n, (src, dst) in enumerate(
            (
                (att_in, att), (qcat_in, qcat), (keys_in, keys), (bias_in, bias), (lse_in, lse), (cos_in, cos),
                (sin_in, sin), (normed_in, normed), (lat_raw_in, lat_raw), (tok_in, tok),
            )
        )
    ]
    home_load = pltpu.make_async_copy(home_in.at[:, width:], home, home_sem)
    home_load.start()
    loads[0].start()
    loads[2].start()
    kv_load.start()
    for c in late:
        c.start()
    for n in (1, 3, 4, 5, 6):
        loads[n].start()
    bar = pltpu.get_barrier_semaphore()
    greet_all(me, core, bar)
    trade = Trade(
        lambda i: trade_in.at[:, pl.ds(pl.multiple_of(i * 128, 128), 128)], trade_out, me, core, as_, ar, ao
    )
    trade.start()
    loads[0].wait()
    g_att, g_moe = read_gains(wlat)
    home_load.wait()
    lane = lax.broadcasted_iota(jnp.int32, (256, 128), 1)

    routed = (lane >= ROPE) & (lane < ROPE + 16)
    logits = jnp.where(routed, mm(moe_low[...], wr[...]), -jnp.inf)
    e = jnp.exp(logits - jnp.max(logits, axis=1, keepdims=True))
    router = e / jnp.sum(e, axis=1, keepdims=True)
    d_router = jnp.where(routed, home[:, width:].astype(jnp.float32), 0.0)
    d_logits = (router * (d_router - jnp.sum(router * d_router, axis=1, keepdims=True))).astype(jnp.bfloat16)

    def norm_back(v, gain, dy):
        r = root(v)
        hat = v * r
        up = dy * gain
        return r * (up - hat * jnp.mean(up * hat, axis=1, keepdims=True)), dy * hat

    def one_lane(n):
        return (lane == n).astype(jnp.bfloat16)

    d_moe = home[:, :width].astype(jnp.float32) + nt(d_logits, wr[...])
    d_norm2, gain_rows = norm_back(middle[...], g_moe, d_moe)
    d_middle = grad[...].astype(jnp.float32) + d_norm2
    dmid[...] = d_middle
    dmid_low[...] = d_middle.astype(jnp.bfloat16)
    gains = gain_rows.astype(jnp.bfloat16)
    small = tn(moe_low[...], d_logits) + tn(gains, one_lane(81))

    loads[2].wait()
    for c in late:
        c.wait()
    d_att[...] = mm(dmid_low[...], wo[...]).astype(jnp.bfloat16)

    def wo_rows(n, _):
        r = pl.ds(pl.multiple_of(n * 256, 256), 256)
        wo[r] = tn(dmid_low[:, r], att[...]).astype(jnp.bfloat16)
        return 0

    lax.fori_loop(0, width // 256, wo_rows, 0)
    stores[2].start()
    kv_load.wait()
    dkr[...] = jnp.zeros_like(dkr)
    dqr[...] = jnp.zeros_like(dqr)

    def head(h, _):
        cols = pl.ds(pl.multiple_of(h * 128, 128), 128)
        nope_at = pl.ds(pl.multiple_of(h * 256, 256), 128)
        value_at = pl.ds(pl.multiple_of(h * 256 + 128, 128), 128)
        pair = pl.ds(pl.multiple_of(h // 2 * 128, 128), 128)
        kc = jnp.concatenate([kv[:, nope_at], keys[:, :, RANK:].reshape(KEYS, 128)], 1)
        p = jnp.exp(nt(qcat[h], kc) * scale + bias[...] - lse[h])
        dv = tn(p.astype(jnp.bfloat16), d_att[:, cols])
        dp = nt(d_att[:, cols], kv[:, value_at])
        ds = (p * (dp - jnp.sum(p * dp, axis=1, keepdims=True))).astype(jnp.bfloat16)
        dqc = mm(ds, kc) * scale
        dkc = tn(ds, qcat[h]) * scale
        dq[:, cols] = dqc[:, :128].astype(jnp.bfloat16)
        dqr[:, pair] += jnp.where((lane < 64) == (h % 2 == 0), dqc[:, 128:], 0.0)
        kv[:, nope_at] = dkc[:, :128].astype(jnp.bfloat16)
        kv[:, value_at] = dv.astype(jnp.bfloat16)
        dkr[...] += dkc[:, 128:]
        return 0

    lax.fori_loop(0, 8, head, 0)
    for n in (3, 4, 5, 6):
        loads[n].wait()

    mine = pl.ds(pl.multiple_of(core * 128, 128), 128)
    others = pl.ds(pl.multiple_of((1 - core) * 128, 128), 128)

    def send(d, to):
        return pltpu.make_async_remote_copy(
            src_ref=dk_out.at[d - 1, mine], dst_ref=dk_in.at[d - 1], send_sem=ks.at[d - 1], recv_sem=kr.at[d - 1],
            device_id=(jnp.clip(to, 0, 15), core), device_id_type=MESH,
        )

    pair = pltpu.make_async_remote_copy(
        src_ref=dk_out.at[:, others], dst_ref=dk_pair, send_sem=ps, recv_sem=pr, device_id=(me, 1 - core), device_id_type=MESH
    )
    for s in range(SLOTS):
        r = slice(s * 256, (s + 1) * 256)
        d = SLOTS - 1 - s if s < SLOTS - 1 else SLOTS
        dk_out[d - 1, :, :RANK] = nt(kv[r], wkv[...].reshape(RANK, 2048)).astype(jnp.bfloat16)
        dk_out[d - 1, :, RANK:] = (dkr[r] + pltpu.roll(dkr[r], 64, 1)).astype(jnp.bfloat16)
    pair.start()
    dq[:, 1024:] = turned(dqr[...], cos[...], -sin[...]).astype(jnp.bfloat16)
    loads[1].wait()

    def normed_cols(n, _):
        r = pl.ds(pl.multiple_of(n * 512, 512), 512)
        v = nt(dq[...], wq[r])
        part[:, r] = v.astype(jnp.bfloat16)
        wq[r] = tn(normed[:, r], dq[...]).astype(jnp.bfloat16)
        return 0

    normed_cols(0, 0)
    pair.wait_recv()
    for d in range(1, SLOTS):
        dk_out[d - 1, mine] = dk_out[d - 1, mine] + dk_pair[d - 1]
        pl.when(me >= d)(lambda d=d: send(d, me - d).start())
    own_dk[...] = dk_out[SLOTS - 1, mine].astype(jnp.float32) + dk_pair[SLOTS - 1].astype(jnp.float32)
    lax.fori_loop(1, 4, normed_cols, 0)
    swap = pltpu.make_async_remote_copy(
        src_ref=part, dst_ref=arrived, send_sem=cs, recv_sem=cr, device_id=(me, 1 - core), device_id_type=MESH
    )
    swap.start()
    stores[1].start()
    latent_all = keys[:, :, :RANK].reshape(KEYS, RANK)
    for c in range(4):
        g = tn(latent_all, kv[:, c * 512 : (c + 1) * 512]).astype(jnp.bfloat16)
        wkv[:, :, c * 512 : (c + 1) * 512] = g.reshape(16, 32, 512)
        stores[3 + c].start()
    for d in range(1, SLOTS):

        @pl.when(me + d < 16)
        def _():
            send(d, me + d).wait_recv()
            own_dk[...] += dk_in[d - 1].astype(jnp.float32)

    d_keys[mine] = own_dk[...].astype(jnp.bfloat16)

    def half(rows):
        return pltpu.make_async_remote_copy(
            src_ref=d_keys.at[rows], dst_ref=d_keys.at[rows], send_sem=hs, recv_sem=hr,
            device_id=(me, 1 - core), device_id_type=MESH,
        )

    half(mine).start()
    swap.wait_recv()
    dnorm[...] = part[...].astype(jnp.float32) + arrived[...].astype(jnp.float32)
    half(others).wait_recv()

    d_first, lat_gain_rows = norm_back(lat_raw[:, :RANK], g_lat[...], d_keys[:, :RANK].astype(jnp.float32))
    d_second = turned(d_keys[:, RANK:].astype(jnp.float32), cos[:, :128], -sin[:, :128])
    d_second = jnp.where(lane < 64, d_second, 0.0)
    d_lat_low = jnp.concatenate([d_first, d_second], 1).astype(jnp.bfloat16)
    d_normed = dnorm[...] + nt(d_lat_low, wlat[...])
    d_norm1, att_gain_rows = norm_back(tok[...].astype(jnp.float32), g_att, d_normed)
    tok_grad[...] = dmid[...] + d_norm1
    small = small + tn(normed[...], d_lat_low[:, RANK:]) + tn(att_gain_rows.astype(jnp.bfloat16), one_lane(80))
    wlat[:, :RANK] = tn(normed[...], d_lat_low[:, :RANK]).astype(jnp.bfloat16)
    wlat[:, RANK:] = small.astype(jnp.bfloat16)
    lat_col = tn(lat_gain_rows.astype(jnp.bfloat16), one_lane(82))
    for b in range(16):
        r = slice(b * 128, b * 128 + 32)
        wlat[r, RANK:] = (small[r] + lat_col[b * 32 : (b + 1) * 32]).astype(jnp.bfloat16)
    stores[0].start()
    for c in stores:
        c.wait()
    trade.wait()
    for d in range(1, SLOTS):
        pl.when(me >= d)(lambda d=d: send(d, me - d).wait_send())
    pair.wait_send()
    swap.wait_send()
    half(mine).wait_send()


def att_bwd(
    weights, home, trade, grad, middle, moe_low, tok, normed, lat_raw, qcat, keys, kv, lse, att, wr, g_lat, cos, sin, bias, cid
):
    low, f32, S, V = jnp.bfloat16, jnp.float32, pltpu.SemaphoreType.DMA, pltpu.VMEM
    any_, vmem = pl.BlockSpec(memory_space=pl.ANY), pl.BlockSpec(memory_space=pltpu.VMEM)
    shape = lambda kind, *s: jax.ShapeDtypeStruct(s, kind)
    rows, width = tok.shape
    pack = weights.shape[1]
    return pl.pallas_call(
        att_bwd_kernel,
        out_shape=[shape(f32, rows, width), shape(low, width, pack - 512), shape(low, 16, 4, 32, 512), shape(low, 16, 288, 128)],
        in_specs=[any_] * 4 + [vmem] * 5 + [any_] * 11,
        out_specs=[vmem, any_, any_, any_],
        scratch_shapes=[
            V((rows, width + 128), low),
            V((rows, width), low), V((rows, width), low), V((rows, 640), f32), V((8, rows, 256), low), V((SLOTS, rows, 640), low),
            V((8, rows, 1), f32), V((rows, 1024), low), V((rows, 512), f32), V((rows, 512), f32), V((rows, KEYS), f32),
            V((KEYS, 2048), low), V((width, 1536), low), V((width, 1024), low), V((16, 32, 2048), low),
            V((width, 640), low), V((rows, width), f32), V((rows, width), f32), V((rows, width), low), V((rows, 1024), low),
            V((rows, 1536), low), V((rows, 512), f32), V((KEYS, 128), f32), V((SLOTS, rows, 640), low), V((SLOTS, rows // 2, 640), low),
            V((4, rows // 2, 640), low), V((rows // 2, 640), f32), V((rows, width), low), V((rows, width), low), V((rows, 640), low),
            S, S((15,)), S((15,)), S, S((10,)), S((7,)), S, S((4,)), S((4,)), S, S, S, S, S, S, S((7,)),
        ],
        compiler_params=pltpu.CompilerParams(collective_id=cid, has_side_effects=True, vmem_limit_bytes=60 << 20),
        cost_estimate=pl.CostEstimate(flops=25 * 10**9, bytes_accessed=70 * 10**6, transcendentals=0),
    )(
        weights.reshape(16, 4, 32, pack), weights, home, trade, grad, middle, moe_low, wr, g_lat, kv,
        tok, normed, lat_raw, qcat, keys, lse, att, cos, sin, bias,
    )


def my_half(v, rows):
    return lax.dynamic_slice_in_dim(v, lax.axis_index("tensor") * rows, rows, 0)


def row_halves(v):
    rows = v.shape[0] // 2
    return my_half(v, rows).reshape(2, rows // 2, v.shape[1])


def nope_first(w):
    heads = w.reshape(w.shape[0], -1, NOPE + ROPE)
    return jnp.concatenate(
        [heads[:, :, :NOPE].reshape(w.shape[0], -1), heads[:, :, NOPE:].reshape(w.shape[0], -1)], 1
    )


def heads_first(w):
    heads = w.shape[1] // (NOPE + ROPE)
    nope = w[:, : heads * NOPE].reshape(w.shape[0], heads, NOPE)
    rope = w[:, heads * NOPE :].reshape(w.shape[0], heads, ROPE)
    return jnp.concatenate([nope, rope], 2).reshape(w.shape[0], -1)


def shards_sixteen(
    tokens,
    out_grad,
    segments,
    routes,
    attn_gain,
    w_query,
    w_latent,
    latent_gain,
    w_keyval,
    w_out,
    moe_gain,
    w_router,
    shared_gate,
    shared_up,
    shared_down,
    expert_gate,
    routed_up_weight,
    expert_down,
):
    n_rows, width = tokens.shape
    dp_count = lax.axis_size("dp")
    dp_index = lax.axis_index("dp")
    seq_len = segments.shape[1]
    total = n_rows * dp_count
    hop_count = (WINDOW - 1) // n_rows + 1
    n_keys = (hop_count + 1) * n_rows
    experts = w_router.shape[1]
    capacity = 4 * n_rows * TOPK // (3 * experts)
    row_start = dp_index * n_rows
    seg_row = segments[0]
    depth = w_query.shape[0]
    q_width, o_width, kv_width = w_query.shape[1], w_out.shape[0], w_keyval.shape[1]
    kv_rows = w_keyval.shape[0]
    kv_cuts = depth // kv_rows
    kv_part = kv_width // kv_cuts
    lat_width = w_latent.shape[1]
    route_width = n_rows * TOPK // depth
    small = (lat_width + experts + 3 + route_width + 127) // 128 * 128

    gains = jnp.stack(
        [attn_gain, moe_gain, jnp.pad(latent_gain, (0, depth - kv_rows))], 1
    )
    packed = jnp.concatenate(
        [
            nope_first(w_query),
            w_out.T,
            w_latent,
            w_router,
            gains,
            routes.reshape(depth, route_width).astype(jnp.bfloat16),
            jnp.zeros((depth, small - lat_width - experts - 3 - route_width), jnp.bfloat16),
            w_keyval.reshape(kv_rows, kv_cuts, kv_part).transpose(1, 0, 2).reshape(depth, kv_part),
        ],
        1,
    )
    pack_width = packed.shape[1]
    weights, grad_all = ag16(
        [packed.reshape(2, depth // 2, pack_width), row_halves(out_grad)], (False, True), 1
    )
    weights = weights.reshape(width, pack_width)
    shared_part = shared_gate.shape[1] // dp_count
    shared_send = jnp.stack(
        [
            shared_gate.reshape(depth, dp_count, shared_part).transpose(1, 2, 0),
            shared_up.reshape(depth, dp_count, shared_part).transpose(1, 2, 0),
            shared_down.reshape(dp_count, shared_part, depth),
        ],
        1,
    )
    shared_send = jnp.pad(shared_send, ((0, 0), (0, 0), (0, 96 - shared_part), (0, 0)))
    moe_wr = weights[:, q_width + o_width + RANK : q_width + o_width + RANK + 128]
    at = ROPE + experts
    gain_latent = (
        moe_wr[:, at + 2].reshape(dp_count, depth)[:, :kv_rows].reshape(-1).astype(jnp.float32)
    )
    all_routes = moe_wr[:, at + 3 : at + 3 + route_width].reshape(total, TOPK).astype(jnp.int32)

    local_heads = q_width // (NOPE + ROPE)
    positions = (row_start + jnp.arange(n_rows, dtype=jnp.int32)).astype(jnp.float32)
    cos_tab, sin_tab = rope_tables(positions)
    cos_lanes, sin_lanes = jnp.tile(cos_tab, (1, 2 * local_heads)), jnp.tile(sin_tab, (1, 2 * local_heads))
    key_pos = row_start - hop_count * n_rows + jnp.arange(n_keys, dtype=jnp.int32)
    query_pos = row_start + jnp.arange(n_rows, dtype=jnp.int32)
    padded_seg = jnp.concatenate([jnp.full((hop_count * n_rows,), -1, jnp.int32), seg_row])
    key_seg = lax.dynamic_slice_in_dim(padded_seg, row_start, n_keys, 0)
    query_seg = lax.dynamic_slice_in_dim(seg_row, row_start, n_rows, 0)
    allowed = (key_pos[None, :] >= 0) & (key_pos[None, :] <= query_pos[:, None])
    allowed = (
        allowed
        & (query_pos[:, None] - key_pos[None, :] < WINDOW)
        & (query_seg[:, None] == key_seg[None, :])
    )

    bias = jnp.where(allowed, 0.0, -jnp.inf)
    middle, moe_low, normed_low, lat_raw, qcat, keys, kv, lse, attended_low, shared_all = att_fwd(
        tokens, weights, shared_send.reshape(dp_count, 3 * 96, depth), gain_latent[None], cos_lanes, sin_lanes, bias, 7
    )
    shared_all = shared_all.reshape(dp_count, 3, 96, depth)[:, :, :shared_part].transpose(1, 2, 0, 3)
    lead = jnp.pad(shared_all.reshape(3, shared_part, width), ((0, 0), (0, 128 - shared_part), (0, 0)))
    shared_in, shared_out = lead[:2].reshape(256, width), lead[2]
    (moe_all,) = ag16([row_halves(moe_low)], (True,), 3)
    chosen = jnp.any(all_routes == dp_index, axis=1).reshape(dp_count, n_rows)
    earlier = jnp.arange(n_rows)[:, None] < jnp.arange(n_rows)[None, :]
    rank = matmul(chosen.astype(jnp.bfloat16), earlier.astype(jnp.bfloat16)).astype(jnp.int32)
    pick = (
        (rank[:, None, :] == jnp.arange(capacity, dtype=jnp.int32)[None, :, None])
        & chosen[:, None, :]
    ).astype(jnp.bfloat16)

    slot_rows = dp_count * capacity
    home, rows_in, rows_grad, scaled_act, d_ea_low, d_eb_low, shared_grads = moe_call(
        moe_all.reshape(dp_count, n_rows, width),
        grad_all.reshape(dp_count, n_rows, width),
        pick,
        pick.transpose(0, 2, 1),
        expert_gate[0].T,
        routed_up_weight[0].T,
        expert_down[0],
        moe_wr,
        shared_in,
        shared_out,
        4,
    )[:7]
    home = home.reshape(n_rows, 2 * width + 128)
    result = (middle + home[:, :width].astype(jnp.float32)).astype(jnp.bfloat16)
    grad_down = matmul_tn(scaled_act, rows_grad)[None]
    grad_gate = matmul_tn(rows_in, d_ea_low)[None]
    grad_up = matmul_tn(rows_in, d_eb_low)[None]
    token_input_gradient, packed_grads, kv_grads, shared_home = att_bwd(
        weights, home, shared_grads, out_grad, middle, moe_low, tokens, normed_low, lat_raw, qcat, keys, kv, lse,
        attended_low, moe_wr, gain_latent[None], cos_lanes, sin_lanes, bias, 8
    )
    mine = rs16(
        packed_grads.reshape(dp_count, 2, depth // 2, pack_width - kv_part),
        kv_grads.reshape(dp_count, 2, depth // 2, kv_part),
        6,
    ).reshape(depth, pack_width)
    shared_home = shared_home.reshape(dp_count, 3, 96, depth)[:, :, :shared_part].astype(jnp.float32)
    grad_sgate = shared_home[:, 0].transpose(2, 0, 1).reshape(depth, -1)
    grad_sup = shared_home[:, 1].transpose(2, 0, 1).reshape(depth, -1)
    grad_sdown = shared_home[:, 2].reshape(-1, depth)
    out_wq = heads_first(mine[:, :q_width])
    at = q_width
    out_wo = mine[:, at : at + o_width].T
    at += o_width
    out_wlat = mine[:, at : at + lat_width]
    at += lat_width
    out_router = mine[:, at : at + experts]
    at += experts
    out_wkv = (
        mine[:, pack_width - kv_part :]
        .reshape(kv_cuts, kv_rows, kv_part)
        .transpose(1, 0, 2)
        .reshape(kv_rows, kv_width)
    )
    return (
        result,
        token_input_gradient,
        mine[:, at],
        out_wq,
        out_wlat,
        mine[:kv_rows, at + 2],
        out_wkv,
        out_wo,
        mine[:, at + 1],
        out_router,
        grad_sgate,
        grad_sup,
        grad_sdown,
        grad_gate,
        grad_up,
        grad_down,
    )


def shards_general(
    tokens,
    out_grad,
    segments,
    routes,
    attn_gain,
    w_query,
    w_latent,
    latent_gain,
    w_keyval,
    w_out,
    moe_gain,
    w_router,
    shared_gate,
    shared_up,
    shared_down,
    expert_gate,
    routed_up_weight,
    expert_down,
):
    n_rows = tokens.shape[0]
    model_width = tokens.shape[1]
    dp_count = lax.axis_size("dp")
    dp_index = lax.axis_index("dp")
    seq_len = segments.shape[1]
    seq_devs = seq_len // n_rows
    hop_count = (WINDOW - 1) // n_rows + 1
    n_keys = (hop_count + 1) * n_rows
    experts = w_router.shape[1]
    local_experts = expert_gate.shape[0]
    capacity = 4 * n_rows * TOPK // (3 * experts)
    slot_total = experts * capacity
    score_scale = (NOPE + ROPE) ** (-0.5)
    row_start = dp_index % seq_devs * n_rows
    seg_row = lax.dynamic_index_in_dim(segments, dp_index // seq_devs, 0, keepdims=False)
    gathered = (
        lax.all_gather(attn_gain, "dp", axis=0, tiled=True),
        lax.all_gather(w_query, "dp", axis=0, tiled=True),
        lax.all_gather(w_latent, "dp", axis=0, tiled=True),
        lax.all_gather(latent_gain, "dp", axis=0, tiled=True),
        lax.all_gather(w_keyval, "dp", axis=0, tiled=True),
        lax.all_gather(w_out, "dp", axis=1, tiled=True),
        lax.all_gather(moe_gain, "dp", axis=0, tiled=True),
        lax.all_gather(w_router, "dp", axis=0, tiled=True),
        lax.all_gather(shared_gate, "dp", axis=0, tiled=True),
        lax.all_gather(shared_up, "dp", axis=0, tiled=True),
        lax.all_gather(shared_down, "dp", axis=1, tiled=True),
    )
    (
        gain_attn,
        wq_full,
        wlat_full,
        gain_latent,
        wkv_full,
        wo_full,
        gain_moe,
        wr_full,
        sgate_full,
        sup_full,
        sdown_full,
    ) = gathered
    local_heads = wq_full.shape[1] // (NOPE + ROPE)
    positions = (row_start + jnp.arange(n_rows, dtype=jnp.int32)).astype(jnp.float32)
    cos_tab, sin_tab = rope_tables(positions)
    resid_in = tokens.astype(jnp.float32)
    normed, attn_norm_back = jax.vjp(rms_scale, resid_in, gain_attn.astype(jnp.float32))
    normed_low = normed.astype(jnp.bfloat16)

    def rope_queries(q_flat):
        shaped = q_flat.reshape(n_rows, local_heads, NOPE + ROPE)
        return jnp.concatenate(
            [shaped[..., :NOPE], rotate(shaped[..., NOPE:], cos_tab[:, None], sin_tab[:, None])], -1
        )

    queries, query_back = jax.vjp(rope_queries, matmul(normed_low, wq_full))
    query_low = queries.astype(jnp.bfloat16)

    def latent_piece(latent_raw, gain_vec):
        return (
            rms_scale(latent_raw[:, :RANK], gain_vec),
            rotate(latent_raw[:, RANK:], cos_tab, sin_tab),
        )

    (latent, key_rope), latent_back = jax.vjp(
        latent_piece, matmul(normed_low, wlat_full), gain_latent.astype(jnp.float32)
    )
    latent_low = latent.astype(jnp.bfloat16)
    rope_low = key_rope.astype(jnp.bfloat16)
    latent_parts = []
    rope_parts = []
    for distance in range(hop_count, 0, -1):
        moved_latent, moved_rope = passed_along((latent_low, rope_low), "dp", distance)
        latent_parts.append(moved_latent)
        rope_parts.append(moved_rope)
    keys_latent = jnp.concatenate(latent_parts + [latent_low], 0)
    keys_rope = jnp.concatenate(rope_parts + [rope_low], 0)
    keyval = (
        matmul(keys_latent, wkv_full).astype(jnp.bfloat16).reshape(n_keys, local_heads, NOPE + VDIM)
    )
    key_nope = keyval[..., :NOPE]
    values = keyval[..., NOPE:]
    key_pos = row_start - hop_count * n_rows + jnp.arange(n_keys, dtype=jnp.int32)
    query_pos = row_start + jnp.arange(n_rows, dtype=jnp.int32)
    padded_seg = jnp.concatenate([jnp.full((hop_count * n_rows,), -1, jnp.int32), seg_row])
    key_seg = lax.dynamic_slice_in_dim(padded_seg, row_start, n_keys, 0)
    query_seg = lax.dynamic_slice_in_dim(seg_row, row_start, n_rows, 0)
    allowed = (key_pos[None, :] >= 0) & (key_pos[None, :] <= query_pos[:, None])
    allowed = (
        allowed
        & (query_pos[:, None] - key_pos[None, :] < WINDOW)
        & (query_seg[:, None] == key_seg[None, :])
    )

    def masked_scores():
        nope_part = jnp.einsum(
            "qhd,khd->hqk", query_low[..., :NOPE], key_nope, preferred_element_type=jnp.float32
        )
        rope_part = jnp.einsum(
            "qhr,kr->hqk", query_low[..., NOPE:], keys_rope, preferred_element_type=jnp.float32
        )
        return jnp.where(allowed[None], score_scale * (nope_part + rope_part), -jnp.inf)

    scores = masked_scores()
    top_score = jnp.max(scores, axis=-1, keepdims=True)
    exp_scores = jnp.exp(scores - top_score)
    denom = jnp.sum(exp_scores, axis=-1, keepdims=True)
    attn_probs = exp_scores / denom
    log_total = top_score + jnp.log(denom)
    attended = jnp.einsum(
        "hqk,khv->qhv", attn_probs.astype(jnp.bfloat16), values, preferred_element_type=jnp.float32
    )
    attended_low = attended.astype(jnp.bfloat16).reshape(n_rows, local_heads * VDIM)
    attn_out = lax.psum(matmul(attended_low, wo_full).astype(jnp.bfloat16), "tensor").astype(
        jnp.float32
    )
    middle = resid_in + attn_out
    moe_normed, moe_norm_back = jax.vjp(rms_scale, middle, gain_moe.astype(jnp.float32))
    moe_low = moe_normed.astype(jnp.bfloat16)
    router, router_back = jax.vjp(
        lambda logit_vals: jax.nn.softmax(logit_vals, axis=-1), matmul(moe_low, wr_full)
    )
    expert_ids = jnp.arange(experts, dtype=jnp.int32)
    route_hot = (routes[:, :, None] == expert_ids[None, None, :]).astype(jnp.float32)
    gate_w = jnp.einsum("te,tke->tk", router, route_hot, precision=highest)
    flat_routes = routes.reshape(-1)
    assign_count = flat_routes.shape[0]
    flat_hot = (flat_routes[:, None] == expert_ids[None, :]).astype(jnp.int32)
    earlier = ranks_before(flat_hot)
    slot_in = jnp.sum(earlier * flat_hot, axis=1)
    target = flat_routes * capacity + slot_in
    assign_ids = jnp.arange(assign_count, dtype=jnp.int32)
    assign_of_slot = jnp.zeros((slot_total,), jnp.int32).at[target].set(assign_ids)
    slot_live = (
        jnp.zeros((slot_total,), jnp.bfloat16)
        .at[target]
        .set(jnp.ones((assign_count,), jnp.bfloat16))
    )
    send_rows = moe_low[assign_of_slot // TOPK] * slot_live[:, None]
    recv_rows = lax.all_to_all(
        send_rows.reshape(dp_count, local_experts * capacity, model_width),
        "dp",
        split_axis=0,
        concat_axis=0,
        tiled=True,
    )
    received_four_parts = recv_rows.reshape(dp_count, local_experts, capacity, model_width)
    exp_gate = jnp.einsum(
        "sjcd,jdf->sjcf", received_four_parts, expert_gate, preferred_element_type=jnp.float32
    )
    exp_up = jnp.einsum(
        "sjcd,jdf->sjcf", received_four_parts, routed_up_weight, preferred_element_type=jnp.float32
    )
    exp_act, exp_act_back = jax.vjp(gated_act, exp_gate, exp_up)
    exp_act_low = exp_act.astype(jnp.bfloat16)
    exp_result = jnp.einsum(
        "sjcf,jfd->sjcd", exp_act_low, expert_down, preferred_element_type=jnp.float32
    )
    returned = lax.all_to_all(
        exp_result.reshape(dp_count, local_experts * capacity, model_width).astype(jnp.bfloat16),
        "dp",
        split_axis=0,
        concat_axis=0,
        tiled=True,
    ).astype(jnp.float32)
    per_assign = returned.reshape(slot_total, model_width)[target].reshape(
        n_rows, TOPK, model_width
    )
    routed = jnp.einsum("tk,tkd->td", gate_w, per_assign, precision=highest)
    shared_a = matmul(moe_low, sgate_full)
    shared_b = matmul(moe_low, sup_full)
    shared_act, shared_back = jax.vjp(gated_act, shared_a, shared_b)
    shared_low = shared_act.astype(jnp.bfloat16)
    moe_out = lax.psum(
        (routed + matmul(shared_low, sdown_full)).astype(jnp.bfloat16), "tensor"
    ).astype(jnp.float32)
    result = (middle + moe_out).astype(jnp.bfloat16)
    grad_y = out_grad.astype(jnp.float32)
    grad_sdown = matmul_tn(shared_low, out_grad)
    d_shared_a, d_shared_b = shared_back(matmul_nt(out_grad, sdown_full))
    d_sa_low = d_shared_a.astype(jnp.bfloat16)
    d_sb_low = d_shared_b.astype(jnp.bfloat16)
    grad_sgate = matmul_tn(moe_low, d_sa_low)
    grad_sup = matmul_tn(moe_low, d_sb_low)
    d_moe = matmul_nt(d_sa_low, sgate_full) + matmul_nt(d_sb_low, sup_full)
    d_gate_part = jnp.einsum("td,tkd->tk", grad_y, per_assign, precision=highest)
    d_assign = (
        (gate_w[:, :, None] * grad_y[:, None, :])
        .astype(jnp.bfloat16)
        .reshape(assign_count, model_width)
    )
    send_grads = d_assign[assign_of_slot] * slot_live[:, None]
    recv_grads = lax.all_to_all(
        send_grads.reshape(dp_count, local_experts * capacity, model_width),
        "dp",
        split_axis=0,
        concat_axis=0,
        tiled=True,
    )
    recv_grads = recv_grads.reshape(dp_count, local_experts, capacity, model_width)
    expert_down_weight_gradient = jnp.einsum(
        "sjcf,sjcd->jfd", exp_act_low, recv_grads, preferred_element_type=jnp.float32
    )
    d_exp_act = jnp.einsum(
        "sjcd,jfd->sjcf", recv_grads, expert_down, preferred_element_type=jnp.float32
    )
    d_exp_gate, expert_up_act_gradient = exp_act_back(d_exp_act)
    d_egate_low = d_exp_gate.astype(jnp.bfloat16)
    expert_up_gradient_lowp = expert_up_act_gradient.astype(jnp.bfloat16)
    expert_gate_weight_gradient = jnp.einsum(
        "bmky,bmkx->myx", received_four_parts, d_egate_low, preferred_element_type=jnp.float32
    )
    expert_up_weight_gradient = jnp.einsum(
        "bmky,bmkx->myx",
        received_four_parts,
        expert_up_gradient_lowp,
        preferred_element_type=jnp.float32,
    )
    d_slots = jnp.einsum(
        "hteg,tmg->htem", d_egate_low, expert_gate, preferred_element_type=jnp.float32
    )
    d_slots = d_slots + jnp.einsum(
        "hteg,tmg->htem",
        expert_up_gradient_lowp,
        routed_up_weight,
        preferred_element_type=jnp.float32,
    )
    back_grads = lax.all_to_all(
        d_slots.reshape(dp_count, local_experts * capacity, model_width).astype(jnp.bfloat16),
        "dp",
        split_axis=0,
        concat_axis=0,
        tiled=True,
    ).astype(jnp.float32)
    d_moe = d_moe + jnp.sum(
        back_grads.reshape(slot_total, model_width)[target].reshape(n_rows, TOPK, model_width),
        axis=1,
    )
    d_moe, d_gate = (
        lax.psum(d_moe.astype(jnp.bfloat16), "tensor").astype(jnp.float32),
        lax.psum(d_gate_part.astype(jnp.bfloat16), "tensor").astype(jnp.float32),
    )
    d_router = jnp.einsum("tk,tke->te", d_gate, route_hot, precision=highest)
    (d_logits,) = router_back(d_router)
    d_logits_low = d_logits.astype(jnp.bfloat16)
    grad_router = matmul_tn(moe_low, d_logits_low)
    d_moe = d_moe + matmul_nt(d_logits_low, wr_full)
    d_mid_norm, grad_gain_moe = moe_norm_back(d_moe)
    d_middle = grad_y + d_mid_norm
    d_middle_low = d_middle.astype(jnp.bfloat16)
    grad_wout = matmul_tn(attended_low, d_middle_low)
    d_att_low = (
        matmul_nt(d_middle_low, wo_full).astype(jnp.bfloat16).reshape(n_rows, local_heads, VDIM)
    )
    again_probs = jnp.exp(masked_scores() - log_total)
    d_values = jnp.einsum(
        "hqk,qhv->khv",
        again_probs.astype(jnp.bfloat16),
        d_att_low,
        preferred_element_type=jnp.float32,
    )
    d_probs = jnp.einsum("qhv,khv->hqk", d_att_low, values, preferred_element_type=jnp.float32)
    d_scores = (
        again_probs * (d_probs - jnp.sum(d_probs * again_probs, axis=-1, keepdims=True))
    ).astype(jnp.bfloat16)
    d_query_nope = score_scale * jnp.einsum(
        "hqk,khd->qhd", d_scores, key_nope, preferred_element_type=jnp.float32
    )
    d_query_rope = score_scale * jnp.einsum(
        "hqk,kr->qhr", d_scores, keys_rope, preferred_element_type=jnp.float32
    )
    d_key_nope = score_scale * jnp.einsum(
        "hqk,qhd->khd", d_scores, query_low[..., :NOPE], preferred_element_type=jnp.float32
    )
    d_key_rope = score_scale * jnp.einsum(
        "hqk,qhr->kr", d_scores, query_low[..., NOPE:], preferred_element_type=jnp.float32
    )
    (d_q_raw,) = query_back(jnp.concatenate([d_query_nope, d_query_rope], -1))
    d_q_low = d_q_raw.astype(jnp.bfloat16)
    grad_wq = matmul_tn(normed_low, d_q_low)
    d_normed = matmul_nt(d_q_low, wq_full)
    d_kv_low = (
        jnp.concatenate([d_key_nope, d_values], -1)
        .astype(jnp.bfloat16)
        .reshape(n_keys, local_heads * (NOPE + VDIM))
    )
    grad_wkv = matmul_tn(keys_latent, d_kv_low)
    d_keys_latent = matmul_nt(d_kv_low, wkv_full)
    own_latent = d_keys_latent[hop_count * n_rows :]
    own_rope = d_key_rope[hop_count * n_rows :]
    for distance in range(hop_count, 0, -1):
        block_index = hop_count - distance
        lower = block_index * n_rows
        home_latent, home_rope = (
            passed_along(
                d_keys_latent[lower : lower + n_rows].astype(jnp.bfloat16), "dp", -distance
            ).astype(jnp.float32),
            passed_along(
                d_key_rope[lower : lower + n_rows].astype(jnp.bfloat16), "dp", -distance
            ).astype(jnp.float32),
        )
        own_latent = own_latent + home_latent
        own_rope = own_rope + home_rope
    d_normed, own_latent, own_rope = (
        lax.psum(d_normed.astype(jnp.bfloat16), "tensor").astype(jnp.float32),
        lax.psum(own_latent.astype(jnp.bfloat16), "tensor").astype(jnp.float32),
        lax.psum(own_rope.astype(jnp.bfloat16), "tensor").astype(jnp.float32),
    )
    d_latent_raw, grad_gain_latent = latent_back((own_latent, own_rope))
    d_latent_low = d_latent_raw.astype(jnp.bfloat16)
    grad_wlat = matmul_tn(normed_low, d_latent_low)
    d_normed = d_normed + matmul_nt(d_latent_low, wlat_full)
    d_tokens_norm, grad_gain_attn = attn_norm_back(d_normed)
    token_input_gradient = d_middle + d_tokens_norm
    reduced_result = tuple(
        (
            lax.psum_scatter(grad_gain_attn, "dp", scatter_dimension=0, tiled=True),
            lax.psum_scatter(grad_wq, "dp", scatter_dimension=0, tiled=True),
            lax.psum_scatter(grad_wlat, "dp", scatter_dimension=0, tiled=True),
            lax.psum_scatter(grad_gain_latent, "dp", scatter_dimension=0, tiled=True),
            lax.psum_scatter(grad_wkv, "dp", scatter_dimension=0, tiled=True),
            lax.psum_scatter(grad_wout, "dp", scatter_dimension=1, tiled=True),
            lax.psum_scatter(grad_gain_moe, "dp", scatter_dimension=0, tiled=True),
            lax.psum_scatter(grad_router, "dp", scatter_dimension=0, tiled=True),
            lax.psum_scatter(grad_sgate, "dp", scatter_dimension=0, tiled=True),
            lax.psum_scatter(grad_sup, "dp", scatter_dimension=0, tiled=True),
            lax.psum_scatter(grad_sdown, "dp", scatter_dimension=1, tiled=True),
        )
    )
    return (
        (result, token_input_gradient)
        + reduced_result
        + (expert_gate_weight_gradient, expert_up_weight_gradient, expert_down_weight_gradient)
    )


def solution(mesh):
    placed = (
        P("dp", None),
        P("dp", None),
        P(),
        P("dp", None),
        P("dp"),
        P("dp", "tensor"),
        P("dp", None),
        P("dp"),
        P("dp", "tensor"),
        P("tensor", "dp"),
        P("dp"),
        P("dp", None),
        P("dp", "tensor"),
        P("dp", "tensor"),
        P("tensor", "dp"),
        P("dp", None, "tensor"),
        P("dp", None, "tensor"),
        P("dp", "tensor", None),
    )
    sixteen = mesh.shape["dp"] == 16 and mesh.shape["tensor"] == 2

    def body(*args):
        fits_sixteen = sixteen and args[2].shape[0] == 1 and args[15].shape[0] == 1 and args[0].shape[0] == 256
        return (shards_sixteen if fits_sixteen else shards_general)(*args)

    return jax.shard_map(
        body,
        mesh=mesh,
        in_specs=placed,
        out_specs=(
            P("dp", None),
            P("dp", None),
            P("dp"),
            P("dp", "tensor"),
            P("dp", None),
            P("dp"),
            P("dp", "tensor"),
            P("tensor", "dp"),
            P("dp"),
            P("dp", None),
            P("dp", "tensor"),
            P("dp", "tensor"),
            P("tensor", "dp"),
            P("dp", None, "tensor"),
            P("dp", None, "tensor"),
            P("dp", "tensor", None),
        ),
        check_vma=False,
    )
```
